128 devices in a mesh: row: 16 (over y, z_hi, core), col: 8 (over z_lo, x).
Axes of the slice: x: 4, y: 4, z: 4 (z_hi: 2, z_lo: 2; z = z_hi * 2 + z_lo), core: 2. Of those that a mesh axis runs over, the one named last changes fastest.
Arguments:
- tokens: bfloat16 [32768, 1024], P(('row', 'col')), may hold values from -6 to 6
- grad_out: bfloat16 [32768, 1024], P(('row', 'col')), may hold values from -6 to 6
- target: int32 [32768], P(('row', 'col')), may hold values from 0 to 32767, as said below
- lengths: int32 [16, 8], P('row'), may hold values from 1 to 1024, 2048 in all within a row
- attn_gain: float32 [1024], replicated, may hold values from 0.1 to 1.9
- ffn_gain: float32 [1024], replicated, may hold values from 0.1 to 1.9
- q_gain: float32 [128], replicated, may hold values from 0.1 to 1.9
- k_gain: float32 [128], replicated, may hold values from 0.1 to 1.9
- w_query: bfloat16 [1024, 2048], P('row', 'col'), may hold values from -0.1875 to 0.1875
- key_matrix: bfloat16 [1024, 1024], P('row', 'col'), may hold values from -0.1875 to 0.1875
- value_matrix: bfloat16 [1024, 1024], P('row', 'col'), may hold values from -0.1875 to 0.1875
- w_out: bfloat16 [2048, 1024], P('col', 'row'), may hold values from -0.5 to 0.5
- w_gate: bfloat16 [1024, 3072], P('row', 'col'), may hold values from -0.1875 to 0.1875
- w_up: bfloat16 [1024, 3072], P('row', 'col'), may hold values from -0.1875 to 0.1875
- w_down: bfloat16 [3072, 1024], P('col', 'row'), may hold values from -0.109375 to 0.109375
Outputs:
- output: bfloat16 [32768, 1024], P(('row', 'col'))
- input_grad: bfloat16 [32768, 1024], P(('row', 'col'))
- grad_attn_gain: float32 [1024], replicated
- grad_ffn_gain: float32 [1024], replicated
- grad_q_gain: float32 [128], replicated
- grad_k_gain: float32 [128], replicated
- grad_w_query: float32 [1024, 2048], P('row', 'col')
- grad_w_key: float32 [1024, 1024], P('row', 'col')
- grad_w_value: float32 [1024, 1024], P('row', 'col')
- grad_w_out: float32 [2048, 1024], P('col', 'row')
- grad_w_gate: float32 [1024, 3072], P('row', 'col')
- grad_w_up: float32 [1024, 3072], P('row', 'col')
- grad_w_down: float32 [3072, 1024], P('col', 'row')
The draws below stay inside these ranges and needn't reach their ends.
Inputs may be any that keep to these rules, and one draw needn't show every extreme that they name: target is a permutation of 0 to 32767. Arrival position a lies on device a // 256 of row+col and slot s on device s // 256; these two devices have the same col index, and every device sends exactly 16 of its tokens to each row group. `lengths`: each row sums to 2048, and its largest entry is 1024.
All inputs are finite; a program needn't handle non-finite values.
Results may differ from the reference program's by a relative error of at most 0.024.
Values may be sent and summed in bfloat16 or wider, within the bound.
A program may use at most 192 MiB of HBM per device.

```python
import math
import jax
import jax.numpy as jnp
import numpy as np
from jax import lax

MODEL_WIDTH = 1024
FF = 3072
QUERY_HEADS = 16
VALUE_HEADS = 8
HEAD_SIZE = 128
LONGEST = 1024
GROUP_TOKENS = 2048
SEQS = 8
ROWS = 256
TOKENS = 32768
QBLOCK = 512
N_ROW = 16
N_COL = 8


def draw_target(key, part):
    key = jax.random.fold_in(key, 7)
    per_group = ROWS // N_ROW
    first_key, second_key = jax.random.split(key)
    devices_all = N_ROW * N_COL
    arrival = jax.vmap(lambda single: jax.random.permutation(single, ROWS))(jax.random.split(first_key, devices_all))
    arrival = arrival.reshape(N_ROW, N_COL, ROWS).astype(jnp.int32)
    target_group = arrival // per_group
    within = jnp.arange(N_ROW, dtype=jnp.int32)[:, None, None] * per_group + arrival % per_group
    layout = jax.vmap(lambda single: jax.random.permutation(single, ROWS))(jax.random.split(second_key, devices_all))
    layout = layout.reshape(N_ROW, N_COL, ROWS).astype(jnp.int32)
    column = jnp.broadcast_to(jnp.arange(N_COL, dtype=jnp.int32)[None, :, None], target_group.shape)
    local_slot = layout[target_group, column, within]
    slots = (target_group * N_COL + column) * ROWS + local_slot
    return slots.reshape(-1).astype(jnp.int32)


def steps_of(rng, shape, pieces, low, largest):
    def one(axis_at, parts):
        heights = jax.random.uniform(jax.random.fold_in(jax.random.fold_in(rng, 6), axis_at), (parts,), jnp.float32, low / len(pieces), largest / len(pieces))
        return jnp.repeat(jnp.exp(heights), shape[axis_at] // parts).reshape((-1,) + (1,) * (len(shape) - axis_at - 1))

    factor_of = one(*pieces[0])
    for cut in pieces[1:]:
        factor_of = factor_of * one(*cut)
    return factor_of


def length_profile(number_of, total, bound, slope):
    portions = [(1 << 20) // math.isqrt(standing ** slope) + 1 for standing in range(2, number_of + 1)]
    spare, given = total - bound - (number_of - 1), [1] * (number_of - 1)
    while spare > 0:
        free = [i for i in range(number_of - 1) if given[i] < bound]
        pool, left = sum([portions[i] for i in free]), spare
        for i in free:
            more = min(bound - given[i], max(1, left * portions[i] // pool), spare)
            given[i] = given[i] + more
            spare = spare - more
    return np.array([bound] + given)


def ragged(stream_key, number_of, total, most, slope):
    if number_of == 2:
        one = jax.random.randint(stream_key, (), max(1, total - most), min(most, total - 1) + 1)
        return jnp.stack([one, total - one])
    tallies = jnp.asarray(length_profile(number_of, total, most, slope), jnp.int32)
    couples = (number_of - 1) // 2
    giver, taker = tallies[1:1 + 2 * couples:2], tallies[2:2 + 2 * couples:2]
    room = jnp.minimum(giver - 1, most - taker)
    moved = jax.random.randint(jax.random.fold_in(stream_key, 1), (couples,), 0, 1 << 20) % (room + 1)
    tallies = tallies.at[1:1 + 2 * couples:2].set(giver - moved).at[2:2 + 2 * couples:2].set(taker + moved)
    return tallies[jax.random.permutation(jax.random.fold_in(stream_key, 2), number_of)]


def scatter_about(own_key, dims, scale, reach, cuts=(), kind=jnp.bfloat16):
    values = scale * jax.random.normal(own_key, dims, jnp.float32)
    if cuts:
        values = values * steps_of(own_key, dims, cuts, -0.22, 0.18)
    return jnp.clip(values, -reach, reach).astype(kind)


def setup_inputs(seed: int = 0) -> dict:
    streams_of = jax.random.split(jax.random.key(seed), 16)
    return {
        "tokens": scatter_about(streams_of[0], (TOKENS, MODEL_WIDTH), 1.0, 6.0, ((0, 128),)),
        "grad_out": scatter_about(streams_of[1], (TOKENS, MODEL_WIDTH), 1.0, 6.0, ((0, 128),)),
        "target": draw_target(jax.random.fold_in(streams_of[15], 71), 0),
        "lengths": jax.vmap(lambda own: ragged(own, SEQS, GROUP_TOKENS, LONGEST, 1))(jax.random.split(streams_of[3], N_ROW)).reshape((N_ROW, SEQS)).astype(jnp.int32),
        "attn_gain": jnp.clip(1.0 + 0.18 * jax.random.normal(streams_of[4], (MODEL_WIDTH,), jnp.float32), 0.1, 1.9),
        "ffn_gain": jnp.clip(1.0 + 0.18 * jax.random.normal(streams_of[5], (MODEL_WIDTH,), jnp.float32), 0.1, 1.9),
        "q_gain": jnp.clip(1.0 + 0.18 * jax.random.normal(streams_of[6], (HEAD_SIZE,), jnp.float32), 0.1, 1.9),
        "k_gain": jnp.clip(1.0 + 0.18 * jax.random.normal(streams_of[7], (HEAD_SIZE,), jnp.float32), 0.1, 1.9),
        "w_query": scatter_about(streams_of[8], (MODEL_WIDTH, QUERY_HEADS * HEAD_SIZE), MODEL_WIDTH ** -0.5, 0.1875, ((0, 16), (1, 8))),
        "key_matrix": scatter_about(streams_of[9], (MODEL_WIDTH, VALUE_HEADS * HEAD_SIZE), MODEL_WIDTH ** -0.5, 0.1875, ((0, 16), (1, 8))),
        "value_matrix": scatter_about(streams_of[10], (MODEL_WIDTH, VALUE_HEADS * HEAD_SIZE), MODEL_WIDTH ** -0.5, 0.1875, ((0, 16), (1, 8))),
        "w_out": scatter_about(streams_of[11], (QUERY_HEADS * HEAD_SIZE, MODEL_WIDTH), (QUERY_HEADS * HEAD_SIZE // 16) ** -0.5, 0.5, ((0, 8), (1, 16))),
        "w_gate": scatter_about(streams_of[12], (MODEL_WIDTH, FF), MODEL_WIDTH ** -0.5, 0.1875, ((0, 16), (1, 8))),
        "w_up": scatter_about(streams_of[13], (MODEL_WIDTH, FF), MODEL_WIDTH ** -0.5, 0.1875, ((0, 16), (1, 8))),
        "w_down": scatter_about(streams_of[14], (FF, MODEL_WIDTH), FF ** -0.5, 0.109375, ((0, 8), (1, 16))),
    }


EPSILON = 1e-06
ROPE_BASE = 1000000.0
EXACT_MODE = lax.Precision.HIGHEST

@jax.custom_vjp
def reduced_cast(v):
    return lax.optimization_barrier(v.astype(jnp.bfloat16)).astype(jnp.float32)

@jax.custom_vjp
def reduced_cast_grad(v):
    return v

def low_keep(v):
    return (reduced_cast(v), None)

def low_pass(kept, grad):
    return (grad,)

def back_keep(v):
    return (v, None)

def back_low(kept, grad):
    return (reduced_cast(grad),)
reduced_cast.defvjp(low_keep, low_pass)
reduced_cast_grad.defvjp(back_keep, back_low)

def rms_scale(values, weights):
    inverse = lax.rsqrt(lax.optimization_barrier(jnp.mean(values * values, axis=-1, keepdims=True)) + EPSILON)
    return values * inverse * weights

def rotate(values, position):
    head_width = values.shape[-1]
    halfway = head_width // 2
    inverse_freq = ROPE_BASE ** (-jnp.arange(halfway, dtype=jnp.float32) * 2.0 / head_width)
    shaped = (values.shape[0],) + (1,) * (values.ndim - 1)
    angles = position.astype(jnp.float32).reshape(shaped) * inverse_freq
    cosine = jnp.cos(angles)
    sine_part = jnp.sin(angles)
    leading = values[..., :halfway]
    trailing = values[..., halfway:]
    return jnp.concatenate([leading * cosine - trailing * sine_part, trailing * cosine + leading * sine_part], axis=-1)

def head_prep(raw_heads, weights, position):
    return rotate(rms_scale(raw_heads, weights), position)

def sequence_layout(seq_lengths, total):
    ends_at = jnp.cumsum(seq_lengths).astype(jnp.int32)
    starts_at = (ends_at - seq_lengths).astype(jnp.int32)
    slot_ids = jnp.arange(total, dtype=jnp.int32)
    segment = lax.optimization_barrier(jnp.sum((slot_ids[:, None] >= ends_at[None, :]).astype(jnp.int32), axis=1)).astype(jnp.int32)
    member = segment[:, None] == jnp.arange(seq_lengths.shape[0], dtype=jnp.int32)[None, :]
    first_slot = lax.optimization_barrier(jnp.sum(jnp.where(member, starts_at[None, :], 0), axis=1)).astype(jnp.int32)
    return (segment, (slot_ids - first_slot).astype(jnp.int32))

def group_layer(inputs, seq_lengths, params):
    attn_gain, ffn_gain, q_gain, k_gain, full_query, complete_keys, complete_values, full_out, full_gate, full_up, full_down = params
    segment, position = sequence_layout(seq_lengths, GROUP_TOKENS)
    first_normalized = reduced_cast(rms_scale(inputs, attn_gain))
    query_raw = reduced_cast_grad(jnp.dot(first_normalized, full_query, precision=EXACT_MODE)).reshape(GROUP_TOKENS, QUERY_HEADS, HEAD_SIZE)
    unrotated_key = reduced_cast_grad(jnp.dot(first_normalized, complete_keys, precision=EXACT_MODE)).reshape(GROUP_TOKENS, VALUE_HEADS, HEAD_SIZE)
    value_heads_rows = reduced_cast_grad(reduced_cast(jnp.dot(first_normalized, complete_values, precision=EXACT_MODE))).reshape(GROUP_TOKENS, VALUE_HEADS, HEAD_SIZE)
    queries = reduced_cast(head_prep(query_raw, q_gain, position))
    keys_rot = reduced_cast(head_prep(unrotated_key, k_gain, position))
    query_per_value_head = QUERY_HEADS // VALUE_HEADS
    keys_all = jnp.repeat(keys_rot, query_per_value_head, axis=1)
    values_all = jnp.repeat(value_heads_rows, query_per_value_head, axis=1)
    blocks = GROUP_TOKENS // QBLOCK
    scale = HEAD_SIZE ** (-0.5)
    slot_ids = jnp.arange(GROUP_TOKENS, dtype=jnp.int32)

    def block(item):
        query_part, segment_part, slot_part = item
        raw_scores = reduced_cast_grad(jnp.einsum('qhd,khd->hqk', query_part, keys_all, precision=EXACT_MODE))
        allowed = (segment_part[:, None] == segment[None, :]) & (slot_ids[None, :] <= slot_part[:, None])
        probs = jax.nn.softmax(jnp.where(allowed[None], raw_scores * scale, -1e+30), axis=-1)
        return jnp.einsum('hqk,khd->qhd', reduced_cast(probs), values_all, precision=EXACT_MODE)
    attended = lax.map(jax.checkpoint(block), (queries.reshape(blocks, QBLOCK, QUERY_HEADS, HEAD_SIZE), segment.reshape(blocks, QBLOCK), slot_ids.reshape(blocks, QBLOCK)))
    attended = reduced_cast_grad(reduced_cast(attended.reshape(GROUP_TOKENS, QUERY_HEADS * HEAD_SIZE)))
    middle = inputs + reduced_cast_grad(jnp.dot(attended, full_out, precision=EXACT_MODE))
    normed_two = reduced_cast(rms_scale(middle, ffn_gain))
    gate_pre = reduced_cast_grad(jnp.dot(normed_two, full_gate, precision=EXACT_MODE))
    up_pre = reduced_cast_grad(jnp.dot(normed_two, full_up, precision=EXACT_MODE))
    hidden = reduced_cast(jax.nn.silu(gate_pre) * up_pre)
    return middle + reduced_cast_grad(jnp.dot(hidden, full_down, precision=EXACT_MODE))

def reference(tokens, grad_out, target, lengths, attn_gain, ffn_gain, q_gain, k_gain, w_query, key_matrix, value_matrix, w_out, w_gate, w_up, w_down):
    width = tokens.shape[1]
    tokens_slot = jnp.zeros_like(tokens).at[target].set(tokens)
    grads_slot = jnp.zeros_like(grad_out).at[target].set(grad_out)
    inputs_all = tokens_slot.astype(jnp.float32).reshape(N_ROW, GROUP_TOKENS, width)
    grads_all = grads_slot.astype(jnp.float32).reshape(N_ROW, GROUP_TOKENS, width)
    params = (attn_gain, ffn_gain, q_gain, k_gain, w_query.astype(jnp.float32), key_matrix.astype(jnp.float32), value_matrix.astype(jnp.float32), w_out.astype(jnp.float32), w_gate.astype(jnp.float32), w_up.astype(jnp.float32), w_down.astype(jnp.float32))

    def forward(inputs_all, params):

        def one_group(item):
            return group_layer(item[0], item[1], params)
        return lax.map(jax.checkpoint(one_group), (inputs_all, lengths))
    outputs_all, pull = jax.vjp(forward, inputs_all, params)
    grad_inputs, grads = pull(grads_all)
    output = outputs_all.reshape(-1, width)[target].astype(jnp.bfloat16)
    input_grad = grad_inputs.reshape(-1, width)[target].astype(jnp.bfloat16)
    return (output, input_grad, grads[0], grads[1], grads[2], grads[3], grads[4], grads[5], grads[6], grads[7], grads[8], grads[9], grads[10])
```

```python
import functools
import math

import jax
import jax.numpy as jnp
from jax import lax
from jax.experimental import pallas as pl
from jax.experimental.pallas import tpu as pltpu
from jax.sharding import PartitionSpec as P

MESH = pl.DeviceIdType.MESH
BF = jnp.bfloat16
F32 = jnp.float32
I32 = jnp.int32
EPSILON = 1e-06
ROPE_BASE = 1000000.0
HEAD = 128
NR = 16
NC = 8
ROWS = 256
WIDTH = 1024
GROUP = 2048
ORDERS = (("x", "y", "z"), ("y", "z", "x"), ("z", "x", "y"))
HBM = pl.BlockSpec(memory_space=pltpu.HBM)
VMEM = pl.BlockSpec(memory_space=pltpu.VMEM)
DMA = pltpu.SemaphoreType.DMA


def sds(shape, dtype=BF):
    return jax.ShapeDtypeStruct(shape, dtype)


def params(cid=None, mib=56, **kw):
    if cid is not None:
        kw.update(collective_id=cid, has_side_effects=True)
    return pltpu.CompilerParams(vmem_limit_bytes=mib << 20, **kw)


def where_am_i():
    r = lax.axis_index("row")
    c = lax.axis_index("col")
    return {"x": c % 4, "y": r // 4, "z": 2 * ((r // 2) % 2) + c // 4, "k": r % 2}


def device(at):
    return (at["y"] * 4 + (at["z"] // 2) * 2 + at["k"], (at["z"] % 2) * 4 + at["x"])


def moved(at, axis, step):
    out = dict(at)
    out[axis] = (at[axis] + step) % 4
    return out


def mate(at):
    out = dict(at)
    out["k"] = 1 - at["k"]
    return out


def meet(peers):
    barrier = pltpu.get_barrier_semaphore()
    for p in peers:
        pl.semaphore_signal(barrier, inc=1, device_id=p, device_id_type=MESH)
    pl.semaphore_wait(barrier, len(peers))


def ring_peers(at):
    return [device(moved(at, a, s)) for a in "xyz" for s in (1, -1)]


def row_peers(at):
    r = lax.axis_index("row")
    c = lax.axis_index("col")
    return [((r + d) % NR, c) for d in range(1, NR)]


def col_peers(at):
    r = lax.axis_index("row")
    c = lax.axis_index("col")
    return [(r, (c + d) % NC) for d in range(1, NC)]


def remote(src, dst, ssem, rsem, to):
    return pltpu.make_async_remote_copy(
        src_ref=src, dst_ref=dst, send_sem=ssem, recv_sem=rsem, device_id=to, device_id_type=MESH
    )


def block_index(sel, with_core=None):
    full = slice(None)
    z = sel.get("z")
    idx = (
        sel.get("x", full),
        full if z is None else z % 2,
        sel.get("y", full),
        full if z is None else z // 2,
    )
    return idx if with_core is None else idx + (with_core,)


def gather_phases(at, locs, outs, sems, late):
    ssem, rsem, msem, nsem = sems
    k = at["k"]
    waits = []

    def region(s, t, pos):
        order = ORDERS[s]
        sel = {a: at[a] for a in order[t + 1 :]}
        sel[order[t]] = pos
        return block_index(sel, k)

    n = len(locs)
    half = locs[0].shape[0] // 2
    for t in range(3):
        firsts = []
        for s in range(n):
            a = ORDERS[s][t]
            p = at[a]
            here = outs[s].at[region(s, t, p)]
            src = locs[s] if t == 0 else here
            pair = []
            for d, step in enumerate((1, -1)):
                cp = remote(
                    src, here, ssem.at[s, t, d], rsem.at[s, t, d], device(moved(at, a, step))
                )
                cp.start()
                pair.append(cp)
            if t == 2:
                cp = remote(here, here, msem.at[s, 0], nsem.at[s, 0], device(mate(at)))
                cp.start()
                late.append(cp)
            firsts.append(pair)
        seconds = []
        for s in range(n):
            a = ORDERS[s][t]
            p = at[a]
            pair = []
            for d, step in enumerate((1, -1)):
                firsts[s][d].wait_recv()
                came = region(s, t, (p - step) % 4)
                rows = pl.ds(d * half, half)
                cp = remote(
                    outs[s].at[came + (rows,)],
                    outs[s].at[came + (rows,)],
                    ssem.at[s, t, 2 + d],
                    rsem.at[s, t, 2 + d],
                    device(moved(at, a, step)),
                )
                cp.start()
                pair.append(cp)
                if t == 2:
                    ref = outs[s].at[came]
                    cp = remote(ref, ref, msem.at[s, 1 + d], nsem.at[s, 1 + d], device(mate(at)))
                    cp.start()
                    late.append(cp)
            seconds.append(pair)
        for s in range(n):
            for cp in seconds[s]:
                cp.wait_recv()
            if t == 2:
                p = at[ORDERS[s][t]]
                ref = outs[s].at[region(s, t, (p + 2) % 4)]
                cp = remote(ref, ref, msem.at[s, 3], nsem.at[s, 3], device(mate(at)))
                cp.start()
                late.append(cp)
        waits += [c for pair in firsts + seconds for c in pair]
    return waits


def gather_sems(n=3):
    return [DMA((n, 3, 4)), DMA((n, 3, 4)), DMA((n, 4)), DMA((n, 4)), DMA((n,))]


def gather_shape(w):
    return sds((4, 2, 4, 2, 2, 64, w))


def run_gather(at, locs, outs, sems):
    ssem, rsem, msem, nsem, lsem = sems
    own = []
    for s in range(len(locs)):
        cp = pltpu.make_async_copy(
            locs[s], outs[s].at[block_index({a: at[a] for a in "xyz"}, at["k"])], lsem.at[s]
        )
        cp.start()
        own.append(cp)
    for cp in own:
        cp.wait()
    late = []
    waits = gather_phases(at, locs, outs, (ssem, rsem, msem, nsem), late)
    for cp in late:
        cp.wait()
    for cp in waits:
        cp.wait_send()


def gather_kernel(l0, l1, l2, g0, g1, g2, *sems):
    at = where_am_i()
    meet(ring_peers(at) + [device(mate(at))])
    run_gather(at, (l0, l1, l2), (g0, g1, g2), sems)


def gather(blocks, cid, name):
    w = blocks[0].shape[1]
    return pl.pallas_call(
        gather_kernel,
        name=name,
        out_shape=[gather_shape(w)] * 3,
        in_specs=[HBM] * 3,
        out_specs=[HBM] * 3,
        scratch_shapes=gather_sems(),
        compiler_params=params(cid),
    )(*blocks)


def lead_shape(axes):
    out = ()
    for a in ("x", "zl", "y", "zh"):
        if a[0] in axes:
            out += (4,) if a in "xy" else (2,)
    return out


def sub_index(sel, axes):
    out = ()
    for a in ("x", "zl", "y", "zh"):
        if a[0] not in axes:
            continue
        pos = sel.get(a[0])
        if pos is None:
            out += (slice(None),)
        elif a == "zl":
            out += (pos % 2,)
        elif a == "zh":
            out += (pos // 2,)
        else:
            out += (pos,)
    return out


def unravel(i, shape):
    out = ()
    for n in reversed(shape):
        out = (i % n,) + out
        i = i // n
    return out


def add_blocks(lead, dst, terms):
    n = math.prod(lead)

    def one(i):
        j = unravel(i, lead)
        total = None
        for ref, pre in terms:
            v = ref[pre(j)].astype(F32)
            total = v if total is None else total + v
        dst[0][dst[1](j)] = total.astype(dst[0].dtype)

    if n == 1:
        one(0)
    else:

        @pl.loop(0, n)
        def _(i):
            one(i)


def scatter_buffers(w, n=3):
    out = []
    for s in range(n):
        for t in range(3):
            lead = lead_shape(ORDERS[s][: 2 - t])
            out.append(pltpu.VMEM((2,) + lead + (32, w), BF))
            out.append(pltpu.VMEM((2,) + lead + (64, w), BF))
            out.append(pltpu.VMEM((2,) + lead + (32, w), BF))
            if t == 0:
                out.append(pltpu.VMEM(lead + (64, w), BF))
            elif t == 1:
                out.append(pltpu.VMEM(lead + (64, w), BF))
    return out


PER_STREAM = 11


def scatter_sems(n=3):
    return [DMA((n, 3, 6)), DMA((n, 3, 6)), DMA((n, 3))]


def run_scatter(at, parts, results, bufs, sems):
    ssem, rsem, lsem = sems
    n = len(parts)
    cur = [(parts[s], "xyz") for s in range(n)]
    waits = []
    lo, hi = pl.ds(0, 32), pl.ds(32, 32)
    for t in range(3):
        st = []
        for s in range(n):
            b = bufs[s * PER_STREAM : (s + 1) * PER_STREAM]
            rel_in, piece_in, rel_out = b[4 * t : 4 * t + 3]
            total = b[4 * t + 3] if t < 2 else None
            a = ORDERS[s][2 - t]
            rem = ORDERS[s][: 2 - t]
            ref, axes = cur[s]
            p = at[a]

            def src(pos, rows, ref=ref, axes=axes, a=a):
                return ref.at[sub_index({a: pos % 4}, axes) + (rows,)]

            right, left = device(moved(at, a, 1)), device(moved(at, a, -1))
            allr = (slice(None),) * len(lead_shape(rem))
            cps = [
                remote(src(p + 2, lo), rel_in.at[0], ssem.at[s, t, 0], rsem.at[s, t, 0], right),
                remote(src(p + 2, hi), rel_in.at[1], ssem.at[s, t, 1], rsem.at[s, t, 1], left),
                remote(
                    src(p + 1, hi),
                    piece_in.at[(0,) + allr + (hi,)],
                    ssem.at[s, t, 2],
                    rsem.at[s, t, 2],
                    right,
                ),
                remote(
                    src(p - 1, lo),
                    piece_in.at[(1,) + allr + (lo,)],
                    ssem.at[s, t, 3],
                    rsem.at[s, t, 3],
                    left,
                ),
            ]
            for cp in cps:
                cp.start()
            loads = []
            if t == 0:
                loads = [
                    pltpu.make_async_copy(src(p + 1, lo), rel_out.at[0], lsem.at[s, 0]),
                    pltpu.make_async_copy(src(p - 1, hi), rel_out.at[1], lsem.at[s, 1]),
                    pltpu.make_async_copy(src(p, slice(None)), total, lsem.at[s, 2]),
                ]
                for cp in loads:
                    cp.start()
            st.append((rel_in, piece_in, rel_out, total, a, rem, right, left, cps, loads, allr))
        for s in range(n):
            rel_in, piece_in, rel_out, total, a, rem, right, left, cps, loads, allr = st[s]
            ref, axes = cur[s]
            lead = lead_shape(rem)
            p = at[a]
            for d, (rows, pos, to) in enumerate(((lo, p + 1, right), (hi, p - 1, left))):
                cps[d].wait_recv()
                if t == 0:
                    loads[d].wait()
                    mine = (rel_out, lambda j, d=d: (d,) + j)
                else:

                    def pick(j, pos=pos, rows=rows, axes=axes, a=a, rem=rem):
                        it = iter(j)
                        out = ()
                        for q in ("x", "zl", "y", "zh"):
                            if q[0] not in axes:
                                continue
                            if q[0] == a:
                                z = pos % 4
                                out += (z % 2 if q == "zl" else z // 2 if q == "zh" else z,)
                            else:
                                out += (next(it),)
                        return out + (rows,)

                    mine = (ref, pick)
                add_blocks(
                    lead,
                    (rel_out, lambda j, d=d: (d,) + j),
                    [mine, (rel_in, lambda j, d=d: (d,) + j)],
                )
                cp = remote(
                    rel_out.at[d],
                    piece_in.at[(d,) + allr + (rows,)],
                    ssem.at[s, t, 4 + d],
                    rsem.at[s, t, 4 + d],
                    to,
                )
                cp.start()
                cps.append(cp)
        for s in range(n):
            rel_in, piece_in, rel_out, total, a, rem, right, left, cps, loads, allr = st[s]
            ref, axes = cur[s]
            lead = lead_shape(rem)
            p = at[a]
            for i in (2, 3, 4, 5):
                cps[i].wait_recv()
            if t == 0:
                loads[2].wait()
                mine = (total, lambda j: j)
            else:

                def pick(j, pos=p, axes=axes, a=a):
                    it = iter(j)
                    out = ()
                    for q in ("x", "zl", "y", "zh"):
                        if q[0] not in axes:
                            continue
                        if q[0] == a:
                            out += (pos % 2 if q == "zl" else pos // 2 if q == "zh" else pos,)
                        else:
                            out += (next(it),)
                    return out

                mine = (ref, pick)
            dst = (total, lambda j: j) if t < 2 else (results[s], lambda j: (slice(None),) * 2)
            add_blocks(
                lead,
                dst,
                [
                    mine,
                    (piece_in, lambda j: (0,) + j),
                    (piece_in, lambda j: (1,) + j),
                ],
            )
            cur[s] = (total, rem)
            waits += cps
    for cp in waits:
        cp.wait_send()


def scatter_kernel(w, p0, p1, p2, r0, r1, r2, *scratch):
    at = where_am_i()
    meet(ring_peers(at))
    bufs, sems = scratch[: 3 * PER_STREAM], scratch[3 * PER_STREAM :]
    run_scatter(at, (p0, p1, p2), (r0, r1, r2), bufs, sems)


def scatter(parts, cid, name):
    w = parts[0].shape[-1]
    return pl.pallas_call(
        functools.partial(scatter_kernel, w),
        name=name,
        out_shape=[sds((64, w), F32)] * 3,
        in_specs=[HBM] * 3,
        out_specs=[VMEM] * 3,
        scratch_shapes=scatter_buffers(w) + scatter_sems(),
        compiler_params=params(cid),
    )(*parts)


def swap_over(axis, src, dst, ssem, rsem, lsem):
    n = NR if axis == "row" else NC
    r = lax.axis_index("row")
    c = lax.axis_index("col")
    me = r if axis == "row" else c
    cps = []
    for d in range(1, n):
        to = (me + d) % n
        cp = remote(
            src.at[to],
            dst.at[me],
            ssem.at[d - 1],
            rsem.at[d - 1],
            (to, c) if axis == "row" else (r, to),
        )
        cp.start()
        cps.append(cp)
    own = pltpu.make_async_copy(src.at[me], dst.at[me], lsem)
    own.start()
    return cps + [own]


def swap_sems(axis):
    n = NR if axis == "row" else NC
    return [DMA((n - 1,)), DMA((n - 1,)), DMA]


def col_swap_kernel(src, dst, ssem, rsem, lsem):
    at = where_am_i()
    meet(col_peers(at))
    for cp in swap_over("col", src, dst, ssem, rsem, lsem):
        cp.wait()


def col_swap(src, cid, name):
    return pl.pallas_call(
        col_swap_kernel,
        name=name,
        out_shape=sds(src.shape),
        in_specs=[HBM],
        out_specs=HBM,
        scratch_shapes=swap_sems("col"),
        compiler_params=params(cid),
    )(src)


def dot(a, b, dims=((1,), (0,))):
    return lax.dot_general(a, b, (dims, ((), ())), preferred_element_type=F32)


NT = ((1,), (1,))
TN = ((0,), (0,))


def iota(shape, dim):
    return lax.broadcasted_iota(I32, shape, dim)


def onehot(cond):
    return cond.astype(F32).astype(BF)


def unrope(g, cos, sin):
    return g * cos - pltpu.roll(g, HEAD // 2, 1) * sin


def mean_square_scale(v):
    return lax.rsqrt(jnp.mean(v * v, axis=-1, keepdims=True) + EPSILON)


def slots_sent(target_row, target_col):
    g_row, g_col = target_row // GROUP, target_col // GROUP
    same = g_row == g_col
    i0, i1 = iota((ROWS, ROWS), 0), iota((ROWS, ROWS), 1)
    before_row = jnp.sum((same & (i0 < i1)).astype(F32), axis=0, keepdims=True).astype(I32)
    before_col = jnp.sum((same & (i1 < i0)).astype(F32), axis=1, keepdims=True).astype(I32)
    return g_row * (ROWS // NR) + before_row, g_col * (ROWS // NR) + before_col


def dispatch_kernel(
    t_row, t_col, tokens, grads, l0, l1, l2, tok, grd, slt, g0, g1, g2, tok_s, grd_s, slt_s, *sems
):
    at = where_am_i()
    meet(ring_peers(at) + row_peers(at))
    place, _ = slots_sent(t_row[...], t_col[...])
    sel = place == iota((ROWS, ROWS), 0)
    pick = onehot(sel)
    tok_s[...] = dot(pick, tokens[...]).astype(BF).reshape(tok_s.shape)
    slot = jnp.sum(jnp.where(sel, t_row[...], 0).astype(F32), axis=1, keepdims=True)
    slt_s[...] = jnp.broadcast_to(slot, (ROWS, HEAD)).astype(I32).reshape(slt_s.shape)
    cps = swap_over("row", tok_s, tok, *sems[0:3])
    cps += swap_over("row", slt_s, slt, *sems[6:9])
    grd_s[...] = dot(pick, grads[...]).astype(BF).reshape(grd_s.shape)
    cps += swap_over("row", grd_s, grd, *sems[3:6])
    run_gather(at, (l0, l1, l2), (g0, g1, g2), sems[9:])
    for cp in cps:
        cp.wait()


def dispatch(target, tokens, grads, blocks):
    w = blocks[0].shape[1]
    return pl.pallas_call(
        dispatch_kernel,
        name="dispatch",
        out_shape=[sds((NR, 16, WIDTH))] * 2
        + [sds((NR, 16, HEAD), I32)]
        + [gather_shape(w)] * 3,
        in_specs=[VMEM] * 4 + [HBM] * 3,
        out_specs=[HBM] * 6,
        scratch_shapes=[pltpu.VMEM((NR, 16, WIDTH), BF)] * 2
        + [pltpu.VMEM((NR, 16, HEAD), I32)]
        + swap_sems("row") * 3
        + gather_sems(),
        compiler_params=params(1),
    )(target.reshape(1, ROWS), target.reshape(ROWS, 1), tokens, grads, *blocks)


def halves_of(v):
    even, odd = [], []
    low = iota((v.shape[0], HEAD), 1) < HEAD // 2
    for m in range(4):
        a, b = v[:, 256 * m : 256 * m + 128], v[:, 256 * m + 128 : 256 * m + 256]
        even.append(jnp.where(low, a, pltpu.roll(b, 64, 1)))
        odd.append(jnp.where(low, pltpu.roll(a, 64, 1), b))
    return jnp.concatenate(even, axis=1), jnp.concatenate(odd, axis=1)


def project_kernel(
    slt, tok, grd, again, qgain, kgain, cos, sin, wq, wkv, out, raw, x_o, dy_o, n1h, dyh, n1_s
):
    c = pl.program_id(0)

    @pl.when(c == 0)
    def _():
        local = slt[...].reshape(ROWS, HEAD)[:, :1] % ROWS
        put = onehot(local == iota((ROWS, ROWS), 1))
        x = dot(put, tok[...].reshape(ROWS, WIDTH), TN)
        dy = dot(put, grd[...].reshape(ROWS, WIDTH), TN)
        x_o[...] = x.astype(BF)
        dy_o[...] = dy.astype(BF)
        n1 = x * mean_square_scale(x) * again[...]
        n1_s[...] = n1.astype(BF)
        a, b = halves_of(n1)
        n1h[0] = a.astype(BF)
        n1h[1] = b.astype(BF)
        a, b = halves_of(dy)
        dyh[0] = a.astype(BF)
        dyh[1] = b.astype(BF)

    n1 = n1_s[...]
    q = dot(n1, wq[0, 0].reshape(WIDTH, 256))
    kv = dot(n1, wkv[0, 0].reshape(WIDTH, 256))
    raw[0, :, 0:256] = q
    raw[0, :, 256:384] = kv[:, :HEAD]
    pieces = ((q[:, :HEAD], qgain), (q[:, HEAD:], qgain), (kv[:, :HEAD], kgain))
    for i, (v, gain) in enumerate(pieces):
        n = v * mean_square_scale(v) * gain[...]
        n = n * cos[...] + pltpu.roll(n, HEAD // 2, 1) * sin[...]
        out[0, :, i * HEAD : (i + 1) * HEAD] = n.astype(BF)
    out[0, :, 3 * HEAD :] = kv[:, HEAD:].astype(BF)


def slab(w):
    return pl.BlockSpec((1, 1, 4, 2, 2, 64, w), lambda c: (c % 4, c // 4, 0, 0, 0, 0, 0))


def whole(shape):
    return pl.BlockSpec(shape, lambda *_: (0,) * len(shape))


def project(slt, tok, grd, again, qgain, kgain, cos, sin, wq, wkv):
    return pl.pallas_call(
        project_kernel,
        name="project",
        grid=(NC,),
        out_shape=[
            sds((NC, ROWS, 512)),
            sds((NC, ROWS, 384), F32),
            sds((ROWS, WIDTH)),
            sds((ROWS, WIDTH)),
            sds((2, ROWS, 512)),
            sds((2, ROWS, 512)),
        ],
        in_specs=[
            whole((NR, 16, HEAD)),
            whole((NR, 16, WIDTH)),
            whole((NR, 16, WIDTH)),
            whole((1, WIDTH)),
            whole((1, HEAD)),
            whole((1, HEAD)),
            whole((ROWS, HEAD)),
            whole((ROWS, HEAD)),
            slab(256),
            slab(256),
        ],
        out_specs=[
            pl.BlockSpec((1, ROWS, 512), lambda c: (c, 0, 0)),
            pl.BlockSpec((1, ROWS, 384), lambda c: (c, 0, 0)),
            whole((ROWS, WIDTH)),
            whole((ROWS, WIDTH)),
            whole((2, ROWS, 512)),
            whole((2, ROWS, 512)),
        ],
        scratch_shapes=[pltpu.VMEM((ROWS, WIDTH), BF)],
        compiler_params=params(),
    )(slt, tok, grd, again, qgain, kgain, cos, sin, wq, wkv)


LOG2E = math.log2(math.e)
QK = 512


def stacked(v):
    return jnp.concatenate([v[:, :HEAD], v[:, HEAD : 2 * HEAD]], axis=0)


def allowed(i, j, first):
    key = j * ROWS + iota((ROWS, QK), 0)
    query = i * ROWS + iota((ROWS, QK), 1) % ROWS
    return (key <= query) & (key >= first)


def attend_kernel(lo, qkv, first, out, o_t, lse):
    i = pl.program_id(0)
    scale = HEAD**-0.5 * LOG2E
    q = stacked(qkv[i, :, 0 : 2 * HEAD])
    start = first[0]

    def scores(j):
        s = dot(qkv[j, :, 2 * HEAD : 3 * HEAD], q, NT) * scale
        return jnp.where(allowed(i, j, start), s, -1e30)

    s = scores(i)
    m = jnp.max(s, axis=0, keepdims=True)
    p = jnp.exp2(s - m)
    total = jnp.sum(p, axis=0, keepdims=True)
    acc = dot(qkv[i, :, 3 * HEAD :], p.astype(BF), TN)

    def step(d, carry):
        m, total, acc = carry
        j = i - 1 - d
        s = scores(j)
        m2 = jnp.maximum(m, jnp.max(s, axis=0, keepdims=True))
        fade = jnp.exp2(m - m2)
        p = jnp.exp2(s - m2)
        total = total * fade + jnp.sum(p, axis=0, keepdims=True)
        acc = acc * fade + dot(qkv[j, :, 3 * HEAD :], p.astype(BF), TN)
        return m2, total, acc

    m, total, acc = lax.fori_loop(0, i - lo[i], step, (m, total, acc))
    o = acc / total
    o_t[0] = o
    lse[0] = m + jnp.log2(total)
    back = o.T
    out[0] = jnp.concatenate([back[:ROWS], back[ROWS:]], axis=1).astype(BF)


def attend(lo, qkv, first):
    return pl.pallas_call(
        attend_kernel,
        name="attend",
        grid_spec=pltpu.PrefetchScalarGridSpec(
            num_scalar_prefetch=1,
            grid=(NC,),
            in_specs=[
                pl.BlockSpec((NC, ROWS, 512), lambda i, lo: (0, 0, 0)),
                pl.BlockSpec((1, 1, QK), lambda i, lo: (i, 0, 0)),
            ],
            out_specs=[
                pl.BlockSpec((1, ROWS, 256), lambda i, lo: (i, 0, 0)),
                pl.BlockSpec((1, HEAD, QK), lambda i, lo: (i, 0, 0)),
                pl.BlockSpec((1, 1, QK), lambda i, lo: (i, 0, 0)),
            ],
        ),
        out_shape=[
            sds((NC, ROWS, 256)),
            sds((NC, HEAD, QK), F32),
            sds((NC, 1, QK), F32),
        ],
        compiler_params=params(),
    )(lo, qkv, first)


def attend_back_kernel(hi, qkv, first, d_o, o_t, lse, out, qs, dos, delta, dq):
    j = pl.program_id(0)
    scale = HEAD**-0.5

    @pl.when(j == 0)
    def _():
        for i in range(NC):
            qs[i] = stacked(qkv[i, :, 0 : 2 * HEAD])
            g = stacked(d_o[i])
            dos[i] = g
            delta[i] = jnp.sum(g.astype(F32).T * o_t[i], axis=0, keepdims=True)
            dq[i] = jnp.zeros((HEAD, QK), F32)

    k = qkv[j, :, 2 * HEAD : 3 * HEAD]
    v = qkv[j, :, 3 * HEAD :]
    k_t = k.astype(F32).T.astype(BF)

    def step(i, carry):
        dk, dv = carry
        s = dot(k, qs[i], NT) * (scale * LOG2E) - lse[i]
        p = jnp.where(allowed(i, j, first[i]), jnp.exp2(s), 0.0)
        ds = (p * (dot(v, dos[i], NT) - delta[i]) * scale).astype(BF)
        dv = dv + dot(p.astype(BF), dos[i])
        dk = dk + dot(ds, qs[i])
        dq[i] += dot(k_t, ds)
        return dk, dv

    zero = jnp.zeros((ROWS, HEAD), F32)
    dk, dv = lax.fori_loop(j, hi[j] + 1, step, (zero, zero))
    done = dq[j].T
    out[0, :, 0:HEAD] = done[:ROWS].astype(BF)
    out[0, :, HEAD : 2 * HEAD] = done[ROWS:].astype(BF)
    out[0, :, 2 * HEAD : 3 * HEAD] = dk.astype(BF)
    out[0, :, 3 * HEAD :] = dv.astype(BF)


def attend_back(hi, qkv, first, d_o, o_t, lse):
    def full(shape):
        return pl.BlockSpec(shape, lambda j, hi: (0,) * len(shape))

    return pl.pallas_call(
        attend_back_kernel,
        name="attend_back",
        grid_spec=pltpu.PrefetchScalarGridSpec(
            num_scalar_prefetch=1,
            grid=(NC,),
            in_specs=[
                full((NC, ROWS, 512)),
                full((NC, 1, QK)),
                full((NC, ROWS, 256)),
                full((NC, HEAD, QK)),
                full((NC, 1, QK)),
            ],
            out_specs=pl.BlockSpec((1, ROWS, 512), lambda j, hi: (j, 0, 0)),
            scratch_shapes=[
                pltpu.VMEM((NC, QK, HEAD), BF),
                pltpu.VMEM((NC, QK, HEAD), BF),
                pltpu.VMEM((NC, 1, QK), F32),
                pltpu.VMEM((NC, HEAD, QK), F32),
            ],
        ),
        out_shape=sds((NC, ROWS, 512)),
        compiler_params=params(),
    )(hi, qkv, first, d_o, o_t, lse)


def middle_kernel(
    slt, x, dy, oa, fgain, wo, wg, wu, wd,
    out_s, dh_o, dhlh, n2h, act, d_o, gain_o,
    h_s, n2_s, acc, dn2, dhl_s,
):
    i = pl.program_id(0)

    @pl.when(i < NC)
    def _():
        part = dot(oa[0], wo[0, 0].reshape(WIDTH, 256), NT)

        @pl.when(i == 0)
        def _():
            acc[...] = x[...].astype(F32) + part

        @pl.when(i > 0)
        def _():
            acc[...] += part

    @pl.when(i == NC)
    def _():
        h = acc[...]
        h_s[...] = h
        n2 = h * mean_square_scale(h) * fgain[...]
        n2_s[...] = n2.astype(BF)
        a, b = halves_of(n2)
        n2h[0] = a.astype(BF)
        n2h[1] = b.astype(BF)
        dn2[...] = jnp.zeros_like(dn2)

    @pl.when((i >= NC) & (i < 2 * NC))
    def _():
        g_w = wg[0, 0].reshape(WIDTH, 384)
        u_w = wu[0, 0].reshape(WIDTH, 384)
        d_w = wd[0, 0].reshape(WIDTH, 384)
        g = dot(n2_s[...], g_w)
        u = dot(n2_s[...], u_w)
        dhid = dot(dy[...], d_w)
        sig = jax.nn.sigmoid(g)
        silu = g * sig
        hid = (silu * u).astype(BF)
        dg = (dhid * u * sig * (1.0 + g * (1.0 - sig))).astype(BF)
        du = (dhid * silu).astype(BF)
        act[0, :, 0:384] = dg
        act[0, :, 384:768] = du
        act[0, :, 768:] = hid
        acc[...] += dot(hid, d_w, NT)
        dn2[...] += dot(dg, g_w, NT) + dot(du, u_w, NT)

    @pl.when(i == 2 * NC - 1)
    def _():
        local = slt[...].reshape(ROWS, HEAD)[:, :1] % ROWS
        take = onehot(local == iota((ROWS, ROWS), 1))
        out_s[...] = dot(take, acc[...].astype(BF)).astype(BF).reshape(out_s.shape)
        h = h_s[...]
        r2 = mean_square_scale(h)
        hn = h * r2
        e = dn2[...]
        gain_o[...] = jnp.sum(e * hn, axis=0, keepdims=True)
        e = e * fgain[...]
        dh = dy[...].astype(F32) + r2 * (e - hn * jnp.mean(e * hn, axis=-1, keepdims=True))
        dh_o[...] = dh
        dhl_s[...] = dh.astype(BF)
        a, b = halves_of(dh)
        dhlh[0] = a.astype(BF)
        dhlh[1] = b.astype(BF)

    @pl.when(i >= 2 * NC)
    def _():
        d_o[0] = dot(dhl_s[...], wo[0, 0].reshape(WIDTH, 256)).astype(BF)


def middle(slt, x, dy, oa, fgain, wo, wg, wu, wd):
    def ffn(w):
        def at(i):
            c = jnp.clip(i - NC, 0, NC - 1)
            return (c % 4, c // 4, 0, 0, 0, 0, 0)

        return pl.BlockSpec((1, 1, 4, 2, 2, 64, w), at)

    def out_at(i):
        c = jnp.where(i < NC, i, jnp.where(i < 2 * NC, NC - 1, i - 2 * NC))
        return (c % 4, c // 4, 0, 0, 0, 0, 0)

    return pl.pallas_call(
        middle_kernel,
        name="middle",
        grid=(3 * NC,),
        out_shape=[
            sds((NR, 16, WIDTH)),
            sds((ROWS, WIDTH), F32),
            sds((2, ROWS, 512)),
            sds((2, ROWS, 512)),
            sds((NC, ROWS, 1152)),
            sds((NC, ROWS, 256)),
            sds((1, WIDTH), F32),
        ],
        in_specs=[
            whole((NR, 16, HEAD)),
            whole((ROWS, WIDTH)),
            whole((ROWS, WIDTH)),
            pl.BlockSpec((1, ROWS, 256), lambda i: (jnp.minimum(i, NC - 1), 0, 0)),
            whole((1, WIDTH)),
            pl.BlockSpec((1, 1, 4, 2, 2, 64, 256), out_at),
            ffn(384),
            ffn(384),
            ffn(384),
        ],
        out_specs=[
            whole((NR, 16, WIDTH)),
            whole((ROWS, WIDTH)),
            whole((2, ROWS, 512)),
            whole((2, ROWS, 512)),
            pl.BlockSpec((1, ROWS, 1152), lambda i: (jnp.clip(i - NC, 0, NC - 1), 0, 0)),
            pl.BlockSpec((1, ROWS, 256), lambda i: (jnp.maximum(i - 2 * NC, 0), 0, 0)),
            whole((1, WIDTH)),
        ],
        scratch_shapes=[
            pltpu.VMEM((ROWS, WIDTH), F32),
            pltpu.VMEM((ROWS, WIDTH), BF),
            pltpu.VMEM((ROWS, WIDTH), F32),
            pltpu.VMEM((ROWS, WIDTH), F32),
            pltpu.VMEM((ROWS, WIDTH), BF),
        ],
        compiler_params=params(),
    )(slt, x, dy, oa, fgain, wo, wg, wu, wd)


def back_swap_kernel(d_o, out_s, act, oa, n2h, dyh, dhlh, *rest):
    outs, sems = rest[:7], rest[7:]
    g_o, got, act_m, oa_m, n2_m, dy_m, dhl_m = outs
    at = where_am_i()
    meet(col_peers(at) + row_peers(at))
    cps = swap_over("col", d_o, g_o, *sems[0:3])
    to = device(mate(at))
    other = 1 - at["k"]
    pairs = (
        (act, act_m),
        (oa, oa_m),
        (n2h.at[other], n2_m),
        (dyh.at[other], dy_m),
        (dhlh.at[other], dhl_m),
    )
    for i, (src, dst) in enumerate(pairs):
        cp = remote(src, dst, sems[6].at[i], sems[7].at[i], to)
        cp.start()
        cps.append(cp)
    cps += swap_over("row", out_s, got, *sems[3:6])
    for cp in cps:
        cp.wait()


def back_swap(d_o, out_s, act, oa, n2h, dyh, dhlh):
    return pl.pallas_call(
        back_swap_kernel,
        name="back_swap",
        out_shape=[sds(d_o.shape), sds(out_s.shape), sds(act.shape), sds(oa.shape)]
        + [sds((ROWS, 512))] * 3,
        in_specs=[HBM] * 7,
        out_specs=[HBM] * 7,
        scratch_shapes=swap_sems("col") + swap_sems("row") + [DMA((5,)), DMA((5,))],
        compiler_params=params(5),
    )(d_o, out_s, act, oa, n2h, dyh, dhlh)


def stack_tokens(k, mine, others, scratch):
    scratch[:, 0:ROWS] = mine[k].astype(F32).T.astype(BF)
    scratch[:, ROWS:] = others[...].astype(F32).T.astype(BF)


def ffn_grads_kernel(n2h, n2_m, dyh, dy_m, act, act_m, g0, g1, g2, n_s, y_s):
    c = pl.program_id(0)

    @pl.when(c == 0)
    def _():
        k = lax.axis_index("row") % 2
        stack_tokens(k, n2h, n2_m, n_s)
        stack_tokens(k, dyh, dy_m, y_s)

    for i, (lhs, out) in enumerate(((n_s, g0), (n_s, g1), (y_s, g2))):
        cols = slice(384 * i, 384 * i + 384)
        rhs = jnp.concatenate([act[0, :, cols], act_m[0, :, cols]], axis=0)
        out[0, 0] = dot(lhs[...], rhs).astype(BF).reshape(4, 2, 64, 384)


def grad_slab(w):
    return pl.BlockSpec((1, 1, 4, 2, 64, w), lambda c: (c % 4, c // 4, 0, 0, 0, 0))


def ffn_grads(n2h, n2_m, dyh, dy_m, act, act_m):
    one = pl.BlockSpec((1, ROWS, 1152), lambda c: (c, 0, 0))
    return pl.pallas_call(
        ffn_grads_kernel,
        name="ffn_grads",
        grid=(NC,),
        out_shape=[sds((4, 2, 4, 2, 64, 384))] * 3,
        in_specs=[whole((2, ROWS, 512)), whole((ROWS, 512))] * 2 + [one, one],
        out_specs=[grad_slab(384)] * 3,
        scratch_shapes=[pltpu.VMEM((512, 2 * ROWS), BF)] * 2,
        compiler_params=params(),
    )(n2h, n2_m, dyh, dy_m, act, act_m)


def attn_grads_kernel(n1h, n1_m, dhlh, dhl_m, dqkv, dqkv_m, oa, oa_m, g0, g1, g2, n_s, h_s):
    c = pl.program_id(0)

    @pl.when(c == 0)
    def _():
        k = lax.axis_index("row") % 2
        stack_tokens(k, n1h, n1_m, n_s)
        stack_tokens(k, dhlh, dhl_m, h_s)

    for i, (lhs, mine, others, out) in enumerate(
        ((n_s, dqkv, dqkv_m, g0), (n_s, dqkv, dqkv_m, g1), (h_s, oa, oa_m, g2))
    ):
        cols = slice(256 * i, 256 * i + 256) if i < 2 else slice(0, 256)
        rhs = jnp.concatenate([mine[0, :, cols], others[0, :, cols]], axis=0)
        out[0, 0] = dot(lhs[...], rhs).astype(BF).reshape(4, 2, 64, 256)


def attn_grads(n1h, n1_m, dhlh, dhl_m, dqkv, dqkv_m, oa, oa_m):
    def one(w):
        return pl.BlockSpec((1, ROWS, w), lambda c: (c, 0, 0))

    return pl.pallas_call(
        attn_grads_kernel,
        name="attn_grads",
        grid=(NC,),
        out_shape=[sds((4, 2, 4, 2, 64, 256))] * 3,
        in_specs=[whole((2, ROWS, 512)), whole((ROWS, 512))] * 2
        + [one(512), one(512), one(256), one(256)],
        out_specs=[grad_slab(256)] * 3,
        scratch_shapes=[pltpu.VMEM((512, 2 * ROWS), BF)] * 2,
        compiler_params=params(),
    )(n1h, n1_m, dhlh, dhl_m, dqkv, dqkv_m, oa, oa_m)


def project_back_kernel(
    slt, x, dh, again, qgain, kgain, cos, sin, raw, dqkv, wq, wkv,
    d_o, dx_s, gain_o, qk_o, acc, gq, gk,
):
    c = pl.program_id(0)

    @pl.when(c == 0)
    def _():
        acc[...] = jnp.zeros_like(acc)
        gq[...] = jnp.zeros_like(gq)
        gk[...] = jnp.zeros_like(gk)

    for i, (gain, g_acc) in enumerate(((qgain, gq), (qgain, gq), (kgain, gk))):
        cols = slice(i * HEAD, (i + 1) * HEAD)
        v = raw[0, :, cols]
        r = mean_square_scale(v)
        xn = v * r
        dn = unrope(dqkv[0, :, cols].astype(F32), cos[...], sin[...])
        g_acc[...] += jnp.sum(dn * xn, axis=0, keepdims=True)
        e = dn * gain[...]
        d_o[0, :, cols] = (r * (e - xn * jnp.mean(e * xn, axis=-1, keepdims=True))).astype(BF)
    d_o[0, :, 3 * HEAD :] = dqkv[0, :, 3 * HEAD :]
    acc[...] += dot(d_o[0, :, 0:256], wq[0, 0].reshape(WIDTH, 256), NT) + dot(
        d_o[0, :, 256:512], wkv[0, 0].reshape(WIDTH, 256), NT
    )

    @pl.when(c == NC - 1)
    def _():
        xv = x[...].astype(F32)
        r1 = mean_square_scale(xv)
        xn = xv * r1
        e = acc[...]
        gain_o[...] = jnp.sum(e * xn, axis=0, keepdims=True)
        e = e * again[...]
        dx = dh[...] + r1 * (e - xn * jnp.mean(e * xn, axis=-1, keepdims=True))
        local = slt[...].reshape(ROWS, HEAD)[:, :1] % ROWS
        take = onehot(local == iota((ROWS, ROWS), 1))
        dx_s[...] = dot(take, dx.astype(BF)).astype(BF).reshape(dx_s.shape)
        qk_o[...] = jnp.concatenate([gq[...], gk[...]], axis=1)


def project_back(slt, x, dh, again, qgain, kgain, cos, sin, raw, dqkv, wq, wkv):
    return pl.pallas_call(
        project_back_kernel,
        name="project_back",
        grid=(NC,),
        out_shape=[
            sds((NC, ROWS, 512)),
            sds((NR, 16, WIDTH)),
            sds((1, WIDTH), F32),
            sds((1, 2 * HEAD), F32),
        ],
        in_specs=[
            whole((NR, 16, HEAD)),
            whole((ROWS, WIDTH)),
            whole((ROWS, WIDTH)),
            whole((1, WIDTH)),
            whole((1, HEAD)),
            whole((1, HEAD)),
            whole((ROWS, HEAD)),
            whole((ROWS, HEAD)),
            pl.BlockSpec((1, ROWS, 384), lambda c: (c, 0, 0)),
            pl.BlockSpec((1, ROWS, 512), lambda c: (c, 0, 0)),
            slab(256),
            slab(256),
        ],
        out_specs=[
            pl.BlockSpec((1, ROWS, 512), lambda c: (c, 0, 0)),
            whole((NR, 16, WIDTH)),
            whole((1, WIDTH)),
            whole((1, 2 * HEAD)),
        ],
        scratch_shapes=[
            pltpu.VMEM((ROWS, WIDTH), F32),
            pltpu.VMEM((1, HEAD), F32),
            pltpu.VMEM((1, HEAD), F32),
        ],
        compiler_params=params(),
    )(slt, x, dh, again, qgain, kgain, cos, sin, raw, dqkv, wq, wkv)


def core_swap_kernel(dqkv, n1h, dqkv_m, n1_m, ssem, rsem):
    at = where_am_i()
    to = device(mate(at))
    meet([to])
    cps = [
        remote(dqkv, dqkv_m, ssem.at[0], rsem.at[0], to),
        remote(n1h.at[1 - at["k"]], n1_m, ssem.at[1], rsem.at[1], to),
    ]
    for cp in cps:
        cp.start()
    for cp in cps:
        cp.wait()


def core_swap(dqkv, n1h):
    return pl.pallas_call(
        core_swap_kernel,
        name="core_swap",
        out_shape=[sds(dqkv.shape), sds((ROWS, 512))],
        in_specs=[HBM] * 2,
        out_specs=[HBM] * 2,
        scratch_shapes=[DMA((2,)), DMA((2,))],
        compiler_params=params(7),
    )(dqkv, n1h)


def last_kernel(p0, p1, p2, dx_s, gains, r0, r1, r2, got, gsum, *scratch):
    nb = 3 * PER_STREAM
    bufs, rest = scratch[:nb], scratch[nb:]
    room, ssem, rsem = rest[:3]
    at = where_am_i()
    far = [device(moved(at, a, 2)) for a in "xyz"]
    meet(ring_peers(at) + far + row_peers(at))
    cps = swap_over("row", dx_s, got, *rest[3:6])
    gsum[...] = gains[...]
    waits = []
    for t, a in enumerate("xyz"):
        p = at[a]
        room[t, p] = gsum[...]
        step = []
        for d in (1, 2, 3):
            cp = remote(
                room.at[t, p], room.at[t, p], ssem.at[t, d - 1], rsem.at[t, d - 1],
                device(moved(at, a, d)),
            )
            cp.start()
            step.append(cp)
        for cp in step:
            cp.wait()
        gsum[...] = room[t, 0] + room[t, 1] + room[t, 2] + room[t, 3]
    k = at["k"]
    room[3, k] = gsum[...]
    cp = remote(room.at[3, k], room.at[3, k], ssem.at[3, 0], rsem.at[3, 0], device(mate(at)))
    cp.start()
    cp.wait()
    gsum[...] = room[3, 0] + room[3, 1]
    run_scatter(at, (p0, p1, p2), (r0, r1, r2), bufs, rest[6:])
    for cp in cps:
        cp.wait()


def last(parts, dx_s, gains):
    w = parts[0].shape[-1]
    return pl.pallas_call(
        last_kernel,
        name="last",
        out_shape=[sds((64, w), F32)] * 3 + [sds(dx_s.shape), sds(gains.shape, F32)],
        in_specs=[HBM] * 4 + [VMEM],
        out_specs=[VMEM] * 3 + [HBM, VMEM],
        scratch_shapes=scatter_buffers(w)
        + [pltpu.VMEM((4, 4) + gains.shape, F32), DMA((4, 3)), DMA((4, 3))]
        + swap_sems("row")
        + scatter_sems(),
        compiler_params=params(8),
    )(*parts, dx_s, gains)


def arrive_kernel(t_row, t_col, out, dx, out_o, dx_o):
    _, place = slots_sent(t_row[...], t_col[...])
    pick = onehot(place == iota((ROWS, ROWS), 1))
    out_o[...] = dot(pick, out[...].reshape(ROWS, WIDTH)).astype(BF)
    dx_o[...] = dot(pick, dx[...].reshape(ROWS, WIDTH)).astype(BF)


def arrive(target, out, dx):
    return pl.pallas_call(
        arrive_kernel,
        name="arrive",
        out_shape=[sds((ROWS, WIDTH))] * 2,
        in_specs=[VMEM] * 4,
        out_specs=[VMEM] * 2,
        compiler_params=params(),
    )(target.reshape(1, ROWS), target.reshape(ROWS, 1), out, dx)


def layout(lengths):
    ends = jnp.cumsum(lengths)
    starts = (ends - lengths).astype(I32)
    slots = jnp.arange(GROUP, dtype=I32)
    first = jnp.max(jnp.where(starts[None, :] <= slots[:, None], starts[None, :], 0), axis=1)
    lo = first[::ROWS] // ROWS
    blocks = jnp.arange(NC, dtype=I32)
    hi = jnp.max(jnp.where(lo[None, :] <= blocks[:, None], blocks[None, :], 0), axis=1)
    return first, lo.astype(I32), hi.astype(I32)


def local(
    tokens, grad_out, target, lengths, attn_gain, ffn_gain, q_gain, k_gain,
    w_query, key_matrix, value_matrix, w_out, w_gate, w_up, w_down,
):
    col = lax.axis_index("col")
    first, lo, hi = layout(lengths[0])
    mine = lax.dynamic_slice(first, (col * ROWS,), (ROWS,))
    pos = (col * ROWS + jnp.arange(ROWS, dtype=I32) - mine).astype(F32)
    freq = ROPE_BASE ** (-jnp.arange(HEAD // 2, dtype=F32) * 2.0 / HEAD)
    angles = pos[:, None] * freq[None, :]
    cos, sin = jnp.cos(angles), jnp.sin(angles)
    cos = jnp.concatenate([cos, cos], axis=1)
    sin = jnp.concatenate([-sin, sin], axis=1)
    first2 = first.reshape(NC, 1, ROWS)
    first2 = jnp.concatenate([first2, first2], axis=2)
    again, fgain = attn_gain.reshape(1, WIDTH), ffn_gain.reshape(1, WIDTH)
    qgain, kgain = q_gain.reshape(1, HEAD), k_gain.reshape(1, HEAD)

    w_kv = jnp.concatenate([key_matrix, value_matrix], axis=1)
    tok, grd, slt, wq, wkv, wo = dispatch(target, tokens, grad_out, [w_query, w_kv, w_out.T])
    wg, wu, wd = gather([w_gate, w_up, w_down.T], 2, "gather_ffn")
    qkv, raw, x, dy, n1h, dyh = project(
        slt, tok, grd, again, qgain, kgain, cos, sin, wq, wkv
    )
    qkv = col_swap(qkv, 3, "swap_qkv")
    o, o_t, lse = attend(lo, qkv, first2)
    oa = col_swap(o, 4, "swap_o")
    out_s, dh, dhlh, n2h, act, d_o, gain_f = middle(slt, x, dy, oa, fgain, wo, wg, wu, wd)
    g_o, got_out, act_m, oa_m, n2_m, dy_m, dhl_m = back_swap(
        d_o, out_s, act, oa, n2h, dyh, dhlh
    )
    parts = ffn_grads(n2h, n2_m, dyh, dy_m, act, act_m)
    r_gate, r_up, r_down = scatter(parts, 6, "scatter_ffn")
    dqkv = attend_back(hi, qkv, first2, g_o, o_t, lse)
    dqkv = col_swap(dqkv, 9, "swap_dqkv")
    draw, dx_s, gain_a, gain_qk = project_back(
        slt, x, dh, again, qgain, kgain, cos, sin, raw, dqkv, wq, wkv
    )
    draw_m, n1_m = core_swap(draw, n1h)
    parts = attn_grads(n1h, n1_m, dhlh, dhl_m, draw, draw_m, oa, oa_m)
    gains = jnp.concatenate([gain_a, gain_f, gain_qk, jnp.zeros((1, 768), F32)], axis=1)
    r_q, r_kv, r_o, got_dx, gains = last(parts, dx_s, gains.reshape(24, HEAD))
    output, input_grad = arrive(target, got_out, got_dx)
    gains = gains.reshape(-1)
    return (
        output,
        input_grad,
        gains[0:1024],
        gains[1024:2048],
        gains[2048:2176],
        gains[2176:2304],
        r_q,
        r_kv[:, :HEAD],
        r_kv[:, HEAD:],
        r_o.T,
        r_gate,
        r_up,
        r_down.T,
    )


def solution(mesh):
    both = P(("row", "col"), None)
    by_row, by_col = P("row", "col"), P("col", "row")
    weights = (by_row, by_row, by_row, by_col, by_row, by_row, by_col)
    return jax.shard_map(
        local,
        mesh=mesh,
        in_specs=(both, both, P(("row", "col")), P("row", None), P(), P(), P(), P()) + weights,
        out_specs=(both, both, P(), P(), P(), P()) + weights,
        check_vma=False,
    )
```

```python
import functools
import math

import jax
import jax.numpy as jnp
import numpy as np
from jax import lax
from jax.experimental import pallas as pl
from jax.experimental.pallas import tpu as pltpu
from jax.sharding import PartitionSpec as P

MESH = pl.DeviceIdType.MESH
BF = jnp.bfloat16
F32 = jnp.float32
I32 = jnp.int32
EPSILON = 1e-06
ROPE_BASE = 1000000.0
HEAD = 128
NR = 16
NC = 8
ROWS = 256
WIDTH = 1024
GROUP = 2048
ORDERS = (("x", "y", "z"), ("y", "z", "x"), ("z", "x", "y"))
HBM = pl.BlockSpec(memory_space=pltpu.HBM)
VMEM = pl.BlockSpec(memory_space=pltpu.VMEM)
DMA = pltpu.SemaphoreType.DMA


def sds(shape, dtype=BF):
    return jax.ShapeDtypeStruct(shape, dtype)


def params(cid=None, mib=56, **kw):
    if cid is not None:
        kw.update(collective_id=cid, has_side_effects=True)
    return pltpu.CompilerParams(vmem_limit_bytes=mib << 20, **kw)


def where_am_i():
    r = lax.axis_index("row")
    c = lax.axis_index("col")
    return {"x": c % 4, "y": r // 4, "z": 2 * ((r // 2) % 2) + c // 4, "k": r % 2}


def device(at):
    return (at["y"] * 4 + (at["z"] // 2) * 2 + at["k"], (at["z"] % 2) * 4 + at["x"])


def moved(at, axis, step):
    out = dict(at)
    out[axis] = (at[axis] + step) % 4
    return out


def mate(at):
    out = dict(at)
    out["k"] = 1 - at["k"]
    return out


def meet(peers):
    barrier = pltpu.get_barrier_semaphore()
    for p in peers:
        pl.semaphore_signal(barrier, inc=1, device_id=p, device_id_type=MESH)
    pl.semaphore_wait(barrier, len(peers))


def ring_peers(at):
    return [device(moved(at, a, s)) for a in "xyz" for s in (1, -1)]


def row_peers(at):
    r = lax.axis_index("row")
    c = lax.axis_index("col")
    return [((r + d) % NR, c) for d in range(1, NR)]


def col_peers(at):
    r = lax.axis_index("row")
    c = lax.axis_index("col")
    return [(r, (c + d) % NC) for d in range(1, NC)]


def remote(src, dst, ssem, rsem, to):
    return pltpu.make_async_remote_copy(
        src_ref=src, dst_ref=dst, send_sem=ssem, recv_sem=rsem, device_id=to, device_id_type=MESH
    )


def block_index(sel, with_core=None):
    full = slice(None)
    z = sel.get("z")
    idx = (
        sel.get("x", full),
        full if z is None else z % 2,
        sel.get("y", full),
        full if z is None else z // 2,
    )
    return idx if with_core is None else idx + (with_core,)


SHIFT = (0, -1, 1, 2)


def piece_index(at, s, t, g, rel):
    order = ORDERS[s]
    sel = {a: at[a] for a in order[t + 1 :]}
    if t > 0 and g is not None:
        sel[order[t - 1]] = (at[order[t - 1]] + SHIFT[g]) % 4
    sel[order[t]] = (at[order[t]] + rel) % 4
    return block_index(sel, at["k"])


class Gather:
    def __init__(self, at, outs, sems):
        self.at, self.outs = at, outs
        self.ssem, self.rsem, self.msem, self.nsem = sems
        self.n = len(outs)
        self.half = outs[0].shape[5] // 2
        self.late, self.sent = [], []

    def copies(self, s, t, g):
        ref = self.outs[s].at[piece_index(self.at, s, t, g, 0)]
        a, i = ORDERS[s][t], t * 4 + (g or 0)
        return [
            remote(ref, ref, self.ssem.at[s, i, d], self.rsem.at[s, i, d], device(moved(self.at, a, step)))
            for d, step in enumerate((1, -1))
        ]

    def forwards(self, s, t, g):
        a, i = ORDERS[s][t], t * 4 + (g or 0)
        out = []
        for d, step in enumerate((1, -1)):
            came = piece_index(self.at, s, t, g, -step) + (pl.ds(d * self.half, self.half),)
            ref = self.outs[s].at[came]
            out.append(
                remote(
                    ref,
                    ref,
                    self.ssem.at[s, i, 2 + d],
                    self.rsem.at[s, i, 2 + d],
                    device(moved(self.at, a, step)),
                )
            )
        return out

    def to_mate(self, s, g, rel):
        slot = 4 * (g or 0) + SHIFT.index(rel)
        ref = self.outs[s].at[piece_index(self.at, s, 2, g, rel)]
        return remote(ref, ref, self.msem.at[s, slot], self.nsem.at[s, slot], device(mate(self.at)))

    def share(self, s, g, rel):
        cp = self.to_mate(s, g, rel)
        cp.start()
        self.late.append(cp)

    def send(self, t, g):
        for s in range(self.n):
            for cp in self.copies(s, t, g):
                cp.start()
                self.sent.append(cp)
            if t == 2:
                self.share(s, g, 0)

    def pass_on(self, t, g):
        for s in range(self.n):
            first = self.copies(s, t, g)
            for d, cp in enumerate(self.forwards(s, t, g)):
                first[d].wait_recv()
                cp.start()
                self.sent.append(cp)
                if t == 2:
                    self.share(s, g, (-1, 1)[d])

    def arrived(self, t, g):
        for s in range(self.n):
            for cp in self.forwards(s, t, g):
                cp.wait_recv()
            if t == 2:
                self.share(s, g, 2)

    def drain(self):
        for cp in self.late:
            cp.wait()
        for cp in self.sent:
            cp.wait_send()

    def lines(self):
        self.send(0, None)
        self.send(1, 0)
        yield
        self.pass_on(0, None)
        self.send(1, 1)
        self.send(1, 2)
        yield
        self.pass_on(1, 0)
        self.arrived(0, None)
        self.send(1, 3)
        yield
        self.pass_on(1, 1)
        self.pass_on(1, 2)
        self.pass_on(1, 3)
        yield
        for g in range(4):
            self.arrived(1, g)

    def all(self):
        self.send(0, None)
        self.send(1, 0)
        yield
        self.pass_on(0, None)
        self.send(1, 1)
        self.send(1, 2)
        yield
        self.pass_on(1, 0)
        self.arrived(0, None)
        self.send(1, 3)
        self.send(2, 0)
        yield
        self.pass_on(1, 1)
        self.pass_on(1, 2)
        self.pass_on(1, 3)
        self.send(2, 1)
        self.send(2, 2)
        yield
        self.pass_on(2, 0)
        for g in range(4):
            self.arrived(1, g)
        self.send(2, 3)
        yield
        self.pass_on(2, 1)
        self.pass_on(2, 2)
        yield
        self.pass_on(2, 3)
        yield
        for g in range(4):
            self.arrived(2, g)


def gather_sems(n=3):
    return [DMA((n, 12, 4)), DMA((n, 12, 4)), DMA((n, 16)), DMA((n, 16))]


def plane_sems(n=3):
    return gather_sems(n)


def gather_shape(w):
    return sds((4, 2, 4, 2, 2, 64, w))


def lead_shape(axes):
    out = ()
    for a in ("x", "zl", "y", "zh"):
        if a[0] in axes:
            out += (4,) if a in "xy" else (2,)
    return out


def sub_index(sel, axes):
    out = ()
    for a in ("x", "zl", "y", "zh"):
        if a[0] not in axes:
            continue
        pos = sel.get(a[0])
        if pos is None:
            out += (slice(None),)
        elif a == "zl":
            out += (pos % 2,)
        elif a == "zh":
            out += (pos // 2,)
        else:
            out += (pos,)
    return out


def unravel(i, shape):
    out = ()
    for n in reversed(shape):
        out = (i % n,) + out
        i = i // n
    return out


def add_blocks(lead, dst, terms):
    n = math.prod(lead)

    def one(i):
        j = unravel(i, lead)
        total = None
        for ref, pre in terms:
            v = ref[pre(j)].astype(F32)
            total = v if total is None else total + v
        dst[0][dst[1](j)] = total.astype(dst[0].dtype)

    if n == 1:
        one(0)
    else:

        @pl.loop(0, n)
        def _(i):
            one(i)


def scatter_leads(s, t):
    return lead_shape(ORDERS[s][: 2 - t])


def scatter_buffers(w, t0=0, n=3):
    out = []
    for s in range(n):
        for t in range(t0, 3):
            lead = scatter_leads(s, t)
            out.append(pltpu.VMEM((2,) + lead + (32, w), BF))
            out.append(pltpu.VMEM((2,) + lead + (64, w), BF))
            out.append(pltpu.VMEM((2,) + lead + (32, w), BF))
            out.append(pltpu.VMEM(lead + (64, w), BF))
    return out


def scatter_sems(n=3):
    return [DMA((n, 3, 6)), DMA((n, 3, 6)), DMA((n, 3))]


LO, HI = pl.ds(0, 32), pl.ds(32, 32)


def part_of(s, t, at, rel, rows):
    a = ORDERS[s][2 - t]
    return sub_index({a: (at[a] + rel) % 4}, ORDERS[s][: 3 - t]) + (rows,)


def first_sends(s, t, at, ref, rel_in, piece_in, ssem, rsem):
    a = ORDERS[s][2 - t]
    right, left = device(moved(at, a, 1)), device(moved(at, a, -1))
    allr = (slice(None),) * len(scatter_leads(s, t))

    def src(rel, rows):
        return ref.at[part_of(s, t, at, rel, rows)]

    return [
        remote(src(2, LO), rel_in.at[0], ssem.at[s, t, 0], rsem.at[s, t, 0], right),
        remote(src(2, HI), rel_in.at[1], ssem.at[s, t, 1], rsem.at[s, t, 1], left),
        remote(
            src(1, HI), piece_in.at[(0,) + allr + (HI,)], ssem.at[s, t, 2], rsem.at[s, t, 2], right
        ),
        remote(
            src(-1, LO), piece_in.at[(1,) + allr + (LO,)], ssem.at[s, t, 3], rsem.at[s, t, 3], left
        ),
    ]


def second_send(s, t, at, d, rel_out, piece_in, ssem, rsem):
    a = ORDERS[s][2 - t]
    allr = (slice(None),) * len(scatter_leads(s, t))
    return remote(
        rel_out.at[d],
        piece_in.at[(d,) + allr + ((LO, HI)[d],)],
        ssem.at[s, t, 4 + d],
        rsem.at[s, t, 4 + d],
        device(moved(at, a, (1, -1)[d])),
    )


def side(d):
    return lambda j: (d,) + j


def same(j):
    return j


def run_scatter(at, parts, results, bufs, sems, t0=0):
    ssem, rsem, lsem = sems
    n = len(parts)
    cur = list(parts)
    waits = []
    per = 4 * (3 - t0)
    for t in range(t0, 3):
        st = []
        for s in range(n):
            i = s * per + 4 * (t - t0)
            rel_in, piece_in, rel_out, total = bufs[i : i + 4]
            cps = first_sends(s, t, at, cur[s], rel_in, piece_in, ssem, rsem)
            for cp in cps:
                cp.start()
            loads = []
            if t == t0:
                for j, (rel, rows, dst) in enumerate(
                    ((1, LO, rel_out.at[0]), (-1, HI, rel_out.at[1]), (0, slice(None), total))
                ):
                    cp = pltpu.make_async_copy(
                        cur[s].at[part_of(s, t, at, rel, rows)], dst, lsem.at[s, j]
                    )
                    cp.start()
                    loads.append(cp)
            st.append((rel_in, piece_in, rel_out, total, cps, loads))
        yield
        for s in range(n):
            rel_in, piece_in, rel_out, total, cps, loads = st[s]
            lead = scatter_leads(s, t)
            for d in range(2):
                cps[d].wait_recv()
                if t == t0:
                    loads[d].wait()
                    mine = (rel_out, side(d))
                else:
                    mine = (cur[s], picker(s, t, at, (1, -1)[d], (LO, HI)[d]))
                add_blocks(lead, (rel_out, side(d)), [mine, (rel_in, side(d))])
                cp = second_send(s, t, at, d, rel_out, piece_in, ssem, rsem)
                cp.start()
                cps.append(cp)
        yield
        for s in range(n):
            rel_in, piece_in, rel_out, total, cps, loads = st[s]
            lead = scatter_leads(s, t)
            for i in (2, 3, 4, 5):
                cps[i].wait_recv()
            if t == t0:
                loads[2].wait()
                mine = (total, same)
            else:
                mine = (cur[s], picker(s, t, at, 0, slice(None)))
            dst = (total, same) if t < 2 else (results[s], lambda j: (slice(None),) * 2)
            add_blocks(lead, dst, [mine, (piece_in, side(0)), (piece_in, side(1))])
            cur[s] = total
            waits += cps
    for cp in waits:
        cp.wait_send()


def picker(s, t, at, rel, rows):
    a, axes = ORDERS[s][2 - t], ORDERS[s][: 3 - t]
    pos = (at[a] + rel) % 4

    def pick(j):
        it = iter(j)
        out = ()
        for q in ("x", "zl", "y", "zh"):
            if q[0] not in axes:
                continue
            if q[0] == a:
                out += (pos % 2 if q == "zl" else pos // 2 if q == "zh" else pos,)
            else:
                out += (next(it),)
        return out + (rows,)

    return pick


def in_turn(*steps):
    live = list(steps)
    while live:
        for it in list(live):
            if next(it, "end") == "end":
                live.remove(it)


def swap_over(axis, src, dst, ssem, rsem, lsem):
    n = NR if axis == "row" else NC
    r = lax.axis_index("row")
    c = lax.axis_index("col")
    me = r if axis == "row" else c
    cps = []
    for d in range(1, n):
        to = (me + d) % n
        cp = remote(
            src.at[to],
            dst.at[me],
            ssem.at[d - 1],
            rsem.at[d - 1],
            (to, c) if axis == "row" else (r, to),
        )
        cp.start()
        cps.append(cp)
    own = pltpu.make_async_copy(src.at[me], dst.at[me], lsem)
    own.start()
    return cps + [own]


def swap_sems(axis):
    n = NR if axis == "row" else NC
    return [DMA((n - 1,)), DMA((n - 1,)), DMA]


def col_swap_kernel(src, dst, ssem, rsem, lsem):
    at = where_am_i()
    meet(col_peers(at))
    for cp in swap_over("col", src, dst, ssem, rsem, lsem):
        cp.wait()


def col_swap(src, cid, name):
    return pl.pallas_call(
        col_swap_kernel,
        name=name,
        out_shape=sds(src.shape),
        in_specs=[HBM],
        out_specs=HBM,
        scratch_shapes=swap_sems("col"),
        compiler_params=params(cid),
    )(src)


def dot(a, b, dims=((1,), (0,))):
    return lax.dot_general(a, b, (dims, ((), ())), preferred_element_type=F32)


NT = ((1,), (1,))
TN = ((0,), (0,))


def iota(shape, dim):
    return lax.broadcasted_iota(I32, shape, dim)


def onehot(cond):
    return cond.astype(F32).astype(BF)


def unrope(g, cos, sin):
    return g * cos - pltpu.roll(g, HEAD // 2, 1) * sin


def mean_square_scale(v):
    return lax.rsqrt(jnp.mean(v * v, axis=-1, keepdims=True) + EPSILON)


def column(row):
    eye = iota((ROWS, ROWS), 0) == iota((ROWS, ROWS), 1)
    return jnp.sum(jnp.where(eye, row.astype(F32), 0.0), axis=1, keepdims=True).astype(I32)


def slots_sent(target_row):
    g_row = target_row // GROUP
    g_col = column(g_row)
    same = g_row == g_col
    i0, i1 = iota((ROWS, ROWS), 0), iota((ROWS, ROWS), 1)
    before_row = jnp.sum((same & (i0 < i1)).astype(F32), axis=0, keepdims=True).astype(I32)
    before_col = jnp.sum((same & (i1 < i0)).astype(F32), axis=1, keepdims=True).astype(I32)
    return g_row * (ROWS // NR) + before_row, g_col * (ROWS // NR) + before_col


def dispatch_kernel(
    t_row, tokens, grads, w_q, w_k, w_v, w_o, w_g, w_u, w_d,
    tok, grd, slt, a0, a1, a2, f0, f1, f2,
    tok_s, grd_s, slt_s, own_sem, *sems,
):
    at = where_am_i()
    here = block_index({a: at[a] for a in "xyz"}, at["k"])
    rows = (slice(None),)
    own = [
        (w_q, a0.at[here]),
        (w_k, a1.at[here + rows + (pl.ds(0, HEAD),)]),
        (w_v, a1.at[here + rows + (pl.ds(HEAD, HEAD),)]),
        (w_o, a2.at[here]),
        (w_g, f0.at[here]),
        (w_u, f1.at[here]),
        (w_d, f2.at[here]),
    ]
    own = [pltpu.make_async_copy(src, dst, own_sem.at[i]) for i, (src, dst) in enumerate(own)]
    for cp in own:
        cp.start()
    meet(ring_peers(at) + row_peers(at))
    for cp in own:
        cp.wait()
    first = Gather(at, (a0, a1, a2), sems[9:13])
    second = Gather(at, (f0, f1, f2), sems[13:17])
    steps = first.all()
    more = second.lines()
    next(steps)
    place, _ = slots_sent(t_row[...])
    sel = place == iota((ROWS, ROWS), 0)
    pick = onehot(sel)
    tok_s[...] = dot(pick, tokens[...]).astype(BF).reshape(tok_s.shape)
    slot = jnp.sum(jnp.where(sel, t_row[...], 0).astype(F32), axis=1, keepdims=True)
    slt_s[...] = jnp.broadcast_to(slot, (ROWS, HEAD)).astype(I32).reshape(slt_s.shape)
    cps = swap_over("row", tok_s, tok, *sems[0:3])
    cps += swap_over("row", slt_s, slt, *sems[6:9])
    next(steps)
    grd_s[...] = dot(pick, grads[...]).astype(BF).reshape(grd_s.shape)
    cps += swap_over("row", grd_s, grd, *sems[3:6])
    in_turn(steps, more)
    for cp in cps:
        cp.wait()
    first.drain()
    second.drain()


def dispatch(target, tokens, grads, w_q, w_k, w_v, w_o, w_g, w_u, w_d):
    return pl.pallas_call(
        dispatch_kernel,
        name="dispatch",
        out_shape=[sds((NR, 16, WIDTH))] * 2
        + [sds((NR, 16, HEAD), I32)]
        + [gather_shape(256)] * 3
        + [gather_shape(384)] * 3,
        in_specs=[VMEM] * 3 + [HBM] * 7,
        out_specs=[HBM] * 9,
        scratch_shapes=[pltpu.VMEM((NR, 16, WIDTH), BF)] * 2
        + [pltpu.VMEM((NR, 16, HEAD), I32)]
        + [DMA((7,))]
        + swap_sems("row") * 3
        + gather_sems()
        + gather_sems(),
        compiler_params=params(1),
    )(
        target.reshape(1, ROWS), tokens, grads,
        w_q, w_k, w_v, w_o, w_g, w_u, w_d,
    )


def halves_of(v):
    even, odd = [], []
    low = iota((v.shape[0], HEAD), 1) < HEAD // 2
    for m in range(4):
        a, b = v[:, 256 * m : 256 * m + 128], v[:, 256 * m + 128 : 256 * m + 256]
        even.append(jnp.where(low, a, pltpu.roll(b, 64, 1)))
        odd.append(jnp.where(low, pltpu.roll(a, 64, 1), b))
    return jnp.concatenate(even, axis=1), jnp.concatenate(odd, axis=1)


def first_slots(lens, slots):
    start = jnp.int32(0)
    out = jnp.zeros_like(slots)
    for j in range(8):
        out = jnp.where(slots >= start, start, out)
        start = start + lens(j)
    return out


def project_kernel(
    lens, slt, tok, grd, again, qgain, kgain, freq, wq, wkv, i0, i1, i2,
    out, raw, x_o, dy_o, n1h, dyh, cos, sin, f0, f1, f2, n1_s, *sems,
):
    c = pl.program_id(0)
    at = where_am_i()
    more = Gather(at, (f0, f1, f2), sems)

    @pl.when(c == 0)
    def _():
        meet(ring_peers(at) + [device(mate(at))])
        more.send(2, None)

    @pl.when(c == 0)
    def _():
        slots = lax.axis_index("col") * ROWS + iota((ROWS, HEAD), 0)
        pos = (slots - first_slots(lambda j: lens[0, j], slots)).astype(F32)
        angle = pos * freq[...]
        cos[...] = jnp.cos(angle)
        sine = jnp.sin(angle)
        sin[...] = jnp.where(iota((ROWS, HEAD), 1) < HEAD // 2, -sine, sine)
        local = slt[...].reshape(ROWS, HEAD)[:, :1] % ROWS
        put = onehot(local == iota((ROWS, ROWS), 1))
        x = dot(put, tok[...].reshape(ROWS, WIDTH), TN)
        dy = dot(put, grd[...].reshape(ROWS, WIDTH), TN)
        x_o[...] = x.astype(BF)
        dy_o[...] = dy.astype(BF)
        n1 = x * mean_square_scale(x) * again[...]
        n1_s[...] = n1.astype(BF)
        a, b = halves_of(n1)
        n1h[0] = a.astype(BF)
        n1h[1] = b.astype(BF)
        a, b = halves_of(dy)
        dyh[0] = a.astype(BF)
        dyh[1] = b.astype(BF)

    n1 = n1_s[...]
    q = dot(n1, wq[0, 0].reshape(WIDTH, 256))
    kv = dot(n1, wkv[0, 0].reshape(WIDTH, 256))
    raw[0, :, 0:256] = q
    raw[0, :, 256:384] = kv[:, :HEAD]
    pieces = ((q[:, :HEAD], qgain), (q[:, HEAD:], qgain), (kv[:, :HEAD], kgain))
    for i, (v, gain) in enumerate(pieces):
        n = v * mean_square_scale(v) * gain[...]
        n = n * cos[...] + pltpu.roll(n, HEAD // 2, 1) * sin[...]
        out[0, :, i * HEAD : (i + 1) * HEAD] = n.astype(BF)
    out[0, :, 3 * HEAD :] = kv[:, HEAD:].astype(BF)

    @pl.when(c == NC - 1)
    def _():
        for s in range(3):
            for cp in more.copies(s, 2, None) + [more.to_mate(s, None, 0)]:
                cp.wait()


def slab(w):
    return pl.BlockSpec((1, 1, 4, 2, 2, 64, w), lambda c: (c % 4, c // 4, 0, 0, 0, 0, 0))


def whole(shape):
    return pl.BlockSpec(shape, lambda *_: (0,) * len(shape))


def project(lens, slt, tok, grd, again, qgain, kgain, wq, wkv, planes):
    freq = ROPE_BASE ** (-(np.arange(HEAD) % (HEAD // 2)).astype(np.float32) * 2.0 / HEAD)
    return pl.pallas_call(
        project_kernel,
        name="project",
        grid=(NC,),
        out_shape=[
            sds((NC, ROWS, 512)),
            sds((NC, ROWS, 384), F32),
            sds((ROWS, WIDTH)),
            sds((ROWS, WIDTH)),
            sds((2, ROWS, 512)),
            sds((2, ROWS, 512)),
            sds((ROWS, HEAD), F32),
            sds((ROWS, HEAD), F32),
        ]
        + [gather_shape(384)] * 3,
        in_specs=[
            pl.BlockSpec(memory_space=pltpu.SMEM),
            whole((NR, 16, HEAD)),
            whole((NR, 16, WIDTH)),
            whole((NR, 16, WIDTH)),
            whole((1, WIDTH)),
            whole((1, HEAD)),
            whole((1, HEAD)),
            whole((1, HEAD)),
            slab(256),
            slab(256),
        ]
        + [HBM] * 3,
        out_specs=[
            pl.BlockSpec((1, ROWS, 512), lambda c: (c, 0, 0)),
            pl.BlockSpec((1, ROWS, 384), lambda c: (c, 0, 0)),
            whole((ROWS, WIDTH)),
            whole((ROWS, WIDTH)),
            whole((2, ROWS, 512)),
            whole((2, ROWS, 512)),
            whole((ROWS, HEAD)),
            whole((ROWS, HEAD)),
        ]
        + [HBM] * 3,
        input_output_aliases={10: 8, 11: 9, 12: 10},
        scratch_shapes=[pltpu.VMEM((ROWS, WIDTH), BF)] + gather_sems(),
        compiler_params=params(2),
    )(
        lens, slt, tok, grd, again, qgain, kgain,
        jnp.asarray(freq.astype(np.float32).reshape(1, HEAD)), wq, wkv, *planes,
    )


def heads_kernel(src, i0, i1, i2, dst, f0, f1, f2, *sems):
    at = where_am_i()
    meet(ring_peers(at) + [device(mate(at))] + col_peers(at))
    more = Gather(at, (f0, f1, f2), sems[3:])
    cps = swap_over("col", src, dst, *sems[:3])
    for s in range(3):
        for d, cp in enumerate(more.forwards(s, 2, None)):
            cp.start()
            more.sent.append(cp)
            more.share(s, None, (-1, 1)[d])
    more.arrived(2, None)
    for cp in cps:
        cp.wait()
    more.drain()


def heads(src, planes):
    return pl.pallas_call(
        heads_kernel,
        name="swap_qkv",
        out_shape=[sds(src.shape)] + [gather_shape(384)] * 3,
        in_specs=[HBM] * 4,
        out_specs=[HBM] * 4,
        input_output_aliases={1: 1, 2: 2, 3: 3},
        scratch_shapes=swap_sems("col") + gather_sems(),
        compiler_params=params(3),
    )(src, *planes)


LOG2E = math.log2(math.e)
QK = 512


def stacked(v):
    return jnp.concatenate([v[:, :HEAD], v[:, HEAD : 2 * HEAD]], axis=0)


def group_slots(i):
    return i * ROWS + iota((1, QK), 1) % ROWS


def first_block(lens, i):
    start, out = jnp.int32(0), jnp.int32(0)
    for j in range(8):
        out = jnp.where(start <= i * ROWS, start, out)
        start = start + lens[j]
    return out // ROWS


def last_block(lens, j):
    end, out = jnp.int32(0), jnp.int32(GROUP)
    for n in range(8):
        end = end + lens[n]
        out = jnp.where(end > (j + 1) * ROWS - 1, jnp.minimum(out, end), out)
    return (out - 1) // ROWS


def allowed(i, j, first):
    key = j * ROWS + iota((ROWS, QK), 0)
    query = i * ROWS + iota((ROWS, QK), 1) % ROWS
    return (key <= query) & (key >= first)


def attend_kernel(lens, qkv, out, o_t, lse):
    i = pl.program_id(0)
    scale = HEAD**-0.5 * LOG2E
    q = stacked(qkv[i, :, 0 : 2 * HEAD])
    start = first_slots(lambda j: lens[j], group_slots(i))

    def scores(j):
        s = dot(qkv[j, :, 2 * HEAD : 3 * HEAD], q, NT) * scale
        return jnp.where(allowed(i, j, start), s, -1e30)

    s = scores(i)
    m = jnp.max(s, axis=0, keepdims=True)
    p = jnp.exp2(s - m)
    total = jnp.sum(p, axis=0, keepdims=True)
    acc = dot(qkv[i, :, 3 * HEAD :], p.astype(BF), TN)

    def step(d, carry):
        m, total, acc = carry
        j = i - 1 - d
        s = scores(j)
        m2 = jnp.maximum(m, jnp.max(s, axis=0, keepdims=True))
        fade = jnp.exp2(m - m2)
        p = jnp.exp2(s - m2)
        total = total * fade + jnp.sum(p, axis=0, keepdims=True)
        acc = acc * fade + dot(qkv[j, :, 3 * HEAD :], p.astype(BF), TN)
        return m2, total, acc

    m, total, acc = lax.fori_loop(0, i - first_block(lens, i), step, (m, total, acc))
    o = acc / total
    o_t[0] = o
    lse[0] = m + jnp.log2(total)
    back = o.T
    out[0] = jnp.concatenate([back[:ROWS], back[ROWS:]], axis=1).astype(BF)


def attend(lens, qkv):
    return pl.pallas_call(
        attend_kernel,
        name="attend",
        grid_spec=pltpu.PrefetchScalarGridSpec(
            num_scalar_prefetch=1,
            grid=(NC,),
            in_specs=[
                pl.BlockSpec((NC, ROWS, 512), lambda i, lo: (0, 0, 0)),
            ],
            out_specs=[
                pl.BlockSpec((1, ROWS, 256), lambda i, lo: (i, 0, 0)),
                pl.BlockSpec((1, HEAD, QK), lambda i, lo: (i, 0, 0)),
                pl.BlockSpec((1, 1, QK), lambda i, lo: (i, 0, 0)),
            ],
        ),
        out_shape=[
            sds((NC, ROWS, 256)),
            sds((NC, HEAD, QK), F32),
            sds((NC, 1, QK), F32),
        ],
        compiler_params=params(),
    )(lens, qkv)


def attend_back_kernel(lens, qkv, d_o, o_t, lse, out, qs, dos, delta, dq, first):
    j = pl.program_id(0)
    scale = HEAD**-0.5

    @pl.when(j == 0)
    def _():
        for i in range(NC):
            qs[i] = stacked(qkv[i, :, 0 : 2 * HEAD])
            g = stacked(d_o[i])
            dos[i] = g
            delta[i] = jnp.sum(g.astype(F32).T * o_t[i], axis=0, keepdims=True)
            dq[i] = jnp.zeros((HEAD, QK), F32)
            first[i] = first_slots(lambda n: lens[n], group_slots(i))

    k = qkv[j, :, 2 * HEAD : 3 * HEAD]
    v = qkv[j, :, 3 * HEAD :]
    k_t = k.astype(F32).T.astype(BF)

    def step(i, carry):
        dk, dv = carry
        s = dot(k, qs[i], NT) * (scale * LOG2E) - lse[i]
        p = jnp.where(allowed(i, j, first[i]), jnp.exp2(s), 0.0)
        ds = (p * (dot(v, dos[i], NT) - delta[i]) * scale).astype(BF)
        dv = dv + dot(p.astype(BF), dos[i])
        dk = dk + dot(ds, qs[i])
        dq[i] += dot(k_t, ds)
        return dk, dv

    zero = jnp.zeros((ROWS, HEAD), F32)
    dk, dv = lax.fori_loop(j, last_block(lens, j) + 1, step, (zero, zero))
    done = dq[j].T
    out[0, :, 0:HEAD] = done[:ROWS].astype(BF)
    out[0, :, HEAD : 2 * HEAD] = done[ROWS:].astype(BF)
    out[0, :, 2 * HEAD : 3 * HEAD] = dk.astype(BF)
    out[0, :, 3 * HEAD :] = dv.astype(BF)


def attend_back(lens, qkv, d_o, o_t, lse):
    def full(shape):
        return pl.BlockSpec(shape, lambda j, hi: (0,) * len(shape))

    return pl.pallas_call(
        attend_back_kernel,
        name="attend_back",
        grid_spec=pltpu.PrefetchScalarGridSpec(
            num_scalar_prefetch=1,
            grid=(NC,),
            in_specs=[
                full((NC, ROWS, 512)),
                full((NC, ROWS, 256)),
                full((NC, HEAD, QK)),
                full((NC, 1, QK)),
            ],
            out_specs=pl.BlockSpec((1, ROWS, 512), lambda j, hi: (j, 0, 0)),
            scratch_shapes=[
                pltpu.VMEM((NC, QK, HEAD), BF),
                pltpu.VMEM((NC, QK, HEAD), BF),
                pltpu.VMEM((NC, 1, QK), F32),
                pltpu.VMEM((NC, HEAD, QK), F32),
                pltpu.VMEM((NC, 1, QK), I32),
            ],
        ),
        out_shape=sds((NC, ROWS, 512)),
        compiler_params=params(),
    )(lens, qkv, d_o, o_t, lse)


def middle_kernel(
    slt, x, dy, oa, fgain, wo, wg, wu, wd,
    out_s, dh_o, dhlh, n2h, act, d_o, gain_o,
    h_s, n2_s, acc, dn2, dhl_s,
):
    i = pl.program_id(0)

    @pl.when(i < NC)
    def _():
        part = dot(oa[0], wo[0, 0].reshape(WIDTH, 256), NT)

        @pl.when(i == 0)
        def _():
            acc[...] = x[...].astype(F32) + part

        @pl.when(i > 0)
        def _():
            acc[...] += part

    @pl.when(i == NC)
    def _():
        h = acc[...]
        h_s[...] = h
        n2 = h * mean_square_scale(h) * fgain[...]
        n2_s[...] = n2.astype(BF)
        a, b = halves_of(n2)
        n2h[0] = a.astype(BF)
        n2h[1] = b.astype(BF)
        dn2[...] = jnp.zeros_like(dn2)

    @pl.when((i >= NC) & (i < 2 * NC))
    def _():
        g_w = wg[0, 0].reshape(WIDTH, 384)
        u_w = wu[0, 0].reshape(WIDTH, 384)
        d_w = wd[0, 0].reshape(WIDTH, 384)
        g = dot(n2_s[...], g_w)
        u = dot(n2_s[...], u_w)
        dhid = dot(dy[...], d_w)
        sig = jax.nn.sigmoid(g)
        silu = g * sig
        hid = (silu * u).astype(BF)
        dg = (dhid * u * sig * (1.0 + g * (1.0 - sig))).astype(BF)
        du = (dhid * silu).astype(BF)
        act[0, :, 0:384] = dg
        act[0, :, 384:768] = du
        act[0, :, 768:] = hid
        acc[...] += dot(hid, d_w, NT)
        dn2[...] += dot(dg, g_w, NT) + dot(du, u_w, NT)

    @pl.when(i == 2 * NC - 1)
    def _():
        local = slt[...].reshape(ROWS, HEAD)[:, :1] % ROWS
        take = onehot(local == iota((ROWS, ROWS), 1))
        out_s[...] = dot(take, acc[...].astype(BF)).astype(BF).reshape(out_s.shape)
        h = h_s[...]
        r2 = mean_square_scale(h)
        hn = h * r2
        e = dn2[...]
        gain_o[...] = jnp.sum(e * hn, axis=0, keepdims=True)
        e = e * fgain[...]
        dh = dy[...].astype(F32) + r2 * (e - hn * jnp.mean(e * hn, axis=-1, keepdims=True))
        dh_o[...] = dh
        dhl_s[...] = dh.astype(BF)
        a, b = halves_of(dh)
        dhlh[0] = a.astype(BF)
        dhlh[1] = b.astype(BF)

    @pl.when(i >= 2 * NC)
    def _():
        d_o[0] = dot(dhl_s[...], wo[0, 0].reshape(WIDTH, 256)).astype(BF)


def middle(slt, x, dy, oa, fgain, wo, wg, wu, wd):
    def ffn(w):
        def at(i):
            c = jnp.clip(i - NC, 0, NC - 1)
            return (c % 4, c // 4, 0, 0, 0, 0, 0)

        return pl.BlockSpec((1, 1, 4, 2, 2, 64, w), at)

    def out_at(i):
        c = jnp.where(i < NC, i, jnp.where(i < 2 * NC, NC - 1, i - 2 * NC))
        return (c % 4, c // 4, 0, 0, 0, 0, 0)

    return pl.pallas_call(
        middle_kernel,
        name="middle",
        grid=(3 * NC,),
        out_shape=[
            sds((NR, 16, WIDTH)),
            sds((ROWS, WIDTH), F32),
            sds((2, ROWS, 512)),
            sds((2, ROWS, 512)),
            sds((NC, ROWS, 1152)),
            sds((NC, ROWS, 256)),
            sds((1, WIDTH), F32),
        ],
        in_specs=[
            whole((NR, 16, HEAD)),
            whole((ROWS, WIDTH)),
            whole((ROWS, WIDTH)),
            pl.BlockSpec((1, ROWS, 256), lambda i: (jnp.minimum(i, NC - 1), 0, 0)),
            whole((1, WIDTH)),
            pl.BlockSpec((1, 1, 4, 2, 2, 64, 256), out_at),
            ffn(384),
            ffn(384),
            ffn(384),
        ],
        out_specs=[
            whole((NR, 16, WIDTH)),
            whole((ROWS, WIDTH)),
            whole((2, ROWS, 512)),
            whole((2, ROWS, 512)),
            pl.BlockSpec((1, ROWS, 1152), lambda i: (jnp.clip(i - NC, 0, NC - 1), 0, 0)),
            pl.BlockSpec((1, ROWS, 256), lambda i: (jnp.maximum(i - 2 * NC, 0), 0, 0)),
            whole((1, WIDTH)),
        ],
        scratch_shapes=[
            pltpu.VMEM((ROWS, WIDTH), F32),
            pltpu.VMEM((ROWS, WIDTH), BF),
            pltpu.VMEM((ROWS, WIDTH), F32),
            pltpu.VMEM((ROWS, WIDTH), F32),
            pltpu.VMEM((ROWS, WIDTH), BF),
        ],
        compiler_params=params(),
    )(slt, x, dy, oa, fgain, wo, wg, wu, wd)


def back_swap_kernel(d_o, out_s, act, oa, n2h, dyh, dhlh, *rest):
    outs, sems = rest[:7], rest[7:]
    g_o, got, act_m, oa_m, n2_m, dy_m, dhl_m = outs
    at = where_am_i()
    meet(col_peers(at) + row_peers(at))
    cps = swap_over("col", d_o, g_o, *sems[0:3])
    to = device(mate(at))
    other = 1 - at["k"]
    pairs = (
        (act, act_m),
        (oa, oa_m),
        (n2h.at[other], n2_m),
        (dyh.at[other], dy_m),
        (dhlh.at[other], dhl_m),
    )
    for i, (src, dst) in enumerate(pairs):
        cp = remote(src, dst, sems[6].at[i], sems[7].at[i], to)
        cp.start()
        cps.append(cp)
    cps += swap_over("row", out_s, got, *sems[3:6])
    for cp in cps:
        cp.wait()


def back_swap(d_o, out_s, act, oa, n2h, dyh, dhlh):
    return pl.pallas_call(
        back_swap_kernel,
        name="back_swap",
        out_shape=[sds(d_o.shape), sds(out_s.shape), sds(act.shape), sds(oa.shape)]
        + [sds((ROWS, 512))] * 3,
        in_specs=[HBM] * 7,
        out_specs=[HBM] * 7,
        scratch_shapes=swap_sems("col") + swap_sems("row") + [DMA((5,)), DMA((5,))],
        compiler_params=params(5),
    )(d_o, out_s, act, oa, n2h, dyh, dhlh)


def stack_tokens(k, mine, others, scratch):
    scratch[:, 0:ROWS] = mine[k].astype(F32).T.astype(BF)
    scratch[:, ROWS:] = others[...].astype(F32).T.astype(BF)


def ffn_grads_kernel(n2h, n2_m, dyh, dy_m, act, act_m, g0, g1, g2, n_s, y_s):
    c = pl.program_id(0)

    @pl.when(c == 0)
    def _():
        k = lax.axis_index("row") % 2
        stack_tokens(k, n2h, n2_m, n_s)
        stack_tokens(k, dyh, dy_m, y_s)

    for i, (lhs, out) in enumerate(((n_s, g0), (n_s, g1), (y_s, g2))):
        cols = slice(384 * i, 384 * i + 384)
        rhs = jnp.concatenate([act[0, :, cols], act_m[0, :, cols]], axis=0)
        out[0, 0] = dot(lhs[...], rhs).astype(BF).reshape(4, 2, 64, 384)


def grad_slab(w):
    return pl.BlockSpec((1, 1, 4, 2, 64, w), lambda c: (c % 4, c // 4, 0, 0, 0, 0))


def ffn_grads(n2h, n2_m, dyh, dy_m, act, act_m):
    one = pl.BlockSpec((1, ROWS, 1152), lambda c: (c, 0, 0))
    return pl.pallas_call(
        ffn_grads_kernel,
        name="ffn_grads",
        grid=(NC,),
        out_shape=[sds((4, 2, 4, 2, 64, 384))] * 3,
        in_specs=[whole((2, ROWS, 512)), whole((ROWS, 512))] * 2 + [one, one],
        out_specs=[grad_slab(384)] * 3,
        scratch_shapes=[pltpu.VMEM((512, 2 * ROWS), BF)] * 2,
        compiler_params=params(),
    )(n2h, n2_m, dyh, dy_m, act, act_m)


def attn_grads_kernel(n1h, n1_m, dhlh, dhl_m, dqkv, dqkv_m, oa, oa_m, g0, g1, g2, n_s, h_s):
    c = pl.program_id(0)

    @pl.when(c == 0)
    def _():
        k = lax.axis_index("row") % 2
        stack_tokens(k, n1h, n1_m, n_s)
        stack_tokens(k, dhlh, dhl_m, h_s)

    for i, (lhs, mine, others, out) in enumerate(
        ((n_s, dqkv, dqkv_m, g0), (n_s, dqkv, dqkv_m, g1), (h_s, oa, oa_m, g2))
    ):
        cols = slice(256 * i, 256 * i + 256) if i < 2 else slice(0, 256)
        rhs = jnp.concatenate([mine[0, :, cols], others[0, :, cols]], axis=0)
        out[0, 0] = dot(lhs[...], rhs).astype(BF).reshape(4, 2, 64, 256)


def attn_grads(n1h, n1_m, dhlh, dhl_m, dqkv, dqkv_m, oa, oa_m):
    def one(w):
        return pl.BlockSpec((1, ROWS, w), lambda c: (c, 0, 0))

    return pl.pallas_call(
        attn_grads_kernel,
        name="attn_grads",
        grid=(NC,),
        out_shape=[sds((4, 2, 4, 2, 64, 256))] * 3,
        in_specs=[whole((2, ROWS, 512)), whole((ROWS, 512))] * 2
        + [one(512), one(512), one(256), one(256)],
        out_specs=[grad_slab(256)] * 3,
        scratch_shapes=[pltpu.VMEM((512, 2 * ROWS), BF)] * 2,
        compiler_params=params(),
    )(n1h, n1_m, dhlh, dhl_m, dqkv, dqkv_m, oa, oa_m)


def later_shapes():
    leads = [scatter_leads(s, 0) for s in range(3)]
    return [sds((2,) + n + (32, 384)) for n in leads], [sds((2,) + n + (64, 384)) for n in leads]


def heads_back_kernel(src, p0, p1, p2, dst, *rest):
    rel_in, piece_in, sems = rest[0:3], rest[3:6], rest[6:]
    at = where_am_i()
    meet(ring_peers(at) + col_peers(at))
    cps = swap_over("col", src, dst, *sems[:3])
    for s, p in enumerate((p0, p1, p2)):
        more = first_sends(s, 0, at, p, rel_in[s], piece_in[s], sems[3], sems[4])
        for cp in more:
            cp.start()
        cps += more
    for cp in cps:
        cp.wait()


def heads_back(src, parts):
    rel, piece = later_shapes()
    return pl.pallas_call(
        heads_back_kernel,
        name="swap_dqkv",
        out_shape=[sds(src.shape)] + rel + piece,
        in_specs=[HBM] * 4,
        out_specs=[HBM] * 7,
        scratch_shapes=swap_sems("col") + scatter_sems()[:2],
        compiler_params=params(6),
    )(src, *parts)


def project_back_kernel(
    slt, x, dh, again, qgain, kgain, cos, sin, raw, dqkv, wq, wkv, p0, p1, p2, r0, r1, r2, i0, i1, i2,
    d_o, dx_s, gain_o, qk_o, q0, q1, q2, acc, gq, gk, *rest,
):
    c = pl.program_id(0)
    at = where_am_i()
    rel_v, own_v, (ssem, rsem, lsem) = rest[0:3], rest[3:6], rest[6:]
    parts, rel_in, piece_in = (p0, p1, p2), (r0, r1, r2), (q0, q1, q2)

    def loads(s):
        out = [pltpu.make_async_copy(rel_in[s], rel_v[s], lsem.at[s, 0])]
        for d, (rel, rows) in enumerate(((1, LO), (-1, HI))):
            src = parts[s].at[part_of(s, 0, at, rel, rows)]
            out.append(pltpu.make_async_copy(src, own_v[s].at[d], lsem.at[s, 1 + d]))
        return out

    def sends(s):
        return [second_send(s, 0, at, d, own_v[s], piece_in[s], ssem, rsem) for d in range(2)]

    @pl.when(c == 0)
    def _():
        for s in range(3):
            for cp in loads(s):
                cp.start()
        meet(ring_peers(at))

    @pl.when(c == 1)
    def _():
        for s in range(3):
            for cp in loads(s):
                cp.wait()
            lead = (2,) + scatter_leads(s, 0)
            add_blocks(lead, (own_v[s], same), [(own_v[s], same), (rel_v[s], same)])
            for cp in sends(s):
                cp.start()

    @pl.when(c == 0)
    def _():
        acc[...] = jnp.zeros_like(acc)
        gq[...] = jnp.zeros_like(gq)
        gk[...] = jnp.zeros_like(gk)

    for i, (gain, g_acc) in enumerate(((qgain, gq), (qgain, gq), (kgain, gk))):
        cols = slice(i * HEAD, (i + 1) * HEAD)
        v = raw[0, :, cols]
        r = mean_square_scale(v)
        xn = v * r
        dn = unrope(dqkv[0, :, cols].astype(F32), cos[...], sin[...])
        g_acc[...] += jnp.sum(dn * xn, axis=0, keepdims=True)
        e = dn * gain[...]
        d_o[0, :, cols] = (r * (e - xn * jnp.mean(e * xn, axis=-1, keepdims=True))).astype(BF)
    d_o[0, :, 3 * HEAD :] = dqkv[0, :, 3 * HEAD :]
    acc[...] += dot(d_o[0, :, 0:256], wq[0, 0].reshape(WIDTH, 256), NT) + dot(
        d_o[0, :, 256:512], wkv[0, 0].reshape(WIDTH, 256), NT
    )

    @pl.when(c == NC - 1)
    def _():
        xv = x[...].astype(F32)
        r1 = mean_square_scale(xv)
        xn = xv * r1
        e = acc[...]
        gain_o[...] = jnp.sum(e * xn, axis=0, keepdims=True)
        e = e * again[...]
        dx = dh[...] + r1 * (e - xn * jnp.mean(e * xn, axis=-1, keepdims=True))
        local = slt[...].reshape(ROWS, HEAD)[:, :1] % ROWS
        take = onehot(local == iota((ROWS, ROWS), 1))
        dx_s[...] = dot(take, dx.astype(BF)).astype(BF).reshape(dx_s.shape)
        qk_o[...] = jnp.concatenate([gq[...], gk[...]], axis=1)
        for s in range(3):
            for cp in sends(s):
                cp.wait()


def project_back(slt, x, dh, again, qgain, kgain, cos, sin, raw, dqkv, wq, wkv, parts, rel, piece):
    return pl.pallas_call(
        project_back_kernel,
        name="project_back",
        grid=(NC,),
        out_shape=[
            sds((NC, ROWS, 512)),
            sds((NR, 16, WIDTH)),
            sds((1, WIDTH), F32),
            sds((1, 2 * HEAD), F32),
        ]
        + later_shapes()[1],
        in_specs=[
            whole((NR, 16, HEAD)),
            whole((ROWS, WIDTH)),
            whole((ROWS, WIDTH)),
            whole((1, WIDTH)),
            whole((1, HEAD)),
            whole((1, HEAD)),
            whole((ROWS, HEAD)),
            whole((ROWS, HEAD)),
            pl.BlockSpec((1, ROWS, 384), lambda c: (c, 0, 0)),
            pl.BlockSpec((1, ROWS, 512), lambda c: (c, 0, 0)),
            slab(256),
            slab(256),
        ]
        + [HBM] * 9,
        out_specs=[
            pl.BlockSpec((1, ROWS, 512), lambda c: (c, 0, 0)),
            whole((NR, 16, WIDTH)),
            whole((1, WIDTH)),
            whole((1, 2 * HEAD)),
        ]
        + [HBM] * 3,
        input_output_aliases={18: 4, 19: 5, 20: 6},
        scratch_shapes=[
            pltpu.VMEM((ROWS, WIDTH), F32),
            pltpu.VMEM((1, HEAD), F32),
            pltpu.VMEM((1, HEAD), F32),
        ]
        + [pltpu.VMEM(r.shape, BF) for r in later_shapes()[0]] * 2
        + scatter_sems(),
        compiler_params=params(7),
    )(slt, x, dh, again, qgain, kgain, cos, sin, raw, dqkv, wq, wkv, *parts, *rel, *piece)


def core_swap_kernel(dqkv, n1h, p0, p1, p2, q0, q1, q2, dqkv_m, n1_m, s0, s1, s2, *rest):
    own_v, piece_v, (ssem, rsem, lsem, osem) = rest[0:3], rest[3:6], rest[6:]
    at = where_am_i()
    loads = []
    for s, (p, q) in enumerate(((p0, q0), (p1, q1), (p2, q2))):
        src = p.at[part_of(s, 0, at, 0, slice(None))]
        pair = [
            pltpu.make_async_copy(src, own_v[s], lsem.at[s, 0]),
            pltpu.make_async_copy(q, piece_v[s], lsem.at[s, 1]),
        ]
        for cp in pair:
            cp.start()
        loads.append(pair)
    to = device(mate(at))
    meet([to])
    cps = [
        remote(dqkv, dqkv_m, ssem.at[0], rsem.at[0], to),
        remote(n1h.at[1 - at["k"]], n1_m, ssem.at[1], rsem.at[1], to),
    ]
    for cp in cps:
        cp.start()
    for s, out in enumerate((s0, s1, s2)):
        for cp in loads[s]:
            cp.wait()
        lead = scatter_leads(s, 0)
        terms = [(own_v[s], same), (piece_v[s], side(0)), (piece_v[s], side(1))]
        add_blocks(lead, (own_v[s], same), terms)
        cp = pltpu.make_async_copy(own_v[s], out, osem.at[s])
        cp.start()
        cps.append(cp)
    for cp in cps:
        cp.wait()


def core_swap(dqkv, n1h, parts, piece):
    sums = [sds(scatter_leads(s, 0) + (64, 384)) for s in range(3)]
    return pl.pallas_call(
        core_swap_kernel,
        name="core_swap",
        out_shape=[sds(dqkv.shape), sds((ROWS, 512))] + sums,
        in_specs=[HBM] * 8,
        out_specs=[HBM] * 5,
        scratch_shapes=[pltpu.VMEM(r.shape, BF) for r in sums]
        + [pltpu.VMEM(r.shape, BF) for r in later_shapes()[1]]
        + [DMA((2,)), DMA((2,)), DMA((3, 2)), DMA((3,))],
        compiler_params=params(8),
    )(dqkv, n1h, *parts, *piece)


def gain_steps(at, pieces, room, total, ssem, rsem):
    p = at["x"]
    lane = 0
    for ref in pieces:
        room[0, p, :, lane : lane + ref.shape[1]] = ref[...]
        lane += ref.shape[1]
    for t, a in enumerate("xyzk"):
        p = at[a]
        others = (1, 2, 3) if a != "k" else (1,)
        if t > 0:
            room[t, p] = total[...]
        step = []
        for d in others:
            to = device(moved(at, a, d)) if a != "k" else device(mate(at))
            sems = ssem.at[t, d - 1], rsem.at[t, d - 1]
            cp = remote(room.at[t, p], room.at[t, p], *sems, to)
            cp.start()
            step.append(cp)
        yield
        for cp in step:
            cp.wait()
        acc = room[t, 0]
        for j in range(1, len(others) + 1):
            acc = acc + room[t, j]
        total[...] = acc


def last_kernel(
    p0, p1, p2, s0, s1, s2, dx_s, ga, gf, gqk, r0, r1, r2, t0, t1, t2, got, gsum, *scratch
):
    na, nf = len(scatter_buffers(256)), len(scatter_buffers(384, 1))
    bufs, more, rest = scratch[:na], scratch[na : na + nf], scratch[na + nf :]
    at = where_am_i()
    far = [device(moved(at, a, 2)) for a in "xyz"]
    meet(ring_peers(at) + far + row_peers(at))
    cps = []

    def rows():
        yield
        cps.extend(swap_over("row", dx_s, got, *rest[3:6]))

    in_turn(
        run_scatter(at, (p0, p1, p2), (r0, r1, r2), bufs, rest[6:9]),
        rows(),
        gain_steps(at, (ga, gf, gqk), rest[0], gsum, rest[1], rest[2]),
        run_scatter(at, (s0, s1, s2), (t0, t1, t2), more, rest[9:12], 1),
    )
    for cp in cps:
        cp.wait()


def last(parts, sums, dx_s, gains):
    total = 2 * WIDTH + 2 * HEAD
    return pl.pallas_call(
        last_kernel,
        name="last",
        out_shape=[sds((64, 256), F32)] * 3
        + [sds((64, 384), F32)] * 3
        + [sds(dx_s.shape), sds((1, total), F32)],
        in_specs=[HBM] * 7 + [VMEM] * 3,
        out_specs=[VMEM] * 6 + [HBM, VMEM],
        scratch_shapes=scatter_buffers(256)
        + scatter_buffers(384, 1)
        + [pltpu.VMEM((4, 4, 1, total), F32), DMA((4, 3)), DMA((4, 3))]
        + swap_sems("row")
        + scatter_sems()
        + scatter_sems(),
        compiler_params=params(9),
    )(*parts, *sums, dx_s, *gains)


def arrive_kernel(
    t_row, out, dx, q, kv, o, g, u, d, gains,
    out_o, dx_o, ga, gf, gq, gk, q_o, k_o, v_o, o_o, g_o, u_o, d_o,
):
    _, place = slots_sent(t_row[...])
    pick = onehot(place == iota((ROWS, ROWS), 1))
    out_o[...] = dot(pick, out[...].reshape(ROWS, WIDTH)).astype(BF)
    dx_o[...] = dot(pick, dx[...].reshape(ROWS, WIDTH)).astype(BF)
    ga[...] = gains[:, 0:WIDTH]
    gf[...] = gains[:, WIDTH : 2 * WIDTH]
    gq[...] = gains[:, 2 * WIDTH : 2 * WIDTH + HEAD]
    gk[...] = gains[:, 2 * WIDTH + HEAD :]
    q_o[...] = q[...]
    k_o[...] = kv[:, :HEAD]
    v_o[...] = kv[:, HEAD:]
    o_o[...] = o[...]
    g_o[...] = g[...]
    u_o[...] = u[...]
    d_o[...] = d[...]


def arrive(target, *args):
    return pl.pallas_call(
        arrive_kernel,
        name="arrive",
        out_shape=[sds((ROWS, WIDTH))] * 2
        + [sds((1, n), F32) for n in (WIDTH, WIDTH, HEAD, HEAD)]
        + [
            sds(n, F32)
            for n in ((64, 256), (64, 128), (64, 128), (64, 256), (64, 384), (64, 384), (64, 384))
        ],
        in_specs=[VMEM] * 10,
        out_specs=[VMEM] * 13,
        compiler_params=params(),
    )(target.reshape(1, ROWS), *args)


def local(
    tokens, grad_out, target, lengths, attn_gain, ffn_gain, q_gain, k_gain,
    w_query, key_matrix, value_matrix, w_out, w_gate, w_up, w_down,
):
    again, fgain = attn_gain.reshape(1, WIDTH), ffn_gain.reshape(1, WIDTH)
    qgain, kgain = q_gain.reshape(1, HEAD), k_gain.reshape(1, HEAD)
    lens = lengths[0]

    tok, grd, slt, wq, wkv, wo, *planes = dispatch(
        target, tokens, grad_out, w_query, key_matrix, value_matrix, w_out.T, w_gate, w_up, w_down.T
    )
    qkv, raw, x, dy, n1h, dyh, cos, sin, *planes = project(
        lengths, slt, tok, grd, again, qgain, kgain, wq, wkv, planes
    )
    qkv, wg, wu, wd = heads(qkv, planes)
    o, o_t, lse = attend(lens, qkv)
    oa = col_swap(o, 4, "swap_o")
    out_s, dh, dhlh, n2h, act, d_o, gain_f = middle(slt, x, dy, oa, fgain, wo, wg, wu, wd)
    g_o, got_out, act_m, oa_m, n2_m, dy_m, dhl_m = back_swap(
        d_o, out_s, act, oa, n2h, dyh, dhlh
    )
    f_parts = ffn_grads(n2h, n2_m, dyh, dy_m, act, act_m)
    dqkv = attend_back(lens, qkv, g_o, o_t, lse)
    dqkv, *later = heads_back(dqkv, f_parts)
    draw, dx_s, gain_a, gain_qk, *piece = project_back(
        slt, x, dh, again, qgain, kgain, cos, sin, raw, dqkv, wq, wkv,
        f_parts, later[:3], later[3:],
    )
    draw_m, n1_m, *sums = core_swap(draw, n1h, f_parts, piece)
    a_parts = attn_grads(n1h, n1_m, dhlh, dhl_m, draw, draw_m, oa, oa_m)
    r_q, r_kv, r_o, r_g, r_u, r_d, got_dx, gains = last(
        a_parts, sums, dx_s, (gain_a, gain_f, gain_qk)
    )
    output, input_grad, ga, gf, gq, gk, g_q, g_k, g_v, g_o, g_g, g_u, g_d = arrive(
        target, got_out, got_dx, r_q, r_kv, r_o, r_g, r_u, r_d, gains
    )
    return (
        output, input_grad, ga[0], gf[0], gq[0], gk[0], g_q, g_k, g_v, g_o.T, g_g, g_u, g_d.T,
    )


def solution(mesh):
    both = P(("row", "col"), None)
    by_row, by_col = P("row", "col"), P("col", "row")
    weights = (by_row, by_row, by_row, by_col, by_row, by_row, by_col)
    return jax.shard_map(
        local,
        mesh=mesh,
        in_specs=(both, both, P(("row", "col")), P("row", None), P(), P(), P(), P()) + weights,
        out_specs=(both, both, P(), P(), P(), P()) + weights,
        check_vma=False,
    )
```

```python
import functools
import math

import jax
import jax.numpy as jnp
import numpy as np
from jax import lax
from jax.experimental import pallas as pl
from jax.experimental.pallas import tpu as pltpu
from jax.sharding import PartitionSpec as P

MESH = pl.DeviceIdType.MESH
BF = jnp.bfloat16
F32 = jnp.float32
I32 = jnp.int32
EPSILON = 1e-06
ROPE_BASE = 1000000.0
HEAD = 128
NR = 16
NC = 8
ROWS = 256
WIDTH = 1024
GROUP = 2048
ORDERS = (("x", "y", "z"), ("y", "z", "x"), ("z", "x", "y"))
HBM = pl.BlockSpec(memory_space=pltpu.HBM)
VMEM = pl.BlockSpec(memory_space=pltpu.VMEM)
DMA = pltpu.SemaphoreType.DMA


def sds(shape, dtype=BF):
    return jax.ShapeDtypeStruct(shape, dtype)


def params(cid=None, mib=56, **kw):
    if cid is not None:
        kw.update(collective_id=cid, has_side_effects=True)
    return pltpu.CompilerParams(vmem_limit_bytes=mib << 20, **kw)


def where_am_i():
    r = lax.axis_index("row")
    c = lax.axis_index("col")
    return {"x": c % 4, "y": r // 4, "z": 2 * ((r // 2) % 2) + c // 4, "k": r % 2}


def device(at):
    return (at["y"] * 4 + (at["z"] // 2) * 2 + at["k"], (at["z"] % 2) * 4 + at["x"])


def moved(at, axis, step):
    out = dict(at)
    out[axis] = (at[axis] + step) % 4
    return out


def mate(at):
    out = dict(at)
    out["k"] = 1 - at["k"]
    return out


def meet(peers):
    barrier = pltpu.get_barrier_semaphore()
    for p in peers:
        pl.semaphore_signal(barrier, inc=1, device_id=p, device_id_type=MESH)
    pl.semaphore_wait(barrier, len(peers))


def ring_peers(at):
    return [device(moved(at, a, s)) for a in "xyz" for s in (1, -1)]


def row_peers(at):
    r = lax.axis_index("row")
    c = lax.axis_index("col")
    return [((r + d) % NR, c) for d in range(1, NR)]


def col_peers(at):
    r = lax.axis_index("row")
    c = lax.axis_index("col")
    return [(r, (c + d) % NC) for d in range(1, NC)]


def remote(src, dst, ssem, rsem, to):
    return pltpu.make_async_remote_copy(
        src_ref=src, dst_ref=dst, send_sem=ssem, recv_sem=rsem, device_id=to, device_id_type=MESH
    )


def block_index(sel, with_core=None):
    full = slice(None)
    z = sel.get("z")
    idx = (
        sel.get("x", full),
        full if z is None else z % 2,
        sel.get("y", full),
        full if z is None else z // 2,
    )
    return idx if with_core is None else idx + (with_core,)


SHIFT = (0, -1, 1, 2)


def piece_index(at, s, t, g, rel):
    order = ORDERS[s]
    sel = {a: at[a] for a in order[t + 1 :]}
    if t > 0 and g is not None:
        sel[order[t - 1]] = (at[order[t - 1]] + SHIFT[g]) % 4
    sel[order[t]] = (at[order[t]] + rel) % 4
    return block_index(sel, at["k"])


class Gather:
    def __init__(self, at, outs, sems, phases=(0, 1, 2), own=None):
        self.at, self.outs, self.own = at, outs, own
        self.base = {t: sum(4 if p == 0 else 16 for p in phases if p < t) for t in phases}
        self.ssem, self.rsem, self.msem, self.nsem = sems
        self.n = len(outs)
        self.half = outs[0].shape[5] // 2
        self.late, self.sent = [], []

    def copies(self, s, t, g):
        ref = self.outs[s].at[piece_index(self.at, s, t, g, 0)]
        a, i = ORDERS[s][t], self.base[t] + 4 * (g or 0)
        src = self.own[s] if self.own and (t == 0 or (t == 1 and g == 0)) else ref
        return [
            remote(src, ref, self.ssem.at[s, i + d], self.rsem.at[s, i + d], device(moved(self.at, a, step)))
            for d, step in enumerate((1, -1))
        ]

    def forwards(self, s, t, g):
        a, i = ORDERS[s][t], self.base[t] + 4 * (g or 0) + 2
        out = []
        for d, step in enumerate((1, -1)):
            came = piece_index(self.at, s, t, g, -step) + (pl.ds(d * self.half, self.half),)
            ref = self.outs[s].at[came]
            out.append(
                remote(
                    ref,
                    ref,
                    self.ssem.at[s, i + d],
                    self.rsem.at[s, i + d],
                    device(moved(self.at, a, step)),
                )
            )
        return out

    def to_mate(self, s, g, rel):
        slot = 4 * (g or 0) + SHIFT.index(rel)
        ref = self.outs[s].at[piece_index(self.at, s, 2, g, rel)]
        return remote(ref, ref, self.msem.at[s, slot], self.nsem.at[s, slot], device(mate(self.at)))

    def share(self, s, g, rel):
        cp = self.to_mate(s, g, rel)
        cp.start()
        self.late.append(cp)

    def send(self, t, g):
        for s in range(self.n):
            for cp in self.copies(s, t, g):
                cp.start()
                self.sent.append(cp)
            if t == 2:
                self.share(s, g, 0)

    def pass_on(self, t, g):
        for s in range(self.n):
            first = self.copies(s, t, g)
            for d, cp in enumerate(self.forwards(s, t, g)):
                first[d].wait_recv()
                cp.start()
                self.sent.append(cp)
                if t == 2:
                    self.share(s, g, (-1, 1)[d])

    def arrived(self, t, g):
        for s in range(self.n):
            for cp in self.forwards(s, t, g):
                cp.wait_recv()
            if t == 2:
                self.share(s, g, 2)

    def drain(self):
        for cp in self.late:
            cp.wait()
        for cp in self.sent:
            cp.wait_send()

    def lines(self):
        self.send(0, None)
        self.send(1, 0)
        yield
        self.pass_on(0, None)
        self.send(1, 1)
        self.send(1, 2)
        yield
        self.pass_on(1, 0)
        self.arrived(0, None)
        self.send(1, 3)
        yield
        self.pass_on(1, 1)
        self.pass_on(1, 2)
        self.pass_on(1, 3)
        yield
        for g in range(4):
            self.arrived(1, g)

    def all(self):
        self.send(0, None)
        self.send(1, 0)
        yield
        self.pass_on(0, None)
        self.send(1, 1)
        self.send(1, 2)
        yield
        self.pass_on(1, 0)
        self.arrived(0, None)
        self.send(1, 3)
        self.send(2, 0)
        yield
        self.pass_on(1, 1)
        self.pass_on(1, 2)
        self.pass_on(1, 3)
        self.send(2, 1)
        self.send(2, 2)
        yield
        self.pass_on(2, 0)
        for g in range(4):
            self.arrived(1, g)
        self.send(2, 3)
        yield
        self.pass_on(2, 1)
        self.pass_on(2, 2)
        yield
        self.pass_on(2, 3)
        yield
        for g in range(4):
            self.arrived(2, g)


def gather_sems(steps, shares, n=3):
    return [DMA((n, steps)), DMA((n, steps)), DMA((n, max(shares, 1))), DMA((n, max(shares, 1)))]


def gather_shape(w):
    return sds((4, 2, 4, 2, 2, 64, w))


def lead_shape(axes):
    out = ()
    for a in ("x", "zl", "y", "zh"):
        if a[0] in axes:
            out += (4,) if a in "xy" else (2,)
    return out


def sub_index(sel, axes):
    out = ()
    for a in ("x", "zl", "y", "zh"):
        if a[0] not in axes:
            continue
        pos = sel.get(a[0])
        if pos is None:
            out += (slice(None),)
        elif a == "zl":
            out += (pos % 2,)
        elif a == "zh":
            out += (pos // 2,)
        else:
            out += (pos,)
    return out


def unravel(i, shape):
    out = ()
    for n in reversed(shape):
        out = (i % n,) + out
        i = i // n
    return out


def add_blocks(lead, dst, terms):
    n = math.prod(lead)

    def one(i):
        j = unravel(i, lead)
        total = None
        for ref, pre in terms:
            v = ref[pre(j)].astype(F32)
            total = v if total is None else total + v
        dst[0][dst[1](j)] = total.astype(dst[0].dtype)

    if n == 1:
        one(0)
    else:

        @pl.loop(0, n)
        def _(i):
            one(i)


def scatter_leads(s, t):
    return lead_shape(ORDERS[s][: 2 - t])


def scatter_buffers(w, t0=0, n=3):
    out = []
    for s in range(n):
        for t in range(t0, 3):
            lead = scatter_leads(s, t)
            out.append(pltpu.VMEM((2,) + lead + (32, w), BF))
            out.append(pltpu.VMEM((2,) + lead + (64, w), BF))
            out.append(pltpu.VMEM((2,) + lead + (32, w), BF))
            out.append(pltpu.VMEM(lead + (64, w), BF))
    return out


def scatter_sems(phases=3, n=3):
    return [DMA((n, phases, 6)), DMA((n, phases, 6)), DMA((n, 3))]


LO, HI = pl.ds(0, 32), pl.ds(32, 32)


def part_of(s, t, at, rel, rows):
    a = ORDERS[s][2 - t]
    return sub_index({a: (at[a] + rel) % 4}, ORDERS[s][: 3 - t]) + (rows,)


def first_sends(s, t, at, ref, rel_in, piece_in, ssem, rsem, t0=0):
    a = ORDERS[s][2 - t]
    right, left = device(moved(at, a, 1)), device(moved(at, a, -1))
    allr = (slice(None),) * len(scatter_leads(s, t))

    def src(rel, rows):
        return ref.at[part_of(s, t, at, rel, rows)]

    return [
        remote(src(2, LO), rel_in.at[0], ssem.at[s, t - t0, 0], rsem.at[s, t - t0, 0], right),
        remote(src(2, HI), rel_in.at[1], ssem.at[s, t - t0, 1], rsem.at[s, t - t0, 1], left),
        remote(
            src(1, HI), piece_in.at[(0,) + allr + (HI,)], ssem.at[s, t - t0, 2], rsem.at[s, t - t0, 2], right
        ),
        remote(
            src(-1, LO), piece_in.at[(1,) + allr + (LO,)], ssem.at[s, t - t0, 3], rsem.at[s, t - t0, 3], left
        ),
    ]


def second_send(s, t, at, d, rel_out, piece_in, ssem, rsem, t0=0):
    a = ORDERS[s][2 - t]
    allr = (slice(None),) * len(scatter_leads(s, t))
    return remote(
        rel_out.at[d],
        piece_in.at[(d,) + allr + ((LO, HI)[d],)],
        ssem.at[s, t - t0, 4 + d],
        rsem.at[s, t - t0, 4 + d],
        device(moved(at, a, (1, -1)[d])),
    )


def side(d):
    return lambda j: (d,) + j


def same(j):
    return j


def run_scatter(at, parts, results, bufs, sems, t0=0):
    ssem, rsem, lsem = sems
    n = len(parts)
    cur = list(parts)
    waits = []
    per = 4 * (3 - t0)
    for t in range(t0, 3):
        st = []
        for s in range(n):
            i = s * per + 4 * (t - t0)
            rel_in, piece_in, rel_out, total = bufs[i : i + 4]
            cps = first_sends(s, t, at, cur[s], rel_in, piece_in, ssem, rsem, t0)
            for cp in cps:
                cp.start()
            loads = []
            if t == t0:
                for j, (rel, rows, dst) in enumerate(
                    ((1, LO, rel_out.at[0]), (-1, HI, rel_out.at[1]), (0, slice(None), total))
                ):
                    cp = pltpu.make_async_copy(
                        cur[s].at[part_of(s, t, at, rel, rows)], dst, lsem.at[s, j]
                    )
                    cp.start()
                    loads.append(cp)
            st.append((rel_in, piece_in, rel_out, total, cps, loads))
        yield
        for s in range(n):
            rel_in, piece_in, rel_out, total, cps, loads = st[s]
            lead = scatter_leads(s, t)
            for d in range(2):
                cps[d].wait_recv()
                if t == t0:
                    loads[d].wait()
                    mine = (rel_out, side(d))
                else:
                    mine = (cur[s], picker(s, t, at, (1, -1)[d], (LO, HI)[d]))
                add_blocks(lead, (rel_out, side(d)), [mine, (rel_in, side(d))])
                cp = second_send(s, t, at, d, rel_out, piece_in, ssem, rsem, t0)
                cp.start()
                cps.append(cp)
        yield
        for s in range(n):
            rel_in, piece_in, rel_out, total, cps, loads = st[s]
            lead = scatter_leads(s, t)
            for i in (2, 3, 4, 5):
                cps[i].wait_recv()
            if t == t0:
                loads[2].wait()
                mine = (total, same)
            else:
                mine = (cur[s], picker(s, t, at, 0, slice(None)))
            dst = (total, same) if t < 2 else (results[s], lambda j: (slice(None),) * 2)
            add_blocks(lead, dst, [mine, (piece_in, side(0)), (piece_in, side(1))])
            cur[s] = total
            waits += cps
    for cp in waits:
        cp.wait_send()


def picker(s, t, at, rel, rows):
    a, axes = ORDERS[s][2 - t], ORDERS[s][: 3 - t]
    pos = (at[a] + rel) % 4

    def pick(j):
        it = iter(j)
        out = ()
        for q in ("x", "zl", "y", "zh"):
            if q[0] not in axes:
                continue
            if q[0] == a:
                out += (pos % 2 if q == "zl" else pos // 2 if q == "zh" else pos,)
            else:
                out += (next(it),)
        return out + (rows,)

    return pick


def in_turn(*steps):
    live = list(steps)
    while live:
        for it in list(live):
            if next(it, "end") == "end":
                live.remove(it)


def swap_over(axis, src, dst, ssem, rsem, lsem):
    n = NR if axis == "row" else NC
    r = lax.axis_index("row")
    c = lax.axis_index("col")
    me = r if axis == "row" else c
    cps = []
    for d in range(1, n):
        to = (me + d) % n
        cp = remote(
            src.at[to],
            dst.at[me],
            ssem.at[d - 1],
            rsem.at[d - 1],
            (to, c) if axis == "row" else (r, to),
        )
        cp.start()
        cps.append(cp)
    own = pltpu.make_async_copy(src.at[me], dst.at[me], lsem)
    own.start()
    return cps + [own]


def swap_sems(axis):
    n = NR if axis == "row" else NC
    return [DMA((n - 1,)), DMA((n - 1,)), DMA]


def col_swap_kernel(src, dst, ssem, rsem, lsem):
    at = where_am_i()
    meet(col_peers(at))
    for cp in swap_over("col", src, dst, ssem, rsem, lsem):
        cp.wait()


def col_swap(src, cid, name):
    return pl.pallas_call(
        col_swap_kernel,
        name=name,
        out_shape=sds(src.shape),
        in_specs=[HBM],
        out_specs=HBM,
        scratch_shapes=swap_sems("col"),
        compiler_params=params(cid),
    )(src)


def dot(a, b, dims=((1,), (0,))):
    return lax.dot_general(a, b, (dims, ((), ())), preferred_element_type=F32)


NT = ((1,), (1,))
TN = ((0,), (0,))


def iota(shape, dim):
    return lax.broadcasted_iota(I32, shape, dim)


def onehot(cond):
    return cond.astype(F32).astype(BF)


def unrope(g, cos, sin):
    return g * cos - pltpu.roll(g, HEAD // 2, 1) * sin


def mean_square_scale(v):
    return lax.rsqrt(jnp.mean(v * v, axis=-1, keepdims=True) + EPSILON)


def column(row):
    eye = iota((ROWS, ROWS), 0) == iota((ROWS, ROWS), 1)
    return jnp.sum(jnp.where(eye, row.astype(F32), 0.0), axis=1, keepdims=True).astype(I32)


def slots_sent(target_row):
    g_row = target_row // GROUP
    g_col = column(g_row)
    same = g_row == g_col
    i0, i1 = iota((ROWS, ROWS), 0), iota((ROWS, ROWS), 1)
    before_row = jnp.sum((same & (i0 < i1)).astype(F32), axis=0, keepdims=True).astype(I32)
    before_col = jnp.sum((same & (i1 < i0)).astype(F32), axis=1, keepdims=True).astype(I32)
    return g_row * (ROWS // NR) + before_row, g_col * (ROWS // NR) + before_col


def halves_of(v):
    even, odd = [], []
    low = iota((v.shape[0], HEAD), 1) < HEAD // 2
    for m in range(4):
        a, b = v[:, 256 * m : 256 * m + 128], v[:, 256 * m + 128 : 256 * m + 256]
        even.append(jnp.where(low, a, pltpu.roll(b, 64, 1)))
        odd.append(jnp.where(low, pltpu.roll(a, 64, 1), b))
    return jnp.concatenate(even, axis=1), jnp.concatenate(odd, axis=1)


def first_slots(lens, slots):
    start = jnp.int32(0)
    out = jnp.zeros_like(slots)
    for j in range(8):
        out = jnp.where(slots >= start, start, out)
        start = start + lens(j)
    return out


def slab(w):
    return pl.BlockSpec((1, 1, 4, 2, 2, 64, w), lambda c: (c % 4, c // 4, 0, 0, 0, 0, 0))


def whole(shape):
    return pl.BlockSpec(shape, lambda *_: (0,) * len(shape))


def front_kernel(
    t_row, lens, tokens, grads, again, qgain, kgain, freq, w_q, w_k, w_v, w_o, w_g, w_u, w_d,
    qkv, raw, x_o, dy_o, n1h, dyh, cos, sin, slt, a0, a1, a2, f0, f1, f2,
    sent, came, kv_s, n1_s, src_s, raw_s, wq_v, wkv_v,
    own_sem, w_sem, raw_sem, out_ssem, out_rsem, out_lsem, *sems,
):
    at = where_am_i()
    row, col = lax.axis_index("row"), lax.axis_index("col")
    here = block_index({a: at[a] for a in "xyz"}, at["k"])
    kv_s[:, :HEAD] = w_k[...]
    kv_s[:, HEAD:] = w_v[...]
    pairs = zip((w_q, kv_s, w_o, w_g, w_u, w_d), (a0, a1, a2, f0, f1, f2))
    own = [
        pltpu.make_async_copy(src, dst.at[here], own_sem.at[i])
        for i, (src, dst) in enumerate(pairs)
    ]
    for cp in own:
        cp.start()
    near = [device(moved(at, "z", 1)), device(moved(at, "z", -1))]
    meet(near + row_peers(at) + col_peers(at))
    first = Gather(at, (a0, a1, a2), sems[3:7], own=(w_q, kv_s, w_o))
    second = Gather(at, (f0, f1, f2), sems[7:11], (0, 1), own=(w_g, w_u, w_d))
    steps = first.all()
    more = second.lines()
    next(steps)
    place, _ = slots_sent(t_row[...])
    sel = place == iota((ROWS, ROWS), 0)
    pick = onehot(sel)
    slot = jnp.sum(jnp.where(sel, t_row[...] % ROWS, 0).astype(F32), axis=1, keepdims=True)
    message = (NR, 16, WIDTH)
    sent[:, :, 0:WIDTH] = dot(pick, tokens[...]).astype(BF).reshape(message)
    sent[:, :, WIDTH : 2 * WIDTH] = dot(pick, grads[...]).astype(BF).reshape(message)
    sent[:, :, 2 * WIDTH :] = (
        jnp.broadcast_to(slot, (ROWS, HEAD)).astype(BF).reshape((NR, 16, HEAD))
    )
    cps = swap_over("row", sent, came, *sems[0:3])
    next(steps)
    for cp in own:
        cp.wait()
    for _ in range(5):
        next(steps)
        next(more, None)

    slots = col * ROWS + iota((ROWS, HEAD), 0)
    pos = (slots - first_slots(lambda j: lens[0, j], slots)).astype(F32)
    angle = pos * freq[...]
    cos[...] = jnp.cos(angle)
    sine = jnp.sin(angle)
    sin[...] = jnp.where(iota((ROWS, HEAD), 1) < HEAD // 2, -sine, sine)
    for cp in cps:
        cp.wait()
    local = came[:, :, 2 * WIDTH :].reshape(ROWS, HEAD)
    slt[...] = local
    put = onehot(local[:, :1].astype(F32).astype(I32) == iota((ROWS, ROWS), 1))
    x = dot(put, came[:, :, 0:WIDTH].reshape(ROWS, WIDTH), TN)
    x_o[...] = x.astype(BF)
    n1 = x * mean_square_scale(x) * again[...]
    n1_s[...] = n1.astype(BF)
    a, b = halves_of(n1)
    n1h[0] = a.astype(BF)
    n1h[1] = b.astype(BF)
    dy = dot(put, came[:, :, WIDTH : 2 * WIDTH].reshape(ROWS, WIDTH), TN)
    dy_o[...] = dy.astype(BF)
    a, b = halves_of(dy)
    dyh[0] = a.astype(BF)
    dyh[1] = b.astype(BF)

    in_turn(steps, more)
    first.drain()
    second.drain()

    def block_at(i):
        return (col + 1 + i) % NC

    def loads(i):
        c, slot = block_at(i), i % 2
        return [
            pltpu.make_async_copy(a0.at[c % 4, c // 4], wq_v.at[slot], w_sem.at[0, slot]),
            pltpu.make_async_copy(a1.at[c % 4, c // 4], wkv_v.at[slot], w_sem.at[1, slot]),
        ]

    def sends(i):
        c = block_at(i)
        return remote(src_s.at[c], qkv.at[col], out_ssem.at[i], out_rsem.at[i], (row, c))

    for cp in loads(0):
        cp.start()

    @pl.loop(0, NC)
    def _(i):
        c = block_at(i)

        @pl.when(i < NC - 1)
        def _():
            for cp in loads(i + 1):
                cp.start()

        for cp in loads(i):
            cp.wait()
        n = n1_s[...]
        q = dot(n, wq_v[i % 2].reshape(WIDTH, 256))
        kv = dot(n, wkv_v[i % 2].reshape(WIDTH, 256))
        raw_s[c, :, 0:256] = q
        raw_s[c, :, 256:384] = kv[:, :HEAD]
        pieces = ((q[:, :HEAD], qgain), (q[:, HEAD:], qgain), (kv[:, :HEAD], kgain))
        for j, (v, gain) in enumerate(pieces):
            v = v * mean_square_scale(v) * gain[...]
            v = v * cos[...] + pltpu.roll(v, HEAD // 2, 1) * sin[...]
            src_s[c, :, j * HEAD : (j + 1) * HEAD] = v.astype(BF)
        src_s[c, :, 3 * HEAD :] = kv[:, HEAD:].astype(BF)

        @pl.when(i < NC - 1)
        def _():
            sends(i).start()

    mine = pltpu.make_async_copy(src_s.at[col], qkv.at[col], out_lsem)
    mine.start()
    keep = pltpu.make_async_copy(raw_s, raw, raw_sem)
    keep.start()
    for i in range(NC - 1):
        sends(i).wait()
    mine.wait()
    keep.wait()


def front(target, lens, tokens, grads, again, qgain, kgain, *weights):
    freq = ROPE_BASE ** (-(np.arange(HEAD) % (HEAD // 2)).astype(np.float32) * 2.0 / HEAD)
    freq = jnp.asarray(freq.astype(np.float32).reshape(1, HEAD))
    rows = pltpu.VMEM((NR, 16, 2 * WIDTH + HEAD), BF)
    return pl.pallas_call(
        front_kernel,
        name="front",
        out_shape=[
            sds((NC, ROWS, 512)),
            sds((NC, ROWS, 384), F32),
            sds((ROWS, WIDTH)),
            sds((ROWS, WIDTH)),
            sds((2, ROWS, 512)),
            sds((2, ROWS, 512)),
            sds((ROWS, HEAD), F32),
            sds((ROWS, HEAD), F32),
            sds((ROWS, HEAD)),
        ]
        + [gather_shape(256)] * 3
        + [gather_shape(384)] * 3,
        in_specs=[VMEM, pl.BlockSpec(memory_space=pltpu.SMEM)]
        + [VMEM] * 6
        + [HBM, VMEM, VMEM]
        + [HBM] * 4,
        out_specs=[HBM] * 2 + [VMEM] * 7 + [HBM] * 6,
        scratch_shapes=[rows, rows, pltpu.VMEM((64, 256), BF)]
        + [
            pltpu.VMEM((ROWS, WIDTH), BF),
            pltpu.VMEM((NC, ROWS, 512), BF),
            pltpu.VMEM((NC, ROWS, 384), F32),
            pltpu.VMEM((2, 4, 2, 2, 64, 256), BF),
            pltpu.VMEM((2, 4, 2, 2, 64, 256), BF),
        ]
        + [DMA((6,)), DMA((2, 2)), DMA, DMA((NC - 1,)), DMA((NC - 1,)), DMA]
        + swap_sems("row")
        + gather_sems(36, 16)
        + gather_sems(20, 0),
        compiler_params=params(1),
    )(target.reshape(1, ROWS), lens, tokens, grads, again, qgain, kgain, freq, *weights)


LOG2E = math.log2(math.e)
QK = 512


def stacked(v):
    return jnp.concatenate([v[:, :HEAD], v[:, HEAD : 2 * HEAD]], axis=0)


SPAN = 5


def group_slots(i):
    return i * ROWS + iota((1, QK), 1) % ROWS


def allowed(i, j, first):
    key = j * ROWS + iota((ROWS, QK), 0)
    return (key <= group_slots(i)) & (key >= first)


def attend_kernel(
    lens, qkv, i0, i1, i2, oa, o_t, lse, f0, f1, f2, o_s, s_v, ssem, rsem, lsem, *sems
):
    at = where_am_i()
    row, col = lax.axis_index("row"), lax.axis_index("col")
    meet(ring_peers(at) + [device(mate(at))] + col_peers(at))
    more = Gather(at, (f0, f1, f2), sems, (2,))
    more.send(2, None)
    scale = HEAD**-0.5 * LOG2E

    def block_at(n):
        return (col + 1 + n) % NC

    def sends(n):
        c = block_at(n)
        return remote(o_s.at[c], oa.at[col], ssem.at[n], rsem.at[n], (row, c))

    @pl.loop(0, NC)
    def _(n):
        i = block_at(n)
        q = stacked(qkv[i, :, 0 : 2 * HEAD])
        start = first_slots(lambda j: lens[0, j], group_slots(i))
        j0 = jnp.maximum(i - (SPAN - 1), 0)
        m = None
        for d in range(SPAN):
            s = dot(qkv[j0 + d, :, 2 * HEAD : 3 * HEAD], q, NT) * scale
            s = jnp.where(allowed(i, j0 + d, start), s, -1e30)
            s_v[d] = s
            top = jnp.max(s, axis=0, keepdims=True)
            m = top if m is None else jnp.maximum(m, top)
        total = jnp.zeros((1, QK), F32)
        acc = jnp.zeros((HEAD, QK), F32)
        for d in range(SPAN):
            p = jnp.exp2(s_v[d] - m)
            total = total + jnp.sum(p, axis=0, keepdims=True)
            acc = acc + dot(qkv[j0 + d, :, 3 * HEAD :], p.astype(BF), TN)
        o = acc / total
        o_t[i] = o
        lse[i] = m + jnp.log2(total)
        back = o.T
        o_s[i] = jnp.concatenate([back[:ROWS], back[ROWS:]], axis=1).astype(BF)

        @pl.when(n < NC - 1)
        def _():
            sends(n).start()

        @pl.when(n == NC - 2)
        def _():
            more.pass_on(2, None)

    mine = pltpu.make_async_copy(o_s.at[col], oa.at[col], lsem)
    mine.start()
    more.arrived(2, None)
    for n in range(NC - 1):
        sends(n).wait()
    mine.wait()
    for s in range(3):
        for cp in more.copies(s, 2, None) + more.forwards(s, 2, None):
            cp.wait_send()
        for rel in SHIFT:
            more.to_mate(s, None, rel).wait()


def attend(lens, qkv, planes):
    return pl.pallas_call(
        attend_kernel,
        name="attend",
        out_shape=[
            sds((NC, ROWS, 256)),
            sds((NC, HEAD, QK), F32),
            sds((NC, 1, QK), F32),
        ]
        + [gather_shape(384)] * 3,
        in_specs=[pl.BlockSpec(memory_space=pltpu.SMEM), VMEM] + [HBM] * 3,
        out_specs=[HBM, VMEM, VMEM] + [HBM] * 3,
        input_output_aliases={2: 3, 3: 4, 4: 5},
        scratch_shapes=[pltpu.VMEM((NC, ROWS, 256), BF), pltpu.VMEM((SPAN, ROWS, QK), F32)]
        + swap_sems("col")
        + gather_sems(4, 4),
        compiler_params=params(2),
    )(lens, qkv, *planes)


def later_shapes():
    leads = [scatter_leads(s, 0) for s in range(3)]
    return [sds((2,) + n + (32, 384)) for n in leads], [sds((2,) + n + (64, 384)) for n in leads]


def attend_back_kernel(lens, qkv, d_o, o_t, lse, p0, p1, p2, dst, *rest):
    rel_in, piece_in, rest = rest[0:3], rest[3:6], rest[6:]
    out_s, qs, dos, delta, dq, first, kv_ssem, kv_rsem, kv_lsem = rest[:9]
    q_ssem, q_rsem, q_lsem, ssem, rsem, _ = rest[9:]
    at = where_am_i()
    row, col = lax.axis_index("row"), lax.axis_index("col")
    meet(ring_peers(at) + col_peers(at))
    cps = []
    for s, p in enumerate((p0, p1, p2)):
        more = first_sends(s, 0, at, p, rel_in[s], piece_in[s], ssem, rsem)
        for cp in more:
            cp.start()
        cps += more
    scale = HEAD**-0.5

    @pl.loop(0, NC)
    def _(i):
        qs[i] = stacked(qkv[i, :, 0 : 2 * HEAD])
        g = stacked(d_o[i])
        dos[i] = g
        delta[i] = jnp.sum(g.astype(F32).T * o_t[i], axis=0, keepdims=True)
        dq[i] = jnp.zeros((HEAD, QK), F32)
        first[i] = first_slots(lambda n: lens[0, n], group_slots(i))

    def block_at(n):
        return (col + 1 + n) % NC

    lanes_q, lanes_kv = pl.ds(0, 2 * HEAD), pl.ds(2 * HEAD, 2 * HEAD)
    whole_rows = (slice(None),)

    def sends(n, lanes, ssem, rsem):
        c = block_at(n)
        return remote(
            out_s.at[(c,) + whole_rows + (lanes,)],
            dst.at[(col,) + whole_rows + (lanes,)],
            ssem.at[n],
            rsem.at[n],
            (row, c),
        )

    def keeps(lanes, sem):
        return pltpu.make_async_copy(
            out_s.at[(col,) + whole_rows + (lanes,)], dst.at[(col,) + whole_rows + (lanes,)], sem
        )

    @pl.loop(0, NC)
    def _(n):
        j = block_at(n)
        k = qkv[j, :, 2 * HEAD : 3 * HEAD]
        v = qkv[j, :, 3 * HEAD :]
        k_t = k.astype(F32).T.astype(BF)

        def step(i, carry):
            dk, dv = carry
            s = dot(k, qs[i], NT) * (scale * LOG2E) - lse[i]
            p = jnp.where(allowed(i, j, first[i]), jnp.exp2(s), 0.0)
            ds = (p * (dot(v, dos[i], NT) - delta[i]) * scale).astype(BF)
            dv = dv + dot(p.astype(BF), dos[i])
            dk = dk + dot(ds, qs[i])
            dq[i] += dot(k_t, ds)
            return dk, dv

        zero = jnp.zeros((ROWS, HEAD), F32)
        dk, dv = lax.fori_loop(j, jnp.minimum(j + SPAN, NC), step, (zero, zero))
        out_s[j, :, 2 * HEAD : 3 * HEAD] = dk.astype(BF)
        out_s[j, :, 3 * HEAD :] = dv.astype(BF)

        @pl.when(n < NC - 1)
        def _():
            sends(n, lanes_kv, kv_ssem, kv_rsem).start()

    @pl.loop(0, NC)
    def _(n):
        i = block_at(n)
        done = dq[i].T
        out_s[i, :, 0:HEAD] = done[:ROWS].astype(BF)
        out_s[i, :, HEAD : 2 * HEAD] = done[ROWS:].astype(BF)

        @pl.when(n < NC - 1)
        def _():
            sends(n, lanes_q, q_ssem, q_rsem).start()

    mine = [keeps(lanes_kv, kv_lsem), keeps(lanes_q, q_lsem)]
    for cp in mine:
        cp.start()
    for cp in mine + cps:
        cp.wait()
    for n in range(NC - 1):
        sends(n, lanes_kv, kv_ssem, kv_rsem).wait()
        sends(n, lanes_q, q_ssem, q_rsem).wait()


def attend_back(lens, qkv, d_o, o_t, lse, parts):
    rel, piece = later_shapes()
    return pl.pallas_call(
        attend_back_kernel,
        name="attend_back",
        out_shape=[sds((NC, ROWS, 512))] + rel + piece,
        in_specs=[pl.BlockSpec(memory_space=pltpu.SMEM)] + [VMEM] * 4 + [HBM] * 3,
        out_specs=[HBM] * 7,
        scratch_shapes=[
            pltpu.VMEM((NC, ROWS, 512), BF),
            pltpu.VMEM((NC, QK, HEAD), BF),
            pltpu.VMEM((NC, QK, HEAD), BF),
            pltpu.VMEM((NC, 1, QK), F32),
            pltpu.VMEM((NC, HEAD, QK), F32),
            pltpu.VMEM((NC, 1, QK), I32),
        ]
        + swap_sems("col") * 2
        + scatter_sems(1),
        compiler_params=params(6),
    )(lens, qkv, d_o, o_t, lse, *parts)


def middle_kernel(
    slt, x, dy, oa, fgain, wo, wg, wu, wd,
    out_s, dh_o, dhlh, n2h, act, d_o, gain_o,
    h_s, n2_s, acc, dn2, dhl_s,
):
    i = pl.program_id(0)

    @pl.when(i < NC)
    def _():
        part = dot(oa[0], wo[0, 0].reshape(WIDTH, 256), NT)

        @pl.when(i == 0)
        def _():
            acc[...] = x[...].astype(F32) + part

        @pl.when(i > 0)
        def _():
            acc[...] += part

    @pl.when(i == NC)
    def _():
        h = acc[...]
        h_s[...] = h
        n2 = h * mean_square_scale(h) * fgain[...]
        n2_s[...] = n2.astype(BF)
        a, b = halves_of(n2)
        n2h[0] = a.astype(BF)
        n2h[1] = b.astype(BF)
        dn2[...] = jnp.zeros_like(dn2)

    @pl.when((i >= NC) & (i < 2 * NC))
    def _():
        g_w = wg[0, 0].reshape(WIDTH, 384)
        u_w = wu[0, 0].reshape(WIDTH, 384)
        d_w = wd[0, 0].reshape(WIDTH, 384)
        g = dot(n2_s[...], g_w)
        u = dot(n2_s[...], u_w)
        dhid = dot(dy[...], d_w)
        sig = jax.nn.sigmoid(g)
        silu = g * sig
        hid = (silu * u).astype(BF)
        dg = (dhid * u * sig * (1.0 + g * (1.0 - sig))).astype(BF)
        du = (dhid * silu).astype(BF)
        act[0, :, 0:384] = dg
        act[0, :, 384:768] = du
        act[0, :, 768:] = hid
        acc[...] += dot(hid, d_w, NT)
        dn2[...] += dot(dg, g_w, NT) + dot(du, u_w, NT)

    @pl.when(i == 2 * NC - 1)
    def _():
        take = onehot(slt[:, :1].astype(F32).astype(I32) == iota((ROWS, ROWS), 1))
        out_s[...] = dot(take, acc[...].astype(BF)).astype(BF).reshape(out_s.shape)
        h = h_s[...]
        r2 = mean_square_scale(h)
        hn = h * r2
        e = dn2[...]
        gain_o[...] = jnp.sum(e * hn, axis=0, keepdims=True)
        e = e * fgain[...]
        dh = dy[...].astype(F32) + r2 * (e - hn * jnp.mean(e * hn, axis=-1, keepdims=True))
        dh_o[...] = dh
        dhl_s[...] = dh.astype(BF)
        a, b = halves_of(dh)
        dhlh[0] = a.astype(BF)
        dhlh[1] = b.astype(BF)

    @pl.when(i >= 2 * NC)
    def _():
        d_o[0] = dot(dhl_s[...], wo[0, 0].reshape(WIDTH, 256)).astype(BF)


def middle(slt, x, dy, oa, fgain, wo, wg, wu, wd):
    def ffn(w):
        def at(i):
            c = jnp.clip(i - NC, 0, NC - 1)
            return (c % 4, c // 4, 0, 0, 0, 0, 0)

        return pl.BlockSpec((1, 1, 4, 2, 2, 64, w), at)

    def out_at(i):
        c = jnp.where(i < NC, i, jnp.where(i < 2 * NC, NC - 1, i - 2 * NC))
        return (c % 4, c // 4, 0, 0, 0, 0, 0)

    return pl.pallas_call(
        middle_kernel,
        name="middle",
        grid=(3 * NC,),
        out_shape=[
            sds((NR, 16, WIDTH)),
            sds((ROWS, WIDTH), F32),
            sds((2, ROWS, 512)),
            sds((2, ROWS, 512)),
            sds((NC, ROWS, 1152)),
            sds((NC, ROWS, 256)),
            sds((1, WIDTH), F32),
        ],
        in_specs=[
            whole((ROWS, HEAD)),
            whole((ROWS, WIDTH)),
            whole((ROWS, WIDTH)),
            pl.BlockSpec((1, ROWS, 256), lambda i: (jnp.minimum(i, NC - 1), 0, 0)),
            whole((1, WIDTH)),
            pl.BlockSpec((1, 1, 4, 2, 2, 64, 256), out_at),
            ffn(384),
            ffn(384),
            ffn(384),
        ],
        out_specs=[
            whole((NR, 16, WIDTH)),
            whole((ROWS, WIDTH)),
            whole((2, ROWS, 512)),
            whole((2, ROWS, 512)),
            pl.BlockSpec((1, ROWS, 1152), lambda i: (jnp.clip(i - NC, 0, NC - 1), 0, 0)),
            pl.BlockSpec((1, ROWS, 256), lambda i: (jnp.maximum(i - 2 * NC, 0), 0, 0)),
            whole((1, WIDTH)),
        ],
        scratch_shapes=[
            pltpu.VMEM((ROWS, WIDTH), F32),
            pltpu.VMEM((ROWS, WIDTH), BF),
            pltpu.VMEM((ROWS, WIDTH), F32),
            pltpu.VMEM((ROWS, WIDTH), F32),
            pltpu.VMEM((ROWS, WIDTH), BF),
        ],
        compiler_params=params(),
    )(slt, x, dy, oa, fgain, wo, wg, wu, wd)


def back_swap_kernel(d_o, out_s, act, oa, n2h, dyh, dhlh, *rest):
    outs, sems = rest[:7], rest[7:]
    g_o, got, act_m, oa_m, n2_m, dy_m, dhl_m = outs
    at = where_am_i()
    meet(col_peers(at) + row_peers(at))
    cps = swap_over("col", d_o, g_o, *sems[0:3])
    to = device(mate(at))
    other = 1 - at["k"]
    pairs = (
        (act, act_m),
        (oa, oa_m),
        (n2h.at[other], n2_m),
        (dyh.at[other], dy_m),
        (dhlh.at[other], dhl_m),
    )
    for i, (src, dst) in enumerate(pairs):
        cp = remote(src, dst, sems[6].at[i], sems[7].at[i], to)
        cp.start()
        cps.append(cp)
    cps += swap_over("row", out_s, got, *sems[3:6])
    for cp in cps:
        cp.wait()


def back_swap(d_o, out_s, act, oa, n2h, dyh, dhlh):
    return pl.pallas_call(
        back_swap_kernel,
        name="back_swap",
        out_shape=[sds(d_o.shape), sds(out_s.shape), sds(act.shape), sds(oa.shape)]
        + [sds((ROWS, 512))] * 3,
        in_specs=[HBM] * 7,
        out_specs=[HBM] * 7,
        scratch_shapes=swap_sems("col") + swap_sems("row") + [DMA((5,)), DMA((5,))],
        compiler_params=params(5),
    )(d_o, out_s, act, oa, n2h, dyh, dhlh)


def stack_tokens(k, mine, others, scratch):
    scratch[:, 0:ROWS] = mine[k].astype(F32).T.astype(BF)
    scratch[:, ROWS:] = others[...].astype(F32).T.astype(BF)


def ffn_grads_kernel(n2h, n2_m, dyh, dy_m, act, act_m, g0, g1, g2, n_s, y_s):
    c = pl.program_id(0)

    @pl.when(c == 0)
    def _():
        k = lax.axis_index("row") % 2
        stack_tokens(k, n2h, n2_m, n_s)
        stack_tokens(k, dyh, dy_m, y_s)

    for i, (lhs, out) in enumerate(((n_s, g0), (n_s, g1), (y_s, g2))):
        cols = slice(384 * i, 384 * i + 384)
        rhs = jnp.concatenate([act[0, :, cols], act_m[0, :, cols]], axis=0)
        out[0, 0] = dot(lhs[...], rhs).astype(BF).reshape(4, 2, 64, 384)


def grad_slab(w):
    return pl.BlockSpec((1, 1, 4, 2, 64, w), lambda c: (c % 4, c // 4, 0, 0, 0, 0))


def ffn_grads(n2h, n2_m, dyh, dy_m, act, act_m):
    one = pl.BlockSpec((1, ROWS, 1152), lambda c: (c, 0, 0))
    return pl.pallas_call(
        ffn_grads_kernel,
        name="ffn_grads",
        grid=(NC,),
        out_shape=[sds((4, 2, 4, 2, 64, 384))] * 3,
        in_specs=[whole((2, ROWS, 512)), whole((ROWS, 512))] * 2 + [one, one],
        out_specs=[grad_slab(384)] * 3,
        scratch_shapes=[pltpu.VMEM((512, 2 * ROWS), BF)] * 2,
        compiler_params=params(),
    )(n2h, n2_m, dyh, dy_m, act, act_m)


def attn_grads_kernel(n1h, n1_m, dhlh, dhl_m, dqkv, dqkv_m, oa, oa_m, g0, g1, g2, n_s, h_s):
    c = pl.program_id(0)

    @pl.when(c == 0)
    def _():
        k = lax.axis_index("row") % 2
        stack_tokens(k, n1h, n1_m, n_s)
        stack_tokens(k, dhlh, dhl_m, h_s)

    for i, (lhs, mine, others, out) in enumerate(
        ((n_s, dqkv, dqkv_m, g0), (n_s, dqkv, dqkv_m, g1), (h_s, oa, oa_m, g2))
    ):
        cols = slice(256 * i, 256 * i + 256) if i < 2 else slice(0, 256)
        rhs = jnp.concatenate([mine[0, :, cols], others[0, :, cols]], axis=0)
        out[0, 0] = dot(lhs[...], rhs).astype(BF).reshape(4, 2, 64, 256)


def attn_grads(n1h, n1_m, dhlh, dhl_m, dqkv, dqkv_m, oa, oa_m):
    def one(w):
        return pl.BlockSpec((1, ROWS, w), lambda c: (c, 0, 0))

    return pl.pallas_call(
        attn_grads_kernel,
        name="attn_grads",
        grid=(NC,),
        out_shape=[sds((4, 2, 4, 2, 64, 256))] * 3,
        in_specs=[whole((2, ROWS, 512)), whole((ROWS, 512))] * 2
        + [one(512), one(512), one(256), one(256)],
        out_specs=[grad_slab(256)] * 3,
        scratch_shapes=[pltpu.VMEM((512, 2 * ROWS), BF)] * 2,
        compiler_params=params(),
    )(n1h, n1_m, dhlh, dhl_m, dqkv, dqkv_m, oa, oa_m)


def project_back_kernel(
    slt, x, dh, again, qgain, kgain, cos, sin, raw, dqkv, wq, wkv, p0, p1, p2, r0, r1, r2, i0, i1, i2,
    d_o, dx_s, gain_o, qk_o, q0, q1, q2, acc, gq, gk, *rest,
):
    c = pl.program_id(0)
    at = where_am_i()
    rel_v, own_v, (ssem, rsem, lsem) = rest[0:3], rest[3:6], rest[6:]
    parts, rel_in, piece_in = (p0, p1, p2), (r0, r1, r2), (q0, q1, q2)

    def loads(s):
        out = [pltpu.make_async_copy(rel_in[s], rel_v[s], lsem.at[s, 0])]
        for d, (rel, rows) in enumerate(((1, LO), (-1, HI))):
            src = parts[s].at[part_of(s, 0, at, rel, rows)]
            out.append(pltpu.make_async_copy(src, own_v[s].at[d], lsem.at[s, 1 + d]))
        return out

    def sends(s):
        return [second_send(s, 0, at, d, own_v[s], piece_in[s], ssem, rsem) for d in range(2)]

    @pl.when(c == 0)
    def _():
        for s in range(3):
            for cp in loads(s):
                cp.start()
        meet(ring_peers(at))

    @pl.when(c == 1)
    def _():
        for s in range(3):
            for cp in loads(s):
                cp.wait()
            lead = (2,) + scatter_leads(s, 0)
            add_blocks(lead, (own_v[s], same), [(own_v[s], same), (rel_v[s], same)])
            for cp in sends(s):
                cp.start()

    @pl.when(c == 0)
    def _():
        acc[...] = jnp.zeros_like(acc)
        gq[...] = jnp.zeros_like(gq)
        gk[...] = jnp.zeros_like(gk)

    for i, (gain, g_acc) in enumerate(((qgain, gq), (qgain, gq), (kgain, gk))):
        cols = slice(i * HEAD, (i + 1) * HEAD)
        v = raw[0, :, cols]
        r = mean_square_scale(v)
        xn = v * r
        dn = unrope(dqkv[0, :, cols].astype(F32), cos[...], sin[...])
        g_acc[...] += jnp.sum(dn * xn, axis=0, keepdims=True)
        e = dn * gain[...]
        d_o[0, :, cols] = (r * (e - xn * jnp.mean(e * xn, axis=-1, keepdims=True))).astype(BF)
    d_o[0, :, 3 * HEAD :] = dqkv[0, :, 3 * HEAD :]
    acc[...] += dot(d_o[0, :, 0:256], wq[0, 0].reshape(WIDTH, 256), NT) + dot(
        d_o[0, :, 256:512], wkv[0, 0].reshape(WIDTH, 256), NT
    )

    @pl.when(c == NC - 1)
    def _():
        xv = x[...].astype(F32)
        r1 = mean_square_scale(xv)
        xn = xv * r1
        e = acc[...]
        gain_o[...] = jnp.sum(e * xn, axis=0, keepdims=True)
        e = e * again[...]
        dx = dh[...] + r1 * (e - xn * jnp.mean(e * xn, axis=-1, keepdims=True))
        take = onehot(slt[:, :1].astype(F32).astype(I32) == iota((ROWS, ROWS), 1))
        dx_s[...] = dot(take, dx.astype(BF)).astype(BF).reshape(dx_s.shape)
        qk_o[...] = jnp.concatenate([gq[...], gk[...]], axis=1)
        for s in range(3):
            for cp in sends(s):
                cp.wait()


def project_back(slt, x, dh, again, qgain, kgain, cos, sin, raw, dqkv, wq, wkv, parts, rel, piece):
    return pl.pallas_call(
        project_back_kernel,
        name="project_back",
        grid=(NC,),
        out_shape=[
            sds((NC, ROWS, 512)),
            sds((NR, 16, WIDTH)),
            sds((1, WIDTH), F32),
            sds((1, 2 * HEAD), F32),
        ]
        + later_shapes()[1],
        in_specs=[
            whole((ROWS, HEAD)),
            whole((ROWS, WIDTH)),
            whole((ROWS, WIDTH)),
            whole((1, WIDTH)),
            whole((1, HEAD)),
            whole((1, HEAD)),
            whole((ROWS, HEAD)),
            whole((ROWS, HEAD)),
            pl.BlockSpec((1, ROWS, 384), lambda c: (c, 0, 0)),
            pl.BlockSpec((1, ROWS, 512), lambda c: (c, 0, 0)),
            slab(256),
            slab(256),
        ]
        + [HBM] * 9,
        out_specs=[
            pl.BlockSpec((1, ROWS, 512), lambda c: (c, 0, 0)),
            whole((NR, 16, WIDTH)),
            whole((1, WIDTH)),
            whole((1, 2 * HEAD)),
        ]
        + [HBM] * 3,
        input_output_aliases={18: 4, 19: 5, 20: 6},
        scratch_shapes=[
            pltpu.VMEM((ROWS, WIDTH), F32),
            pltpu.VMEM((1, HEAD), F32),
            pltpu.VMEM((1, HEAD), F32),
        ]
        + [pltpu.VMEM(r.shape, BF) for r in later_shapes()[0]] * 2
        + scatter_sems(1),
        compiler_params=params(7),
    )(slt, x, dh, again, qgain, kgain, cos, sin, raw, dqkv, wq, wkv, *parts, *rel, *piece)


def core_swap_kernel(dqkv, n1h, p0, p1, p2, q0, q1, q2, dqkv_m, n1_m, s0, s1, s2, *rest):
    own_v, piece_v, (ssem, rsem, lsem, osem) = rest[0:3], rest[3:6], rest[6:]
    at = where_am_i()
    loads = []
    for s, (p, q) in enumerate(((p0, q0), (p1, q1), (p2, q2))):
        src = p.at[part_of(s, 0, at, 0, slice(None))]
        pair = [
            pltpu.make_async_copy(src, own_v[s], lsem.at[s, 0]),
            pltpu.make_async_copy(q, piece_v[s], lsem.at[s, 1]),
        ]
        for cp in pair:
            cp.start()
        loads.append(pair)
    to = device(mate(at))
    meet([to])
    cps = [
        remote(dqkv, dqkv_m, ssem.at[0], rsem.at[0], to),
        remote(n1h.at[1 - at["k"]], n1_m, ssem.at[1], rsem.at[1], to),
    ]
    for cp in cps:
        cp.start()
    for s, out in enumerate((s0, s1, s2)):
        for cp in loads[s]:
            cp.wait()
        lead = scatter_leads(s, 0)
        terms = [(own_v[s], same), (piece_v[s], side(0)), (piece_v[s], side(1))]
        add_blocks(lead, (own_v[s], same), terms)
        cp = pltpu.make_async_copy(own_v[s], out, osem.at[s])
        cp.start()
        cps.append(cp)
    for cp in cps:
        cp.wait()


def core_swap(dqkv, n1h, parts, piece):
    sums = [sds(scatter_leads(s, 0) + (64, 384)) for s in range(3)]
    return pl.pallas_call(
        core_swap_kernel,
        name="core_swap",
        out_shape=[sds(dqkv.shape), sds((ROWS, 512))] + sums,
        in_specs=[HBM] * 8,
        out_specs=[HBM] * 5,
        scratch_shapes=[pltpu.VMEM(r.shape, BF) for r in sums]
        + [pltpu.VMEM(r.shape, BF) for r in later_shapes()[1]]
        + [DMA((2,)), DMA((2,)), DMA((3, 2)), DMA((3,))],
        compiler_params=params(8),
    )(dqkv, n1h, *parts, *piece)


def gain_steps(at, pieces, room, total, ssem, rsem):
    p = at["x"]
    lane = 0
    for ref in pieces:
        room[0, p, :, lane : lane + ref.shape[1]] = ref[...]
        lane += ref.shape[1]
    for t, a in enumerate("xyzk"):
        p = at[a]
        others = (1, 2, 3) if a != "k" else (1,)
        if t > 0:
            room[t, p] = total[...]
        step = []
        for d in others:
            to = device(moved(at, a, d)) if a != "k" else device(mate(at))
            sems = ssem.at[t, d - 1], rsem.at[t, d - 1]
            cp = remote(room.at[t, p], room.at[t, p], *sems, to)
            cp.start()
            step.append(cp)
        yield
        for cp in step:
            cp.wait()
        acc = room[t, 0]
        for j in range(1, len(others) + 1):
            acc = acc + room[t, j]
        total[...] = acc


def last_kernel(
    p0, p1, p2, s0, s1, s2, dx_s, ga, gf, gqk, r0, r1, r2, t0, t1, t2, got, gsum, *scratch
):
    na, nf = len(scatter_buffers(256)), len(scatter_buffers(384, 1))
    bufs, more, rest = scratch[:na], scratch[na : na + nf], scratch[na + nf :]
    at = where_am_i()
    far = [device(moved(at, a, 2)) for a in "xyz"]
    meet(ring_peers(at) + far + row_peers(at))
    cps = []

    def rows():
        yield
        cps.extend(swap_over("row", dx_s, got, *rest[3:6]))

    in_turn(
        run_scatter(at, (p0, p1, p2), (r0, r1, r2), bufs, rest[6:9]),
        rows(),
        gain_steps(at, (ga, gf, gqk), rest[0], gsum, rest[1], rest[2]),
        run_scatter(at, (s0, s1, s2), (t0, t1, t2), more, rest[9:12], 1),
    )
    for cp in cps:
        cp.wait()


def last(parts, sums, dx_s, gains):
    total = 2 * WIDTH + 2 * HEAD
    return pl.pallas_call(
        last_kernel,
        name="last",
        out_shape=[sds((64, 256), F32)] * 3
        + [sds((64, 384), F32)] * 3
        + [sds(dx_s.shape), sds((1, total), F32)],
        in_specs=[HBM] * 7 + [VMEM] * 3,
        out_specs=[VMEM] * 6 + [HBM, VMEM],
        scratch_shapes=scatter_buffers(256)
        + scatter_buffers(384, 1)
        + [pltpu.VMEM((4, 4, 1, total), F32), DMA((4, 3)), DMA((4, 3))]
        + swap_sems("row")
        + scatter_sems()
        + scatter_sems(2),
        compiler_params=params(9),
    )(*parts, *sums, dx_s, *gains)


def arrive_kernel(
    t_row, out, dx, q, kv, o, g, u, d, gains,
    out_o, dx_o, ga, gf, gq, gk, q_o, k_o, v_o, o_o, g_o, u_o, d_o,
):
    _, place = slots_sent(t_row[...])
    pick = onehot(place == iota((ROWS, ROWS), 1))
    out_o[...] = dot(pick, out[...].reshape(ROWS, WIDTH)).astype(BF)
    dx_o[...] = dot(pick, dx[...].reshape(ROWS, WIDTH)).astype(BF)
    ga[...] = gains[:, 0:WIDTH]
    gf[...] = gains[:, WIDTH : 2 * WIDTH]
    gq[...] = gains[:, 2 * WIDTH : 2 * WIDTH + HEAD]
    gk[...] = gains[:, 2 * WIDTH + HEAD :]
    q_o[...] = q[...]
    k_o[...] = kv[:, :HEAD]
    v_o[...] = kv[:, HEAD:]
    o_o[...] = o[...]
    g_o[...] = g[...]
    u_o[...] = u[...]
    d_o[...] = d[...]


def arrive(target, *args):
    return pl.pallas_call(
        arrive_kernel,
        name="arrive",
        out_shape=[sds((ROWS, WIDTH))] * 2
        + [sds((1, n), F32) for n in (WIDTH, WIDTH, HEAD, HEAD)]
        + [
            sds(n, F32)
            for n in ((64, 256), (64, 128), (64, 128), (64, 256), (64, 384), (64, 384), (64, 384))
        ],
        in_specs=[VMEM] * 10,
        out_specs=[VMEM] * 13,
        compiler_params=params(),
    )(target.reshape(1, ROWS), *args)


def local(
    tokens, grad_out, target, lengths, attn_gain, ffn_gain, q_gain, k_gain,
    w_query, key_matrix, value_matrix, w_out, w_gate, w_up, w_down,
):
    again, fgain = attn_gain.reshape(1, WIDTH), ffn_gain.reshape(1, WIDTH)
    qgain, kgain = q_gain.reshape(1, HEAD), k_gain.reshape(1, HEAD)

    qkv, raw, x, dy, n1h, dyh, cos, sin, slt, wq, wkv, wo, *planes = front(
        target, lengths, tokens, grad_out, again, qgain, kgain,
        w_query, key_matrix, value_matrix, w_out.T, w_gate, w_up, w_down.T,
    )
    oa, o_t, lse, wg, wu, wd = attend(lengths, qkv, planes)
    out_s, dh, dhlh, n2h, act, d_o, gain_f = middle(slt, x, dy, oa, fgain, wo, wg, wu, wd)
    g_o, got_out, act_m, oa_m, n2_m, dy_m, dhl_m = back_swap(
        d_o, out_s, act, oa, n2h, dyh, dhlh
    )
    f_parts = ffn_grads(n2h, n2_m, dyh, dy_m, act, act_m)
    dqkv, *later = attend_back(lengths, qkv, g_o, o_t, lse, f_parts)
    draw, dx_s, gain_a, gain_qk, *piece = project_back(
        slt, x, dh, again, qgain, kgain, cos, sin, raw, dqkv, wq, wkv,
        f_parts, later[:3], later[3:],
    )
    draw_m, n1_m, *sums = core_swap(draw, n1h, f_parts, piece)
    a_parts = attn_grads(n1h, n1_m, dhlh, dhl_m, draw, draw_m, oa, oa_m)
    r_q, r_kv, r_o, r_g, r_u, r_d, got_dx, gains = last(
        a_parts, sums, dx_s, (gain_a, gain_f, gain_qk)
    )
    output, input_grad, ga, gf, gq, gk, g_q, g_k, g_v, g_o, g_g, g_u, g_d = arrive(
        target, got_out, got_dx, r_q, r_kv, r_o, r_g, r_u, r_d, gains
    )
    return (
        output, input_grad, ga[0], gf[0], gq[0], gk[0], g_q, g_k, g_v, g_o.T, g_g, g_u, g_d.T,
    )


def solution(mesh):
    both = P(("row", "col"), None)
    by_row, by_col = P("row", "col"), P("col", "row")
    weights = (by_row, by_row, by_row, by_col, by_row, by_row, by_col)
    return jax.shard_map(
        local,
        mesh=mesh,
        in_specs=(both, both, P(("row", "col")), P("row", None), P(), P(), P(), P()) + weights,
        out_specs=(both, both, P(), P(), P(), P()) + weights,
        check_vma=False,
    )
```

```python
import functools
import math

import jax
import jax.numpy as jnp
import numpy as np
from jax import lax
from jax.experimental import pallas as pl
from jax.experimental.pallas import tpu as pltpu
from jax.sharding import PartitionSpec as P

MESH = pl.DeviceIdType.MESH
BF = jnp.bfloat16
F32 = jnp.float32
I32 = jnp.int32
EPSILON = 1e-06
ROPE_BASE = 1000000.0
HEAD = 128
NR = 16
NC = 8
ROWS = 256
WIDTH = 1024
GROUP = 2048
ORDERS = (("x", "y", "z"), ("y", "z", "x"), ("z", "x", "y"))
HBM = pl.BlockSpec(memory_space=pltpu.HBM)
VMEM = pl.BlockSpec(memory_space=pltpu.VMEM)
DMA = pltpu.SemaphoreType.DMA


def sds(shape, dtype=BF):
    return jax.ShapeDtypeStruct(shape, dtype)


def params(cid=None, mib=56, **kw):
    if cid is not None:
        kw.update(collective_id=cid, has_side_effects=True)
    return pltpu.CompilerParams(vmem_limit_bytes=mib << 20, **kw)


def where_am_i():
    r = lax.axis_index("row")
    c = lax.axis_index("col")
    return {"x": c % 4, "y": r // 4, "z": 2 * ((r // 2) % 2) + c // 4, "k": r % 2}


def device(at):
    return (at["y"] * 4 + (at["z"] // 2) * 2 + at["k"], (at["z"] % 2) * 4 + at["x"])


def moved(at, axis, step):
    out = dict(at)
    out[axis] = (at[axis] + step) % 4
    return out


def mate(at):
    out = dict(at)
    out["k"] = 1 - at["k"]
    return out


def meet(peers):
    barrier = pltpu.get_barrier_semaphore()
    for p in peers:
        pl.semaphore_signal(barrier, inc=1, device_id=p, device_id_type=MESH)
    pl.semaphore_wait(barrier, len(peers))


def ring_peers(at):
    return [device(moved(at, a, s)) for a in "xyz" for s in (1, -1)]


def row_peers(at):
    r = lax.axis_index("row")
    c = lax.axis_index("col")
    return [((r + d) % NR, c) for d in range(1, NR)]


def col_peers(at):
    r = lax.axis_index("row")
    c = lax.axis_index("col")
    return [(r, (c + d) % NC) for d in range(1, NC)]


def remote(src, dst, ssem, rsem, to):
    return pltpu.make_async_remote_copy(
        src_ref=src, dst_ref=dst, send_sem=ssem, recv_sem=rsem, device_id=to, device_id_type=MESH
    )


def block_index(sel, with_core=None):
    full = slice(None)
    z = sel.get("z")
    idx = (
        sel.get("x", full),
        full if z is None else z % 2,
        sel.get("y", full),
        full if z is None else z // 2,
    )
    return idx if with_core is None else idx + (with_core,)


SHIFT = (0, -1, 1, 2)


def piece_index(at, s, t, g, rel):
    order = ORDERS[s]
    sel = {a: at[a] for a in order[t + 1 :]}
    if t > 0 and g is not None:
        sel[order[t - 1]] = (at[order[t - 1]] + SHIFT[g]) % 4
    sel[order[t]] = (at[order[t]] + rel) % 4
    return block_index(sel, at["k"])


class Gather:
    def __init__(self, at, outs, sems, phases=(0, 1, 2), own=None):
        self.at, self.outs, self.own = at, outs, own
        self.base = {t: sum(4 if p == 0 else 16 for p in phases if p < t) for t in phases}
        self.ssem, self.rsem, self.msem, self.nsem = sems
        self.n = len(outs)
        self.half = outs[0].shape[5] // 2
        self.late, self.sent = [], []

    def copies(self, s, t, g):
        ref = self.outs[s].at[piece_index(self.at, s, t, g, 0)]
        a, i = ORDERS[s][t], self.base[t] + 4 * (g or 0)
        src = self.own[s] if self.own and (t == 0 or (t == 1 and g == 0)) else ref
        return [
            remote(src, ref, self.ssem.at[s, i + d], self.rsem.at[s, i + d], device(moved(self.at, a, step)))
            for d, step in enumerate((1, -1))
        ]

    def forwards(self, s, t, g):
        a, i = ORDERS[s][t], self.base[t] + 4 * (g or 0) + 2
        out = []
        for d, step in enumerate((1, -1)):
            came = piece_index(self.at, s, t, g, -step) + (pl.ds(d * self.half, self.half),)
            ref = self.outs[s].at[came]
            out.append(
                remote(
                    ref,
                    ref,
                    self.ssem.at[s, i + d],
                    self.rsem.at[s, i + d],
                    device(moved(self.at, a, step)),
                )
            )
        return out

    def to_mate(self, s, g, rel):
        slot = 4 * (g or 0) + SHIFT.index(rel)
        ref = self.outs[s].at[piece_index(self.at, s, 2, g, rel)]
        return remote(ref, ref, self.msem.at[s, slot], self.nsem.at[s, slot], device(mate(self.at)))

    def share(self, s, g, rel):
        cp = self.to_mate(s, g, rel)
        cp.start()
        self.late.append(cp)

    def send(self, t, g):
        for s in range(self.n):
            for cp in self.copies(s, t, g):
                cp.start()
                self.sent.append(cp)
            if t == 2:
                self.share(s, g, 0)

    def pass_on(self, t, g):
        for s in range(self.n):
            first = self.copies(s, t, g)
            for d, cp in enumerate(self.forwards(s, t, g)):
                first[d].wait_recv()
                cp.start()
                self.sent.append(cp)
                if t == 2:
                    self.share(s, g, (-1, 1)[d])

    def arrived(self, t, g):
        for s in range(self.n):
            for cp in self.forwards(s, t, g):
                cp.wait_recv()
            if t == 2:
                self.share(s, g, 2)

    def drain(self):
        for cp in self.late:
            cp.wait()
        for cp in self.sent:
            cp.wait_send()

    def lines(self):
        self.send(0, None)
        self.send(1, 0)
        yield
        self.pass_on(0, None)
        self.send(1, 1)
        self.send(1, 2)
        yield
        self.pass_on(1, 0)
        self.arrived(0, None)
        self.send(1, 3)
        yield
        self.pass_on(1, 1)
        self.pass_on(1, 2)
        self.pass_on(1, 3)
        yield
        for g in range(4):
            self.arrived(1, g)

    def all(self):
        self.send(0, None)
        self.send(1, 0)
        yield
        self.pass_on(0, None)
        self.send(1, 1)
        self.send(1, 2)
        yield
        self.pass_on(1, 0)
        self.arrived(0, None)
        self.send(1, 3)
        self.send(2, 0)
        yield
        self.pass_on(1, 1)
        self.pass_on(1, 2)
        self.pass_on(1, 3)
        self.send(2, 1)
        self.send(2, 2)
        yield
        self.pass_on(2, 0)
        for g in range(4):
            self.arrived(1, g)
        self.send(2, 3)
        yield
        self.pass_on(2, 1)
        self.pass_on(2, 2)
        yield
        self.pass_on(2, 3)
        yield
        for g in range(4):
            self.arrived(2, g)


def gather_sems(steps, shares, n=3):
    return [DMA((n, steps)), DMA((n, steps)), DMA((n, max(shares, 1))), DMA((n, max(shares, 1)))]


def gather_shape(w):
    return sds((4, 2, 4, 2, 2, 64, w))


def lead_shape(axes):
    out = ()
    for a in ("x", "zl", "y", "zh"):
        if a[0] in axes:
            out += (4,) if a in "xy" else (2,)
    return out


def sub_index(sel, axes):
    out = ()
    for a in ("x", "zl", "y", "zh"):
        if a[0] not in axes:
            continue
        pos = sel.get(a[0])
        if pos is None:
            out += (slice(None),)
        elif a == "zl":
            out += (pos % 2,)
        elif a == "zh":
            out += (pos // 2,)
        else:
            out += (pos,)
    return out


def unravel(i, shape):
    out = ()
    for n in reversed(shape):
        out = (i % n,) + out
        i = i // n
    return out


def add_blocks(lead, dst, terms):
    n = math.prod(lead)

    def one(i):
        j = unravel(i, lead)
        total = None
        for ref, pre in terms:
            v = ref[pre(j)].astype(F32)
            total = v if total is None else total + v
        dst[0][dst[1](j)] = total.astype(dst[0].dtype)

    if n == 1:
        one(0)
    else:

        @pl.loop(0, n)
        def _(i):
            one(i)


def scatter_leads(s, t):
    return lead_shape(ORDERS[s][: 2 - t])


def scatter_buffers(w, t0=0, n=3):
    out = []
    for s in range(n):
        for t in range(t0, 3):
            lead = scatter_leads(s, t)
            out.append(pltpu.VMEM((2,) + lead + (32, w), BF))
            out.append(pltpu.VMEM((2,) + lead + (64, w), BF))
            out.append(pltpu.VMEM((2,) + lead + (32, w), BF))
            out.append(pltpu.VMEM(lead + (64, w), BF))
    return out


def scatter_sems(phases=3, n=3):
    return [DMA((n, phases, 6)), DMA((n, phases, 6)), DMA((n, 3))]


LO, HI = pl.ds(0, 32), pl.ds(32, 32)


def part_of(s, t, at, rel, rows):
    a = ORDERS[s][2 - t]
    return sub_index({a: (at[a] + rel) % 4}, ORDERS[s][: 3 - t]) + (rows,)


def first_sends(s, t, at, ref, rel_in, piece_in, ssem, rsem, t0=0):
    a = ORDERS[s][2 - t]
    right, left = device(moved(at, a, 1)), device(moved(at, a, -1))
    allr = (slice(None),) * len(scatter_leads(s, t))

    def src(rel, rows):
        return ref.at[part_of(s, t, at, rel, rows)]

    return [
        remote(src(2, LO), rel_in.at[0], ssem.at[s, t - t0, 0], rsem.at[s, t - t0, 0], right),
        remote(src(2, HI), rel_in.at[1], ssem.at[s, t - t0, 1], rsem.at[s, t - t0, 1], left),
        remote(
            src(1, HI), piece_in.at[(0,) + allr + (HI,)], ssem.at[s, t - t0, 2], rsem.at[s, t - t0, 2], right
        ),
        remote(
            src(-1, LO), piece_in.at[(1,) + allr + (LO,)], ssem.at[s, t - t0, 3], rsem.at[s, t - t0, 3], left
        ),
    ]


def second_send(s, t, at, d, rel_out, piece_in, ssem, rsem, t0=0):
    a = ORDERS[s][2 - t]
    allr = (slice(None),) * len(scatter_leads(s, t))
    return remote(
        rel_out.at[d],
        piece_in.at[(d,) + allr + ((LO, HI)[d],)],
        ssem.at[s, t - t0, 4 + d],
        rsem.at[s, t - t0, 4 + d],
        device(moved(at, a, (1, -1)[d])),
    )


def side(d):
    return lambda j: (d,) + j


def same(j):
    return j


def run_scatter(at, parts, results, bufs, sems, resident=False):
    ssem, rsem, lsem = sems
    t0 = 0
    n = len(parts)
    cur = list(parts)
    waits = []
    per = 4 * (3 - t0)
    for t in range(t0, 3):
        st = []
        for s in range(n):
            i = s * per + 4 * (t - t0)
            rel_in, piece_in, rel_out, total = bufs[i : i + 4]
            cps = first_sends(s, t, at, cur[s], rel_in, piece_in, ssem, rsem, t0)
            for cp in cps:
                cp.start()
            loads = []
            if t == t0 and not resident:
                for j, (rel, rows, dst) in enumerate(
                    ((1, LO, rel_out.at[0]), (-1, HI, rel_out.at[1]), (0, slice(None), total))
                ):
                    cp = pltpu.make_async_copy(
                        cur[s].at[part_of(s, t, at, rel, rows)], dst, lsem.at[s, j]
                    )
                    cp.start()
                    loads.append(cp)
            st.append((rel_in, piece_in, rel_out, total, cps, loads))
        yield
        for s in range(n):
            rel_in, piece_in, rel_out, total, cps, loads = st[s]
            lead = scatter_leads(s, t)
            for d in range(2):
                cps[d].wait_recv()
                if loads:
                    loads[d].wait()
                    mine = (rel_out, side(d))
                else:
                    mine = (cur[s], picker(s, t, at, (1, -1)[d], (LO, HI)[d]))
                add_blocks(lead, (rel_out, side(d)), [mine, (rel_in, side(d))])
                cp = second_send(s, t, at, d, rel_out, piece_in, ssem, rsem, t0)
                cp.start()
                cps.append(cp)
        yield
        for s in range(n):
            rel_in, piece_in, rel_out, total, cps, loads = st[s]
            lead = scatter_leads(s, t)
            for i in (2, 3, 4, 5):
                cps[i].wait_recv()
            if loads:
                loads[2].wait()
                mine = (total, same)
            else:
                mine = (cur[s], picker(s, t, at, 0, slice(None)))
            dst = (total, same) if t < 2 else (results[s], lambda j: (slice(None),) * 2)
            add_blocks(lead, dst, [mine, (piece_in, side(0)), (piece_in, side(1))])
            cur[s] = total
            waits += cps
    for cp in waits:
        cp.wait_send()


def picker(s, t, at, rel, rows):
    a, axes = ORDERS[s][2 - t], ORDERS[s][: 3 - t]
    pos = (at[a] + rel) % 4

    def pick(j):
        it = iter(j)
        out = ()
        for q in ("x", "zl", "y", "zh"):
            if q[0] not in axes:
                continue
            if q[0] == a:
                out += (pos % 2 if q == "zl" else pos // 2 if q == "zh" else pos,)
            else:
                out += (next(it),)
        return out + (rows,)

    return pick


def in_turn(*steps):
    live = list(steps)
    while live:
        for it in list(live):
            if next(it, "end") == "end":
                live.remove(it)


def swap_over(axis, src, dst, ssem, rsem, lsem):
    n = NR if axis == "row" else NC
    r = lax.axis_index("row")
    c = lax.axis_index("col")
    me = r if axis == "row" else c
    cps = []
    for d in range(1, n):
        to = (me + d) % n
        cp = remote(
            src.at[to],
            dst.at[me],
            ssem.at[d - 1],
            rsem.at[d - 1],
            (to, c) if axis == "row" else (r, to),
        )
        cp.start()
        cps.append(cp)
    own = pltpu.make_async_copy(src.at[me], dst.at[me], lsem)
    own.start()
    return cps + [own]


def swap_sems(axis):
    n = NR if axis == "row" else NC
    return [DMA((n - 1,)), DMA((n - 1,)), DMA]


def col_swap_kernel(src, dst, ssem, rsem, lsem):
    at = where_am_i()
    meet(col_peers(at))
    for cp in swap_over("col", src, dst, ssem, rsem, lsem):
        cp.wait()


def col_swap(src, cid, name):
    return pl.pallas_call(
        col_swap_kernel,
        name=name,
        out_shape=sds(src.shape),
        in_specs=[HBM],
        out_specs=HBM,
        scratch_shapes=swap_sems("col"),
        compiler_params=params(cid),
    )(src)


def dot(a, b, dims=((1,), (0,))):
    return lax.dot_general(a, b, (dims, ((), ())), preferred_element_type=F32)


NT = ((1,), (1,))
TN = ((0,), (0,))


def iota(shape, dim):
    return lax.broadcasted_iota(I32, shape, dim)


def onehot(cond):
    return cond.astype(F32).astype(BF)


def unrope(g, cos, sin):
    return g * cos - pltpu.roll(g, HEAD // 2, 1) * sin


def mean_square_scale(v):
    return lax.rsqrt(jnp.mean(v * v, axis=-1, keepdims=True) + EPSILON)


def column(row):
    eye = iota((ROWS, ROWS), 0) == iota((ROWS, ROWS), 1)
    return jnp.sum(jnp.where(eye, row.astype(F32), 0.0), axis=1, keepdims=True).astype(I32)


def slots_sent(target_row):
    g_row = target_row // GROUP
    g_col = column(g_row)
    same = g_row == g_col
    i0, i1 = iota((ROWS, ROWS), 0), iota((ROWS, ROWS), 1)
    before_row = jnp.sum((same & (i0 < i1)).astype(F32), axis=0, keepdims=True).astype(I32)
    before_col = jnp.sum((same & (i1 < i0)).astype(F32), axis=1, keepdims=True).astype(I32)
    return g_row * (ROWS // NR) + before_row, g_col * (ROWS // NR) + before_col


def halves_of(v):
    even, odd = [], []
    low = iota((v.shape[0], HEAD), 1) < HEAD // 2
    for m in range(4):
        a, b = v[:, 256 * m : 256 * m + 128], v[:, 256 * m + 128 : 256 * m + 256]
        even.append(jnp.where(low, a, pltpu.roll(b, 64, 1)))
        odd.append(jnp.where(low, pltpu.roll(a, 64, 1), b))
    return jnp.concatenate(even, axis=1), jnp.concatenate(odd, axis=1)


def first_slots(lens, slots):
    start = jnp.int32(0)
    out = jnp.zeros_like(slots)
    for j in range(8):
        out = jnp.where(slots >= start, start, out)
        start = start + lens(j)
    return out


def place(c):
    return (c % 4) * 2 + c // 4


def as_slabs(g):
    return g.reshape(NC, -1, g.shape[-1])


def front_kernel(
    t_row, lens, tokens, grads, again, qgain, kgain, freq, w_q, w_k, w_v, w_o, w_g, w_u, w_d,
    qkv, raw, x_o, dy_o, n1h, dyh, cos, sin, slt, a0, a1, a2, f0, f1, f2,
    sent, came, kv_s, n1_s, src_s, raw_s, wq_v, wkv_v,
    own_sem, w_sem, raw_sem, out_ssem, out_rsem, out_lsem, *sems,
):
    at = where_am_i()
    row, col = lax.axis_index("row"), lax.axis_index("col")
    here = block_index({a: at[a] for a in "xyz"}, at["k"])
    kv_s[:, :HEAD] = w_k[...]
    kv_s[:, HEAD:] = w_v[...]
    pairs = zip((w_q, kv_s, w_o, w_g, w_u, w_d), (a0, a1, a2, f0, f1, f2))
    own = [
        pltpu.make_async_copy(src, dst.at[here], own_sem.at[i])
        for i, (src, dst) in enumerate(pairs)
    ]
    for cp in own:
        cp.start()
    near = [device(moved(at, "z", 1)), device(moved(at, "z", -1))]
    meet(near + row_peers(at) + col_peers(at))
    first = Gather(at, (a0, a1, a2), sems[3:7], own=(w_q, kv_s, w_o))
    second = Gather(at, (f0, f1, f2), sems[7:11], (0, 1), own=(w_g, w_u, w_d))
    steps = first.all()
    more = second.lines()
    next(steps)
    place, _ = slots_sent(t_row[...])
    sel = place == iota((ROWS, ROWS), 0)
    pick = onehot(sel)
    slot = jnp.sum(jnp.where(sel, t_row[...] % ROWS, 0).astype(F32), axis=1, keepdims=True)
    message = (NR, 16, WIDTH)
    sent[:, :, 0:WIDTH] = dot(pick, tokens[...]).astype(BF).reshape(message)
    sent[:, :, WIDTH : 2 * WIDTH] = dot(pick, grads[...]).astype(BF).reshape(message)
    sent[:, :, 2 * WIDTH :] = (
        jnp.broadcast_to(slot, (ROWS, HEAD)).astype(BF).reshape((NR, 16, HEAD))
    )
    cps = swap_over("row", sent, came, *sems[0:3])
    next(steps)
    for cp in own:
        cp.wait()
    for _ in range(5):
        next(steps)
        next(more, None)

    slots = col * ROWS + iota((ROWS, HEAD), 0)
    pos = (slots - first_slots(lambda j: lens[0, j], slots)).astype(F32)
    angle = pos * freq[...]
    cos[...] = jnp.cos(angle)
    sine = jnp.sin(angle)
    sin[...] = jnp.where(iota((ROWS, HEAD), 1) < HEAD // 2, -sine, sine)
    for cp in cps:
        cp.wait()
    local = came[:, :, 2 * WIDTH :].reshape(ROWS, HEAD)
    slt[...] = local
    put = onehot(local[:, :1].astype(F32).astype(I32) == iota((ROWS, ROWS), 1))
    x = dot(put, came[:, :, 0:WIDTH].reshape(ROWS, WIDTH), TN)
    x_o[...] = x.astype(BF)
    n1 = x * mean_square_scale(x) * again[...]
    n1_s[...] = n1.astype(BF)
    a, b = halves_of(n1)
    n1h[0] = a.astype(BF)
    n1h[1] = b.astype(BF)
    dy = dot(put, came[:, :, WIDTH : 2 * WIDTH].reshape(ROWS, WIDTH), TN)
    dy_o[...] = dy.astype(BF)
    a, b = halves_of(dy)
    dyh[0] = a.astype(BF)
    dyh[1] = b.astype(BF)

    in_turn(steps, more)
    first.drain()
    second.drain()

    def block_at(i):
        return (col + 1 + i) % NC

    def loads(i):
        c, slot = block_at(i), i % 2
        return [
            pltpu.make_async_copy(a0.at[c % 4, c // 4], wq_v.at[slot], w_sem.at[0, slot]),
            pltpu.make_async_copy(a1.at[c % 4, c // 4], wkv_v.at[slot], w_sem.at[1, slot]),
        ]

    def sends(i):
        c = block_at(i)
        return remote(src_s.at[c], qkv.at[col], out_ssem.at[i], out_rsem.at[i], (row, c))

    for cp in loads(0):
        cp.start()

    @pl.loop(0, NC)
    def _(i):
        c = block_at(i)

        @pl.when(i < NC - 1)
        def _():
            for cp in loads(i + 1):
                cp.start()

        for cp in loads(i):
            cp.wait()
        n = n1_s[...]
        q = dot(n, wq_v[i % 2].reshape(WIDTH, 256))
        kv = dot(n, wkv_v[i % 2].reshape(WIDTH, 256))
        raw_s[c, :, 0:256] = q
        raw_s[c, :, 256:384] = kv[:, :HEAD]
        pieces = ((q[:, :HEAD], qgain), (q[:, HEAD:], qgain), (kv[:, :HEAD], kgain))
        for j, (v, gain) in enumerate(pieces):
            v = v * mean_square_scale(v) * gain[...]
            v = v * cos[...] + pltpu.roll(v, HEAD // 2, 1) * sin[...]
            src_s[c, :, j * HEAD : (j + 1) * HEAD] = v.astype(BF)
        src_s[c, :, 3 * HEAD :] = kv[:, HEAD:].astype(BF)

        @pl.when(i < NC - 1)
        def _():
            sends(i).start()

    mine = pltpu.make_async_copy(src_s.at[col], qkv.at[col], out_lsem)
    mine.start()
    keep = pltpu.make_async_copy(raw_s, raw, raw_sem)
    keep.start()
    for i in range(NC - 1):
        sends(i).wait()
    mine.wait()
    keep.wait()


def front(target, lens, tokens, grads, again, qgain, kgain, *weights):
    freq = ROPE_BASE ** (-(np.arange(HEAD) % (HEAD // 2)).astype(np.float32) * 2.0 / HEAD)
    freq = jnp.asarray(freq.astype(np.float32).reshape(1, HEAD))
    rows = pltpu.VMEM((NR, 16, 2 * WIDTH + HEAD), BF)
    return pl.pallas_call(
        front_kernel,
        name="front",
        out_shape=[
            sds((NC, ROWS, 512)),
            sds((NC, ROWS, 384), F32),
            sds((ROWS, WIDTH)),
            sds((ROWS, WIDTH)),
            sds((2, ROWS, 512)),
            sds((2, ROWS, 512)),
            sds((ROWS, HEAD), F32),
            sds((ROWS, HEAD), F32),
            sds((ROWS, HEAD)),
        ]
        + [gather_shape(256)] * 3
        + [gather_shape(384)] * 3,
        in_specs=[VMEM, pl.BlockSpec(memory_space=pltpu.SMEM)]
        + [VMEM] * 6
        + [HBM, VMEM, VMEM]
        + [HBM] * 4,
        out_specs=[HBM] * 2 + [VMEM] * 7 + [HBM] * 6,
        scratch_shapes=[rows, rows, pltpu.VMEM((64, 256), BF)]
        + [
            pltpu.VMEM((ROWS, WIDTH), BF),
            pltpu.VMEM((NC, ROWS, 512), BF),
            pltpu.VMEM((NC, ROWS, 384), F32),
            pltpu.VMEM((2, 4, 2, 2, 64, 256), BF),
            pltpu.VMEM((2, 4, 2, 2, 64, 256), BF),
        ]
        + [DMA((6,)), DMA((2, 2)), DMA, DMA((NC - 1,)), DMA((NC - 1,)), DMA]
        + swap_sems("row")
        + gather_sems(36, 16)
        + gather_sems(20, 0),
        compiler_params=params(1),
    )(target.reshape(1, ROWS), lens, tokens, grads, again, qgain, kgain, freq, *weights)


LOG2E = math.log2(math.e)
QK = 512


def stacked(v):
    return jnp.concatenate([v[:, :HEAD], v[:, HEAD : 2 * HEAD]], axis=0)


SPAN = 5


def group_slots(i):
    return i * ROWS + iota((1, QK), 1) % ROWS


def allowed(i, j, first):
    key = j * ROWS + iota((ROWS, QK), 0)
    return (key <= group_slots(i)) & (key >= first)


def attend_kernel(
    lens, qkv, i0, i1, i2, oa, o_t, lse, f0, f1, f2, o_s, s_v, ssem, rsem, lsem, *sems
):
    at = where_am_i()
    row, col = lax.axis_index("row"), lax.axis_index("col")
    meet(ring_peers(at) + [device(mate(at))] + col_peers(at))
    more = Gather(at, (f0, f1, f2), sems, (2,))
    more.send(2, None)
    scale = HEAD**-0.5 * LOG2E

    def block_at(n):
        return (col + 1 + n) % NC

    def sends(n):
        c = block_at(n)
        return remote(o_s.at[c], oa.at[col], ssem.at[n], rsem.at[n], (row, c))

    @pl.loop(0, NC)
    def _(n):
        i = block_at(n)
        q = stacked(qkv[i, :, 0 : 2 * HEAD])
        start = first_slots(lambda j: lens[0, j], group_slots(i))
        j0 = jnp.maximum(i - (SPAN - 1), 0)
        m = None
        for d in range(SPAN):
            s = dot(qkv[j0 + d, :, 2 * HEAD : 3 * HEAD], q, NT) * scale
            s = jnp.where(allowed(i, j0 + d, start), s, -1e30)
            s_v[d] = s
            top = jnp.max(s, axis=0, keepdims=True)
            m = top if m is None else jnp.maximum(m, top)
        total = jnp.zeros((1, QK), F32)
        acc = jnp.zeros((HEAD, QK), F32)
        for d in range(SPAN):
            p = jnp.exp2(s_v[d] - m)
            total = total + jnp.sum(p, axis=0, keepdims=True)
            acc = acc + dot(qkv[j0 + d, :, 3 * HEAD :], p.astype(BF), TN)
        o = acc / total
        o_t[i] = o
        lse[i] = m + jnp.log2(total)
        back = o.T
        o_s[i] = jnp.concatenate([back[:ROWS], back[ROWS:]], axis=1).astype(BF)

        @pl.when(n < NC - 1)
        def _():
            sends(n).start()

        @pl.when(n == NC - 2)
        def _():
            more.pass_on(2, None)

    mine = pltpu.make_async_copy(o_s.at[col], oa.at[col], lsem)
    mine.start()
    more.arrived(2, None)
    for n in range(NC - 1):
        sends(n).wait()
    mine.wait()
    for s in range(3):
        for cp in more.copies(s, 2, None) + more.forwards(s, 2, None):
            cp.wait_send()
        for rel in SHIFT:
            more.to_mate(s, None, rel).wait()


def attend(lens, qkv, planes):
    return pl.pallas_call(
        attend_kernel,
        name="attend",
        out_shape=[
            sds((NC, ROWS, 256)),
            sds((NC, HEAD, QK), F32),
            sds((NC, 1, QK), F32),
        ]
        + [gather_shape(384)] * 3,
        in_specs=[pl.BlockSpec(memory_space=pltpu.SMEM), VMEM] + [HBM] * 3,
        out_specs=[HBM, VMEM, VMEM] + [HBM] * 3,
        input_output_aliases={2: 3, 3: 4, 4: 5},
        scratch_shapes=[pltpu.VMEM((NC, ROWS, 256), BF), pltpu.VMEM((SPAN, ROWS, QK), F32)]
        + swap_sems("col")
        + gather_sems(4, 4),
        compiler_params=params(2),
    )(lens, qkv, *planes)


PAIR = 768
STEPS = 4


def stack_tokens(k, mine, others, scratch):
    scratch[:, 0:ROWS] = mine[k].astype(F32).T.astype(BF)
    scratch[:, ROWS:] = others[...].astype(F32).T.astype(BF)


def middle_kernel(
    slt, x, dy, dyh, fgain, oa, wo, wg, wu, wd,
    dh_o, dhlh, gain_o, g_o, got, oa_m, dhl_m, p0, p1, p2,
    oa_v, wo_v, w_v, acc, dn2, h_s, n2_s, dhl_s, act, n2h, n2_m, dy_m, do_s, out_s, nt_s, yt_s, g_v,
    oa_sem, wo_sem, w_sem, g_sem, act_ssem, act_rsem, m_ssem, m_rsem, do_ssem, do_rsem, do_lsem,
    *row_sems,
):
    at = where_am_i()
    row, col, k = lax.axis_index("row"), lax.axis_index("col"), at["k"]
    to = device(mate(at))
    lead = []
    for p in range(NC):
        c = (p % 2) * 4 + p // 2
        lanes = pl.ds(256 * p, 256)
        lead.append(pltpu.make_async_copy(oa.at[c], oa_v.at[:, lanes], oa_sem.at[p]))
        lead.append(pltpu.make_async_copy(wo.at[p], wo_v.at[:, lanes], wo_sem.at[p]))
    for cp in lead:
        cp.start()

    def loads(t):
        slot = t % 2
        return [
            pltpu.make_async_copy(
                w.at[2 * t + j],
                w_v.at[slot, :, pl.ds(PAIR * i + 384 * j, 384)],
                w_sem.at[slot, 2 * i + j],
            )
            for i, w in enumerate((wg, wu, wd))
            for j in range(2)
        ]

    def act_send(t):
        rows = pl.ds(0, ROWS), pl.ds(ROWS, ROWS)
        return remote(act.at[t, rows[0]], act.at[t, rows[1]], act_ssem.at[t], act_rsem.at[t], to)

    def mate_send(i, src, dst):
        return remote(src, dst, m_ssem.at[i], m_rsem.at[i], to)

    for cp in loads(0):
        cp.start()
    meet(col_peers(at) + row_peers(at))
    to_mate = [mate_send(0, dyh.at[1 - k], dy_m), mate_send(1, oa, oa_m)]
    for cp in to_mate:
        cp.start()
    for cp in lead:
        cp.wait()

    @pl.loop(0, 4)
    def _(n):
        cols = pl.ds(pl.multiple_of(256 * n, 256), 256)
        acc[:, cols] = x[:, cols].astype(F32) + dot(oa_v[...], wo_v[cols, :], NT)

    h = acc[...]
    h_s[...] = h
    n2 = h * mean_square_scale(h) * fgain[...]
    n2_s[...] = n2.astype(BF)
    a, b = halves_of(n2)
    n2h[0] = a.astype(BF)
    n2h[1] = b.astype(BF)
    cp = mate_send(2, n2h.at[1 - k], n2_m)
    cp.start()
    to_mate.append(cp)
    dn2[...] = jnp.zeros_like(dn2)

    @pl.loop(0, STEPS)
    def _(t):
        slot = t % 2

        @pl.when(t < STEPS - 1)
        def _():
            for cp in loads(t + 1):
                cp.start()

        for cp in loads(t):
            cp.wait()
        g = dot(n2_s[...], w_v[slot, :, 0:PAIR])
        u = dot(n2_s[...], w_v[slot, :, PAIR : 2 * PAIR])
        dhid = dot(dy[...], w_v[slot, :, 2 * PAIR :])
        sig = jax.nn.sigmoid(g)
        silu = g * sig
        act[t, 0:ROWS, 2 * PAIR :] = (silu * u).astype(BF)
        act[t, 0:ROWS, 0:PAIR] = (dhid * u * sig * (1.0 + g * (1.0 - sig))).astype(BF)
        act[t, 0:ROWS, PAIR : 2 * PAIR] = (dhid * silu).astype(BF)
        act_send(t).start()
        acc[...] += dot(act[t, 0:ROWS, 2 * PAIR :], w_v[slot, :, 2 * PAIR :], NT)
        dn2[...] += dot(act[t, 0:ROWS, 0 : 2 * PAIR], w_v[slot, :, 0 : 2 * PAIR], NT)

    h = h_s[...]
    r2 = mean_square_scale(h)
    hn = h * r2
    e = dn2[...]
    gain_o[...] = jnp.sum(e * hn, axis=0, keepdims=True)
    e = e * fgain[...]
    dh = dy[...].astype(F32) + r2 * (e - hn * jnp.mean(e * hn, axis=-1, keepdims=True))
    dh_o[...] = dh
    dhl_s[...] = dh.astype(BF)

    def block_at(n):
        return (col + 1 + n) % NC

    def do_send(n):
        c = block_at(n)
        return remote(do_s.at[c], g_o.at[col], do_ssem.at[n], do_rsem.at[n], (row, c))

    @pl.loop(0, NC)
    def _(n):
        c = block_at(n)
        cols = pl.ds(pl.multiple_of(256 * place(c), 256), 256)
        do_s[c] = dot(dhl_s[...], wo_v[:, cols]).astype(BF)

        @pl.when(n < NC - 1)
        def _():
            do_send(n).start()

    mine = pltpu.make_async_copy(do_s.at[col], g_o.at[col], do_lsem)
    mine.start()
    take = onehot(slt[:, :1].astype(F32).astype(I32) == iota((ROWS, ROWS), 1))
    out_s[...] = dot(take, acc[...].astype(BF)).astype(BF).reshape(out_s.shape)
    back = swap_over("row", out_s, got, *row_sems)
    a, b = halves_of(dhl_s[...].astype(F32))
    dhlh[0] = a.astype(BF)
    dhlh[1] = b.astype(BF)
    cp = mate_send(3, dhlh.at[1 - k], dhl_m)
    cp.start()
    to_mate.append(cp)
    for cp in to_mate:
        cp.wait()
    stack_tokens(k, n2h, n2_m, nt_s)
    stack_tokens(k, dyh, dy_m, yt_s)

    def stores(t):
        slot = t % 2
        return [
            pltpu.make_async_copy(
                g_v.at[slot, :, pl.ds(PAIR * i + 384 * j, 384)],
                p.at[2 * t + j],
                g_sem.at[slot, 2 * i + j],
            )
            for i, p in enumerate((p0, p1, p2))
            for j in range(2)
        ]

    @pl.loop(0, STEPS)
    def _(t):
        slot = t % 2

        @pl.when(t >= 2)
        def _():
            for cp in stores(t - 2):
                cp.wait()

        act_send(t).wait()
        gu = 2 * PAIR
        g_v[slot, :, 0:gu] = dot(nt_s[...], act[t, :, 0:gu]).astype(BF)
        g_v[slot, :, gu:] = dot(yt_s[...], act[t, :, gu:]).astype(BF)
        for cp in stores(t):
            cp.start()

    for t in (STEPS - 2, STEPS - 1):
        for cp in stores(t):
            cp.wait()
    for n in range(NC - 1):
        do_send(n).wait()
    for cp in [mine] + back:
        cp.wait()


def middle(slt, x, dy, dyh, fgain, oa, wo, wg, wu, wd):
    vm = pltpu.VMEM
    return pl.pallas_call(
        middle_kernel,
        name="middle",
        out_shape=[
            sds((ROWS, WIDTH), F32),
            sds((2, ROWS, 512)),
            sds((1, WIDTH), F32),
            sds((NC, ROWS, 256)),
            sds((NR, 16, WIDTH)),
            sds((NC, ROWS, 256)),
            sds((ROWS, 512)),
        ]
        + [sds((NC, 512, 384))] * 3,
        in_specs=[VMEM] * 5 + [HBM] * 5,
        out_specs=[VMEM] * 3 + [HBM] * 7,
        scratch_shapes=[
            vm((ROWS, 2048), BF),
            vm((WIDTH, 2048), BF),
            vm((2, WIDTH, 3 * PAIR), BF),
            vm((ROWS, WIDTH), F32),
            vm((ROWS, WIDTH), F32),
            vm((ROWS, WIDTH), F32),
            vm((ROWS, WIDTH), BF),
            vm((ROWS, WIDTH), BF),
            vm((STEPS, 2 * ROWS, 3 * PAIR), BF),
            vm((2, ROWS, 512), BF),
            vm((ROWS, 512), BF),
            vm((ROWS, 512), BF),
            vm((NC, ROWS, 256), BF),
            vm((NR, 16, WIDTH), BF),
            vm((512, 2 * ROWS), BF),
            vm((512, 2 * ROWS), BF),
            vm((2, 512, 3 * PAIR), BF),
            DMA((NC,)),
            DMA((NC,)),
            DMA((2, 6)),
            DMA((2, 6)),
            DMA((STEPS,)),
            DMA((STEPS,)),
            DMA((4,)),
            DMA((4,)),
        ]
        + swap_sems("col")
        + swap_sems("row"),
        compiler_params=params(5),
    )(slt, x, dy, dyh, fgain, oa, *map(as_slabs, (wo, wg, wu, wd)))


def gain_steps(at, pieces, room, total, ssem, rsem):
    p = at["x"]
    lane = 0
    for ref in pieces:
        room[0, p, :, lane : lane + ref.shape[1]] = ref[...]
        lane += ref.shape[1]
    for t, a in enumerate("xyzk"):
        p = at[a]
        others = (1, 2, 3) if a != "k" else (1,)
        if t > 0:
            room[t, p] = total[...]
        step = []
        for d in others:
            to = device(moved(at, a, d)) if a != "k" else device(mate(at))
            sems = ssem.at[t, d - 1], rsem.at[t, d - 1]
            cp = remote(room.at[t, p], room.at[t, p], *sems, to)
            cp.start()
            step.append(cp)
        yield
        for cp in step:
            cp.wait()
        acc = room[t, 0]
        for j in range(1, len(others) + 1):
            acc = acc + room[t, j]
        total[...] = acc


def back_kernel(
    lens, qkv, d_o, o_t, lse, slt, x, dh, again, qgain, kgain, cos, sin, gain_f, n1h, dhlh, dhl_m,
    raw, wq, wkv, oa, oa_m, p0, p1, p2,
    r0, r1, r2, t0, t1, t2, got, gsum,
    out_s, qs, dos, delta, dq, first, came, draw, w_v, raw_v, acc, dx_s, gain_a, gain_qk,
    n1_m, nt_s, ht_s, oa_v, a0, a1, a2, room,
    kv_ssem, kv_rsem, kv_lsem, q_ssem, q_rsem, q_lsem, w_sem, m_ssem, m_rsem, n_ssem, n_rsem, oa_sem,
    g_ssem, g_rsem, *rest,
):
    at = where_am_i()
    row, col, k = lax.axis_index("row"), lax.axis_index("col"), at["k"]
    to = device(mate(at))
    row_sems, rest = rest[:3], rest[3:]
    a_sems, f_sems, rest = rest[:3], rest[3:6], rest[6:]
    na = len(scatter_buffers(256))
    a_bufs, f_bufs = rest[:na], rest[na:]
    near = [device(moved(at, "z", 1)), device(moved(at, "z", -1))]
    meet(near + row_peers(at) + col_peers(at))
    ffn = run_scatter(at, (p0, p1, p2), (t0, t1, t2), f_bufs, f_sems)
    next(ffn)
    swap_n1 = remote(n1h.at[1 - k], n1_m, n_ssem, n_rsem, to)
    swap_n1.start()

    scale = HEAD**-0.5

    @pl.loop(0, NC)
    def _(i):
        qs[i] = stacked(qkv[i, :, 0 : 2 * HEAD])
        g = stacked(d_o[i])
        dos[i] = g
        delta[i] = jnp.sum(g.astype(F32).T * o_t[i], axis=0, keepdims=True)
        dq[i] = jnp.zeros((HEAD, QK), F32)
        first[i] = first_slots(lambda n: lens[0, n], group_slots(i))

    def block_at(n):
        return (col + 1 + n) % NC

    lanes_q, lanes_kv = pl.ds(0, 2 * HEAD), pl.ds(2 * HEAD, 2 * HEAD)
    every = (slice(None),)

    def sends(n, lanes, ssem, rsem):
        c = block_at(n)
        src, dst = out_s.at[(c,) + every + (lanes,)], came.at[(col,) + every + (lanes,)]
        return remote(src, dst, ssem.at[n], rsem.at[n], (row, c))

    def sends_kv(n):
        return sends(n, lanes_kv, kv_ssem, kv_rsem)

    def sends_q(n):
        return sends(n, lanes_q, q_ssem, q_rsem)

    def keys(n):
        j = block_at(n)
        key = qkv[j, :, 2 * HEAD : 3 * HEAD]
        value = qkv[j, :, 3 * HEAD :]
        key_t = key.astype(F32).T.astype(BF)

        def step(i, carry):
            dk, dv = carry
            s = dot(key, qs[i], NT) * (scale * LOG2E) - lse[i]
            p = jnp.where(allowed(i, j, first[i]), jnp.exp2(s), 0.0)
            ds = (p * (dot(value, dos[i], NT) - delta[i]) * scale).astype(BF)
            dv = dv + dot(p.astype(BF), dos[i])
            dk = dk + dot(ds, qs[i])
            dq[i] += dot(key_t, ds)
            return dk, dv

        zero = jnp.zeros((ROWS, HEAD), F32)
        dk, dv = lax.fori_loop(j, jnp.minimum(j + SPAN, NC), step, (zero, zero))
        out_s[j, :, 2 * HEAD : 3 * HEAD] = dk.astype(BF)
        out_s[j, :, 3 * HEAD :] = dv.astype(BF)

        @pl.when(n < NC - 1)
        def _():
            sends_kv(n).start()

    pl.loop(0, 6)(keys)
    next(ffn)
    pl.loop(6, NC)(keys)

    @pl.loop(0, NC)
    def _(n):
        i = block_at(n)
        done = dq[i].T
        out_s[i, :, 0:HEAD] = done[:ROWS].astype(BF)
        out_s[i, :, HEAD : 2 * HEAD] = done[ROWS:].astype(BF)

        @pl.when(n < NC - 1)
        def _():
            sends_q(n).start()

    mine = []
    for lanes, sem in ((lanes_kv, kv_lsem), (lanes_q, q_lsem)):
        here = (col,) + every + (lanes,)
        mine.append(pltpu.make_async_copy(out_s.at[here], came.at[here], sem))
    for cp in mine:
        cp.start()

    def comes_from(n):
        return (col - 1 - n + NC) % NC

    def loads(n):
        c, slot = comes_from(n), n % 2
        return [
            pltpu.make_async_copy(wq.at[place(c)], w_v.at[slot, :, pl.ds(0, 256)], w_sem.at[0, slot]),
            pltpu.make_async_copy(
                wkv.at[place(c)], w_v.at[slot, :, pl.ds(256, 256)], w_sem.at[1, slot]
            ),
            pltpu.make_async_copy(raw.at[c], raw_v.at[slot], w_sem.at[2, slot]),
        ]

    def to_mate(n):
        c = comes_from(n)
        src, dst = draw.at[c, pl.ds(0, ROWS)], draw.at[c, pl.ds(ROWS, ROWS)]
        return remote(src, dst, m_ssem.at[n], m_rsem.at[n], to)

    for cp in loads(0):
        cp.start()
    next(ffn)
    acc[...] = jnp.zeros_like(acc)
    gain_qk[...] = jnp.zeros_like(gain_qk)

    def columns(n):
        c, slot = comes_from(n), n % 2

        @pl.when(n < NC - 1)
        def _():
            for cp in loads(n + 1):
                cp.start()
            sends_kv(n).wait_recv()
            sends_q(n).wait_recv()

        @pl.when(n == NC - 1)
        def _():
            for cp in mine:
                cp.wait()

        for cp in loads(n):
            cp.wait()
        for i, gain in enumerate((qgain, qgain, kgain)):
            cols = slice(i * HEAD, (i + 1) * HEAD)
            v = raw_v[slot, :, cols]
            r = mean_square_scale(v)
            xn = v * r
            dn = unrope(came[c, :, cols].astype(F32), cos[...], sin[...])
            lanes = slice(0, HEAD) if i < 2 else slice(HEAD, 2 * HEAD)
            gain_qk[:, lanes] += jnp.sum(dn * xn, axis=0, keepdims=True)
            e = dn * gain[...]
            e = r * (e - xn * jnp.mean(e * xn, axis=-1, keepdims=True))
            draw[c, 0:ROWS, cols] = e.astype(BF)
        draw[c, 0:ROWS, 3 * HEAD :] = came[c, :, 3 * HEAD :]
        to_mate(n).start()
        acc[...] += dot(draw[c, 0:ROWS, :], w_v[slot], NT)

    pl.loop(0, 4)(columns)
    next(ffn)
    pl.loop(4, NC)(columns)

    xv = x[...].astype(F32)
    inverse = mean_square_scale(xv)
    xn = xv * inverse
    e = acc[...]
    gain_a[...] = jnp.sum(e * xn, axis=0, keepdims=True)
    gains = gain_steps(at, (gain_a, gain_f, gain_qk), room, gsum, g_ssem, g_rsem)
    next(gains)
    e = e * again[...]
    dx = dh[...] + inverse * (e - xn * jnp.mean(e * xn, axis=-1, keepdims=True))
    take = onehot(slt[:, :1].astype(F32).astype(I32) == iota((ROWS, ROWS), 1))
    dx_s[...] = dot(take, dx.astype(BF)).astype(BF).reshape(dx_s.shape)
    back = swap_over("row", dx_s, got, *row_sems)

    def oa_loads(n):
        c, slot = comes_from(n), n % 2
        return [
            pltpu.make_async_copy(src.at[c], oa_v.at[slot, pl.ds(ROWS * i, ROWS)], oa_sem.at[i, slot])
            for i, src in enumerate((oa, oa_m))
        ]

    for cp in oa_loads(0):
        cp.start()
    stack_tokens(k, dhlh, dhl_m, ht_s)
    swap_n1.wait()
    stack_tokens(k, n1h, n1_m, nt_s)
    next(gains)

    @pl.loop(0, NC)
    def _(n):
        c, slot = comes_from(n), n % 2

        @pl.when(n < NC - 1)
        def _():
            for cp in oa_loads(n + 1):
                cp.start()

        to_mate(n).wait()
        g = dot(nt_s[...], draw[c]).astype(BF)
        a0[c % 4, c // 4] = g[:, 0:256].reshape(4, 2, 64, 256)
        a1[c % 4, c // 4] = g[:, 256:].reshape(4, 2, 64, 256)
        for cp in oa_loads(n):
            cp.wait()
        a2[c % 4, c // 4] = dot(ht_s[...], oa_v[slot]).astype(BF).reshape(4, 2, 64, 256)

    in_turn(
        run_scatter(at, (a0, a1, a2), (r0, r1, r2), a_bufs, a_sems, True),
        gains,
        ffn,
    )
    for n in range(NC - 1):
        sends_kv(n).wait_send()
        sends_q(n).wait_send()
    for cp in back:
        cp.wait()


def back(
    lens, qkv, d_o, o_t, lse, slt, x, dh, again, qgain, kgain, cos, sin, gain_f, n1h, dhlh, dhl_m,
    raw, wq, wkv, oa, oa_m, f_parts,
):
    vm = pltpu.VMEM
    total = 2 * WIDTH + 2 * HEAD
    return pl.pallas_call(
        back_kernel,
        name="back",
        out_shape=[sds((64, 256), F32)] * 3
        + [sds((64, 384), F32)] * 3
        + [sds((NR, 16, WIDTH)), sds((1, total), F32)],
        in_specs=[pl.BlockSpec(memory_space=pltpu.SMEM)] + [VMEM] * 16 + [HBM] * 8,
        out_specs=[VMEM] * 6 + [HBM, VMEM],
        scratch_shapes=[
            vm((NC, ROWS, 512), BF),
            vm((NC, QK, HEAD), BF),
            vm((NC, QK, HEAD), BF),
            vm((NC, 1, QK), F32),
            vm((NC, HEAD, QK), F32),
            vm((NC, 1, QK), I32),
            vm((NC, ROWS, 512), BF),
            vm((NC, 2 * ROWS, 512), BF),
            vm((2, WIDTH, 512), BF),
            vm((2, ROWS, 384), F32),
            vm((ROWS, WIDTH), F32),
            vm((NR, 16, WIDTH), BF),
            vm((1, WIDTH), F32),
            vm((1, 2 * HEAD), F32),
            vm((ROWS, 512), BF),
            vm((512, 2 * ROWS), BF),
            vm((512, 2 * ROWS), BF),
            vm((2, 2 * ROWS, 256), BF),
        ]
        + [vm((4, 2, 4, 2, 64, 256), BF)] * 3
        + [vm((4, 4, 1, total), F32)]
        + swap_sems("col") * 2
        + [DMA((3, 2)), DMA((NC,)), DMA((NC,)), DMA, DMA, DMA((2, 2)), DMA((4, 3)), DMA((4, 3))]
        + swap_sems("row")
        + scatter_sems()
        + scatter_sems()
        + scatter_buffers(256)
        + scatter_buffers(384),
        compiler_params=params(6, 63),
    )(
        lens, qkv, d_o, o_t, lse, slt, x, dh, again, qgain, kgain, cos, sin, gain_f, n1h, dhlh,
        dhl_m, raw, as_slabs(wq), as_slabs(wkv), oa, oa_m, *f_parts,
    )


def arrive_kernel(
    t_row, out, dx, q, kv, o, g, u, d, gains,
    out_o, dx_o, ga, gf, gq, gk, q_o, k_o, v_o, o_o, g_o, u_o, d_o,
):
    _, place = slots_sent(t_row[...])
    pick = onehot(place == iota((ROWS, ROWS), 1))
    out_o[...] = dot(pick, out[...].reshape(ROWS, WIDTH)).astype(BF)
    dx_o[...] = dot(pick, dx[...].reshape(ROWS, WIDTH)).astype(BF)
    ga[...] = gains[:, 0:WIDTH]
    gf[...] = gains[:, WIDTH : 2 * WIDTH]
    gq[...] = gains[:, 2 * WIDTH : 2 * WIDTH + HEAD]
    gk[...] = gains[:, 2 * WIDTH + HEAD :]
    q_o[...] = q[...]
    k_o[...] = kv[:, :HEAD]
    v_o[...] = kv[:, HEAD:]
    o_o[...] = o[...]
    g_o[...] = g[...]
    u_o[...] = u[...]
    d_o[...] = d[...]


def arrive(target, *args):
    return pl.pallas_call(
        arrive_kernel,
        name="arrive",
        out_shape=[sds((ROWS, WIDTH))] * 2
        + [sds((1, n), F32) for n in (WIDTH, WIDTH, HEAD, HEAD)]
        + [
            sds(n, F32)
            for n in ((64, 256), (64, 128), (64, 128), (64, 256), (64, 384), (64, 384), (64, 384))
        ],
        in_specs=[VMEM] * 10,
        out_specs=[VMEM] * 13,
        compiler_params=params(),
    )(target.reshape(1, ROWS), *args)


def local(
    tokens, grad_out, target, lengths, attn_gain, ffn_gain, q_gain, k_gain,
    w_query, key_matrix, value_matrix, w_out, w_gate, w_up, w_down,
):
    again, fgain = attn_gain.reshape(1, WIDTH), ffn_gain.reshape(1, WIDTH)
    qgain, kgain = q_gain.reshape(1, HEAD), k_gain.reshape(1, HEAD)

    qkv, raw, x, dy, n1h, dyh, cos, sin, slt, wq, wkv, wo, *planes = front(
        target, lengths, tokens, grad_out, again, qgain, kgain,
        w_query, key_matrix, value_matrix, w_out.T, w_gate, w_up, w_down.T,
    )
    oa, o_t, lse, wg, wu, wd = attend(lengths, qkv, planes)
    dh, dhlh, gain_f, g_o, got_out, oa_m, dhl_m, *f_parts = middle(
        slt, x, dy, dyh, fgain, oa, wo, wg, wu, wd
    )
    f_parts = [p.reshape(4, 2, 4, 2, 64, 384) for p in f_parts]
    r_q, r_kv, r_o, r_g, r_u, r_d, got_dx, gains = back(
        lengths, qkv, g_o, o_t, lse, slt, x, dh, again, qgain, kgain, cos, sin, gain_f, n1h, dhlh,
        dhl_m, raw, wq, wkv, oa, oa_m, f_parts,
    )
    output, input_grad, ga, gf, gq, gk, g_q, g_k, g_v, g_o, g_g, g_u, g_d = arrive(
        target, got_out, got_dx, r_q, r_kv, r_o, r_g, r_u, r_d, gains
    )
    return (
        output, input_grad, ga[0], gf[0], gq[0], gk[0], g_q, g_k, g_v, g_o.T, g_g, g_u, g_d.T,
    )


def solution(mesh):
    both = P(("row", "col"), None)
    by_row, by_col = P("row", "col"), P("col", "row")
    weights = (by_row, by_row, by_row, by_col, by_row, by_row, by_col)
    return jax.shard_map(
        local,
        mesh=mesh,
        in_specs=(both, both, P(("row", "col")), P("row", None), P(), P(), P(), P()) + weights,
        out_specs=(both, both, P(), P(), P(), P()) + weights,
        check_vma=False,
    )
```

```python
import functools
import math

import jax
import jax.numpy as jnp
import numpy as np
from jax import lax
from jax.experimental import pallas as pl
from jax.experimental.pallas import tpu as pltpu
from jax.sharding import PartitionSpec as P

MESH = pl.DeviceIdType.MESH
BF = jnp.bfloat16
F32 = jnp.float32
I32 = jnp.int32
EPSILON = 1e-06
ROPE_BASE = 1000000.0
HEAD = 128
NR = 16
NC = 8
ROWS = 256
WIDTH = 1024
GROUP = 2048
ORDERS = (("x", "y", "z"), ("y", "z", "x"), ("z", "x", "y"))
ATTN = (256, 256, 256)
FFN = (256, 256, 640)
HBM = pl.BlockSpec(memory_space=pltpu.HBM)
VMEM = pl.BlockSpec(memory_space=pltpu.VMEM)
DMA = pltpu.SemaphoreType.DMA


def sds(shape, dtype=BF):
    return jax.ShapeDtypeStruct(shape, dtype)


def params(cid=None, mib=56, **kw):
    if cid is not None:
        kw.update(collective_id=cid, has_side_effects=True)
    return pltpu.CompilerParams(vmem_limit_bytes=mib << 20, **kw)


def where_am_i():
    r = lax.axis_index("row")
    c = lax.axis_index("col")
    return {"x": c % 4, "y": r // 4, "z": 2 * ((r // 2) % 2) + c // 4, "k": r % 2}


def device(at):
    return (at["y"] * 4 + (at["z"] // 2) * 2 + at["k"], (at["z"] % 2) * 4 + at["x"])


def moved(at, axis, step):
    out = dict(at)
    out[axis] = (at[axis] + step) % 4
    return out


def mate(at):
    out = dict(at)
    out["k"] = 1 - at["k"]
    return out


def greet(peers):
    barrier = pltpu.get_barrier_semaphore()
    for p in peers:
        pl.semaphore_signal(barrier, inc=1, device_id=p, device_id_type=MESH)


def met(peers):
    pl.semaphore_wait(pltpu.get_barrier_semaphore(), len(peers))


def ring_peers(at):
    return [device(moved(at, a, s)) for a in "xyz" for s in (1, -1)]


def row_peers(at):
    r = lax.axis_index("row")
    c = lax.axis_index("col")
    return [((r + d) % NR, c) for d in range(1, NR)]


def col_peers(at):
    r = lax.axis_index("row")
    c = lax.axis_index("col")
    return [(r, (c + d) % NC) for d in range(1, NC)]


def remote(src, dst, ssem, rsem, to):
    return pltpu.make_async_remote_copy(
        src_ref=src, dst_ref=dst, send_sem=ssem, recv_sem=rsem, device_id=to, device_id_type=MESH
    )


def block_index(sel, with_core=None):
    full = slice(None)
    z = sel.get("z")
    idx = (
        sel.get("x", full),
        full if z is None else z % 2,
        sel.get("y", full),
        full if z is None else z // 2,
    )
    return idx if with_core is None else idx + (with_core,)


SHIFT = (0, -1, 1, 2)


def piece_index(at, order, t, g, rel):
    sel = {a: at[a] for a in order[t + 1 :]}
    if t > 0 and g is not None:
        sel[order[t - 1]] = (at[order[t - 1]] + SHIFT[g]) % 4
    sel[order[t]] = (at[order[t]] + rel) % 4
    return block_index(sel, at["k"])


class Gather:
    def __init__(self, at, outs, sems, phases=(0, 1, 2), own=None, orders=ORDERS, split=False):
        self.at, self.outs, self.own, self.orders = at, outs, own, orders
        self.base = {t: sum(4 if p == 0 or not split else 16 for p in phases if p < t) for t in phases}
        self.ssem, self.rsem, self.msem, self.nsem = sems
        self.n = len(outs)
        self.half = outs[0].shape[5] // 2
        self.late, self.sent = [], []

    def copies(self, s, t, g):
        ref = self.outs[s].at[piece_index(self.at, self.orders[s], t, g, 0)]
        a, i = self.orders[s][t], self.base[t] + 4 * (g or 0)
        src = self.own[s] if self.own and (t == 0 or (t == 1 and g == 0)) else ref
        return [
            remote(src, ref, self.ssem.at[s, i + d], self.rsem.at[s, i + d], device(moved(self.at, a, step)))
            for d, step in enumerate((1, -1))
        ]

    def forwards(self, s, t, g):
        a, i = self.orders[s][t], self.base[t] + 4 * (g or 0) + 2
        out = []
        for d, step in enumerate((1, -1)):
            came = piece_index(self.at, self.orders[s], t, g, -step) + (pl.ds(d * self.half, self.half),)
            ref = self.outs[s].at[came]
            out.append(
                remote(
                    ref,
                    ref,
                    self.ssem.at[s, i + d],
                    self.rsem.at[s, i + d],
                    device(moved(self.at, a, step)),
                )
            )
        return out

    def to_mate(self, s, g, rel):
        slot = 4 * (g or 0) + SHIFT.index(rel)
        ref = self.outs[s].at[piece_index(self.at, self.orders[s], 2, g, rel)]
        return remote(ref, ref, self.msem.at[s, slot], self.nsem.at[s, slot], device(mate(self.at)))

    def share(self, s, g, rel):
        cp = self.to_mate(s, g, rel)
        cp.start()
        self.late.append(cp)

    def send(self, t, g):
        for s in range(self.n):
            for cp in self.copies(s, t, g):
                cp.start()
                self.sent.append(cp)
            if t == 2:
                self.share(s, g, 0)

    def pass_on(self, t, g, wait=True):
        for s in range(self.n):
            first = self.copies(s, t, g) if wait else None
            for d, cp in enumerate(self.forwards(s, t, g)):
                if wait:
                    first[d].wait_recv()
                cp.start()
                self.sent.append(cp)
                if t == 2:
                    self.share(s, g, (-1, 1)[d])

    def arrived(self, t, g):
        for s in range(self.n):
            for cp in self.forwards(s, t, g):
                cp.wait_recv()
            if t == 2:
                self.share(s, g, 2)

    def drain(self):
        for cp in self.late:
            cp.wait()
        for cp in self.sent:
            cp.wait_send()

    def lines(self):
        for t in (0, 1):
            self.send(t, None)
            yield
            self.pass_on(t, None)
            yield
            self.arrived(t, None)

    def all(self):
        self.send(0, None)
        self.send(1, 0)
        yield
        self.pass_on(0, None)
        self.send(1, 1)
        self.send(1, 2)
        yield
        self.pass_on(1, 0)
        self.arrived(0, None)
        self.send(1, 3)
        self.send(2, 0)
        yield
        self.pass_on(1, 1)
        self.pass_on(1, 2)
        self.pass_on(1, 3)
        self.send(2, 1)
        self.send(2, 2)
        yield
        self.pass_on(2, 0)
        for g in range(4):
            self.arrived(1, g)
        self.send(2, 3)
        yield
        self.pass_on(2, 1)
        self.pass_on(2, 2)
        yield
        self.pass_on(2, 3)
        yield
        for g in range(4):
            self.arrived(2, g)


def gather_sems(steps, shares, n=3):
    return [DMA((n, steps)), DMA((n, steps)), DMA((n, max(shares, 1))), DMA((n, max(shares, 1)))]


def gather_shape(w):
    return sds((4, 2, 4, 2, 2, 64, w))


def lead_shape(axes):
    out = ()
    for a in ("x", "zl", "y", "zh"):
        if a[0] in axes:
            out += (4,) if a in "xy" else (2,)
    return out


def sub_index(sel, axes):
    out = ()
    for a in ("x", "zl", "y", "zh"):
        if a[0] not in axes:
            continue
        pos = sel.get(a[0])
        if pos is None:
            out += (slice(None),)
        elif a == "zl":
            out += (pos % 2,)
        elif a == "zh":
            out += (pos // 2,)
        else:
            out += (pos,)
    return out


def add_up(dst, terms):
    total = None
    if len(terms) == 2:
        total = terms[0][0][terms[0][1]] + terms[1][0][terms[1][1]]
    else:
        for ref, at in terms:
            v = ref[at].astype(F32)
            total = v if total is None else total + v
    dst[0][dst[1]] = total.astype(dst[0].dtype)


def scatter_leads(s, t):
    return lead_shape(ORDERS[s][: 2 - t])


def scatter_buffers(widths, t0=0, n=3):
    out = []
    for s in range(n):
        for t in range(t0, 3):
            lead, w = scatter_leads(s, t), widths[s]
            out.append(pltpu.VMEM((2,) + lead + (32, w), BF))
            out.append(pltpu.VMEM((2,) + lead + (64, w), BF))
            out.append(pltpu.VMEM((2,) + lead + (32, w), BF))
            out.append(pltpu.VMEM(lead + (64, w), BF))
    return out


def scatter_sems(phases=3, n=3):
    return [DMA((n, phases, 6)), DMA((n, phases, 6)), DMA((n, 3))]


LO, HI = pl.ds(0, 32), pl.ds(32, 32)


def part_of(s, t, at, rel, rows):
    a = ORDERS[s][2 - t]
    return sub_index({a: (at[a] + rel) % 4}, ORDERS[s][: 3 - t]) + (rows,)


def first_sends(s, t, at, ref, rel_in, piece_in, ssem, rsem, t0=0):
    a = ORDERS[s][2 - t]
    right, left = device(moved(at, a, 1)), device(moved(at, a, -1))
    allr = (slice(None),) * len(scatter_leads(s, t))

    def src(rel, rows):
        return ref.at[part_of(s, t, at, rel, rows)]

    return [
        remote(src(2, LO), rel_in.at[0], ssem.at[s, t - t0, 0], rsem.at[s, t - t0, 0], right),
        remote(src(2, HI), rel_in.at[1], ssem.at[s, t - t0, 1], rsem.at[s, t - t0, 1], left),
        remote(
            src(1, HI), piece_in.at[(0,) + allr + (HI,)], ssem.at[s, t - t0, 2], rsem.at[s, t - t0, 2], right
        ),
        remote(
            src(-1, LO), piece_in.at[(1,) + allr + (LO,)], ssem.at[s, t - t0, 3], rsem.at[s, t - t0, 3], left
        ),
    ]


def second_send(s, t, at, d, rel_out, piece_in, ssem, rsem, t0=0):
    a = ORDERS[s][2 - t]
    allr = (slice(None),) * len(scatter_leads(s, t))
    return remote(
        rel_out.at[d],
        piece_in.at[(d,) + allr + ((LO, HI)[d],)],
        ssem.at[s, t - t0, 4 + d],
        rsem.at[s, t - t0, 4 + d],
        device(moved(at, a, (1, -1)[d])),
    )


def run_scatter(at, parts, results, bufs, sems, resident=False):
    ssem, rsem, lsem = sems
    t0 = 0
    n = len(parts)
    cur = list(parts)
    waits = []
    per = 4 * (3 - t0)
    for t in range(t0, 3):
        st = []
        for s in range(n):
            i = s * per + 4 * (t - t0)
            rel_in, piece_in, rel_out, total = bufs[i : i + 4]
            cps = first_sends(s, t, at, cur[s], rel_in, piece_in, ssem, rsem, t0)
            for cp in cps:
                cp.start()
            loads = []
            if t == t0 and not resident:
                for j, (rel, rows, dst) in enumerate(
                    ((1, LO, rel_out.at[0]), (-1, HI, rel_out.at[1]), (0, slice(None), total))
                ):
                    cp = pltpu.make_async_copy(
                        cur[s].at[part_of(s, t, at, rel, rows)], dst, lsem.at[s, j]
                    )
                    cp.start()
                    loads.append(cp)
            st.append((rel_in, piece_in, rel_out, total, cps, loads))
        yield
        for s in range(n):
            rel_in, piece_in, rel_out, total, cps, loads = st[s]
            for d in range(2):
                cps[d].wait_recv()
                if loads:
                    loads[d].wait()
                    mine = (rel_out, d)
                else:
                    mine = (cur[s], part_of(s, t, at, (1, -1)[d], (LO, HI)[d]))
                add_up((rel_out, d), [mine, (rel_in, d)])
                cp = second_send(s, t, at, d, rel_out, piece_in, ssem, rsem, t0)
                cp.start()
                cps.append(cp)
        yield
        for s in range(n):
            rel_in, piece_in, rel_out, total, cps, loads = st[s]
            for i in (2, 3, 4, 5):
                cps[i].wait_recv()
            if loads:
                loads[2].wait()
                mine = (total, ...)
            else:
                mine = (cur[s], part_of(s, t, at, 0, slice(None)))
            dst = (total if t < 2 else results[s], ...)
            add_up(dst, [mine, (piece_in, 0), (piece_in, 1)])
            cur[s] = total
            waits += cps
    for cp in waits:
        cp.wait_send()


def in_turn(*steps):
    live = list(steps)
    while live:
        for it in list(live):
            if next(it, "end") == "end":
                live.remove(it)


def swap_over(axis, src, dst, ssem, rsem, lsem):
    n = NR if axis == "row" else NC
    r = lax.axis_index("row")
    c = lax.axis_index("col")
    me = r if axis == "row" else c
    cps = []
    for d in range(1, n):
        to = (me + d) % n
        cp = remote(
            src.at[to],
            dst.at[me],
            ssem.at[d - 1],
            rsem.at[d - 1],
            (to, c) if axis == "row" else (r, to),
        )
        cp.start()
        cps.append(cp)
    own = pltpu.make_async_copy(src.at[me], dst.at[me], lsem)
    own.start()
    return cps + [own]


def swap_sems(axis):
    n = NR if axis == "row" else NC
    return [DMA((n - 1,)), DMA((n - 1,)), DMA]


def dot(a, b, dims=((1,), (0,))):
    return lax.dot_general(a, b, (dims, ((), ())), preferred_element_type=F32)


NT = ((1,), (1,))
TN = ((0,), (0,))


def iota(shape, dim):
    return lax.broadcasted_iota(I32, shape, dim)


def onehot(cond):
    return cond.astype(F32).astype(BF)


def unrope(g, cos, sin):
    return g * cos - pltpu.roll(g, HEAD // 2, 1) * sin


def mean_square_scale(v):
    return lax.rsqrt(jnp.mean(v * v, axis=-1, keepdims=True) + EPSILON)


def column(row):
    eye = iota((ROWS, ROWS), 0) == iota((ROWS, ROWS), 1)
    return jnp.sum(jnp.where(eye, row.astype(F32), 0.0), axis=1, keepdims=True).astype(I32)


def slots_sent(target_row):
    g_row = target_row // GROUP
    g_col = column(g_row)
    same = g_row == g_col
    i0, i1 = iota((ROWS, ROWS), 0), iota((ROWS, ROWS), 1)
    before_row = jnp.sum((same & (i0 < i1)).astype(F32), axis=0, keepdims=True).astype(I32)
    before_col = jnp.sum((same & (i1 < i0)).astype(F32), axis=1, keepdims=True).astype(I32)
    return g_row * (ROWS // NR) + before_row, g_col * (ROWS // NR) + before_col


def halves_of(v):
    even, odd = [], []
    low = iota((v.shape[0], HEAD), 1) < HEAD // 2
    for m in range(4):
        a, b = v[:, 256 * m : 256 * m + 128], v[:, 256 * m + 128 : 256 * m + 256]
        even.append(jnp.where(low, a, pltpu.roll(b, 64, 1)))
        odd.append(jnp.where(low, pltpu.roll(a, 64, 1), b))
    return jnp.concatenate(even, axis=1), jnp.concatenate(odd, axis=1)


def first_slots(lens, slots):
    start = jnp.int32(0)
    out = jnp.zeros_like(slots)
    for j in range(8):
        out = jnp.where(slots >= start, start, out)
        start = start + lens(j)
    return out


def place(c):
    return (c % 4) * 2 + c // 4


def as_slabs(g):
    return g.reshape(NC, -1, g.shape[-1])


LOG2E = math.log2(math.e)
QK = 512


def stacked(v):
    return jnp.concatenate([v[:, :HEAD], v[:, HEAD : 2 * HEAD]], axis=0)


SPAN = 5


def group_slots(i):
    return i * ROWS + iota((1, QK), 1) % ROWS


def allowed(i, j, first):
    key = j * ROWS + iota((ROWS, QK), 0)
    return (key <= group_slots(i)) & (key >= first)


def front_kernel(
    t_row, lens, tokens, grads, again, qgain, kgain, freq, w_q, w_k, w_v, w_o, w_g, w_u, w_d,
    oa, raw, x_o, dy_o, n1h, dyh, cos, sin, slt, qkv_o, o_t, lse, a0, a1, a2, f0, f1, f2,
    sent, came, kv_s, u0_s, u1_s, u2_s, n1_s, src_s, raw_s, wq_v, wkv_v, qkv, o_s, s_v,
    own_sem, w_sem, keep_sem, out_ssem, out_rsem, out_lsem, o_ssem, o_rsem, o_lsem, *sems,
):
    at = where_am_i()
    row, col = lax.axis_index("row"), lax.axis_index("col")
    here = block_index({a: at[a] for a in "xyz"}, at["k"])
    near = [device(moved(at, "z", 1)), device(moved(at, "z", -1))]
    peers = near + row_peers(at) + col_peers(at)
    greet(peers)
    kv_s[:, :HEAD] = w_k[...]
    kv_s[:, HEAD:] = w_v[...]
    u0_s[...] = w_g[:, 0:256]
    u1_s[...] = w_u[:, 0:256]
    u2_s[:, 0:128] = w_g[:, 256:]
    u2_s[:, 128:256] = w_u[:, 256:]
    u2_s[:, 256:] = w_d[...]
    pairs = zip((w_q, kv_s, w_o, u0_s, u1_s, u2_s), (a0, a1, a2, f0, f1, f2))
    own = [
        pltpu.make_async_copy(src, dst.at[here], own_sem.at[i])
        for i, (src, dst) in enumerate(pairs)
    ]
    for cp in own:
        cp.start()
    place, _ = slots_sent(t_row[...])
    sel = place == iota((ROWS, ROWS), 0)
    pick = onehot(sel)
    slot = jnp.sum(jnp.where(sel, t_row[...] % ROWS, 0).astype(F32), axis=1, keepdims=True)
    message = (NR, 16, WIDTH)
    sent[0, :, :, 0:WIDTH] = dot(pick, tokens[...]).astype(BF).reshape(message)
    sent[0, :, :, WIDTH:] = (
        jnp.broadcast_to(slot, (ROWS, HEAD)).astype(BF).reshape((NR, 16, HEAD))
    )
    met(peers)
    attn = Gather(at, (a0, a1, a2), sems[6:10], own=(w_q, kv_s, w_o), split=True)
    lines = Gather(at, (f0, f1, f2), sems[10:14], (0, 1), own=(u0_s, u1_s, u2_s))
    planes = [
        Gather(at, (f0, f1), sems[14:18], (2,), orders=ORDERS[:2]),
        Gather(at, (f2,), sems[18:22], (2,), orders=ORDERS[2:]),
    ]
    steps = attn.all()
    more = lines.lines()
    next(steps)
    next(more)
    cps = swap_over("row", sent.at[0], came.at[0], *sems[0:3])
    next(steps)
    next(more)
    for cp in own:
        cp.wait()
    for _ in range(5):
        next(steps)
        next(more, None)
    slots = col * ROWS + iota((ROWS, HEAD), 0)
    pos = (slots - first_slots(lambda j: lens[0, j], slots)).astype(F32)
    angle = pos * freq[...]
    cos[...] = jnp.cos(angle)
    sine = jnp.sin(angle)
    sin[...] = jnp.where(iota((ROWS, HEAD), 1) < HEAD // 2, -sine, sine)
    sent[1, :, :, 0:WIDTH] = dot(pick, grads[...]).astype(BF).reshape(message)
    for cp in cps:
        cp.wait()
    local = came[0, :, :, WIDTH:].reshape(ROWS, HEAD)
    slt[...] = local
    put = onehot(local[:, :1].astype(F32).astype(I32) == iota((ROWS, ROWS), 1))
    x = dot(put, came[0, :, :, 0:WIDTH].reshape(ROWS, WIDTH), TN)
    x_o[...] = x.astype(BF)
    n1 = x * mean_square_scale(x) * again[...]
    n1_s[...] = n1.astype(BF)
    a, b = halves_of(n1)
    n1h[0] = a.astype(BF)
    n1h[1] = b.astype(BF)
    in_turn(steps, more)

    def block_at(i):
        return (col + 1 + i) % NC

    def loads(i):
        c, slot = block_at(i), i % 2
        return [
            pltpu.make_async_copy(a0.at[c % 4, c // 4], wq_v.at[slot], w_sem.at[0, slot]),
            pltpu.make_async_copy(a1.at[c % 4, c // 4], wkv_v.at[slot], w_sem.at[1, slot]),
        ]

    def sends(i):
        c = block_at(i)
        return remote(src_s.at[c], qkv.at[col], out_ssem.at[i], out_rsem.at[i], (row, c))

    attn.drain()
    planes[1].send(2, None)
    for cp in loads(0):
        cp.start()

    def columns(i):
        c = block_at(i)

        @pl.when(i < NC - 1)
        def _():
            for cp in loads(i + 1):
                cp.start()

        for cp in loads(i):
            cp.wait()
        n = n1_s[...]
        q = dot(n, wq_v[i % 2].reshape(WIDTH, 256))
        kv = dot(n, wkv_v[i % 2].reshape(WIDTH, 256))
        raw_s[c, :, 0:256] = q
        raw_s[c, :, 256:384] = kv[:, :HEAD]
        pieces = ((q[:, :HEAD], qgain), (q[:, HEAD:], qgain), (kv[:, :HEAD], kgain))
        for j, (v, gain) in enumerate(pieces):
            v = v * mean_square_scale(v) * gain[...]
            v = v * cos[...] + pltpu.roll(v, HEAD // 2, 1) * sin[...]
            src_s[c, :, j * HEAD : (j + 1) * HEAD] = v.astype(BF)
        src_s[c, :, 3 * HEAD :] = kv[:, HEAD:].astype(BF)

        @pl.when(i < NC - 1)
        def _():
            sends(i).start()

    pl.loop(0, NC)(columns)
    mine = pltpu.make_async_copy(src_s.at[col], qkv.at[col], out_lsem)
    mine.start()
    keep = [pltpu.make_async_copy(raw_s, raw, keep_sem.at[0])]
    keep[0].start()
    cps = swap_over("row", sent.at[1, :, :, pl.ds(0, WIDTH)], came.at[1, :, :, pl.ds(0, WIDTH)], *sems[3:6])
    for i in range(NC - 1):
        sends(i).wait()
    planes[0].send(2, None)
    mine.wait()
    keep.append(pltpu.make_async_copy(qkv, qkv_o, keep_sem.at[1]))
    keep[1].start()

    scale = HEAD**-0.5 * LOG2E

    def o_sends(n):
        c = block_at(n)
        return remote(o_s.at[c], oa.at[col], o_ssem.at[n], o_rsem.at[n], (row, c))

    def queries(n):
        i = block_at(n)
        q = stacked(qkv[i, :, 0 : 2 * HEAD])
        start = first_slots(lambda j: lens[0, j], group_slots(i))
        j0 = jnp.maximum(i - (SPAN - 1), 0)
        m = None
        for d in range(SPAN):
            s = dot(qkv[j0 + d, :, 2 * HEAD : 3 * HEAD], q, NT) * scale
            s = jnp.where(allowed(i, j0 + d, start), s, -1e30)
            s_v[d] = s
            top = jnp.max(s, axis=0, keepdims=True)
            m = top if m is None else jnp.maximum(m, top)
        total = jnp.zeros((1, QK), F32)
        acc = jnp.zeros((HEAD, QK), F32)
        for d in range(SPAN):
            p = jnp.exp2(s_v[d] - m)
            total = total + jnp.sum(p, axis=0, keepdims=True)
            acc = acc + dot(qkv[j0 + d, :, 3 * HEAD :], p.astype(BF), TN)
        o = acc / total
        o_t[i] = o
        lse[i] = m + jnp.log2(total)
        back = o.T
        o_s[i] = jnp.concatenate([back[:ROWS], back[ROWS:]], axis=1).astype(BF)

        @pl.when(n < NC - 1)
        def _():
            o_sends(n).start()

    pl.loop(0, 6)(queries)
    planes[1].pass_on(2, None)
    planes[0].pass_on(2, None)
    pl.loop(6, NC)(queries)
    mine = pltpu.make_async_copy(o_s.at[col], oa.at[col], o_lsem)
    mine.start()
    for cp in cps:
        cp.wait()
    dy = dot(put, came[1, :, :, 0:WIDTH].reshape(ROWS, WIDTH), TN)
    dy_o[...] = dy.astype(BF)
    a, b = halves_of(dy)
    dyh[0] = a.astype(BF)
    dyh[1] = b.astype(BF)
    planes[0].arrived(2, None)
    planes[1].arrived(2, None)
    for n in range(NC - 1):
        o_sends(n).wait()
    for cp in [mine] + keep:
        cp.wait()
    for g in [lines] + planes:
        g.drain()


def front(target, lens, tokens, grads, again, qgain, kgain, *weights):
    freq = ROPE_BASE ** (-(np.arange(HEAD) % (HEAD // 2)).astype(np.float32) * 2.0 / HEAD)
    freq = jnp.asarray(freq.astype(np.float32).reshape(1, HEAD))
    vm = pltpu.VMEM
    return pl.pallas_call(
        front_kernel,
        name="front",
        out_shape=[
            sds((NC, ROWS, 256)),
            sds((NC, ROWS, 384), F32),
            sds((ROWS, WIDTH)),
            sds((ROWS, WIDTH)),
            sds((2, ROWS, 512)),
            sds((2, ROWS, 512)),
            sds((ROWS, HEAD), F32),
            sds((ROWS, HEAD), F32),
            sds((ROWS, HEAD)),
            sds((NC, ROWS, 512)),
            sds((NC, HEAD, QK), F32),
            sds((NC, 1, QK), F32),
        ]
        + [gather_shape(w) for w in ATTN + FFN],
        in_specs=[VMEM, pl.BlockSpec(memory_space=pltpu.SMEM)]
        + [VMEM] * 6
        + [HBM, VMEM, VMEM, HBM]
        + [VMEM] * 3,
        out_specs=[HBM] * 2 + [VMEM] * 7 + [HBM] + [VMEM] * 2 + [HBM] * 6,
        scratch_shapes=[vm((2, NR, 16, WIDTH + HEAD), BF)] * 2
        + [vm((64, w), BF) for w in (256,) + FFN]
        + [
            vm((ROWS, WIDTH), BF),
            vm((NC, ROWS, 512), BF),
            vm((NC, ROWS, 384), F32),
            vm((2, 4, 2, 2, 64, 256), BF),
            vm((2, 4, 2, 2, 64, 256), BF),
            vm((NC, ROWS, 512), BF),
            vm((NC, ROWS, 256), BF),
            vm((SPAN, ROWS, QK), F32),
        ]
        + [DMA((6,)), DMA((2, 2)), DMA((2,))]
        + swap_sems("col") * 2
        + swap_sems("row") * 2
        + gather_sems(36, 16)
        + gather_sems(8, 0)
        + gather_sems(4, 4, 2)
        + gather_sems(4, 4, 1),
        compiler_params=params(1),
    )(target.reshape(1, ROWS), lens, tokens, grads, again, qgain, kgain, freq, *weights)


PAIR = 768
STEPS = 4


def stack_tokens(k, mine, others, scratch):
    scratch[:, 0:ROWS] = mine[k].astype(F32).T.astype(BF)
    scratch[:, ROWS:] = others[...].astype(F32).T.astype(BF)


def lanes_of(j):
    at = 384 * j
    return (
        (0, pl.ds(0, 256), pl.ds(at, 256)),
        (2, pl.ds(0, 128), pl.ds(at + 256, 128)),
        (1, pl.ds(0, 256), pl.ds(PAIR + at, 256)),
        (2, pl.ds(128, 128), pl.ds(PAIR + at + 256, 128)),
        (2, pl.ds(256, 384), pl.ds(2 * PAIR + at, 384)),
    )


def middle_kernel(
    slt, x, dy, dyh, fgain, oa, wo, f0, f1, f2,
    dh_o, dhlh, gain_o, g_o, got, oa_m, dhl_m, p0, p1, p2,
    oa_v, wo_v, w_v, acc, dn2, h_s, n2_s, dhl_s, act, n2h, n2_m, dy_m, do_s, out_s, nt_s, yt_s, g_v,
    oa_sem, wo_sem, w_sem, g_sem, act_ssem, act_rsem, m_ssem, m_rsem, do_ssem, do_rsem, do_lsem,
    *row_sems,
):
    at = where_am_i()
    row, col, k = lax.axis_index("row"), lax.axis_index("col"), at["k"]
    to = device(mate(at))
    peers = col_peers(at) + row_peers(at)
    greet(peers)
    lead = []
    for p in range(NC):
        c = (p % 2) * 4 + p // 2
        lanes = pl.ds(256 * p, 256)
        lead.append(pltpu.make_async_copy(oa.at[c], oa_v.at[:, lanes], oa_sem.at[p]))
        lead.append(pltpu.make_async_copy(wo.at[p], wo_v.at[:, lanes], wo_sem.at[p]))
    for cp in lead:
        cp.start()

    def loads(t):
        slot = t % 2
        return [
            pltpu.make_async_copy(
                (f0, f1, f2)[i].at[2 * t + j, :, src],
                w_v.at[slot, :, dst],
                w_sem.at[slot, 5 * j + n],
            )
            for j in range(2)
            for n, (i, src, dst) in enumerate(lanes_of(j))
        ]

    def act_send(t):
        rows = pl.ds(0, ROWS), pl.ds(ROWS, ROWS)
        return remote(act.at[t, rows[0]], act.at[t, rows[1]], act_ssem.at[t], act_rsem.at[t], to)

    def mate_send(i, src, dst):
        return remote(src, dst, m_ssem.at[i], m_rsem.at[i], to)

    for cp in loads(0):
        cp.start()
    for cp in lead:
        cp.wait()

    @pl.loop(0, 4)
    def _(n):
        cols = pl.ds(pl.multiple_of(256 * n, 256), 256)
        acc[:, cols] = x[:, cols].astype(F32) + dot(oa_v[...], wo_v[cols, :], NT)

    h = acc[...]
    h_s[...] = h
    n2 = h * mean_square_scale(h) * fgain[...]
    n2_s[...] = n2.astype(BF)
    a, b = halves_of(n2)
    n2h[0] = a.astype(BF)
    n2h[1] = b.astype(BF)
    met(peers)
    pairs = ((dyh.at[1 - k], dy_m), (oa, oa_m), (n2h.at[1 - k], n2_m))
    to_mate = [mate_send(i, src, dst) for i, (src, dst) in enumerate(pairs)]
    for cp in to_mate:
        cp.start()
    dn2[...] = jnp.zeros_like(dn2)

    @pl.loop(0, STEPS)
    def _(t):
        slot = t % 2

        @pl.when(t < STEPS - 1)
        def _():
            for cp in loads(t + 1):
                cp.start()

        for cp in loads(t):
            cp.wait()
        g = dot(n2_s[...], w_v[slot, :, 0:PAIR])
        u = dot(n2_s[...], w_v[slot, :, PAIR : 2 * PAIR])
        dhid = dot(dy[...], w_v[slot, :, 2 * PAIR :])
        sig = jax.nn.sigmoid(g)
        silu = g * sig
        act[t, 0:ROWS, 2 * PAIR :] = (silu * u).astype(BF)
        act[t, 0:ROWS, 0:PAIR] = (dhid * u * sig * (1.0 + g * (1.0 - sig))).astype(BF)
        act[t, 0:ROWS, PAIR : 2 * PAIR] = (dhid * silu).astype(BF)
        act_send(t).start()
        acc[...] += dot(act[t, 0:ROWS, 2 * PAIR :], w_v[slot, :, 2 * PAIR :], NT)
        dn2[...] += dot(act[t, 0:ROWS, 0 : 2 * PAIR], w_v[slot, :, 0 : 2 * PAIR], NT)

    h = h_s[...]
    r2 = mean_square_scale(h)
    hn = h * r2
    e = dn2[...]
    gain_o[...] = jnp.sum(e * hn, axis=0, keepdims=True)
    e = e * fgain[...]
    dh = dy[...].astype(F32) + r2 * (e - hn * jnp.mean(e * hn, axis=-1, keepdims=True))
    dh_o[...] = dh
    dhl_s[...] = dh.astype(BF)

    def block_at(n):
        return (col + 1 + n) % NC

    def do_send(n):
        c = block_at(n)
        return remote(do_s.at[c], g_o.at[col], do_ssem.at[n], do_rsem.at[n], (row, c))

    @pl.loop(0, NC)
    def _(n):
        c = block_at(n)
        cols = pl.ds(pl.multiple_of(256 * place(c), 256), 256)
        do_s[c] = dot(dhl_s[...], wo_v[:, cols]).astype(BF)

        @pl.when(n < NC - 1)
        def _():
            do_send(n).start()

    mine = pltpu.make_async_copy(do_s.at[col], g_o.at[col], do_lsem)
    mine.start()
    take = onehot(slt[:, :1].astype(F32).astype(I32) == iota((ROWS, ROWS), 1))
    out_s[...] = dot(take, acc[...].astype(BF)).astype(BF).reshape(out_s.shape)
    back = swap_over("row", out_s, got, *row_sems)
    a, b = halves_of(dhl_s[...].astype(F32))
    dhlh[0] = a.astype(BF)
    dhlh[1] = b.astype(BF)
    cp = mate_send(3, dhlh.at[1 - k], dhl_m)
    cp.start()
    to_mate.append(cp)
    for cp in to_mate:
        cp.wait()
    stack_tokens(k, n2h, n2_m, nt_s)
    stack_tokens(k, dyh, dy_m, yt_s)

    def stores(t):
        slot = t % 2
        return [
            pltpu.make_async_copy(
                g_v.at[slot, :, src],
                (p0, p1, p2)[i].at[2 * t + j, :, dst],
                g_sem.at[slot, 5 * j + n],
            )
            for j in range(2)
            for n, (i, dst, src) in enumerate(lanes_of(j))
        ]

    @pl.loop(0, STEPS)
    def _(t):
        slot = t % 2

        @pl.when(t >= 2)
        def _():
            for cp in stores(t - 2):
                cp.wait()

        act_send(t).wait()
        gu = 2 * PAIR
        g_v[slot, :, 0:gu] = dot(nt_s[...], act[t, :, 0:gu]).astype(BF)
        g_v[slot, :, gu:] = dot(yt_s[...], act[t, :, gu:]).astype(BF)
        for cp in stores(t):
            cp.start()

    for t in (STEPS - 2, STEPS - 1):
        for cp in stores(t):
            cp.wait()
    for n in range(NC - 1):
        do_send(n).wait()
    for cp in [mine] + back:
        cp.wait()


def middle(slt, x, dy, dyh, fgain, oa, wo, *planes):
    vm = pltpu.VMEM
    return pl.pallas_call(
        middle_kernel,
        name="middle",
        out_shape=[
            sds((ROWS, WIDTH), F32),
            sds((2, ROWS, 512)),
            sds((1, WIDTH), F32),
            sds((NC, ROWS, 256)),
            sds((NR, 16, WIDTH)),
            sds((NC, ROWS, 256)),
            sds((ROWS, 512)),
        ]
        + [sds((NC, 512, w)) for w in FFN],
        in_specs=[VMEM] * 5 + [HBM] * 5,
        out_specs=[VMEM] * 3 + [HBM] * 7,
        scratch_shapes=[
            vm((ROWS, 2048), BF),
            vm((WIDTH, 2048), BF),
            vm((2, WIDTH, 3 * PAIR), BF),
            vm((ROWS, WIDTH), F32),
            vm((ROWS, WIDTH), F32),
            vm((ROWS, WIDTH), F32),
            vm((ROWS, WIDTH), BF),
            vm((ROWS, WIDTH), BF),
            vm((STEPS, 2 * ROWS, 3 * PAIR), BF),
            vm((2, ROWS, 512), BF),
            vm((ROWS, 512), BF),
            vm((ROWS, 512), BF),
            vm((NC, ROWS, 256), BF),
            vm((NR, 16, WIDTH), BF),
            vm((512, 2 * ROWS), BF),
            vm((512, 2 * ROWS), BF),
            vm((2, 512, 3 * PAIR), BF),
            DMA((NC,)),
            DMA((NC,)),
            DMA((2, 10)),
            DMA((2, 10)),
            DMA((STEPS,)),
            DMA((STEPS,)),
            DMA((4,)),
            DMA((4,)),
        ]
        + swap_sems("col")
        + swap_sems("row"),
        compiler_params=params(5),
    )(slt, x, dy, dyh, fgain, oa, *map(as_slabs, (wo,) + planes))


def gain_steps(at, pieces, room, total, ssem, rsem):
    p = at["x"]
    lane = 0
    for ref in pieces:
        room[0, p, :, lane : lane + ref.shape[1]] = ref[...]
        lane += ref.shape[1]
    for t, a in enumerate("xyzk"):
        p = at[a]
        others = (1, 2, 3) if a != "k" else (1,)
        if t > 0:
            room[t, p] = total[...]
        step = []
        for d in others:
            to = device(moved(at, a, d)) if a != "k" else device(mate(at))
            sems = ssem.at[t, d - 1], rsem.at[t, d - 1]
            cp = remote(room.at[t, p], room.at[t, p], *sems, to)
            cp.start()
            step.append(cp)
        yield
        for cp in step:
            cp.wait()
        acc = room[t, 0]
        for j in range(1, len(others) + 1):
            acc = acc + room[t, j]
        total[...] = acc


def back_kernel(
    lens, qkv, d_o, lse, slt, x, dh, again, qgain, kgain, cos, sin, gain_f, n1h, dhlh, dhl_m,
    o_t, raw, wq, wkv, oa, oa_m, p0, p1, p2,
    r0, r1, r2, t0, t1, t2, got, gsum,
    out_s, qs, dos, delta, dq, first, came, draw, w_v, raw_v, acc, dx_s, gain_a, gain_qk,
    n1_m, nt_s, ht_s, oa_v, o_v, a0, a1, a2, room,
    kv_ssem, kv_rsem, kv_lsem, q_ssem, q_rsem, q_lsem, w_sem, m_ssem, m_rsem, n_ssem, n_rsem, oa_sem, o_sem,
    g_ssem, g_rsem, *rest,
):
    at = where_am_i()
    row, col, k = lax.axis_index("row"), lax.axis_index("col"), at["k"]
    to = device(mate(at))
    row_sems, rest = rest[:3], rest[3:]
    a_sems, f_sems, rest = rest[:3], rest[3:6], rest[6:]
    na = len(scatter_buffers(ATTN))
    a_bufs, f_bufs = rest[:na], rest[na:]
    near = [device(moved(at, "z", 1)), device(moved(at, "z", -1))]
    peers = near + row_peers(at) + col_peers(at)
    greet(peers)

    scale = HEAD**-0.5

    def o_load(i):
        return pltpu.make_async_copy(o_t.at[i], o_v.at[i % 2], o_sem.at[i % 2])

    o_load(0).start()

    @pl.loop(0, NC)
    def _(i):
        @pl.when(i < NC - 1)
        def _():
            o_load(i + 1).start()

        qs[i] = stacked(qkv[i, :, 0 : 2 * HEAD])
        g = stacked(d_o[i])
        dos[i] = g
        o_load(i).wait()
        delta[i] = jnp.sum(g.astype(F32).T * o_v[i % 2], axis=0, keepdims=True)
        dq[i] = jnp.zeros((HEAD, QK), F32)
        first[i] = first_slots(lambda n: lens[0, n], group_slots(i))

    met(peers)
    ffn = run_scatter(at, (p0, p1, p2), (t0, t1, t2), f_bufs, f_sems)
    next(ffn)
    swap_n1 = remote(n1h.at[1 - k], n1_m, n_ssem, n_rsem, to)
    swap_n1.start()

    def block_at(n):
        return (col + 1 + n) % NC

    lanes_q, lanes_kv = pl.ds(0, 2 * HEAD), pl.ds(2 * HEAD, 2 * HEAD)
    every = (slice(None),)

    def sends(n, lanes, ssem, rsem):
        c = block_at(n)
        src, dst = out_s.at[(c,) + every + (lanes,)], came.at[(col,) + every + (lanes,)]
        return remote(src, dst, ssem.at[n], rsem.at[n], (row, c))

    def sends_kv(n):
        return sends(n, lanes_kv, kv_ssem, kv_rsem)

    def sends_q(n):
        return sends(n, lanes_q, q_ssem, q_rsem)

    def keys(n):
        j = block_at(n)
        key = qkv[j, :, 2 * HEAD : 3 * HEAD]
        value = qkv[j, :, 3 * HEAD :]
        key_t = key.astype(F32).T.astype(BF)

        def step(i, carry):
            dk, dv = carry
            s = dot(key, qs[i], NT) * (scale * LOG2E) - lse[i]
            p = jnp.where(allowed(i, j, first[i]), jnp.exp2(s), 0.0)
            ds = (p * (dot(value, dos[i], NT) - delta[i]) * scale).astype(BF)
            dv = dv + dot(p.astype(BF), dos[i])
            dk = dk + dot(ds, qs[i])
            dq[i] += dot(key_t, ds)
            return dk, dv

        zero = jnp.zeros((ROWS, HEAD), F32)
        dk, dv = lax.fori_loop(j, jnp.minimum(j + SPAN, NC), step, (zero, zero))
        out_s[j, :, 2 * HEAD : 3 * HEAD] = dk.astype(BF)
        out_s[j, :, 3 * HEAD :] = dv.astype(BF)

        @pl.when(n < NC - 1)
        def _():
            sends_kv(n).start()

    pl.loop(0, NC)(keys)

    @pl.loop(0, NC)
    def _(n):
        i = block_at(n)
        done = dq[i].T
        out_s[i, :, 0:HEAD] = done[:ROWS].astype(BF)
        out_s[i, :, HEAD : 2 * HEAD] = done[ROWS:].astype(BF)

        @pl.when(n < NC - 1)
        def _():
            sends_q(n).start()

    mine = []
    for lanes, sem in ((lanes_kv, kv_lsem), (lanes_q, q_lsem)):
        here = (col,) + every + (lanes,)
        mine.append(pltpu.make_async_copy(out_s.at[here], came.at[here], sem))
    for cp in mine:
        cp.start()

    def comes_from(n):
        return (col - 1 - n + NC) % NC

    def loads(n):
        c, slot = comes_from(n), n % 2
        return [
            pltpu.make_async_copy(wq.at[place(c)], w_v.at[slot, :, pl.ds(0, 256)], w_sem.at[0, slot]),
            pltpu.make_async_copy(
                wkv.at[place(c)], w_v.at[slot, :, pl.ds(256, 256)], w_sem.at[1, slot]
            ),
            pltpu.make_async_copy(raw.at[c], raw_v.at[slot], w_sem.at[2, slot]),
        ]

    def to_mate(n):
        c = comes_from(n)
        src, dst = draw.at[c, pl.ds(0, ROWS)], draw.at[c, pl.ds(ROWS, ROWS)]
        return remote(src, dst, m_ssem.at[n], m_rsem.at[n], to)

    for cp in loads(0):
        cp.start()
    next(ffn)
    acc[...] = jnp.zeros_like(acc)
    gain_qk[...] = jnp.zeros_like(gain_qk)

    def columns(n):
        c, slot = comes_from(n), n % 2

        @pl.when(n < NC - 1)
        def _():
            for cp in loads(n + 1):
                cp.start()
            sends_kv(n).wait_recv()
            sends_q(n).wait_recv()

        @pl.when(n == NC - 1)
        def _():
            for cp in mine:
                cp.wait()

        for cp in loads(n):
            cp.wait()
        for i, gain in enumerate((qgain, qgain, kgain)):
            cols = slice(i * HEAD, (i + 1) * HEAD)
            v = raw_v[slot, :, cols]
            r = mean_square_scale(v)
            xn = v * r
            dn = unrope(came[c, :, cols].astype(F32), cos[...], sin[...])
            lanes = slice(0, HEAD) if i < 2 else slice(HEAD, 2 * HEAD)
            gain_qk[:, lanes] += jnp.sum(dn * xn, axis=0, keepdims=True)
            e = dn * gain[...]
            e = r * (e - xn * jnp.mean(e * xn, axis=-1, keepdims=True))
            draw[c, 0:ROWS, cols] = e.astype(BF)
        draw[c, 0:ROWS, 3 * HEAD :] = came[c, :, 3 * HEAD :]
        to_mate(n).start()
        acc[...] += dot(draw[c, 0:ROWS, :], w_v[slot], NT)

    pl.loop(0, NC)(columns)

    xv = x[...].astype(F32)
    inverse = mean_square_scale(xv)
    xn = xv * inverse
    e = acc[...]
    gain_a[...] = jnp.sum(e * xn, axis=0, keepdims=True)
    gains = gain_steps(at, (gain_a, gain_f, gain_qk), room, gsum, g_ssem, g_rsem)
    next(gains)
    e = e * again[...]
    dx = dh[...] + inverse * (e - xn * jnp.mean(e * xn, axis=-1, keepdims=True))
    take = onehot(slt[:, :1].astype(F32).astype(I32) == iota((ROWS, ROWS), 1))
    dx_s[...] = dot(take, dx.astype(BF)).astype(BF).reshape(dx_s.shape)
    back = swap_over("row", dx_s, got, *row_sems)
    next(ffn)

    def oa_loads(n):
        c, slot = comes_from(n), n % 2
        return [
            pltpu.make_async_copy(src.at[c], oa_v.at[slot, pl.ds(ROWS * i, ROWS)], oa_sem.at[i, slot])
            for i, src in enumerate((oa, oa_m))
        ]

    for cp in oa_loads(0):
        cp.start()
    stack_tokens(k, dhlh, dhl_m, ht_s)
    swap_n1.wait()
    stack_tokens(k, n1h, n1_m, nt_s)
    next(gains)

    @pl.loop(0, NC)
    def _(n):
        c, slot = comes_from(n), n % 2

        @pl.when(n < NC - 1)
        def _():
            for cp in oa_loads(n + 1):
                cp.start()

        to_mate(n).wait()
        g = dot(nt_s[...], draw[c]).astype(BF)
        a0[c % 4, c // 4] = g[:, 0:256].reshape(4, 2, 64, 256)
        a1[c % 4, c // 4] = g[:, 256:].reshape(4, 2, 64, 256)
        for cp in oa_loads(n):
            cp.wait()
        a2[c % 4, c // 4] = dot(ht_s[...], oa_v[slot]).astype(BF).reshape(4, 2, 64, 256)

    in_turn(
        run_scatter(at, (a0, a1, a2), (r0, r1, r2), a_bufs, a_sems, True),
        gains,
        ffn,
    )
    for n in range(NC - 1):
        sends_kv(n).wait_send()
        sends_q(n).wait_send()
    for cp in back:
        cp.wait()


def back(
    lens, qkv, d_o, o_t, lse, slt, x, dh, again, qgain, kgain, cos, sin, gain_f, n1h, dhlh, dhl_m,
    raw, wq, wkv, oa, oa_m, f_parts,
):
    vm = pltpu.VMEM
    total = 2 * WIDTH + 2 * HEAD
    return pl.pallas_call(
        back_kernel,
        name="back",
        out_shape=[sds((64, 256), F32)] * 3
        + [sds((64, w), F32) for w in FFN]
        + [sds((NR, 16, WIDTH)), sds((1, total), F32)],
        in_specs=[pl.BlockSpec(memory_space=pltpu.SMEM)] + [VMEM] * 15 + [HBM] * 9,
        out_specs=[VMEM] * 6 + [HBM, VMEM],
        scratch_shapes=[
            vm((NC, ROWS, 512), BF),
            vm((NC, QK, HEAD), BF),
            vm((NC, QK, HEAD), BF),
            vm((NC, 1, QK), F32),
            vm((NC, HEAD, QK), F32),
            vm((NC, 1, QK), I32),
            vm((NC, ROWS, 512), BF),
            vm((NC, 2 * ROWS, 512), BF),
            vm((2, WIDTH, 512), BF),
            vm((2, ROWS, 384), F32),
            vm((ROWS, WIDTH), F32),
            vm((NR, 16, WIDTH), BF),
            vm((1, WIDTH), F32),
            vm((1, 2 * HEAD), F32),
            vm((ROWS, 512), BF),
            vm((512, 2 * ROWS), BF),
            vm((512, 2 * ROWS), BF),
            vm((2, 2 * ROWS, 256), BF),
            vm((2, HEAD, QK), F32),
        ]
        + [vm((4, 2, 4, 2, 64, 256), BF)] * 3
        + [vm((4, 4, 1, total), F32)]
        + swap_sems("col") * 2
        + [DMA((3, 2)), DMA((NC,)), DMA((NC,)), DMA, DMA, DMA((2, 2)), DMA((2,))]
        + [DMA((4, 3)), DMA((4, 3))]
        + swap_sems("row")
        + scatter_sems()
        + scatter_sems()
        + scatter_buffers(ATTN)
        + scatter_buffers(FFN),
        compiler_params=params(6, 63),
    )(
        lens, qkv, d_o, lse, slt, x, dh, again, qgain, kgain, cos, sin, gain_f, n1h, dhlh,
        dhl_m, o_t, raw, as_slabs(wq), as_slabs(wkv), oa, oa_m, *f_parts,
    )


def arrive_kernel(
    t_row, out, dx, q, kv, o, g, u, d, gains,
    out_o, dx_o, ga, gf, gq, gk, q_o, k_o, v_o, o_o, g_o, u_o, d_o,
):
    _, place = slots_sent(t_row[...])
    pick = onehot(place == iota((ROWS, ROWS), 1))
    out_o[...] = dot(pick, out[...].reshape(ROWS, WIDTH)).astype(BF)
    dx_o[...] = dot(pick, dx[...].reshape(ROWS, WIDTH)).astype(BF)
    ga[...] = gains[:, 0:WIDTH]
    gf[...] = gains[:, WIDTH : 2 * WIDTH]
    gq[...] = gains[:, 2 * WIDTH : 2 * WIDTH + HEAD]
    gk[...] = gains[:, 2 * WIDTH + HEAD :]
    q_o[...] = q[...]
    k_o[...] = kv[:, :HEAD]
    v_o[...] = kv[:, HEAD:]
    o_o[...] = o[...]
    g_o[:, 0:256] = g[...]
    g_o[:, 256:] = d[:, 0:128]
    u_o[:, 0:256] = u[...]
    u_o[:, 256:] = d[:, 128:256]
    d_o[...] = d[:, 256:]


def arrive(target, *args):
    return pl.pallas_call(
        arrive_kernel,
        name="arrive",
        out_shape=[sds((ROWS, WIDTH))] * 2
        + [sds((1, n), F32) for n in (WIDTH, WIDTH, HEAD, HEAD)]
        + [
            sds(n, F32)
            for n in ((64, 256), (64, 128), (64, 128), (64, 256), (64, 384), (64, 384), (64, 384))
        ],
        in_specs=[VMEM] * 10,
        out_specs=[VMEM] * 13,
        compiler_params=params(),
    )(target.reshape(1, ROWS), *args)


def local(
    tokens, grad_out, target, lengths, attn_gain, ffn_gain, q_gain, k_gain,
    w_query, key_matrix, value_matrix, w_out, w_gate, w_up, w_down,
):
    again, fgain = attn_gain.reshape(1, WIDTH), ffn_gain.reshape(1, WIDTH)
    qgain, kgain = q_gain.reshape(1, HEAD), k_gain.reshape(1, HEAD)

    oa, raw, x, dy, n1h, dyh, cos, sin, slt, qkv, o_t, lse, wq, wkv, wo, *planes = front(
        target, lengths, tokens, grad_out, again, qgain, kgain,
        w_query, key_matrix, value_matrix, w_out.T, w_gate, w_up, w_down.T,
    )
    dh, dhlh, gain_f, g_o, got_out, oa_m, dhl_m, *f_parts = middle(
        slt, x, dy, dyh, fgain, oa, wo, *planes
    )
    f_parts = [p.reshape(4, 2, 4, 2, 64, -1) for p in f_parts]
    r_q, r_kv, r_o, r_g, r_u, r_d, got_dx, gains = back(
        lengths, qkv, g_o, o_t, lse, slt, x, dh, again, qgain, kgain, cos, sin, gain_f, n1h, dhlh,
        dhl_m, raw, wq, wkv, oa, oa_m, f_parts,
    )
    output, input_grad, ga, gf, gq, gk, g_q, g_k, g_v, g_o, g_g, g_u, g_d = arrive(
        target, got_out, got_dx, r_q, r_kv, r_o, r_g, r_u, r_d, gains
    )
    return (
        output, input_grad, ga[0], gf[0], gq[0], gk[0], g_q, g_k, g_v, g_o.T, g_g, g_u, g_d.T,
    )


def solution(mesh):
    both = P(("row", "col"), None)
    by_row, by_col = P("row", "col"), P("col", "row")
    weights = (by_row, by_row, by_row, by_col, by_row, by_row, by_col)
    return jax.shard_map(
        local,
        mesh=mesh,
        in_specs=(both, both, P(("row", "col")), P("row", None), P(), P(), P(), P()) + weights,
        out_specs=(both, both, P(), P(), P(), P()) + weights,
        check_vma=False,
    )
```

```python
import functools
import math

import jax
import jax.numpy as jnp
import numpy as np
from jax import lax
from jax.experimental import pallas as pl
from jax.experimental.pallas import tpu as pltpu
from jax.sharding import PartitionSpec as P

MESH = pl.DeviceIdType.MESH
BF = jnp.bfloat16
F32 = jnp.float32
I32 = jnp.int32
EPSILON = 1e-06
ROPE_BASE = 1000000.0
HEAD = 128
NR = 16
NC = 8
ROWS = 256
WIDTH = 1024
GROUP = 2048
ORDERS = (("x", "y", "z"), ("y", "z", "x"), ("z", "x", "y"))
ATTN = (256, 256, 256)
FFN = (256, 256, 640)
HBM = pl.BlockSpec(memory_space=pltpu.HBM)
VMEM = pl.BlockSpec(memory_space=pltpu.VMEM)
DMA = pltpu.SemaphoreType.DMA


def sds(shape, dtype=BF):
    return jax.ShapeDtypeStruct(shape, dtype)


def params(cid=None, mib=56, **kw):
    if cid is not None:
        kw.update(collective_id=cid, has_side_effects=True)
    return pltpu.CompilerParams(vmem_limit_bytes=mib << 20, **kw)


def where_am_i():
    r = lax.axis_index("row")
    c = lax.axis_index("col")
    return {"x": c % 4, "y": r // 4, "z": 2 * ((r // 2) % 2) + c // 4, "k": r % 2}


def device(at):
    return (at["y"] * 4 + (at["z"] // 2) * 2 + at["k"], (at["z"] % 2) * 4 + at["x"])


def moved(at, axis, step):
    out = dict(at)
    out[axis] = (at[axis] + step) % 4
    return out


def mate(at):
    out = dict(at)
    out["k"] = 1 - at["k"]
    return out


def greet(peers):
    barrier = pltpu.get_barrier_semaphore()
    for p in peers:
        pl.semaphore_signal(barrier, inc=1, device_id=p, device_id_type=MESH)


def met(peers):
    pl.semaphore_wait(pltpu.get_barrier_semaphore(), len(peers))


def ring_peers(at):
    return [device(moved(at, a, s)) for a in "xyz" for s in (1, -1)]


def row_peers(at):
    r = lax.axis_index("row")
    c = lax.axis_index("col")
    return [((r + d) % NR, c) for d in range(1, NR)]


def col_peers(at):
    r = lax.axis_index("row")
    c = lax.axis_index("col")
    return [(r, (c + d) % NC) for d in range(1, NC)]


def remote(src, dst, ssem, rsem, to):
    return pltpu.make_async_remote_copy(
        src_ref=src, dst_ref=dst, send_sem=ssem, recv_sem=rsem, device_id=to, device_id_type=MESH
    )


def block_index(sel, with_core=None):
    full = slice(None)
    z = sel.get("z")
    idx = (
        sel.get("x", full),
        full if z is None else z % 2,
        sel.get("y", full),
        full if z is None else z // 2,
    )
    return idx if with_core is None else idx + (with_core,)


SHIFT = (0, -1, 1, 2)


def piece_index(at, order, t, g, rel):
    sel = {a: at[a] for a in order[t + 1 :]}
    if t > 0 and g is not None:
        sel[order[t - 1]] = (at[order[t - 1]] + SHIFT[g]) % 4
    sel[order[t]] = (at[order[t]] + rel) % 4
    return block_index(sel, at["k"])


class Gather:
    def __init__(self, at, outs, sems, phases=(0, 1, 2), own=None, orders=ORDERS, split=False):
        self.at, self.outs, self.own, self.orders = at, outs, own, orders
        self.base = {t: sum(4 if p == 0 or not split else 16 for p in phases if p < t) for t in phases}
        self.ssem, self.rsem, self.msem, self.nsem = sems
        self.n = len(outs)
        self.half = outs[0].shape[5] // 2
        self.late, self.sent = [], []

    def copies(self, s, t, g):
        ref = self.outs[s].at[piece_index(self.at, self.orders[s], t, g, 0)]
        a, i = self.orders[s][t], self.base[t] + 4 * (g or 0)
        src = self.own[s] if self.own and (t == 0 or (t == 1 and g == 0)) else ref
        return [
            remote(src, ref, self.ssem.at[s, i + d], self.rsem.at[s, i + d], device(moved(self.at, a, step)))
            for d, step in enumerate((1, -1))
        ]

    def forwards(self, s, t, g):
        a, i = self.orders[s][t], self.base[t] + 4 * (g or 0) + 2
        out = []
        for d, step in enumerate((1, -1)):
            came = piece_index(self.at, self.orders[s], t, g, -step) + (pl.ds(d * self.half, self.half),)
            ref = self.outs[s].at[came]
            out.append(
                remote(
                    ref,
                    ref,
                    self.ssem.at[s, i + d],
                    self.rsem.at[s, i + d],
                    device(moved(self.at, a, step)),
                )
            )
        return out

    def to_mate(self, s, g, rel):
        slot = 4 * (g or 0) + SHIFT.index(rel)
        ref = self.outs[s].at[piece_index(self.at, self.orders[s], 2, g, rel)]
        return remote(ref, ref, self.msem.at[s, slot], self.nsem.at[s, slot], device(mate(self.at)))

    def share(self, s, g, rel):
        cp = self.to_mate(s, g, rel)
        cp.start()
        self.late.append(cp)

    def send(self, t, g):
        for s in range(self.n):
            for cp in self.copies(s, t, g):
                cp.start()
                self.sent.append(cp)
            if t == 2:
                self.share(s, g, 0)

    def pass_on(self, t, g, wait=True):
        for s in range(self.n):
            first = self.copies(s, t, g) if wait else None
            for d, cp in enumerate(self.forwards(s, t, g)):
                if wait:
                    first[d].wait_recv()
                cp.start()
                self.sent.append(cp)
                if t == 2:
                    self.share(s, g, (-1, 1)[d])

    def arrived(self, t, g):
        for s in range(self.n):
            for cp in self.forwards(s, t, g):
                cp.wait_recv()
            if t == 2:
                self.share(s, g, 2)

    def drain(self):
        for cp in self.late:
            cp.wait()
        for cp in self.sent:
            cp.wait_send()

    def lines(self):
        for t in (0, 1):
            self.send(t, None)
            yield
            self.pass_on(t, None)
            yield
            self.arrived(t, None)

    def all(self):
        self.send(0, None)
        self.send(1, 0)
        yield
        self.pass_on(0, None)
        self.send(1, 1)
        self.send(1, 2)
        yield
        self.pass_on(1, 0)
        self.arrived(0, None)
        self.send(1, 3)
        self.send(2, 0)
        yield
        self.pass_on(1, 1)
        self.pass_on(1, 2)
        self.pass_on(1, 3)
        self.send(2, 1)
        self.send(2, 2)
        yield
        self.pass_on(2, 0)
        for g in range(4):
            self.arrived(1, g)
        self.send(2, 3)
        yield
        self.pass_on(2, 1)
        self.pass_on(2, 2)
        yield
        self.pass_on(2, 3)
        yield
        for g in range(4):
            self.arrived(2, g)


def gather_sems(steps, shares, n=3):
    return [DMA((n, steps)), DMA((n, steps)), DMA((n, max(shares, 1))), DMA((n, max(shares, 1)))]


def gather_shape(w):
    return sds((4, 2, 4, 2, 2, 64, w))


def lead_shape(axes):
    out = ()
    for a in ("x", "zl", "y", "zh"):
        if a[0] in axes:
            out += (4,) if a in "xy" else (2,)
    return out


def sub_index(sel, axes):
    out = ()
    for a in ("x", "zl", "y", "zh"):
        if a[0] not in axes:
            continue
        pos = sel.get(a[0])
        if pos is None:
            out += (slice(None),)
        elif a == "zl":
            out += (pos % 2,)
        elif a == "zh":
            out += (pos // 2,)
        else:
            out += (pos,)
    return out


def add_up(dst, terms):
    total = None
    if len(terms) == 2:
        total = terms[0][0][terms[0][1]] + terms[1][0][terms[1][1]]
    else:
        for ref, at in terms:
            v = ref[at].astype(F32)
            total = v if total is None else total + v
    dst[0][dst[1]] = total.astype(dst[0].dtype)


def scatter_leads(s, t):
    return lead_shape(ORDERS[s][: 2 - t])


def scatter_buffers(widths, t0=0, n=3):
    out = []
    for s in range(n):
        for t in range(t0, 3):
            lead, w = scatter_leads(s, t), widths[s]
            out.append(pltpu.VMEM((2,) + lead + (32, w), BF))
            out.append(pltpu.VMEM((2,) + lead + (64, w), BF))
            out.append(pltpu.VMEM((2,) + lead + (32, w), BF))
            out.append(pltpu.VMEM(lead + (64, w), BF))
    return out


def scatter_sems(phases=3, n=3):
    return [DMA((n, phases, 6)), DMA((n, phases, 6)), DMA((n, 3))]


LO, HI = pl.ds(0, 32), pl.ds(32, 32)


def part_of(s, t, at, rel, rows):
    a = ORDERS[s][2 - t]
    return sub_index({a: (at[a] + rel) % 4}, ORDERS[s][: 3 - t]) + (rows,)


def first_sends(s, t, at, ref, rel_in, piece_in, ssem, rsem, t0=0):
    a = ORDERS[s][2 - t]
    right, left = device(moved(at, a, 1)), device(moved(at, a, -1))
    allr = (slice(None),) * len(scatter_leads(s, t))

    def src(rel, rows):
        return ref.at[part_of(s, t, at, rel, rows)]

    return [
        remote(src(2, LO), rel_in.at[0], ssem.at[s, t - t0, 0], rsem.at[s, t - t0, 0], right),
        remote(src(2, HI), rel_in.at[1], ssem.at[s, t - t0, 1], rsem.at[s, t - t0, 1], left),
        remote(
            src(1, HI), piece_in.at[(0,) + allr + (HI,)], ssem.at[s, t - t0, 2], rsem.at[s, t - t0, 2], right
        ),
        remote(
            src(-1, LO), piece_in.at[(1,) + allr + (LO,)], ssem.at[s, t - t0, 3], rsem.at[s, t - t0, 3], left
        ),
    ]


def second_send(s, t, at, d, rel_out, piece_in, ssem, rsem, t0=0):
    a = ORDERS[s][2 - t]
    allr = (slice(None),) * len(scatter_leads(s, t))
    return remote(
        rel_out.at[d],
        piece_in.at[(d,) + allr + ((LO, HI)[d],)],
        ssem.at[s, t - t0, 4 + d],
        rsem.at[s, t - t0, 4 + d],
        device(moved(at, a, (1, -1)[d])),
    )


def run_scatter(at, parts, results, bufs, sems, resident=False):
    ssem, rsem, lsem = sems
    t0 = 0
    n = len(parts)
    cur = list(parts)
    waits = []
    per = 4 * (3 - t0)
    for t in range(t0, 3):
        st = []
        for s in range(n):
            i = s * per + 4 * (t - t0)
            rel_in, piece_in, rel_out, total = bufs[i : i + 4]
            cps = first_sends(s, t, at, cur[s], rel_in, piece_in, ssem, rsem, t0)
            for cp in cps:
                cp.start()
            loads = []
            if t == t0 and not resident:
                for j, (rel, rows, dst) in enumerate(
                    ((1, LO, rel_out.at[0]), (-1, HI, rel_out.at[1]), (0, slice(None), total))
                ):
                    cp = pltpu.make_async_copy(
                        cur[s].at[part_of(s, t, at, rel, rows)], dst, lsem.at[s, j]
                    )
                    cp.start()
                    loads.append(cp)
            st.append((rel_in, piece_in, rel_out, total, cps, loads))
        yield
        for s in range(n):
            rel_in, piece_in, rel_out, total, cps, loads = st[s]
            for d in range(2):
                cps[d].wait_recv()
                if loads:
                    loads[d].wait()
                    mine = (rel_out, d)
                else:
                    mine = (cur[s], part_of(s, t, at, (1, -1)[d], (LO, HI)[d]))
                add_up((rel_out, d), [mine, (rel_in, d)])
                cp = second_send(s, t, at, d, rel_out, piece_in, ssem, rsem, t0)
                cp.start()
                cps.append(cp)
        yield
        for s in range(n):
            rel_in, piece_in, rel_out, total, cps, loads = st[s]
            for i in (2, 3, 4, 5):
                cps[i].wait_recv()
            if loads:
                loads[2].wait()
                mine = (total, ...)
            else:
                mine = (cur[s], part_of(s, t, at, 0, slice(None)))
            dst = (total if t < 2 else results[s], ...)
            add_up(dst, [mine, (piece_in, 0), (piece_in, 1)])
            cur[s] = total
            waits += cps
    for cp in waits:
        cp.wait_send()


def in_turn(*steps):
    live = list(steps)
    while live:
        for it in list(live):
            if next(it, "end") == "end":
                live.remove(it)


def swap_over(axis, src, dst, ssem, rsem, lsem):
    n = NR if axis == "row" else NC
    r = lax.axis_index("row")
    c = lax.axis_index("col")
    me = r if axis == "row" else c
    cps = []
    for d in range(1, n):
        to = (me + d) % n
        cp = remote(
            src.at[to],
            dst.at[me],
            ssem.at[d - 1],
            rsem.at[d - 1],
            (to, c) if axis == "row" else (r, to),
        )
        cp.start()
        cps.append(cp)
    own = pltpu.make_async_copy(src.at[me], dst.at[me], lsem)
    own.start()
    return cps + [own]


def swap_sems(axis):
    n = NR if axis == "row" else NC
    return [DMA((n - 1,)), DMA((n - 1,)), DMA]


def dot(a, b, dims=((1,), (0,))):
    return lax.dot_general(a, b, (dims, ((), ())), preferred_element_type=F32)


NT = ((1,), (1,))
TN = ((0,), (0,))


def iota(shape, dim):
    return lax.broadcasted_iota(I32, shape, dim)


def onehot(cond):
    return cond.astype(F32).astype(BF)


def unrope(g, cos, sin):
    return g * cos - pltpu.roll(g, HEAD // 2, 1) * sin


def mean_square_scale(v):
    return lax.rsqrt(jnp.mean(v * v, axis=-1, keepdims=True) + EPSILON)


def column(row):
    eye = iota((ROWS, ROWS), 0) == iota((ROWS, ROWS), 1)
    return jnp.sum(jnp.where(eye, row.astype(F32), 0.0), axis=1, keepdims=True).astype(I32)


def slots_sent(target_row):
    g_row = target_row // GROUP
    g_col = column(g_row)
    same = g_row == g_col
    i0, i1 = iota((ROWS, ROWS), 0), iota((ROWS, ROWS), 1)
    before_row = jnp.sum((same & (i0 < i1)).astype(F32), axis=0, keepdims=True).astype(I32)
    before_col = jnp.sum((same & (i1 < i0)).astype(F32), axis=1, keepdims=True).astype(I32)
    return g_row * (ROWS // NR) + before_row, g_col * (ROWS // NR) + before_col


def halves_of(v):
    even, odd = [], []
    low = iota((v.shape[0], HEAD), 1) < HEAD // 2
    for m in range(4):
        a, b = v[:, 256 * m : 256 * m + 128], v[:, 256 * m + 128 : 256 * m + 256]
        even.append(jnp.where(low, a, pltpu.roll(b, 64, 1)))
        odd.append(jnp.where(low, pltpu.roll(a, 64, 1), b))
    return jnp.concatenate(even, axis=1), jnp.concatenate(odd, axis=1)


def first_slots(lens, slots):
    start = jnp.int32(0)
    out = jnp.zeros_like(slots)
    for j in range(8):
        out = jnp.where(slots >= start, start, out)
        start = start + lens(j)
    return out


def place(c):
    return (c % 4) * 2 + c // 4


def as_slabs(g):
    return g.reshape(NC, -1, g.shape[-1])


LOG2E = math.log2(math.e)
QK = 512


def stacked(v):
    return jnp.concatenate([v[:, :HEAD], v[:, HEAD : 2 * HEAD]], axis=0)


SPAN = 5


def group_slots(i):
    return i * ROWS + iota((1, QK), 1) % ROWS


def allowed(i, j, first):
    key = j * ROWS + iota((ROWS, QK), 0)
    return (key <= group_slots(i)) & (key >= first)


PAIR = 768
STEPS = 4


def stack_tokens(k, mine, others, scratch):
    scratch[:, 0:ROWS] = mine[k].astype(F32).T.astype(BF)
    scratch[:, ROWS:] = others[...].astype(F32).T.astype(BF)


def lanes_of(j):
    at = 384 * j
    return (
        (0, pl.ds(0, 256), pl.ds(at, 256)),
        (2, pl.ds(0, 128), pl.ds(at + 256, 128)),
        (1, pl.ds(0, 256), pl.ds(PAIR + at, 256)),
        (2, pl.ds(128, 128), pl.ds(PAIR + at + 256, 128)),
        (2, pl.ds(256, 384), pl.ds(2 * PAIR + at, 384)),
    )


def middle_steps(
    at, slt, x, dy, dyh, fgain, oa, wo, f0, f1, f2,
    dh_o, dhlh, gain_o, g_o, got, oa_m, dhl_m, p0, p1, p2,
    oa_v, wo_v, w_v, acc, dn2, h_s, n2_s, dhl_s, act, n2h, n2_m, dy_m, do_s, out_s, nt_s, yt_s,
    oa_sem, wo_sem, w_sem, g_sem, act_ssem, act_rsem, m_ssem, m_rsem, do_ssem, do_rsem, do_lsem,
    *row_sems,
):
    row, col, k = lax.axis_index("row"), lax.axis_index("col"), at["k"]
    to = device(mate(at))
    lead, more = [], []
    flat = [f.reshape(NC, WIDTH, w) for f, w in zip((f0, f1, f2), FFN)]
    parts = [p.reshape(NC, 512, w) for p, w in zip((p0, p1, p2), FFN)]
    for p in range(NC):
        c = (p % 2) * 4 + p // 2
        lanes = pl.ds(256 * p, 256)
        lead.append(pltpu.make_async_copy(wo.reshape(NC, WIDTH, 256).at[p], wo_v.at[:, lanes], wo_sem.at[p]))
        more.append(pltpu.make_async_copy(oa.at[c], oa_v.at[:, lanes], oa_sem.at[p]))
    for cp in lead:
        cp.start()
    yield
    for cp in more:
        cp.start()
    lead += more

    def loads(t):
        slot = t % 2
        return [
            pltpu.make_async_copy(
                flat[i].at[2 * t + j, :, src],
                w_v.at[slot, :, dst],
                w_sem.at[slot, 5 * j + n],
            )
            for j in range(2)
            for n, (i, src, dst) in enumerate(lanes_of(j))
        ]

    def weights(slot, start, stop):
        return w_v[slot, :, start:stop]

    def act_send(t):
        rows = pl.ds(0, ROWS), pl.ds(ROWS, ROWS)
        return remote(act.at[t, rows[0]], act.at[t, rows[1]], act_ssem.at[t], act_rsem.at[t], to)

    def mate_send(i, src, dst):
        return remote(src, dst, m_ssem.at[i], m_rsem.at[i], to)

    for cp in lead:
        cp.wait()

    @pl.loop(0, 4)
    def _(n):
        cols = pl.ds(pl.multiple_of(256 * n, 256), 256)
        acc[:, cols] = x[:, cols].astype(F32) + dot(oa_v[...], wo_v[cols, :], NT)

    h = acc[...]
    h_s[...] = h
    n2 = h * mean_square_scale(h) * fgain[...]
    n2_s[...] = n2.astype(BF)
    a, b = halves_of(n2)
    n2h[0] = a.astype(BF)
    n2h[1] = b.astype(BF)
    pairs = ((dyh.at[1 - k], dy_m), (oa, oa_m), (n2h.at[1 - k], n2_m))
    to_mate = [mate_send(i, src, dst) for i, (src, dst) in enumerate(pairs)]
    for cp in to_mate:
        cp.start()
    dn2[...] = jnp.zeros_like(dn2)
    yield
    for cp in loads(0):
        cp.start()

    @pl.loop(0, STEPS)
    def _(t):
        slot = t % 2

        @pl.when(t < STEPS - 1)
        def _():
            for cp in loads(t + 1):
                cp.start()

        for cp in loads(t):
            cp.wait()
        g = dot(n2_s[...], weights(slot, 0, PAIR))
        u = dot(n2_s[...], weights(slot, PAIR, 2 * PAIR))
        dhid = dot(dy[...], weights(slot, 2 * PAIR, 3 * PAIR))
        sig = jax.nn.sigmoid(g)
        silu = g * sig
        act[t, 0:ROWS, 2 * PAIR :] = (silu * u).astype(BF)
        act[t, 0:ROWS, 0:PAIR] = (dhid * u * sig * (1.0 + g * (1.0 - sig))).astype(BF)
        act[t, 0:ROWS, PAIR : 2 * PAIR] = (dhid * silu).astype(BF)
        act_send(t).start()
        acc[...] += dot(act[t, 0:ROWS, 2 * PAIR :], weights(slot, 2 * PAIR, 3 * PAIR), NT)
        dn2[...] += dot(act[t, 0:ROWS, 0 : 2 * PAIR], weights(slot, 0, 2 * PAIR), NT)

    h = h_s[...]
    r2 = mean_square_scale(h)
    hn = h * r2
    e = dn2[...]
    gain_o[...] = jnp.sum(e * hn, axis=0, keepdims=True)
    e = e * fgain[...]
    dh = dy[...].astype(F32) + r2 * (e - hn * jnp.mean(e * hn, axis=-1, keepdims=True))
    dh_o[...] = dh
    dhl_s[...] = dh.astype(BF)

    def block_at(n):
        return (col + 1 + n) % NC

    def do_send(n):
        c = block_at(n)
        return remote(do_s.at[c], g_o.at[col], do_ssem.at[n], do_rsem.at[n], (row, c))

    @pl.loop(0, NC)
    def _(n):
        c = block_at(n)
        cols = pl.ds(pl.multiple_of(256 * place(c), 256), 256)
        do_s[c] = dot(dhl_s[...], wo_v[:, cols]).astype(BF)

        @pl.when(n < NC - 1)
        def _():
            do_send(n).start()

    mine = pltpu.make_async_copy(do_s.at[col], g_o.at[col], do_lsem)
    mine.start()
    take = onehot(slt[:, :1].astype(F32).astype(I32) == iota((ROWS, ROWS), 1))
    out_s[...] = dot(take, acc[...].astype(BF)).astype(BF).reshape(out_s.shape)
    back = swap_over("row", out_s, got, *row_sems)
    a, b = halves_of(dhl_s[...].astype(F32))
    dhlh[0] = a.astype(BF)
    dhlh[1] = b.astype(BF)
    cp = mate_send(3, dhlh.at[1 - k], dhl_m)
    cp.start()
    to_mate.append(cp)
    for cp in to_mate:
        cp.wait()
    stack_tokens(k, n2h, n2_m, nt_s)
    stack_tokens(k, dyh, dy_m, yt_s)

    def stores(t):
        slot = t % 2
        return [
            pltpu.make_async_copy(
                w_v.at[slot, pl.ds(0, 512), src],
                parts[i].at[2 * t + j, :, dst],
                g_sem.at[slot, 5 * j + n],
            )
            for j in range(2)
            for n, (i, dst, src) in enumerate(lanes_of(j))
        ]

    @pl.loop(0, STEPS)
    def _(t):
        slot = t % 2

        @pl.when(t >= 2)
        def _():
            for cp in stores(t - 2):
                cp.wait()

        act_send(t).wait()
        gu = 2 * PAIR
        g = dot(nt_s[...], act[t, :, 0:gu]).astype(BF)
        w_v[slot, 0:512, 0:gu] = g
        g = dot(yt_s[...], act[t, :, gu:]).astype(BF)
        w_v[slot, 0:512, gu:] = g
        for cp in stores(t):
            cp.start()

    for t in (STEPS - 2, STEPS - 1):
        for cp in stores(t):
            cp.wait()
    for n in range(NC - 1):
        do_send(n).wait()
    for cp in [mine] + back:
        cp.wait()


def front_kernel(
    t_row, lens, tokens, grads, again, fgain, qgain, kgain, freq, w_q, w_k, w_v, w_o, w_g, w_u, w_d,
    oa, raw, x_o, n1h, cos, sin, slt, qkv_o, o_t, lse, a0, a1, a2,
    dh_o, dhlh, gain_o, g_o, got, oa_m, dhl_m, p0, p1, p2, f0, f1, f2,
    sent, came, dy_s, dyh, kv_s, u0_s, u1_s, u2_s, n1_s, src_s, raw_s, wq_v, wkv_v, qkv, o_s, s_v,
    own_sem, w_sem, keep_sem, out_ssem, out_rsem, out_lsem, o_ssem, o_rsem, o_lsem, *rest,
):
    at = where_am_i()
    sems, rest = rest[:22], rest[22:]
    row, col = lax.axis_index("row"), lax.axis_index("col")
    here = block_index({a: at[a] for a in "xyz"}, at["k"])
    near = [device(moved(at, "z", 1)), device(moved(at, "z", -1))]
    peers = near + row_peers(at) + col_peers(at)
    greet(peers)
    kv_s[:, :HEAD] = w_k[...]
    kv_s[:, HEAD:] = w_v[...]
    u0_s[...] = w_g[:, 0:256]
    u1_s[...] = w_u[:, 0:256]
    u2_s[:, 0:128] = w_g[:, 256:]
    u2_s[:, 128:256] = w_u[:, 256:]
    u2_s[:, 256:] = w_d[...]
    pairs = zip((w_q, kv_s, w_o, u0_s, u1_s, u2_s), (a0, a1, a2, f0, f1, f2))
    own = [
        pltpu.make_async_copy(src, dst.at[here], own_sem.at[i])
        for i, (src, dst) in enumerate(pairs)
    ]
    for cp in own:
        cp.start()
    spot, _ = slots_sent(t_row[...])
    sel = spot == iota((ROWS, ROWS), 0)
    pick = onehot(sel)
    slot = jnp.sum(jnp.where(sel, t_row[...] % ROWS, 0).astype(F32), axis=1, keepdims=True)
    message = (NR, 16, WIDTH)
    sent[0, :, :, 0:WIDTH] = dot(pick, tokens[...]).astype(BF).reshape(message)
    sent[0, :, :, WIDTH:] = (
        jnp.broadcast_to(slot, (ROWS, HEAD)).astype(BF).reshape((NR, 16, HEAD))
    )
    met(peers)
    attn = Gather(at, (a0, a1, a2), sems[6:10], own=(w_q, kv_s, w_o), split=True)
    lines = Gather(at, (f0, f1, f2), sems[10:14], (0, 1), own=(u0_s, u1_s, u2_s))
    planes = [
        Gather(at, (f0, f1), sems[14:18], (2,), orders=ORDERS[:2]),
        Gather(at, (f2,), sems[18:22], (2,), orders=ORDERS[2:]),
    ]
    steps = attn.all()
    more = lines.lines()
    next(steps)
    next(more)
    cps = swap_over("row", sent.at[0], came.at[0], *sems[0:3])
    next(steps)
    next(more)
    for cp in own:
        cp.wait()
    for _ in range(5):
        next(steps)
        next(more, None)
    slots = col * ROWS + iota((ROWS, HEAD), 0)
    pos = (slots - first_slots(lambda j: lens[0, j], slots)).astype(F32)
    angle = pos * freq[...]
    cos[...] = jnp.cos(angle)
    sine = jnp.sin(angle)
    sin[...] = jnp.where(iota((ROWS, HEAD), 1) < HEAD // 2, -sine, sine)
    sent[1, :, :, 0:WIDTH] = dot(pick, grads[...]).astype(BF).reshape(message)
    for cp in cps:
        cp.wait()
    local = came[0, :, :, WIDTH:].reshape(ROWS, HEAD)
    slt[...] = local
    put = onehot(local[:, :1].astype(F32).astype(I32) == iota((ROWS, ROWS), 1))
    x = dot(put, came[0, :, :, 0:WIDTH].reshape(ROWS, WIDTH), TN)
    x_o[...] = x.astype(BF)
    n1 = x * mean_square_scale(x) * again[...]
    n1_s[...] = n1.astype(BF)
    a, b = halves_of(n1)
    n1h[0] = a.astype(BF)
    n1h[1] = b.astype(BF)
    in_turn(steps, more)

    def block_at(i):
        return (col + 1 + i) % NC

    slabs = [a.reshape(NC, WIDTH, 256) for a in (a0, a1)]

    def loads(i):
        c, slot = block_at(i), i % 2
        return [
            pltpu.make_async_copy(slabs[0].at[place(c)], wq_v.at[slot], w_sem.at[0, slot]),
            pltpu.make_async_copy(slabs[1].at[place(c)], wkv_v.at[slot], w_sem.at[1, slot]),
        ]

    def sends(i):
        c = block_at(i)
        return remote(src_s.at[c], qkv.at[col], out_ssem.at[i], out_rsem.at[i], (row, c))

    attn.drain()
    planes[1].send(2, None)
    for cp in loads(0):
        cp.start()

    def columns(i):
        c = block_at(i)

        @pl.when(i < NC - 1)
        def _():
            for cp in loads(i + 1):
                cp.start()

        for cp in loads(i):
            cp.wait()
        n = n1_s[...]
        q = dot(n, wq_v[i % 2])
        kv = dot(n, wkv_v[i % 2])
        raw_s[c, :, 0:256] = q
        raw_s[c, :, 256:384] = kv[:, :HEAD]
        pieces = ((q[:, :HEAD], qgain), (q[:, HEAD:], qgain), (kv[:, :HEAD], kgain))
        for j, (v, gain) in enumerate(pieces):
            v = v * mean_square_scale(v) * gain[...]
            v = v * cos[...] + pltpu.roll(v, HEAD // 2, 1) * sin[...]
            src_s[c, :, j * HEAD : (j + 1) * HEAD] = v.astype(BF)
        src_s[c, :, 3 * HEAD :] = kv[:, HEAD:].astype(BF)

        @pl.when(i < NC - 1)
        def _():
            sends(i).start()

    pl.loop(0, NC)(columns)
    mine = pltpu.make_async_copy(src_s.at[col], qkv.at[col], out_lsem)
    mine.start()
    keep = [pltpu.make_async_copy(raw_s, raw, keep_sem.at[0])]
    keep[0].start()
    cps = swap_over("row", sent.at[1, :, :, pl.ds(0, WIDTH)], came.at[1, :, :, pl.ds(0, WIDTH)], *sems[3:6])
    planes[0].send(2, None)
    for i in range(NC - 1):
        sends(i).wait()
    mine.wait()
    keep.append(pltpu.make_async_copy(qkv, qkv_o, keep_sem.at[1]))
    keep[1].start()

    scale = HEAD**-0.5 * LOG2E

    def o_sends(n):
        c = block_at(n)
        return remote(o_s.at[c], oa.at[col], o_ssem.at[n], o_rsem.at[n], (row, c))

    def queries(n):
        i = block_at(n)
        q = stacked(qkv[i, :, 0 : 2 * HEAD])
        start = first_slots(lambda j: lens[0, j], group_slots(i))
        j0 = jnp.maximum(i - (SPAN - 1), 0)
        m = None
        for d in range(SPAN):
            s = dot(qkv[j0 + d, :, 2 * HEAD : 3 * HEAD], q, NT) * scale
            s = jnp.where(allowed(i, j0 + d, start), s, -1e30)
            s_v[d] = s
            top = jnp.max(s, axis=0, keepdims=True)
            m = top if m is None else jnp.maximum(m, top)
        total = jnp.zeros((1, QK), F32)
        acc = jnp.zeros((HEAD, QK), F32)
        for d in range(SPAN):
            p = jnp.exp2(s_v[d] - m)
            total = total + jnp.sum(p, axis=0, keepdims=True)
            acc = acc + dot(qkv[j0 + d, :, 3 * HEAD :], p.astype(BF), TN)
        o = acc / total
        o_t[i] = o
        lse[i] = m + jnp.log2(total)
        back = o.T
        o_s[i] = jnp.concatenate([back[:ROWS], back[ROWS:]], axis=1).astype(BF)

        @pl.when(n < NC - 1)
        def _():
            o_sends(n).start()

    ffn = middle_steps(
        at, slt, x_o, dy_s, dyh, fgain, oa, a2, f0, f1, f2,
        dh_o, dhlh, gain_o, g_o, got, oa_m, dhl_m, p0, p1, p2, *rest,
    )
    next(ffn)
    pl.loop(0, NC)(queries)
    planes[1].pass_on(2, None)
    planes[0].pass_on(2, None)
    mine = pltpu.make_async_copy(o_s.at[col], oa.at[col], o_lsem)
    mine.start()
    for cp in cps:
        cp.wait()
    dy = dot(put, came[1, :, :, 0:WIDTH].reshape(ROWS, WIDTH), TN)
    dy_s[...] = dy.astype(BF)
    a, b = halves_of(dy)
    dyh[0] = a.astype(BF)
    dyh[1] = b.astype(BF)
    for n in range(NC - 1):
        o_sends(n).wait()
    for cp in [mine] + keep:
        cp.wait()
    next(ffn)
    planes[0].arrived(2, None)
    planes[1].arrived(2, None)
    for g in [lines] + planes:
        g.drain()
    next(ffn, None)


def front(target, lens, tokens, grads, again, fgain, qgain, kgain, *weights):
    freq = ROPE_BASE ** (-(np.arange(HEAD) % (HEAD // 2)).astype(np.float32) * 2.0 / HEAD)
    freq = jnp.asarray(freq.astype(np.float32).reshape(1, HEAD))
    vm = pltpu.VMEM
    outs = [
        (HBM, sds((NC, ROWS, 256))),
        (HBM, sds((NC, ROWS, 384), F32)),
        (VMEM, sds((ROWS, WIDTH))),
        (VMEM, sds((2, ROWS, 512))),
        (VMEM, sds((ROWS, HEAD), F32)),
        (VMEM, sds((ROWS, HEAD), F32)),
        (VMEM, sds((ROWS, HEAD))),
        (HBM, sds((NC, ROWS, 512))),
        (VMEM, sds((NC, HEAD, QK), F32)),
        (VMEM, sds((NC, 1, QK), F32)),
    ]
    outs += [(HBM, gather_shape(w)) for w in ATTN]
    outs += [
        (VMEM, sds((ROWS, WIDTH), F32)),
        (VMEM, sds((2, ROWS, 512))),
        (VMEM, sds((1, WIDTH), F32)),
        (HBM, sds((NC, ROWS, 256))),
        (HBM, sds((NR, 16, WIDTH))),
        (HBM, sds((NC, ROWS, 256))),
        (HBM, sds((ROWS, 512))),
    ]
    outs += [(HBM, sds((4, 2, 4, 2, 64, w))) for w in FFN]
    outs += [(HBM, gather_shape(w)) for w in FFN]
    return pl.pallas_call(
        front_kernel,
        name="front",
        out_shape=[shape for _, shape in outs],
        in_specs=[VMEM, pl.BlockSpec(memory_space=pltpu.SMEM)]
        + [VMEM] * 7
        + [HBM, VMEM, VMEM, HBM]
        + [VMEM] * 3,
        out_specs=[space for space, _ in outs],
        scratch_shapes=[vm((2, NR, 16, WIDTH + HEAD), BF)] * 2
        + [vm((ROWS, WIDTH), BF), vm((2, ROWS, 512), BF)]
        + [vm((64, w), BF) for w in (256,) + FFN]
        + [
            vm((ROWS, WIDTH), BF),
            vm((NC, ROWS, 512), BF),
            vm((NC, ROWS, 384), F32),
            vm((2, WIDTH, 256), BF),
            vm((2, WIDTH, 256), BF),
            vm((NC, ROWS, 512), BF),
            vm((NC, ROWS, 256), BF),
            vm((SPAN, ROWS, QK), F32),
        ]
        + [DMA((6,)), DMA((2, 2)), DMA((2,))]
        + swap_sems("col") * 2
        + swap_sems("row") * 2
        + gather_sems(36, 16)
        + gather_sems(8, 0)
        + gather_sems(4, 4, 2)
        + gather_sems(4, 4, 1)
        + [
            vm((ROWS, 2048), BF),
            vm((WIDTH, 2048), BF),
            vm((2, WIDTH, 3 * PAIR), BF),
            vm((ROWS, WIDTH), F32),
            vm((ROWS, WIDTH), F32),
            vm((ROWS, WIDTH), F32),
            vm((ROWS, WIDTH), BF),
            vm((ROWS, WIDTH), BF),
            vm((STEPS, 2 * ROWS, 3 * PAIR), BF),
            vm((2, ROWS, 512), BF),
            vm((ROWS, 512), BF),
            vm((ROWS, 512), BF),
            vm((NC, ROWS, 256), BF),
            vm((NR, 16, WIDTH), BF),
            vm((512, 2 * ROWS), BF),
            vm((512, 2 * ROWS), BF),
            DMA((NC,)),
            DMA((NC,)),
            DMA((2, 10)),
            DMA((2, 10)),
            DMA((STEPS,)),
            DMA((STEPS,)),
            DMA((4,)),
            DMA((4,)),
        ]
        + swap_sems("col")
        + swap_sems("row"),
        compiler_params=params(1, 63),
    )(target.reshape(1, ROWS), lens, tokens, grads, again, fgain, qgain, kgain, freq, *weights)


def gain_steps(at, pieces, room, total, ssem, rsem):
    p = at["x"]
    lane = 0
    for ref in pieces:
        room[0, p, :, lane : lane + ref.shape[1]] = ref[...]
        lane += ref.shape[1]
    for t, a in enumerate("xyzk"):
        p = at[a]
        others = (1, 2, 3) if a != "k" else (1,)
        if t > 0:
            room[t, p] = total[...]
        step = []
        for d in others:
            to = device(moved(at, a, d)) if a != "k" else device(mate(at))
            sems = ssem.at[t, d - 1], rsem.at[t, d - 1]
            cp = remote(room.at[t, p], room.at[t, p], *sems, to)
            cp.start()
            step.append(cp)
        yield
        for cp in step:
            cp.wait()
        acc = room[t, 0]
        for j in range(1, len(others) + 1):
            acc = acc + room[t, j]
        total[...] = acc


def back_kernel(
    lens, qkv, d_o, lse, slt, x, dh, again, qgain, kgain, cos, sin, gain_f, n1h, dhlh, dhl_m,
    o_t, raw, wq, wkv, oa, oa_m, p0, p1, p2,
    r0, r1, r2, t0, t1, t2, got, gsum,
    out_s, qs, dos, delta, dq, first, came, draw, w_v, raw_v, acc, dx_s, gain_a, gain_qk,
    n1_m, nt_s, ht_s, oa_v, o_v, a0, a1, a2, room,
    kv_ssem, kv_rsem, kv_lsem, q_ssem, q_rsem, q_lsem, w_sem, m_ssem, m_rsem, n_ssem, n_rsem, oa_sem, o_sem,
    g_ssem, g_rsem, *rest,
):
    at = where_am_i()
    row, col, k = lax.axis_index("row"), lax.axis_index("col"), at["k"]
    to = device(mate(at))
    row_sems, rest = rest[:3], rest[3:]
    a_sems, f_sems, rest = rest[:3], rest[3:6], rest[6:]
    na = len(scatter_buffers(ATTN))
    a_bufs, f_bufs = rest[:na], rest[na:]
    near = [device(moved(at, "z", 1)), device(moved(at, "z", -1))]
    peers = near + row_peers(at) + col_peers(at)
    greet(peers)

    scale = HEAD**-0.5

    def o_load(i):
        return pltpu.make_async_copy(o_t.at[i], o_v.at[i % 2], o_sem.at[i % 2])

    o_load(0).start()

    @pl.loop(0, NC)
    def _(i):
        @pl.when(i < NC - 1)
        def _():
            o_load(i + 1).start()

        qs[i] = stacked(qkv[i, :, 0 : 2 * HEAD])
        g = stacked(d_o[i])
        dos[i] = g
        o_load(i).wait()
        delta[i] = jnp.sum(g.astype(F32).T * o_v[i % 2], axis=0, keepdims=True)
        dq[i] = jnp.zeros((HEAD, QK), F32)
        first[i] = first_slots(lambda n: lens[0, n], group_slots(i))

    met(peers)
    ffn = run_scatter(at, (p0, p1, p2), (t0, t1, t2), f_bufs, f_sems)
    next(ffn)
    swap_n1 = remote(n1h.at[1 - k], n1_m, n_ssem, n_rsem, to)
    swap_n1.start()

    def block_at(n):
        return (col + 1 + n) % NC

    lanes_q, lanes_kv = pl.ds(0, 2 * HEAD), pl.ds(2 * HEAD, 2 * HEAD)
    every = (slice(None),)

    def sends(n, lanes, ssem, rsem):
        c = block_at(n)
        src, dst = out_s.at[(c,) + every + (lanes,)], came.at[(col,) + every + (lanes,)]
        return remote(src, dst, ssem.at[n], rsem.at[n], (row, c))

    def sends_kv(n):
        return sends(n, lanes_kv, kv_ssem, kv_rsem)

    def sends_q(n):
        return sends(n, lanes_q, q_ssem, q_rsem)

    def keys(n):
        j = block_at(n)
        key = qkv[j, :, 2 * HEAD : 3 * HEAD]
        value = qkv[j, :, 3 * HEAD :]
        key_t = key.astype(F32).T.astype(BF)

        def step(i, carry):
            dk, dv = carry
            s = dot(key, qs[i], NT) * (scale * LOG2E) - lse[i]
            p = jnp.where(allowed(i, j, first[i]), jnp.exp2(s), 0.0)
            ds = (p * (dot(value, dos[i], NT) - delta[i]) * scale).astype(BF)
            dv = dv + dot(p.astype(BF), dos[i])
            dk = dk + dot(ds, qs[i])
            dq[i] += dot(key_t, ds)
            return dk, dv

        zero = jnp.zeros((ROWS, HEAD), F32)
        dk, dv = lax.fori_loop(j, jnp.minimum(j + SPAN, NC), step, (zero, zero))
        out_s[j, :, 2 * HEAD : 3 * HEAD] = dk.astype(BF)
        out_s[j, :, 3 * HEAD :] = dv.astype(BF)

        @pl.when(n < NC - 1)
        def _():
            sends_kv(n).start()

        pl.when(complete(n))(lambda: queries(n))

    start = block_at(0)

    def complete(n):
        j = block_at(n)
        return (j < start) | (jnp.maximum(j - (SPAN - 1), 0) >= start)

    def queries(n):
        i = block_at(n)
        done = dq[i].T
        out_s[i, :, 0:HEAD] = done[:ROWS].astype(BF)
        out_s[i, :, HEAD : 2 * HEAD] = done[ROWS:].astype(BF)

        @pl.when(n < NC - 1)
        def _():
            sends_q(n).start()

    pl.loop(0, NC)(keys)

    @pl.loop(0, NC)
    def _(n):
        pl.when(jnp.logical_not(complete(n)))(lambda: queries(n))

    mine = []
    for lanes, sem in ((lanes_kv, kv_lsem), (lanes_q, q_lsem)):
        here = (col,) + every + (lanes,)
        mine.append(pltpu.make_async_copy(out_s.at[here], came.at[here], sem))
    for cp in mine:
        cp.start()

    def comes_from(n):
        return (col - 1 - n + NC) % NC

    def oa_loads(n):
        slot = n % 2
        return [
            pltpu.make_async_copy(src.at[n], oa_v.at[slot, pl.ds(ROWS * i, ROWS)], oa_sem.at[i, slot])
            for i, src in enumerate((oa, oa_m))
        ]

    def loads(n):
        c, slot = comes_from(n), n % 2
        return [
            pltpu.make_async_copy(wq.at[place(c)], w_v.at[slot, :, pl.ds(0, 256)], w_sem.at[0, slot]),
            pltpu.make_async_copy(
                wkv.at[place(c)], w_v.at[slot, :, pl.ds(256, 256)], w_sem.at[1, slot]
            ),
            pltpu.make_async_copy(raw.at[c], raw_v.at[slot], w_sem.at[2, slot]),
        ]

    for cp in oa_loads(0) + loads(0):
        cp.start()
    stack_tokens(k, dhlh, dhl_m, ht_s)

    @pl.loop(0, NC)
    def _(n):
        @pl.when(n < NC - 1)
        def _():
            for cp in oa_loads(n + 1):
                cp.start()

        for cp in oa_loads(n):
            cp.wait()
        a2[n % 4, n // 4] = dot(ht_s[...], oa_v[n % 2]).astype(BF).reshape(4, 2, 64, 256)

    swap_n1.wait()
    stack_tokens(k, n1h, n1_m, nt_s)
    acc[...] = jnp.zeros_like(acc)
    gain_qk[...] = jnp.zeros_like(gain_qk)
    next(ffn)

    def to_mate(n):
        c = comes_from(n)
        src, dst = draw.at[c, pl.ds(0, ROWS)], draw.at[c, pl.ds(ROWS, ROWS)]
        return remote(src, dst, m_ssem.at[n], m_rsem.at[n], to)

    def weights_of(n):
        c = comes_from(n)
        to_mate(n).wait()
        g = dot(nt_s[...], draw[c]).astype(BF)
        a0[c % 4, c // 4] = g[:, 0:256].reshape(4, 2, 64, 256)
        a1[c % 4, c // 4] = g[:, 256:].reshape(4, 2, 64, 256)

    @pl.loop(0, NC)
    def _(n):
        c, slot = comes_from(n), n % 2

        @pl.when(n < NC - 1)
        def _():
            for cp in loads(n + 1):
                cp.start()
            sends_kv(n).wait_recv()
            sends_q(n).wait_recv()

        @pl.when(n == NC - 1)
        def _():
            for cp in mine:
                cp.wait()

        for cp in loads(n):
            cp.wait()
        for i, gain in enumerate((qgain, qgain, kgain)):
            cols = slice(i * HEAD, (i + 1) * HEAD)
            v = raw_v[slot, :, cols]
            r = mean_square_scale(v)
            xn = v * r
            dn = unrope(came[c, :, cols].astype(F32), cos[...], sin[...])
            lanes = slice(0, HEAD) if i < 2 else slice(HEAD, 2 * HEAD)
            gain_qk[:, lanes] += jnp.sum(dn * xn, axis=0, keepdims=True)
            e = dn * gain[...]
            e = r * (e - xn * jnp.mean(e * xn, axis=-1, keepdims=True))
            draw[c, 0:ROWS, cols] = e.astype(BF)
        draw[c, 0:ROWS, 3 * HEAD :] = came[c, :, 3 * HEAD :]
        to_mate(n).start()
        acc[...] += dot(draw[c, 0:ROWS, :], w_v[slot], NT)

        @pl.when(n > 0)
        def _():
            weights_of(n - 1)

    weights_of(NC - 1)
    attn = run_scatter(at, (a0, a1, a2), (r0, r1, r2), a_bufs, a_sems, True)
    next(attn)

    xv = x[...].astype(F32)
    inverse = mean_square_scale(xv)
    xn = xv * inverse
    e = acc[...]
    gain_a[...] = jnp.sum(e * xn, axis=0, keepdims=True)
    gains = gain_steps(at, (gain_a, gain_f, gain_qk), room, gsum, g_ssem, g_rsem)
    next(gains)
    e = e * again[...]
    dx = dh[...] + inverse * (e - xn * jnp.mean(e * xn, axis=-1, keepdims=True))
    take = onehot(slt[:, :1].astype(F32).astype(I32) == iota((ROWS, ROWS), 1))
    dx_s[...] = dot(take, dx.astype(BF)).astype(BF).reshape(dx_s.shape)
    back = swap_over("row", dx_s, got, *row_sems)
    in_turn(attn, gains, ffn)
    for n in range(NC - 1):
        sends_kv(n).wait_send()
        sends_q(n).wait_send()
    for cp in back:
        cp.wait()


def back(
    lens, qkv, d_o, o_t, lse, slt, x, dh, again, qgain, kgain, cos, sin, gain_f, n1h, dhlh, dhl_m,
    raw, wq, wkv, oa, oa_m, f_parts,
):
    vm = pltpu.VMEM
    total = 2 * WIDTH + 2 * HEAD
    return pl.pallas_call(
        back_kernel,
        name="back",
        out_shape=[sds((64, 256), F32)] * 3
        + [sds((64, w), F32) for w in FFN]
        + [sds((NR, 16, WIDTH)), sds((1, total), F32)],
        in_specs=[pl.BlockSpec(memory_space=pltpu.SMEM)] + [VMEM] * 15 + [HBM] * 9,
        out_specs=[VMEM] * 6 + [HBM, VMEM],
        scratch_shapes=[
            vm((NC, ROWS, 512), BF),
            vm((NC, QK, HEAD), BF),
            vm((NC, QK, HEAD), BF),
            vm((NC, 1, QK), F32),
            vm((NC, HEAD, QK), F32),
            vm((NC, 1, QK), I32),
            vm((NC, ROWS, 512), BF),
            vm((NC, 2 * ROWS, 512), BF),
            vm((2, WIDTH, 512), BF),
            vm((2, ROWS, 384), F32),
            vm((ROWS, WIDTH), F32),
            vm((NR, 16, WIDTH), BF),
            vm((1, WIDTH), F32),
            vm((1, 2 * HEAD), F32),
            vm((ROWS, 512), BF),
            vm((512, 2 * ROWS), BF),
            vm((512, 2 * ROWS), BF),
            vm((2, 2 * ROWS, 256), BF),
            vm((2, HEAD, QK), F32),
        ]
        + [vm((4, 2, 4, 2, 64, 256), BF)] * 3
        + [vm((4, 4, 1, total), F32)]
        + swap_sems("col") * 2
        + [DMA((3, 2)), DMA((NC,)), DMA((NC,)), DMA, DMA, DMA((2, 2)), DMA((2,))]
        + [DMA((4, 3)), DMA((4, 3))]
        + swap_sems("row")
        + scatter_sems()
        + scatter_sems()
        + scatter_buffers(ATTN)
        + scatter_buffers(FFN),
        compiler_params=params(6, 63),
    )(
        lens, qkv, d_o, lse, slt, x, dh, again, qgain, kgain, cos, sin, gain_f, n1h, dhlh,
        dhl_m, o_t, raw, as_slabs(wq), as_slabs(wkv), oa, oa_m, *f_parts,
    )


def arrive_kernel(
    t_row, out, dx, q, kv, o, g, u, d, gains,
    out_o, dx_o, ga, gf, gq, gk, q_o, k_o, v_o, o_o, g_o, u_o, d_o,
):
    _, spot = slots_sent(t_row[...])
    pick = onehot(spot == iota((ROWS, ROWS), 1))
    out_o[...] = dot(pick, out[...].reshape(ROWS, WIDTH)).astype(BF)
    dx_o[...] = dot(pick, dx[...].reshape(ROWS, WIDTH)).astype(BF)
    ga[...] = gains[:, 0:WIDTH]
    gf[...] = gains[:, WIDTH : 2 * WIDTH]
    gq[...] = gains[:, 2 * WIDTH : 2 * WIDTH + HEAD]
    gk[...] = gains[:, 2 * WIDTH + HEAD :]
    q_o[...] = q[...]
    k_o[...] = kv[:, :HEAD]
    v_o[...] = kv[:, HEAD:]
    o_o[...] = o[...]
    g_o[:, 0:256] = g[...]
    g_o[:, 256:] = d[:, 0:128]
    u_o[:, 0:256] = u[...]
    u_o[:, 256:] = d[:, 128:256]
    d_o[...] = d[:, 256:]


def arrive(target, *args):
    return pl.pallas_call(
        arrive_kernel,
        name="arrive",
        out_shape=[sds((ROWS, WIDTH))] * 2
        + [sds((1, n), F32) for n in (WIDTH, WIDTH, HEAD, HEAD)]
        + [
            sds(n, F32)
            for n in ((64, 256), (64, 128), (64, 128), (64, 256), (64, 384), (64, 384), (64, 384))
        ],
        in_specs=[VMEM] * 10,
        out_specs=[VMEM] * 13,
        compiler_params=params(),
    )(target.reshape(1, ROWS), *args)


def local(
    tokens, grad_out, target, lengths, attn_gain, ffn_gain, q_gain, k_gain,
    w_query, key_matrix, value_matrix, w_out, w_gate, w_up, w_down,
):
    again, fgain = attn_gain.reshape(1, WIDTH), ffn_gain.reshape(1, WIDTH)
    qgain, kgain = q_gain.reshape(1, HEAD), k_gain.reshape(1, HEAD)

    oa, raw, x, n1h, cos, sin, slt, qkv, o_t, lse, wq, wkv, _, dh, dhlh, gain_f, g_o, got_out, oa_m, dhl_m, *rest = front(
        target, lengths, tokens, grad_out, again, fgain, qgain, kgain,
        w_query, key_matrix, value_matrix, w_out.T, w_gate, w_up, w_down.T,
    )
    f_parts = rest[:3]
    r_q, r_kv, r_o, r_g, r_u, r_d, got_dx, gains = back(
        lengths, qkv, g_o, o_t, lse, slt, x, dh, again, qgain, kgain, cos, sin, gain_f, n1h, dhlh,
        dhl_m, raw, wq, wkv, oa, oa_m, f_parts,
    )
    output, input_grad, ga, gf, gq, gk, g_q, g_k, g_v, g_o, g_g, g_u, g_d = arrive(
        target, got_out, got_dx, r_q, r_kv, r_o, r_g, r_u, r_d, gains
    )
    return (
        output, input_grad, ga[0], gf[0], gq[0], gk[0], g_q, g_k, g_v, g_o.T, g_g, g_u, g_d.T,
    )


def solution(mesh):
    both = P(("row", "col"), None)
    by_row, by_col = P("row", "col"), P("col", "row")
    weights = (by_row, by_row, by_row, by_col, by_row, by_row, by_col)
    return jax.shard_map(
        local,
        mesh=mesh,
        in_specs=(both, both, P(("row", "col")), P("row", None), P(), P(), P(), P()) + weights,
        out_specs=(both, both, P(), P(), P(), P()) + weights,
        check_vma=False,
    )
```

```python
import functools
import math

import jax
import jax.numpy as jnp
import numpy as np
from jax import lax
from jax.experimental import pallas as pl
from jax.experimental.pallas import tpu as pltpu
from jax.sharding import PartitionSpec as P

MESH = pl.DeviceIdType.MESH
BF = jnp.bfloat16
F32 = jnp.float32
I32 = jnp.int32
EPSILON = 1e-06
ROPE_BASE = 1000000.0
HEAD = 128
NR = 16
NC = 8
ROWS = 256
WIDTH = 1024
GROUP = 2048
ORDERS = (("x", "y", "z"), ("y", "z", "x"), ("z", "x", "y"))
ATTN = (256, 256, 256)
FFN = (256, 256, 640)
FFN_GRADS = (256, 256, 640)
HBM = pl.BlockSpec(memory_space=pltpu.HBM)
VMEM = pl.BlockSpec(memory_space=pltpu.VMEM)
DMA = pltpu.SemaphoreType.DMA


def sds(shape, dtype=BF):
    return jax.ShapeDtypeStruct(shape, dtype)


def params(cid=None, mib=56, **kw):
    if cid is not None:
        kw.update(collective_id=cid, has_side_effects=True)
    return pltpu.CompilerParams(vmem_limit_bytes=mib << 20, **kw)


def where_am_i():
    r = lax.axis_index("row")
    c = lax.axis_index("col")
    return {"x": c % 4, "y": r // 4, "z": 2 * ((r // 2) % 2) + c // 4, "k": r % 2}


def device(at):
    return (at["y"] * 4 + (at["z"] // 2) * 2 + at["k"], (at["z"] % 2) * 4 + at["x"])


def moved(at, axis, step):
    out = dict(at)
    out[axis] = (at[axis] + step) % 4
    return out


def mate(at):
    out = dict(at)
    out["k"] = 1 - at["k"]
    return out


def greet(peers):
    barrier = pltpu.get_barrier_semaphore()
    for p in peers:
        pl.semaphore_signal(barrier, inc=1, device_id=p, device_id_type=MESH)


def met(peers):
    pl.semaphore_wait(pltpu.get_barrier_semaphore(), len(peers))


def ring_peers(at):
    return [device(moved(at, a, s)) for a in "xyz" for s in (1, -1)]


def row_peers(at):
    r = lax.axis_index("row")
    c = lax.axis_index("col")
    return [((r + d) % NR, c) for d in range(1, NR)]


def col_peers(at):
    r = lax.axis_index("row")
    c = lax.axis_index("col")
    return [(r, (c + d) % NC) for d in range(1, NC)]


def remote(src, dst, ssem, rsem, to):
    return pltpu.make_async_remote_copy(
        src_ref=src, dst_ref=dst, send_sem=ssem, recv_sem=rsem, device_id=to, device_id_type=MESH
    )


def block_index(sel, with_core=None):
    full = slice(None)
    z = sel.get("z")
    idx = (
        sel.get("x", full),
        full if z is None else z % 2,
        sel.get("y", full),
        full if z is None else z // 2,
    )
    return idx if with_core is None else idx + (with_core,)


SHIFT = (0, -1, 1, 2)


def piece_index(at, order, t, g, rel):
    sel = {a: at[a] for a in order[t + 1 :]}
    if t > 0 and g is not None:
        sel[order[t - 1]] = (at[order[t - 1]] + SHIFT[g]) % 4
    sel[order[t]] = (at[order[t]] + rel) % 4
    return block_index(sel, at["k"])


class Gather:
    def __init__(self, at, outs, sems, phases=(0, 1, 2), own=None, orders=ORDERS, split=False):
        self.at, self.outs, self.own, self.orders = at, outs, own, orders
        self.base = {t: sum(4 if p == 0 or not split else 16 for p in phases if p < t) for t in phases}
        self.ssem, self.rsem, self.msem, self.nsem = sems
        self.n = len(outs)
        self.half = outs[0].shape[5] // 2
        self.late, self.sent = [], []

    def copies(self, s, t, g):
        ref = self.outs[s].at[piece_index(self.at, self.orders[s], t, g, 0)]
        a, i = self.orders[s][t], self.base[t] + 4 * (g or 0)
        src = self.own[s] if self.own and (t == 0 or (t == 1 and g == 0)) else ref
        return [
            remote(src, ref, self.ssem.at[s, i + d], self.rsem.at[s, i + d], device(moved(self.at, a, step)))
            for d, step in enumerate((1, -1))
        ]

    def forwards(self, s, t, g):
        a, i = self.orders[s][t], self.base[t] + 4 * (g or 0) + 2
        out = []
        for d, step in enumerate((1, -1)):
            came = piece_index(self.at, self.orders[s], t, g, -step) + (pl.ds(d * self.half, self.half),)
            ref = self.outs[s].at[came]
            out.append(
                remote(
                    ref,
                    ref,
                    self.ssem.at[s, i + d],
                    self.rsem.at[s, i + d],
                    device(moved(self.at, a, step)),
                )
            )
        return out

    def to_mate(self, s, g, rel):
        slot = 4 * (g or 0) + SHIFT.index(rel)
        ref = self.outs[s].at[piece_index(self.at, self.orders[s], 2, g, rel)]
        return remote(ref, ref, self.msem.at[s, slot], self.nsem.at[s, slot], device(mate(self.at)))

    def share(self, s, g, rel):
        cp = self.to_mate(s, g, rel)
        cp.start()
        self.late.append(cp)

    def send(self, t, g):
        for s in range(self.n):
            for cp in self.copies(s, t, g):
                cp.start()
                self.sent.append(cp)
            if t == 2:
                self.share(s, g, 0)

    def pass_on(self, t, g, wait=True):
        for s in range(self.n):
            first = self.copies(s, t, g) if wait else None
            for d, cp in enumerate(self.forwards(s, t, g)):
                if wait:
                    first[d].wait_recv()
                cp.start()
                self.sent.append(cp)
                if t == 2:
                    self.share(s, g, (-1, 1)[d])

    def arrived(self, t, g):
        for s in range(self.n):
            for cp in self.forwards(s, t, g):
                cp.wait_recv()
            if t == 2:
                self.share(s, g, 2)

    def drain(self):
        for cp in self.late:
            cp.wait()
        for cp in self.sent:
            cp.wait_send()

    def lines(self):
        self.send(0, None)
        self.send(1, 0)
        yield
        self.pass_on(0, None)
        self.send(1, 1)
        self.send(1, 2)
        yield
        self.pass_on(1, 0)
        self.arrived(0, None)
        self.send(1, 3)
        yield
        for g in (1, 2, 3):
            self.pass_on(1, g)
        yield
        for g in range(4):
            self.arrived(1, g)

    def all(self):
        self.send(0, None)
        self.send(1, 0)
        yield
        self.pass_on(0, None)
        self.send(1, 1)
        self.send(1, 2)
        yield
        self.pass_on(1, 0)
        self.arrived(0, None)
        self.send(1, 3)
        self.send(2, 0)
        yield
        self.pass_on(1, 1)
        self.pass_on(1, 2)
        self.pass_on(1, 3)
        self.send(2, 1)
        self.send(2, 2)
        yield
        self.pass_on(2, 0)
        for g in range(4):
            self.arrived(1, g)
        self.send(2, 3)
        yield
        self.pass_on(2, 1)
        self.pass_on(2, 2)
        yield
        self.pass_on(2, 3)
        yield
        for g in range(4):
            self.arrived(2, g)


def gather_sems(steps, shares, n=3):
    return [DMA((n, steps)), DMA((n, steps)), DMA((n, max(shares, 1))), DMA((n, max(shares, 1)))]


def gather_shape(w):
    return sds((4, 2, 4, 2, 2, 64, w))


def lead_shape(axes):
    out = ()
    for a in ("x", "zl", "y", "zh"):
        if a[0] in axes:
            out += (4,) if a in "xy" else (2,)
    return out


def sub_index(sel, axes):
    out = ()
    for a in ("x", "zl", "y", "zh"):
        if a[0] not in axes:
            continue
        pos = sel.get(a[0])
        if pos is None:
            out += (slice(None),)
        elif a == "zl":
            out += (pos % 2,)
        elif a == "zh":
            out += (pos // 2,)
        else:
            out += (pos,)
    return out


def add_up(dst, terms):
    total = None
    if len(terms) == 2:
        total = terms[0][0][terms[0][1]] + terms[1][0][terms[1][1]]
    else:
        for ref, at in terms:
            v = ref[at].astype(F32)
            total = v if total is None else total + v
    dst[0][dst[1]] = total.astype(dst[0].dtype)


def scatter_leads(s, t):
    return lead_shape(ORDERS[s][: 2 - t])


def scatter_buffers(widths, t0=0, n=3):
    out = []
    for s in range(n):
        for t in range(t0, 3):
            lead, w = scatter_leads(s, t), widths[s]
            out.append(pltpu.VMEM((2,) + lead + (32, w), BF))
            out.append(pltpu.VMEM((2,) + lead + (64, w), BF))
            out.append(pltpu.VMEM((2,) + lead + (32, w), BF))
            out.append(pltpu.VMEM(lead + (64, w), BF))
    return out


def scatter_sems(phases=3, n=3):
    return [DMA((n, phases, 6)), DMA((n, phases, 6)), DMA((n, 3))]


LO, HI = pl.ds(0, 32), pl.ds(32, 32)


def part_of(s, t, at, rel, rows):
    a = ORDERS[s][2 - t]
    return sub_index({a: (at[a] + rel) % 4}, ORDERS[s][: 3 - t]) + (rows,)


def first_sends(s, t, at, ref, rel_in, piece_in, ssem, rsem, t0=0):
    a = ORDERS[s][2 - t]
    right, left = device(moved(at, a, 1)), device(moved(at, a, -1))
    allr = (slice(None),) * len(scatter_leads(s, t))

    def src(rel, rows):
        return ref.at[part_of(s, t, at, rel, rows)]

    return [
        remote(src(2, LO), rel_in.at[0], ssem.at[s, t - t0, 0], rsem.at[s, t - t0, 0], right),
        remote(src(2, HI), rel_in.at[1], ssem.at[s, t - t0, 1], rsem.at[s, t - t0, 1], left),
        remote(
            src(1, HI), piece_in.at[(0,) + allr + (HI,)], ssem.at[s, t - t0, 2], rsem.at[s, t - t0, 2], right
        ),
        remote(
            src(-1, LO), piece_in.at[(1,) + allr + (LO,)], ssem.at[s, t - t0, 3], rsem.at[s, t - t0, 3], left
        ),
    ]


def second_send(s, t, at, d, rel_out, piece_in, ssem, rsem, t0=0):
    a = ORDERS[s][2 - t]
    allr = (slice(None),) * len(scatter_leads(s, t))
    return remote(
        rel_out.at[d],
        piece_in.at[(d,) + allr + ((LO, HI)[d],)],
        ssem.at[s, t - t0, 4 + d],
        rsem.at[s, t - t0, 4 + d],
        device(moved(at, a, (1, -1)[d])),
    )


def run_scatter(at, parts, results, bufs, sems, resident=False):
    ssem, rsem, lsem = sems
    t0 = 0
    n = len(parts)
    cur = list(parts)
    waits = []
    per = 4 * (3 - t0)
    for t in range(t0, 3):
        st = []
        for s in range(n):
            i = s * per + 4 * (t - t0)
            rel_in, piece_in, rel_out, total = bufs[i : i + 4]
            cps = first_sends(s, t, at, cur[s], rel_in, piece_in, ssem, rsem, t0)
            for cp in cps:
                cp.start()
            loads = []
            if t == t0 and not resident:
                for j, (rel, rows, dst) in enumerate(
                    ((1, LO, rel_out.at[0]), (-1, HI, rel_out.at[1]), (0, slice(None), total))
                ):
                    cp = pltpu.make_async_copy(
                        cur[s].at[part_of(s, t, at, rel, rows)], dst, lsem.at[s, j]
                    )
                    cp.start()
                    loads.append(cp)
            st.append((rel_in, piece_in, rel_out, total, cps, loads))
        yield
        for s in range(n):
            rel_in, piece_in, rel_out, total, cps, loads = st[s]
            for d in range(2):
                cps[d].wait_recv()
                if loads:
                    loads[d].wait()
                    mine = (rel_out, d)
                else:
                    mine = (cur[s], part_of(s, t, at, (1, -1)[d], (LO, HI)[d]))
                add_up((rel_out, d), [mine, (rel_in, d)])
                cp = second_send(s, t, at, d, rel_out, piece_in, ssem, rsem, t0)
                cp.start()
                cps.append(cp)
        yield
        for s in range(n):
            rel_in, piece_in, rel_out, total, cps, loads = st[s]
            for i in (2, 3, 4, 5):
                cps[i].wait_recv()
            if loads:
                loads[2].wait()
                mine = (total, ...)
            else:
                mine = (cur[s], part_of(s, t, at, 0, slice(None)))
            dst = (total if t < 2 else results[s], ...)
            add_up(dst, [mine, (piece_in, 0), (piece_in, 1)])
            cur[s] = total
            waits += cps
    for cp in waits:
        cp.wait_send()


def in_turn(*steps):
    live = list(steps)
    while live:
        for it in list(live):
            if next(it, "end") == "end":
                live.remove(it)


def swap_over(axis, src, dst, ssem, rsem, lsem):
    n = NR if axis == "row" else NC
    r = lax.axis_index("row")
    c = lax.axis_index("col")
    me = r if axis == "row" else c
    cps = []
    for d in range(1, n):
        to = (me + d) % n
        cp = remote(
            src.at[to],
            dst.at[me],
            ssem.at[d - 1],
            rsem.at[d - 1],
            (to, c) if axis == "row" else (r, to),
        )
        cp.start()
        cps.append(cp)
    own = pltpu.make_async_copy(src.at[me], dst.at[me], lsem)
    own.start()
    return cps + [own]


def swap_sems(axis):
    n = NR if axis == "row" else NC
    return [DMA((n - 1,)), DMA((n - 1,)), DMA]


def dot(a, b, dims=((1,), (0,))):
    return lax.dot_general(a, b, (dims, ((), ())), preferred_element_type=F32)


NT = ((1,), (1,))
TN = ((0,), (0,))


def iota(shape, dim):
    return lax.broadcasted_iota(I32, shape, dim)


def onehot(cond):
    return cond.astype(F32).astype(BF)


def unrope(g, cos, sin):
    return g * cos - pltpu.roll(g, HEAD // 2, 1) * sin


def mean_square_scale(v):
    return lax.rsqrt(jnp.mean(v * v, axis=-1, keepdims=True) + EPSILON)


def column(row):
    eye = iota((ROWS, ROWS), 0) == iota((ROWS, ROWS), 1)
    return jnp.sum(jnp.where(eye, row.astype(F32), 0.0), axis=1, keepdims=True).astype(I32)


def slots_sent(target_row):
    g_row = target_row // GROUP
    g_col = column(g_row)
    same = g_row == g_col
    i0, i1 = iota((ROWS, ROWS), 0), iota((ROWS, ROWS), 1)
    before_row = jnp.sum((same & (i0 < i1)).astype(F32), axis=0, keepdims=True).astype(I32)
    before_col = jnp.sum((same & (i1 < i0)).astype(F32), axis=1, keepdims=True).astype(I32)
    return g_row * (ROWS // NR) + before_row, g_col * (ROWS // NR) + before_col


def halves_of(v):
    even, odd = [], []
    low = iota((v.shape[0], HEAD), 1) < HEAD // 2
    for m in range(4):
        a, b = v[:, 256 * m : 256 * m + 128], v[:, 256 * m + 128 : 256 * m + 256]
        even.append(jnp.where(low, a, pltpu.roll(b, 64, 1)))
        odd.append(jnp.where(low, pltpu.roll(a, 64, 1), b))
    return jnp.concatenate(even, axis=1), jnp.concatenate(odd, axis=1)


def first_slots(lens, slots):
    start = jnp.int32(0)
    out = jnp.zeros_like(slots)
    for j in range(8):
        out = jnp.where(slots >= start, start, out)
        start = start + lens(j)
    return out


def place(c):
    return (c % 4) * 2 + c // 4


def as_slabs(g):
    return g.reshape(NC, -1, g.shape[-1])


LOG2E = math.log2(math.e)
QK = 512


def stacked(v):
    return jnp.concatenate([v[:, :HEAD], v[:, HEAD : 2 * HEAD]], axis=0)


SPAN = 5


def group_slots(i):
    return i * ROWS + iota((1, QK), 1) % ROWS


def allowed(i, j, first):
    key = j * ROWS + iota((ROWS, QK), 0)
    return (key <= group_slots(i)) & (key >= first)


PAIR = 768
STEPS = 4


def stack_tokens(k, mine, others, scratch):
    scratch[:, 0:ROWS] = mine[k].astype(F32).T.astype(BF)
    scratch[:, ROWS:] = others[...].astype(F32).T.astype(BF)


def pieces_of(widths):
    w0, w1, _ = widths
    out = (
        (0, 0, 0, 0, w0),
        (2, 0, 0, w0, 384 - w0),
        (1, 0, 1, 0, w1),
        (2, 384 - w0, 1, w1, 384 - w1),
        (2, 768 - w0 - w1, 2, 0, 384),
    )
    return [p for p in out if p[4] > 0]


def lanes_of(widths, j):
    return [
        (s, pl.ds(a, n), pl.ds(PAIR * part + 384 * j + b, n))
        for s, a, part, b, n in pieces_of(widths)
    ]


def middle_steps(
    at, slt, x, dy, dyh, fgain, oa, wo, f0, f1, f2,
    dh_o, dhlh, gain_o, g_o, got, oa_m, dhl_m, p0, p1, p2,
    oa_v, wo_v, w_v, acc, dn2, h_s, n2_s, dhl_s, act, n2h, n2_m, dy_m, do_s, out_s, nt_s, yt_s,
    oa_sem, wo_sem, w_sem, g_sem, act_ssem, act_rsem, m_ssem, m_rsem, do_ssem, do_rsem, do_lsem,
    *row_sems,
):
    row, col, k = lax.axis_index("row"), lax.axis_index("col"), at["k"]
    to = device(mate(at))
    lead, more = [], []
    flat = [f.reshape(NC, WIDTH, w) for f, w in zip((f0, f1, f2), FFN)]
    parts = [p.reshape(NC, 512, w) for p, w in zip((p0, p1, p2), FFN_GRADS)]
    for p in range(NC):
        c = (p % 2) * 4 + p // 2
        lanes = pl.ds(256 * p, 256)
        lead.append(pltpu.make_async_copy(wo.reshape(NC, WIDTH, 256).at[p], wo_v.at[:, lanes], wo_sem.at[p]))
        more.append(pltpu.make_async_copy(oa.at[c], oa_v.at[:, lanes], oa_sem.at[p]))
    for cp in lead:
        cp.start()
    yield
    for cp in more:
        cp.start()
    lead += more

    def loads(t):
        slot = t % 2
        return [
            pltpu.make_async_copy(
                flat[i].at[2 * t + j, :, src],
                w_v.at[slot, :, dst],
                w_sem.at[slot, 5 * j + n],
            )
            for j in range(2)
            for n, (i, src, dst) in enumerate(lanes_of(FFN, j))
        ]

    def weights(slot, start, stop):
        return w_v[slot, :, start:stop]

    def act_send(t):
        rows = pl.ds(0, ROWS), pl.ds(ROWS, ROWS)
        return remote(act.at[t, rows[0]], act.at[t, rows[1]], act_ssem.at[t], act_rsem.at[t], to)

    def mate_send(i, src, dst):
        return remote(src, dst, m_ssem.at[i], m_rsem.at[i], to)

    for cp in lead:
        cp.wait()

    @pl.loop(0, 4)
    def _(n):
        cols = pl.ds(pl.multiple_of(256 * n, 256), 256)
        acc[:, cols] = x[:, cols].astype(F32) + dot(oa_v[...], wo_v[cols, :], NT)

    h = acc[...]
    h_s[...] = h
    n2 = h * mean_square_scale(h) * fgain[...]
    n2_s[...] = n2.astype(BF)
    a, b = halves_of(n2)
    n2h[0] = a.astype(BF)
    n2h[1] = b.astype(BF)
    dn2[...] = jnp.zeros_like(dn2)
    yield
    for cp in loads(0):
        cp.start()
    pairs = ((dyh.at[1 - k], dy_m), (oa, oa_m), (n2h.at[1 - k], n2_m))
    to_mate = [mate_send(i, src, dst) for i, (src, dst) in enumerate(pairs)]
    for cp in to_mate:
        cp.start()

    @pl.loop(0, STEPS)
    def _(t):
        slot = t % 2

        @pl.when(t < STEPS - 1)
        def _():
            for cp in loads(t + 1):
                cp.start()

        for cp in loads(t):
            cp.wait()
        g = dot(n2_s[...], weights(slot, 0, PAIR))
        u = dot(n2_s[...], weights(slot, PAIR, 2 * PAIR))
        dhid = dot(dy[...], weights(slot, 2 * PAIR, 3 * PAIR))
        sig = jax.nn.sigmoid(g)
        silu = g * sig
        act[t, 0:ROWS, 2 * PAIR :] = (silu * u).astype(BF)
        act[t, 0:ROWS, 0:PAIR] = (dhid * u * sig * (1.0 + g * (1.0 - sig))).astype(BF)
        act[t, 0:ROWS, PAIR : 2 * PAIR] = (dhid * silu).astype(BF)
        act_send(t).start()
        acc[...] += dot(act[t, 0:ROWS, 2 * PAIR :], weights(slot, 2 * PAIR, 3 * PAIR), NT)
        dn2[...] += dot(act[t, 0:ROWS, 0 : 2 * PAIR], weights(slot, 0, 2 * PAIR), NT)

    h = h_s[...]
    r2 = mean_square_scale(h)
    hn = h * r2
    e = dn2[...]
    gain_o[...] = jnp.sum(e * hn, axis=0, keepdims=True)
    e = e * fgain[...]
    dh = dy[...].astype(F32) + r2 * (e - hn * jnp.mean(e * hn, axis=-1, keepdims=True))
    dh_o[...] = dh
    dhl_s[...] = dh.astype(BF)

    def block_at(n):
        return (col + 1 + n) % NC

    def do_send(n):
        c = block_at(n)
        return remote(do_s.at[c], g_o.at[col], do_ssem.at[n], do_rsem.at[n], (row, c))

    @pl.loop(0, NC)
    def _(n):
        c = block_at(n)
        cols = pl.ds(pl.multiple_of(256 * place(c), 256), 256)
        do_s[c] = dot(dhl_s[...], wo_v[:, cols]).astype(BF)

        @pl.when(n < NC - 1)
        def _():
            do_send(n).start()

    mine = pltpu.make_async_copy(do_s.at[col], g_o.at[col], do_lsem)
    mine.start()
    take = onehot(slt[:, :1].astype(F32).astype(I32) == iota((ROWS, ROWS), 1))
    out_s[...] = dot(take, acc[...].astype(BF)).astype(BF).reshape(out_s.shape)
    back = swap_over("row", out_s, got, *row_sems)
    a, b = halves_of(dhl_s[...].astype(F32))
    dhlh[0] = a.astype(BF)
    dhlh[1] = b.astype(BF)
    cp = mate_send(3, dhlh.at[1 - k], dhl_m)
    cp.start()
    to_mate.append(cp)
    for cp in to_mate:
        cp.wait()
    stack_tokens(k, n2h, n2_m, nt_s)
    stack_tokens(k, dyh, dy_m, yt_s)

    def stores(t):
        slot = t % 2
        return [
            pltpu.make_async_copy(
                w_v.at[slot, pl.ds(0, 512), src],
                parts[i].at[2 * t + j, :, dst],
                g_sem.at[slot, 5 * j + n],
            )
            for j in range(2)
            for n, (i, dst, src) in enumerate(lanes_of(FFN_GRADS, j))
        ]

    @pl.loop(0, STEPS)
    def _(t):
        slot = t % 2

        @pl.when(t >= 2)
        def _():
            for cp in stores(t - 2):
                cp.wait()

        act_send(t).wait()
        gu = 2 * PAIR
        g = dot(nt_s[...], act[t, :, 0:gu]).astype(BF)
        w_v[slot, 0:512, 0:gu] = g
        g = dot(yt_s[...], act[t, :, gu:]).astype(BF)
        w_v[slot, 0:512, gu:] = g
        for cp in stores(t):
            cp.start()

    for t in (STEPS - 2, STEPS - 1):
        for cp in stores(t):
            cp.wait()
    for n in range(NC - 1):
        do_send(n).wait()
    for cp in [mine] + back:
        cp.wait()


def front_kernel(
    t_row, lens, tokens, grads, again, fgain, qgain, kgain, freq, w_q, w_k, w_v, w_o, w_g, w_u, w_d,
    oa, raw, x_o, n1h, cos, sin, slt, qkv_o, o_t, lse, a0, a1, a2,
    dh_o, dhlh, gain_o, g_o, got, oa_m, dhl_m, p0, p1, p2, f0, f1, f2,
    sent, came, dy_s, dyh, kv_s, u0_s, u1_s, u2_s, n1_s, src_s, raw_s, wq_v, wkv_v, qkv, o_s, s_v,
    own_sem, w_sem, keep_sem, out_ssem, out_rsem, out_lsem, o_ssem, o_rsem, o_lsem, *rest,
):
    at = where_am_i()
    sems, rest = rest[:22], rest[22:]
    row, col = lax.axis_index("row"), lax.axis_index("col")
    here = block_index({a: at[a] for a in "xyz"}, at["k"])
    near = [device(moved(at, "z", 1)), device(moved(at, "z", -1))]
    peers = near + row_peers(at) + col_peers(at)
    greet(peers)
    kv_s[:, :HEAD] = w_k[...]
    kv_s[:, HEAD:] = w_v[...]
    for i, at_lane, part, lane, n in pieces_of(FFN):
        src = (w_g, w_u, w_d)[part]
        (u0_s, u1_s, u2_s)[i][:, at_lane : at_lane + n] = src[:, lane : lane + n]
    pairs = zip((w_q, kv_s, w_o, u0_s, u1_s, u2_s), (a0, a1, a2, f0, f1, f2))
    own = [
        pltpu.make_async_copy(src, dst.at[here], own_sem.at[i])
        for i, (src, dst) in enumerate(pairs)
    ]
    for cp in own:
        cp.start()
    spot, _ = slots_sent(t_row[...])
    sel = spot == iota((ROWS, ROWS), 0)
    pick = onehot(sel)
    slot = jnp.sum(jnp.where(sel, t_row[...] % ROWS, 0).astype(F32), axis=1, keepdims=True)
    met(peers)
    attn = Gather(at, (a0, a1, a2), sems[6:10], own=(w_q, kv_s, w_o), split=True)
    lines = Gather(at, (f0, f1, f2), sems[10:14], (0, 1), own=(u0_s, u1_s, u2_s), split=True)
    planes = [
        Gather(at, (f0, f1), sems[14:18], (2,), orders=ORDERS[:2]),
        Gather(at, (f2,), sems[18:22], (2,), orders=ORDERS[2:]),
    ]
    steps = attn.all()
    more = lines.lines()
    next(steps)
    next(more)
    message = (NR, 16, WIDTH)
    sent[0, :, :, 0:WIDTH] = dot(pick, tokens[...]).astype(BF).reshape(message)
    sent[0, :, :, WIDTH:] = (
        jnp.broadcast_to(slot, (ROWS, HEAD)).astype(BF).reshape((NR, 16, HEAD))
    )
    cps = swap_over("row", sent.at[0], came.at[0], *sems[0:3])
    next(steps)
    next(more)
    for cp in own:
        cp.wait()
    for _ in range(5):
        next(steps)
        next(more, None)
    slots = col * ROWS + iota((ROWS, HEAD), 0)
    pos = (slots - first_slots(lambda j: lens[0, j], slots)).astype(F32)
    angle = pos * freq[...]
    cos[...] = jnp.cos(angle)
    sine = jnp.sin(angle)
    sin[...] = jnp.where(iota((ROWS, HEAD), 1) < HEAD // 2, -sine, sine)
    sent[1, :, :, 0:WIDTH] = dot(pick, grads[...]).astype(BF).reshape(message)
    for cp in cps:
        cp.wait()
    local = came[0, :, :, WIDTH:].reshape(ROWS, HEAD)
    slt[...] = local
    put = onehot(local[:, :1].astype(F32).astype(I32) == iota((ROWS, ROWS), 1))
    x = dot(put, came[0, :, :, 0:WIDTH].reshape(ROWS, WIDTH), TN)
    x_o[...] = x.astype(BF)
    n1 = x * mean_square_scale(x) * again[...]
    n1_s[...] = n1.astype(BF)
    a, b = halves_of(n1)
    n1h[0] = a.astype(BF)
    n1h[1] = b.astype(BF)
    in_turn(steps, more)

    def block_at(i):
        return (col + 1 + i) % NC

    slabs = [a.reshape(NC, WIDTH, 256) for a in (a0, a1)]

    def loads(i):
        c, slot = block_at(i), i % 2
        return [
            pltpu.make_async_copy(slabs[0].at[place(c)], wq_v.at[slot], w_sem.at[0, slot]),
            pltpu.make_async_copy(slabs[1].at[place(c)], wkv_v.at[slot], w_sem.at[1, slot]),
        ]

    def sends(i):
        c = block_at(i)
        return remote(src_s.at[c], qkv.at[col], out_ssem.at[i], out_rsem.at[i], (row, c))

    for cp in attn.late:
        cp.wait()
    planes[1].send(2, None)
    for cp in loads(0):
        cp.start()

    def columns(i):
        c = block_at(i)

        @pl.when(i < NC - 1)
        def _():
            for cp in loads(i + 1):
                cp.start()

        for cp in loads(i):
            cp.wait()
        n = n1_s[...]
        q = dot(n, wq_v[i % 2])
        kv = dot(n, wkv_v[i % 2])
        raw_s[c, :, 0:256] = q
        raw_s[c, :, 256:384] = kv[:, :HEAD]
        pieces = ((q[:, :HEAD], qgain), (q[:, HEAD:], qgain), (kv[:, :HEAD], kgain))
        for j, (v, gain) in enumerate(pieces):
            v = v * mean_square_scale(v) * gain[...]
            v = v * cos[...] + pltpu.roll(v, HEAD // 2, 1) * sin[...]
            src_s[c, :, j * HEAD : (j + 1) * HEAD] = v.astype(BF)
        src_s[c, :, 3 * HEAD :] = kv[:, HEAD:].astype(BF)

        @pl.when(i < NC - 1)
        def _():
            sends(i).start()

    pl.loop(0, NC)(columns)
    mine = pltpu.make_async_copy(src_s.at[col], qkv.at[col], out_lsem)
    mine.start()
    keep = [pltpu.make_async_copy(raw_s, raw, keep_sem.at[0])]
    keep[0].start()
    cps = swap_over("row", sent.at[1, :, :, pl.ds(0, WIDTH)], came.at[1, :, :, pl.ds(0, WIDTH)], *sems[3:6])
    planes[0].send(2, None)
    for i in range(NC - 1):
        sends(i).wait()
    mine.wait()
    keep.append(pltpu.make_async_copy(qkv, qkv_o, keep_sem.at[1]))
    keep[1].start()

    scale = HEAD**-0.5 * LOG2E

    def o_sends(n):
        c = block_at(n)
        return remote(o_s.at[c], oa.at[col], o_ssem.at[n], o_rsem.at[n], (row, c))

    def queries(n):
        i = block_at(n)
        q = stacked(qkv[i, :, 0 : 2 * HEAD])
        start = first_slots(lambda j: lens[0, j], group_slots(i))
        j0 = jnp.maximum(i - (SPAN - 1), 0)
        m = None
        for d in range(SPAN):
            s = dot(qkv[j0 + d, :, 2 * HEAD : 3 * HEAD], q, NT) * scale
            s = jnp.where(allowed(i, j0 + d, start), s, -1e30)
            s_v[d] = s
            top = jnp.max(s, axis=0, keepdims=True)
            m = top if m is None else jnp.maximum(m, top)
        total = jnp.zeros((1, QK), F32)
        acc = jnp.zeros((HEAD, QK), F32)
        for d in range(SPAN):
            p = jnp.exp2(s_v[d] - m)
            total = total + jnp.sum(p, axis=0, keepdims=True)
            acc = acc + dot(qkv[j0 + d, :, 3 * HEAD :], p.astype(BF), TN)
        o = acc / total
        o_t[i] = o
        lse[i] = m + jnp.log2(total)
        back = o.T
        o_s[i] = jnp.concatenate([back[:ROWS], back[ROWS:]], axis=1).astype(BF)

        @pl.when(n < NC - 1)
        def _():
            o_sends(n).start()

    ffn = middle_steps(
        at, slt, x_o, dy_s, dyh, fgain, oa, a2, f0, f1, f2,
        dh_o, dhlh, gain_o, g_o, got, oa_m, dhl_m, p0, p1, p2, *rest,
    )
    next(ffn)
    pl.loop(0, NC)(queries)
    planes[1].pass_on(2, None)
    planes[0].pass_on(2, None)
    mine = pltpu.make_async_copy(o_s.at[col], oa.at[col], o_lsem)
    mine.start()
    for cp in cps:
        cp.wait()
    dy = dot(put, came[1, :, :, 0:WIDTH].reshape(ROWS, WIDTH), TN)
    dy_s[...] = dy.astype(BF)
    a, b = halves_of(dy)
    dyh[0] = a.astype(BF)
    dyh[1] = b.astype(BF)
    for n in range(NC - 1):
        o_sends(n).wait()
    for cp in [mine] + keep:
        cp.wait()
    next(ffn)
    planes[0].arrived(2, None)
    planes[1].arrived(2, None)
    for g in [lines] + planes:
        g.drain()
    for cp in attn.sent:
        cp.wait_send()
    next(ffn, None)


def front(target, lens, tokens, grads, again, fgain, qgain, kgain, *weights):
    freq = ROPE_BASE ** (-(np.arange(HEAD) % (HEAD // 2)).astype(np.float32) * 2.0 / HEAD)
    freq = jnp.asarray(freq.astype(np.float32).reshape(1, HEAD))
    vm = pltpu.VMEM
    outs = [
        (HBM, sds((NC, ROWS, 256))),
        (HBM, sds((NC, ROWS, 384), F32)),
        (VMEM, sds((ROWS, WIDTH))),
        (VMEM, sds((2, ROWS, 512))),
        (VMEM, sds((ROWS, HEAD), F32)),
        (VMEM, sds((ROWS, HEAD), F32)),
        (VMEM, sds((ROWS, HEAD))),
        (HBM, sds((NC, ROWS, 512))),
        (VMEM, sds((NC, HEAD, QK), F32)),
        (VMEM, sds((NC, 1, QK), F32)),
    ]
    outs += [(HBM, gather_shape(w)) for w in ATTN]
    outs += [
        (VMEM, sds((ROWS, WIDTH), F32)),
        (VMEM, sds((2, ROWS, 512))),
        (VMEM, sds((1, WIDTH), F32)),
        (HBM, sds((NC, ROWS, 256))),
        (HBM, sds((NR, 16, WIDTH))),
        (HBM, sds((NC, ROWS, 256))),
        (HBM, sds((ROWS, 512))),
    ]
    outs += [(HBM, sds((4, 2, 4, 2, 64, w))) for w in FFN_GRADS]
    outs += [(HBM, gather_shape(w)) for w in FFN]
    return pl.pallas_call(
        front_kernel,
        name="front",
        out_shape=[shape for _, shape in outs],
        in_specs=[VMEM, pl.BlockSpec(memory_space=pltpu.SMEM)]
        + [VMEM] * 7
        + [HBM, VMEM, VMEM, HBM]
        + [VMEM] * 3,
        out_specs=[space for space, _ in outs],
        scratch_shapes=[vm((2, NR, 16, WIDTH + HEAD), BF)] * 2
        + [vm((ROWS, WIDTH), BF), vm((2, ROWS, 512), BF)]
        + [vm((64, w), BF) for w in (256,) + FFN]
        + [
            vm((ROWS, WIDTH), BF),
            vm((NC, ROWS, 512), BF),
            vm((NC, ROWS, 384), F32),
            vm((2, WIDTH, 256), BF),
            vm((2, WIDTH, 256), BF),
            vm((NC, ROWS, 512), BF),
            vm((NC, ROWS, 256), BF),
            vm((SPAN, ROWS, QK), F32),
        ]
        + [DMA((6,)), DMA((2, 2)), DMA((2,))]
        + swap_sems("col") * 2
        + swap_sems("row") * 2
        + gather_sems(36, 16)
        + gather_sems(20, 0)
        + gather_sems(4, 4, 2)
        + gather_sems(4, 4, 1)
        + [
            vm((ROWS, 2048), BF),
            vm((WIDTH, 2048), BF),
            vm((2, WIDTH, 3 * PAIR), BF),
            vm((ROWS, WIDTH), F32),
            vm((ROWS, WIDTH), F32),
            vm((ROWS, WIDTH), F32),
            vm((ROWS, WIDTH), BF),
            vm((ROWS, WIDTH), BF),
            vm((STEPS, 2 * ROWS, 3 * PAIR), BF),
            vm((2, ROWS, 512), BF),
            vm((ROWS, 512), BF),
            vm((ROWS, 512), BF),
            vm((NC, ROWS, 256), BF),
            vm((NR, 16, WIDTH), BF),
            vm((512, 2 * ROWS), BF),
            vm((512, 2 * ROWS), BF),
            DMA((NC,)),
            DMA((NC,)),
            DMA((2, 10)),
            DMA((2, 10)),
            DMA((STEPS,)),
            DMA((STEPS,)),
            DMA((4,)),
            DMA((4,)),
        ]
        + swap_sems("col")
        + swap_sems("row"),
        compiler_params=params(1, 63),
    )(target.reshape(1, ROWS), lens, tokens, grads, again, fgain, qgain, kgain, freq, *weights)


def gain_steps(at, pieces, room, total, ssem, rsem):
    p = at["x"]
    lane = 0
    for ref in pieces:
        room[0, p, :, lane : lane + ref.shape[1]] = ref[...]
        lane += ref.shape[1]
    for t, a in enumerate("xyzk"):
        p = at[a]
        others = (1, 2, 3) if a != "k" else (1,)
        if t > 0:
            room[t, p] = total[...]
        step = []
        for d in others:
            to = device(moved(at, a, d)) if a != "k" else device(mate(at))
            sems = ssem.at[t, d - 1], rsem.at[t, d - 1]
            cp = remote(room.at[t, p], room.at[t, p], *sems, to)
            cp.start()
            step.append(cp)
        yield
        for cp in step:
            cp.wait()
        acc = room[t, 0]
        for j in range(1, len(others) + 1):
            acc = acc + room[t, j]
        total[...] = acc


def back_kernel(
    lens, qkv, d_o, lse, slt, x, dh, again, qgain, kgain, cos, sin, gain_f, n1h, dhlh, dhl_m,
    o_t, raw, wq, wkv, oa, oa_m, p0, p1, p2,
    r0, r1, r2, t0, t1, t2, got, gsum,
    out_s, qs, dos, delta, dq, first, came, draw, w_v, raw_v, acc, dx_s, gain_a, gain_qk,
    n1_m, nt_s, ht_s, oa_v, o_v, a0, a1, a2, room,
    kv_ssem, kv_rsem, kv_lsem, q_ssem, q_rsem, q_lsem, w_sem, m_ssem, m_rsem, n_ssem, n_rsem, oa_sem, o_sem,
    g_ssem, g_rsem, *rest,
):
    at = where_am_i()
    row, col, k = lax.axis_index("row"), lax.axis_index("col"), at["k"]
    to = device(mate(at))
    row_sems, rest = rest[:3], rest[3:]
    a_sems, f_sems, rest = rest[:3], rest[3:6], rest[6:]
    na = len(scatter_buffers(ATTN))
    a_bufs, f_bufs = rest[:na], rest[na:]
    near = [device(moved(at, "z", 1)), device(moved(at, "z", -1))]
    peers = near + row_peers(at) + col_peers(at)
    greet(peers)

    scale = HEAD**-0.5

    def o_load(i):
        return pltpu.make_async_copy(o_t.at[i], o_v.at[i % 2], o_sem.at[i % 2])

    o_load(0).start()

    @pl.loop(0, NC)
    def _(i):
        @pl.when(i < NC - 1)
        def _():
            o_load(i + 1).start()

        qs[i] = stacked(qkv[i, :, 0 : 2 * HEAD])
        g = stacked(d_o[i])
        dos[i] = g
        o_load(i).wait()
        delta[i] = jnp.sum(g.astype(F32).T * o_v[i % 2], axis=0, keepdims=True)
        dq[i] = jnp.zeros((HEAD, QK), F32)
        first[i] = first_slots(lambda n: lens[0, n], group_slots(i))

    met(peers)
    ffn = run_scatter(at, (p0, p1, p2), (t0, t1, t2), f_bufs, f_sems)
    next(ffn)
    swap_n1 = remote(n1h.at[1 - k], n1_m, n_ssem, n_rsem, to)
    swap_n1.start()

    def block_at(n):
        return (col + 1 + n) % NC

    lanes_q, lanes_kv = pl.ds(0, 2 * HEAD), pl.ds(2 * HEAD, 2 * HEAD)
    every = (slice(None),)

    def sends(n, lanes, ssem, rsem):
        c = block_at(n)
        src, dst = out_s.at[(c,) + every + (lanes,)], came.at[(col,) + every + (lanes,)]
        return remote(src, dst, ssem.at[n], rsem.at[n], (row, c))

    def sends_kv(n):
        return sends(n, lanes_kv, kv_ssem, kv_rsem)

    def sends_q(n):
        return sends(n, lanes_q, q_ssem, q_rsem)

    def keys(n):
        j = block_at(n)
        key = qkv[j, :, 2 * HEAD : 3 * HEAD]
        value = qkv[j, :, 3 * HEAD :]
        key_t = key.astype(F32).T.astype(BF)

        def step(i, carry):
            dk, dv = carry
            s = dot(key, qs[i], NT) * (scale * LOG2E) - lse[i]
            p = jnp.where(allowed(i, j, first[i]), jnp.exp2(s), 0.0)
            ds = (p * (dot(value, dos[i], NT) - delta[i]) * scale).astype(BF)
            dv = dv + dot(p.astype(BF), dos[i])
            dk = dk + dot(ds, qs[i])
            dq[i] += dot(key_t, ds)
            return dk, dv

        zero = jnp.zeros((ROWS, HEAD), F32)
        dk, dv = lax.fori_loop(j, jnp.minimum(j + SPAN, NC), step, (zero, zero))
        out_s[j, :, 2 * HEAD : 3 * HEAD] = dk.astype(BF)
        out_s[j, :, 3 * HEAD :] = dv.astype(BF)

        @pl.when(n < NC - 1)
        def _():
            sends_kv(n).start()

        pl.when(complete(n))(lambda: queries(n))

    start = block_at(0)

    def complete(n):
        j = block_at(n)
        return (j < start) | (jnp.maximum(j - (SPAN - 1), 0) >= start)

    def queries(n):
        i = block_at(n)
        done = dq[i].T
        out_s[i, :, 0:HEAD] = done[:ROWS].astype(BF)
        out_s[i, :, HEAD : 2 * HEAD] = done[ROWS:].astype(BF)

        @pl.when(n < NC - 1)
        def _():
            sends_q(n).start()

    pl.loop(0, NC)(keys)

    @pl.loop(0, NC)
    def _(n):
        pl.when(jnp.logical_not(complete(n)))(lambda: queries(n))

    mine = []
    for lanes, sem in ((lanes_kv, kv_lsem), (lanes_q, q_lsem)):
        here = (col,) + every + (lanes,)
        mine.append(pltpu.make_async_copy(out_s.at[here], came.at[here], sem))
    for cp in mine:
        cp.start()

    def comes_from(n):
        return (col - 1 - n + NC) % NC

    def oa_loads(n):
        slot = n % 2
        return [
            pltpu.make_async_copy(src.at[n], oa_v.at[slot, pl.ds(ROWS * i, ROWS)], oa_sem.at[i, slot])
            for i, src in enumerate((oa, oa_m))
        ]

    def loads(n):
        c, slot = comes_from(n), n % 2
        return [
            pltpu.make_async_copy(wq.at[place(c)], w_v.at[slot, :, pl.ds(0, 256)], w_sem.at[0, slot]),
            pltpu.make_async_copy(
                wkv.at[place(c)], w_v.at[slot, :, pl.ds(256, 256)], w_sem.at[1, slot]
            ),
            pltpu.make_async_copy(raw.at[c], raw_v.at[slot], w_sem.at[2, slot]),
        ]

    for cp in oa_loads(0) + loads(0):
        cp.start()
    stack_tokens(k, dhlh, dhl_m, ht_s)

    @pl.loop(0, NC)
    def _(n):
        @pl.when(n < NC - 1)
        def _():
            for cp in oa_loads(n + 1):
                cp.start()

        for cp in oa_loads(n):
            cp.wait()
        a2[n % 4, n // 4] = dot(ht_s[...], oa_v[n % 2]).astype(BF).reshape(4, 2, 64, 256)

    swap_n1.wait()
    stack_tokens(k, n1h, n1_m, nt_s)
    acc[...] = jnp.zeros_like(acc)
    gain_qk[...] = jnp.zeros_like(gain_qk)
    next(ffn)

    def to_mate(n):
        c = comes_from(n)
        src, dst = draw.at[c, pl.ds(0, ROWS)], draw.at[c, pl.ds(ROWS, ROWS)]
        return remote(src, dst, m_ssem.at[n], m_rsem.at[n], to)

    def weights_of(n):
        c = comes_from(n)
        to_mate(n).wait()
        g = dot(nt_s[...], draw[c]).astype(BF)
        a0[c % 4, c // 4] = g[:, 0:256].reshape(4, 2, 64, 256)
        a1[c % 4, c // 4] = g[:, 256:].reshape(4, 2, 64, 256)

    @pl.loop(0, NC)
    def _(n):
        c, slot = comes_from(n), n % 2

        @pl.when(n < NC - 1)
        def _():
            for cp in loads(n + 1):
                cp.start()
            sends_kv(n).wait_recv()
            sends_q(n).wait_recv()

        @pl.when(n == NC - 1)
        def _():
            for cp in mine:
                cp.wait()

        for cp in loads(n):
            cp.wait()
        for i, gain in enumerate((qgain, qgain, kgain)):
            cols = slice(i * HEAD, (i + 1) * HEAD)
            v = raw_v[slot, :, cols]
            r = mean_square_scale(v)
            xn = v * r
            dn = unrope(came[c, :, cols].astype(F32), cos[...], sin[...])
            lanes = slice(0, HEAD) if i < 2 else slice(HEAD, 2 * HEAD)
            gain_qk[:, lanes] += jnp.sum(dn * xn, axis=0, keepdims=True)
            e = dn * gain[...]
            e = r * (e - xn * jnp.mean(e * xn, axis=-1, keepdims=True))
            draw[c, 0:ROWS, cols] = e.astype(BF)
        draw[c, 0:ROWS, 3 * HEAD :] = came[c, :, 3 * HEAD :]
        to_mate(n).start()
        acc[...] += dot(draw[c, 0:ROWS, :], w_v[slot], NT)

        @pl.when(n > 0)
        def _():
            weights_of(n - 1)

    weights_of(NC - 1)
    attn = run_scatter(at, (a0, a1, a2), (r0, r1, r2), a_bufs, a_sems, True)
    next(attn)

    xv = x[...].astype(F32)
    inverse = mean_square_scale(xv)
    xn = xv * inverse
    e = acc[...]
    gain_a[...] = jnp.sum(e * xn, axis=0, keepdims=True)
    gains = gain_steps(at, (gain_a, gain_f, gain_qk), room, gsum, g_ssem, g_rsem)
    next(gains)
    e = e * again[...]
    dx = dh[...] + inverse * (e - xn * jnp.mean(e * xn, axis=-1, keepdims=True))
    take = onehot(slt[:, :1].astype(F32).astype(I32) == iota((ROWS, ROWS), 1))
    dx_s[...] = dot(take, dx.astype(BF)).astype(BF).reshape(dx_s.shape)
    back = swap_over("row", dx_s, got, *row_sems)
    in_turn(attn, gains, ffn)
    for n in range(NC - 1):
        sends_kv(n).wait_send()
        sends_q(n).wait_send()
    for cp in back:
        cp.wait()


def back(
    lens, qkv, d_o, o_t, lse, slt, x, dh, again, qgain, kgain, cos, sin, gain_f, n1h, dhlh, dhl_m,
    raw, wq, wkv, oa, oa_m, f_parts,
):
    vm = pltpu.VMEM
    total = 2 * WIDTH + 2 * HEAD
    return pl.pallas_call(
        back_kernel,
        name="back",
        out_shape=[sds((64, 256), F32)] * 3
        + [sds((64, w), F32) for w in FFN_GRADS]
        + [sds((NR, 16, WIDTH)), sds((1, total), F32)],
        in_specs=[pl.BlockSpec(memory_space=pltpu.SMEM)] + [VMEM] * 15 + [HBM] * 9,
        out_specs=[VMEM] * 6 + [HBM, VMEM],
        scratch_shapes=[
            vm((NC, ROWS, 512), BF),
            vm((NC, QK, HEAD), BF),
            vm((NC, QK, HEAD), BF),
            vm((NC, 1, QK), F32),
            vm((NC, HEAD, QK), F32),
            vm((NC, 1, QK), I32),
            vm((NC, ROWS, 512), BF),
            vm((NC, 2 * ROWS, 512), BF),
            vm((2, WIDTH, 512), BF),
            vm((2, ROWS, 384), F32),
            vm((ROWS, WIDTH), F32),
            vm((NR, 16, WIDTH), BF),
            vm((1, WIDTH), F32),
            vm((1, 2 * HEAD), F32),
            vm((ROWS, 512), BF),
            vm((512, 2 * ROWS), BF),
            vm((512, 2 * ROWS), BF),
            vm((2, 2 * ROWS, 256), BF),
            vm((2, HEAD, QK), F32),
        ]
        + [vm((4, 2, 4, 2, 64, 256), BF)] * 3
        + [vm((4, 4, 1, total), F32)]
        + swap_sems("col") * 2
        + [DMA((3, 2)), DMA((NC,)), DMA((NC,)), DMA, DMA, DMA((2, 2)), DMA((2,))]
        + [DMA((4, 3)), DMA((4, 3))]
        + swap_sems("row")
        + scatter_sems()
        + scatter_sems()
        + scatter_buffers(ATTN)
        + scatter_buffers(FFN_GRADS),
        compiler_params=params(6, 63),
    )(
        lens, qkv, d_o, lse, slt, x, dh, again, qgain, kgain, cos, sin, gain_f, n1h, dhlh,
        dhl_m, o_t, raw, as_slabs(wq), as_slabs(wkv), oa, oa_m, *f_parts,
    )


def arrive_kernel(
    t_row, out, dx, q, kv, o, g, u, d, gains,
    out_o, dx_o, ga, gf, gq, gk, q_o, k_o, v_o, o_o, g_o, u_o, d_o,
):
    _, spot = slots_sent(t_row[...])
    pick = onehot(spot == iota((ROWS, ROWS), 1))
    out_o[...] = dot(pick, out[...].reshape(ROWS, WIDTH)).astype(BF)
    dx_o[...] = dot(pick, dx[...].reshape(ROWS, WIDTH)).astype(BF)
    ga[...] = gains[:, 0:WIDTH]
    gf[...] = gains[:, WIDTH : 2 * WIDTH]
    gq[...] = gains[:, 2 * WIDTH : 2 * WIDTH + HEAD]
    gk[...] = gains[:, 2 * WIDTH + HEAD :]
    q_o[...] = q[...]
    k_o[...] = kv[:, :HEAD]
    v_o[...] = kv[:, HEAD:]
    o_o[...] = o[...]
    for i, at_lane, part, lane, n in pieces_of(FFN_GRADS):
        (g_o, u_o, d_o)[part][:, lane : lane + n] = (g, u, d)[i][:, at_lane : at_lane + n]


def arrive(target, *args):
    return pl.pallas_call(
        arrive_kernel,
        name="arrive",
        out_shape=[sds((ROWS, WIDTH))] * 2
        + [sds((1, n), F32) for n in (WIDTH, WIDTH, HEAD, HEAD)]
        + [
            sds(n, F32)
            for n in ((64, 256), (64, 128), (64, 128), (64, 256), (64, 384), (64, 384), (64, 384))
        ],
        in_specs=[VMEM] * 10,
        out_specs=[VMEM] * 13,
        compiler_params=params(),
    )(target.reshape(1, ROWS), *args)


def local(
    tokens, grad_out, target, lengths, attn_gain, ffn_gain, q_gain, k_gain,
    w_query, key_matrix, value_matrix, w_out, w_gate, w_up, w_down,
):
    again, fgain = attn_gain.reshape(1, WIDTH), ffn_gain.reshape(1, WIDTH)
    qgain, kgain = q_gain.reshape(1, HEAD), k_gain.reshape(1, HEAD)

    oa, raw, x, n1h, cos, sin, slt, qkv, o_t, lse, wq, wkv, _, dh, dhlh, gain_f, g_o, got_out, oa_m, dhl_m, *rest = front(
        target, lengths, tokens, grad_out, again, fgain, qgain, kgain,
        w_query, key_matrix, value_matrix, w_out.T, w_gate, w_up, w_down.T,
    )
    f_parts = rest[:3]
    r_q, r_kv, r_o, r_g, r_u, r_d, got_dx, gains = back(
        lengths, qkv, g_o, o_t, lse, slt, x, dh, again, qgain, kgain, cos, sin, gain_f, n1h, dhlh,
        dhl_m, raw, wq, wkv, oa, oa_m, f_parts,
    )
    output, input_grad, ga, gf, gq, gk, g_q, g_k, g_v, g_o, g_g, g_u, g_d = arrive(
        target, got_out, got_dx, r_q, r_kv, r_o, r_g, r_u, r_d, gains
    )
    return (
        output, input_grad, ga[0], gf[0], gq[0], gk[0], g_q, g_k, g_v, g_o.T, g_g, g_u, g_d.T,
    )


def solution(mesh):
    both = P(("row", "col"), None)
    by_row, by_col = P("row", "col"), P("col", "row")
    weights = (by_row, by_row, by_row, by_col, by_row, by_row, by_col)
    return jax.shard_map(
        local,
        mesh=mesh,
        in_specs=(both, both, P(("row", "col")), P("row", None), P(), P(), P(), P()) + weights,
        out_specs=(both, both, P(), P(), P(), P()) + weights,
        check_vma=False,
    )
```

```python
import functools
import math

import jax
import jax.numpy as jnp
import numpy as np
from jax import lax
from jax.experimental import pallas as pl
from jax.experimental.pallas import tpu as pltpu
from jax.sharding import PartitionSpec as P

MESH = pl.DeviceIdType.MESH
BF = jnp.bfloat16
F32 = jnp.float32
I32 = jnp.int32
EPSILON = 1e-06
ROPE_BASE = 1000000.0
HEAD = 128
NR = 16
NC = 8
ROWS = 256
WIDTH = 1024
GROUP = 2048
ORDERS = (("x", "y", "z"), ("y", "z", "x"), ("z", "x", "y"))
ATTN = (256, 256, 256)
FFN = (256, 256, 640)
FFN_GRADS = (256, 256, 640)
HBM = pl.BlockSpec(memory_space=pltpu.HBM)
VMEM = pl.BlockSpec(memory_space=pltpu.VMEM)
DMA = pltpu.SemaphoreType.DMA


def sds(shape, dtype=BF):
    return jax.ShapeDtypeStruct(shape, dtype)


def params(cid=None, mib=56, **kw):
    if cid is not None:
        kw.update(collective_id=cid, has_side_effects=True)
    return pltpu.CompilerParams(vmem_limit_bytes=mib << 20, **kw)


def where_am_i():
    r = lax.axis_index("row")
    c = lax.axis_index("col")
    return {"x": c % 4, "y": r // 4, "z": 2 * ((r // 2) % 2) + c // 4, "k": r % 2}


def device(at):
    return (at["y"] * 4 + (at["z"] // 2) * 2 + at["k"], (at["z"] % 2) * 4 + at["x"])


def moved(at, axis, step):
    out = dict(at)
    out[axis] = (at[axis] + step) % 4
    return out


def mate(at):
    out = dict(at)
    out["k"] = 1 - at["k"]
    return out


def greet(peers):
    barrier = pltpu.get_barrier_semaphore()
    for p in peers:
        pl.semaphore_signal(barrier, inc=1, device_id=p, device_id_type=MESH)


def met(peers):
    pl.semaphore_wait(pltpu.get_barrier_semaphore(), len(peers))


def ring_peers(at):
    return [device(moved(at, a, s)) for a in "xyz" for s in (1, -1)]


def row_peers(at):
    r = lax.axis_index("row")
    c = lax.axis_index("col")
    return [((r + d) % NR, c) for d in range(1, NR)]


def col_peers(at):
    r = lax.axis_index("row")
    c = lax.axis_index("col")
    return [(r, (c + d) % NC) for d in range(1, NC)]


def remote(src, dst, ssem, rsem, to):
    return pltpu.make_async_remote_copy(
        src_ref=src, dst_ref=dst, send_sem=ssem, recv_sem=rsem, device_id=to, device_id_type=MESH
    )


def block_index(sel, with_core=None):
    full = slice(None)
    z = sel.get("z")
    idx = (
        sel.get("x", full),
        full if z is None else z % 2,
        sel.get("y", full),
        full if z is None else z // 2,
    )
    return idx if with_core is None else idx + (with_core,)


SHIFT = (0, -1, 1, 2)


def piece_index(at, order, t, g, rel):
    sel = {a: at[a] for a in order[t + 1 :]}
    if t > 0 and g is not None:
        sel[order[t - 1]] = (at[order[t - 1]] + SHIFT[g]) % 4
    sel[order[t]] = (at[order[t]] + rel) % 4
    return block_index(sel, at["k"])


class Gather:
    def __init__(self, at, outs, sems, phases=(0, 1, 2), own=None, orders=ORDERS, split=False):
        self.at, self.outs, self.own, self.orders = at, outs, own, orders
        self.base = {t: sum(4 if p == 0 or not split else 16 for p in phases if p < t) for t in phases}
        self.ssem, self.rsem, self.msem, self.nsem = sems
        self.n = len(outs)
        self.half = outs[0].shape[5] // 2
        self.late, self.sent = [], []

    def copies(self, s, t, g):
        ref = self.outs[s].at[piece_index(self.at, self.orders[s], t, g, 0)]
        a, i = self.orders[s][t], self.base[t] + 4 * (g or 0)
        src = self.own[s] if self.own and (t == 0 or (t == 1 and g == 0)) else ref
        return [
            remote(src, ref, self.ssem.at[s, i + d], self.rsem.at[s, i + d], device(moved(self.at, a, step)))
            for d, step in enumerate((1, -1))
        ]

    def forwards(self, s, t, g):
        a, i = self.orders[s][t], self.base[t] + 4 * (g or 0) + 2
        out = []
        for d, step in enumerate((1, -1)):
            came = piece_index(self.at, self.orders[s], t, g, -step) + (pl.ds(d * self.half, self.half),)
            ref = self.outs[s].at[came]
            out.append(
                remote(
                    ref,
                    ref,
                    self.ssem.at[s, i + d],
                    self.rsem.at[s, i + d],
                    device(moved(self.at, a, step)),
                )
            )
        return out

    def to_mate(self, s, g, rel):
        slot = 4 * (g or 0) + SHIFT.index(rel)
        ref = self.outs[s].at[piece_index(self.at, self.orders[s], 2, g, rel)]
        return remote(ref, ref, self.msem.at[s, slot], self.nsem.at[s, slot], device(mate(self.at)))

    def share(self, s, g, rel):
        cp = self.to_mate(s, g, rel)
        cp.start()
        self.late.append(cp)

    def send(self, t, g):
        for s in range(self.n):
            for cp in self.copies(s, t, g):
                cp.start()
                self.sent.append(cp)
            if t == 2:
                self.share(s, g, 0)

    def pass_on(self, t, g, wait=True):
        for s in range(self.n):
            first = self.copies(s, t, g) if wait else None
            for d, cp in enumerate(self.forwards(s, t, g)):
                if wait:
                    first[d].wait_recv()
                cp.start()
                self.sent.append(cp)
                if t == 2:
                    self.share(s, g, (-1, 1)[d])

    def arrived(self, t, g):
        for s in range(self.n):
            for cp in self.forwards(s, t, g):
                cp.wait_recv()
            if t == 2:
                self.share(s, g, 2)

    def drain(self):
        for cp in self.late:
            cp.wait()
        for cp in self.sent:
            cp.wait_send()

    def lines(self):
        self.send(0, None)
        self.send(1, 0)
        yield
        self.pass_on(0, None)
        self.send(1, 1)
        self.send(1, 2)
        yield
        self.pass_on(1, 0)
        self.arrived(0, None)
        self.send(1, 3)
        yield
        for g in (1, 2, 3):
            self.pass_on(1, g)
        yield
        for g in range(4):
            self.arrived(1, g)

    def all(self):
        self.send(0, None)
        self.send(1, 0)
        yield
        self.pass_on(0, None)
        self.send(1, 1)
        self.send(1, 2)
        yield
        self.pass_on(1, 0)
        self.arrived(0, None)
        self.send(1, 3)
        self.send(2, 0)
        yield
        self.pass_on(1, 1)
        self.pass_on(1, 2)
        self.pass_on(1, 3)
        self.send(2, 1)
        self.send(2, 2)
        yield
        self.pass_on(2, 0)
        for g in range(4):
            self.arrived(1, g)
        self.send(2, 3)
        yield
        self.pass_on(2, 1)
        self.pass_on(2, 2)
        yield
        self.pass_on(2, 3)
        yield
        for g in range(4):
            self.arrived(2, g)


def gather_sems(steps, shares, n=3):
    return [DMA((n, steps)), DMA((n, steps)), DMA((n, max(shares, 1))), DMA((n, max(shares, 1)))]


def gather_shape(w):
    return sds((4, 2, 4, 2, 2, 64, w))


def lead_shape(axes):
    out = ()
    for a in ("x", "zl", "y", "zh"):
        if a[0] in axes:
            out += (4,) if a in "xy" else (2,)
    return out


def sub_index(sel, axes):
    out = ()
    for a in ("x", "zl", "y", "zh"):
        if a[0] not in axes:
            continue
        pos = sel.get(a[0])
        if pos is None:
            out += (slice(None),)
        elif a == "zl":
            out += (pos % 2,)
        elif a == "zh":
            out += (pos // 2,)
        else:
            out += (pos,)
    return out


def add_up(dst, terms):
    total = None
    if len(terms) == 2:
        total = terms[0][0][terms[0][1]] + terms[1][0][terms[1][1]]
    else:
        for ref, at in terms:
            v = ref[at].astype(F32)
            total = v if total is None else total + v
    dst[0][dst[1]] = total.astype(dst[0].dtype)


def scatter_leads(s, t):
    return lead_shape(ORDERS[s][: 2 - t])


def scatter_buffers(widths, t0=0, n=3):
    out = []
    for s in range(n):
        for t in range(t0, 3):
            lead, w = scatter_leads(s, t), widths[s]
            out.append(pltpu.VMEM((2,) + lead + (32, w), BF))
            out.append(pltpu.VMEM((2,) + lead + (64, w), BF))
            out.append(pltpu.VMEM((2,) + lead + (32, w), BF))
            out.append(pltpu.VMEM(lead + (64, w), BF))
    return out


def scatter_sems(phases=3, n=3):
    return [DMA((n, phases, 6)), DMA((n, phases, 6)), DMA((n, 3))]


LO, HI = pl.ds(0, 32), pl.ds(32, 32)


def part_of(s, t, at, rel, rows):
    a = ORDERS[s][2 - t]
    return sub_index({a: (at[a] + rel) % 4}, ORDERS[s][: 3 - t]) + (rows,)


def first_sends(s, t, at, ref, rel_in, piece_in, ssem, rsem, t0=0):
    a = ORDERS[s][2 - t]
    right, left = device(moved(at, a, 1)), device(moved(at, a, -1))
    allr = (slice(None),) * len(scatter_leads(s, t))

    def src(rel, rows):
        return ref.at[part_of(s, t, at, rel, rows)]

    return [
        remote(src(2, LO), rel_in.at[0], ssem.at[s, t - t0, 0], rsem.at[s, t - t0, 0], right),
        remote(src(2, HI), rel_in.at[1], ssem.at[s, t - t0, 1], rsem.at[s, t - t0, 1], left),
        remote(
            src(1, HI), piece_in.at[(0,) + allr + (HI,)], ssem.at[s, t - t0, 2], rsem.at[s, t - t0, 2], right
        ),
        remote(
            src(-1, LO), piece_in.at[(1,) + allr + (LO,)], ssem.at[s, t - t0, 3], rsem.at[s, t - t0, 3], left
        ),
    ]


def second_send(s, t, at, d, rel_out, piece_in, ssem, rsem, t0=0):
    a = ORDERS[s][2 - t]
    allr = (slice(None),) * len(scatter_leads(s, t))
    return remote(
        rel_out.at[d],
        piece_in.at[(d,) + allr + ((LO, HI)[d],)],
        ssem.at[s, t - t0, 4 + d],
        rsem.at[s, t - t0, 4 + d],
        device(moved(at, a, (1, -1)[d])),
    )


def run_scatter(at, parts, results, bufs, sems, resident=False):
    ssem, rsem, lsem = sems
    t0 = 0
    n = len(parts)
    cur = list(parts)
    waits = []
    per = 4 * (3 - t0)
    for t in range(t0, 3):
        st = []
        for s in range(n):
            i = s * per + 4 * (t - t0)
            rel_in, piece_in, rel_out, total = bufs[i : i + 4]
            cps = first_sends(s, t, at, cur[s], rel_in, piece_in, ssem, rsem, t0)
            for cp in cps:
                cp.start()
            loads = []
            if t == t0 and not resident:
                for j, (rel, rows, dst) in enumerate(
                    ((1, LO, rel_out.at[0]), (-1, HI, rel_out.at[1]), (0, slice(None), total))
                ):
                    cp = pltpu.make_async_copy(
                        cur[s].at[part_of(s, t, at, rel, rows)], dst, lsem.at[s, j]
                    )
                    cp.start()
                    loads.append(cp)
            st.append((rel_in, piece_in, rel_out, total, cps, loads))
        yield
        for s in range(n):
            rel_in, piece_in, rel_out, total, cps, loads = st[s]
            for d in range(2):
                cps[d].wait_recv()
                if loads:
                    loads[d].wait()
                    mine = (rel_out, d)
                else:
                    mine = (cur[s], part_of(s, t, at, (1, -1)[d], (LO, HI)[d]))
                add_up((rel_out, d), [mine, (rel_in, d)])
                cp = second_send(s, t, at, d, rel_out, piece_in, ssem, rsem, t0)
                cp.start()
                cps.append(cp)
        yield
        for s in range(n):
            rel_in, piece_in, rel_out, total, cps, loads = st[s]
            for i in (2, 3, 4, 5):
                cps[i].wait_recv()
            if loads:
                loads[2].wait()
                mine = (total, ...)
            else:
                mine = (cur[s], part_of(s, t, at, 0, slice(None)))
            dst = (total if t < 2 else results[s], ...)
            add_up(dst, [mine, (piece_in, 0), (piece_in, 1)])
            cur[s] = total
            waits += cps
    for cp in waits:
        cp.wait_send()


def in_turn(*steps):
    live = list(steps)
    while live:
        for it in list(live):
            if next(it, "end") == "end":
                live.remove(it)


def swap_over(axis, src, dst, ssem, rsem, lsem):
    n = NR if axis == "row" else NC
    r = lax.axis_index("row")
    c = lax.axis_index("col")
    me = r if axis == "row" else c
    cps = []
    for d in range(1, n):
        to = (me + d) % n
        cp = remote(
            src.at[to],
            dst.at[me],
            ssem.at[d - 1],
            rsem.at[d - 1],
            (to, c) if axis == "row" else (r, to),
        )
        cp.start()
        cps.append(cp)
    own = pltpu.make_async_copy(src.at[me], dst.at[me], lsem)
    own.start()
    return cps + [own]


def swap_sems(axis):
    n = NR if axis == "row" else NC
    return [DMA((n - 1,)), DMA((n - 1,)), DMA]


def dot(a, b, dims=((1,), (0,))):
    return lax.dot_general(a, b, (dims, ((), ())), preferred_element_type=F32)


NT = ((1,), (1,))
TN = ((0,), (0,))


def iota(shape, dim):
    return lax.broadcasted_iota(I32, shape, dim)


def onehot(cond):
    return cond.astype(F32).astype(BF)


def unrope(g, cos, sin):
    return g * cos - pltpu.roll(g, HEAD // 2, 1) * sin


def mean_square_scale(v):
    return lax.rsqrt(jnp.mean(v * v, axis=-1, keepdims=True) + EPSILON)


def column(row):
    eye = iota((ROWS, ROWS), 0) == iota((ROWS, ROWS), 1)
    return jnp.sum(jnp.where(eye, row.astype(F32), 0.0), axis=1, keepdims=True).astype(I32)


def slots_sent(target_row):
    g_row = target_row // GROUP
    g_col = column(g_row)
    same = g_row == g_col
    i0, i1 = iota((ROWS, ROWS), 0), iota((ROWS, ROWS), 1)
    before_row = jnp.sum((same & (i0 < i1)).astype(F32), axis=0, keepdims=True).astype(I32)
    before_col = jnp.sum((same & (i1 < i0)).astype(F32), axis=1, keepdims=True).astype(I32)
    return g_row * (ROWS // NR) + before_row, g_col * (ROWS // NR) + before_col


def halves_of(v):
    even, odd = [], []
    low = iota((v.shape[0], HEAD), 1) < HEAD // 2
    for m in range(4):
        a, b = v[:, 256 * m : 256 * m + 128], v[:, 256 * m + 128 : 256 * m + 256]
        even.append(jnp.where(low, a, pltpu.roll(b, 64, 1)))
        odd.append(jnp.where(low, pltpu.roll(a, 64, 1), b))
    return jnp.concatenate(even, axis=1), jnp.concatenate(odd, axis=1)


def first_slots(lens, slots):
    start = jnp.int32(0)
    out = jnp.zeros_like(slots)
    for j in range(8):
        out = jnp.where(slots >= start, start, out)
        start = start + lens(j)
    return out


def place(c):
    return (c % 4) * 2 + c // 4


def as_slabs(g):
    return g.reshape(NC, -1, g.shape[-1])


LOG2E = math.log2(math.e)
QK = 512


def stacked(v):
    return jnp.concatenate([v[:, :HEAD], v[:, HEAD : 2 * HEAD]], axis=0)


SPAN = 5


def group_slots(i):
    return i * ROWS + iota((1, QK), 1) % ROWS


def allowed(i, j, first):
    key = j * ROWS + iota((ROWS, QK), 0)
    return (key <= group_slots(i)) & (key >= first)


PAIR = 768
STEPS = 4


def stack_tokens(k, mine, others, scratch):
    scratch[:, 0:ROWS] = mine[k].astype(F32).T.astype(BF)
    scratch[:, ROWS:] = others[...].astype(F32).T.astype(BF)


def pieces_of(widths):
    w0, w1, _ = widths
    out = (
        (0, 0, 0, 0, w0),
        (2, 0, 0, w0, 384 - w0),
        (1, 0, 1, 0, w1),
        (2, 384 - w0, 1, w1, 384 - w1),
        (2, 768 - w0 - w1, 2, 0, 384),
    )
    return [p for p in out if p[4] > 0]


def lanes_of(widths, j):
    return [
        (s, pl.ds(a, n), pl.ds(PAIR * part + 384 * j + b, n))
        for s, a, part, b, n in pieces_of(widths)
    ]


def middle_steps(
    at, slt, x, dy, dyh, fgain, oa, wo, f0, f1, f2,
    dh_o, dhlh, gain_o, g_o, got, oa_m, dhl_m, p0, p1, p2,
    oa_v, wo_v, w_v, acc, dn2, h_s, n2_s, dhl_s, act, n2h, n2_m, dy_m, do_s, out_s, nt_s, yt_s,
    oa_sem, wo_sem, w_sem, g_sem, act_ssem, act_rsem, m_ssem, m_rsem, do_ssem, do_rsem, do_lsem,
    *row_sems,
):
    row, col, k = lax.axis_index("row"), lax.axis_index("col"), at["k"]
    to = device(mate(at))
    lead, more = [], []
    flat = [f.reshape(NC, WIDTH, w) for f, w in zip((f0, f1, f2), FFN)]
    parts = [p.reshape(NC, 512, w) for p, w in zip((p0, p1, p2), FFN_GRADS)]
    for p in range(NC):
        c = (p % 2) * 4 + p // 2
        lanes = pl.ds(256 * p, 256)
        lead.append(pltpu.make_async_copy(wo.reshape(NC, WIDTH, 256).at[p], wo_v.at[:, lanes], wo_sem.at[p]))
        more.append(pltpu.make_async_copy(oa.at[c], oa_v.at[:, lanes], oa_sem.at[p]))
    for cp in lead:
        cp.start()
    yield
    for cp in more:
        cp.start()
    lead += more

    def loads(t):
        slot = t % 2
        return [
            pltpu.make_async_copy(
                flat[i].at[2 * t + j, :, src],
                w_v.at[slot, :, dst],
                w_sem.at[slot, 5 * j + n],
            )
            for j in range(2)
            for n, (i, src, dst) in enumerate(lanes_of(FFN, j))
        ]

    def weights(slot, start, stop):
        return w_v[slot, :, start:stop]

    def act_send(t):
        rows = pl.ds(0, ROWS), pl.ds(ROWS, ROWS)
        return remote(act.at[t, rows[0]], act.at[t, rows[1]], act_ssem.at[t], act_rsem.at[t], to)

    def mate_send(i, src, dst):
        return remote(src, dst, m_ssem.at[i], m_rsem.at[i], to)

    for cp in lead:
        cp.wait()

    @pl.loop(0, 4)
    def _(n):
        cols = pl.ds(pl.multiple_of(256 * n, 256), 256)
        acc[:, cols] = x[:, cols].astype(F32) + dot(oa_v[...], wo_v[cols, :], NT)

    h = acc[...]
    h_s[...] = h
    n2 = h * mean_square_scale(h) * fgain[...]
    n2_s[...] = n2.astype(BF)
    a, b = halves_of(n2)
    n2h[0] = a.astype(BF)
    n2h[1] = b.astype(BF)
    dn2[...] = jnp.zeros_like(dn2)
    yield
    for cp in loads(0):
        cp.start(priority=1)
    pairs = ((dyh.at[1 - k], dy_m), (oa, oa_m), (n2h.at[1 - k], n2_m))
    to_mate = [mate_send(i, src, dst) for i, (src, dst) in enumerate(pairs)]
    for cp in to_mate:
        cp.start()

    @pl.loop(0, STEPS)
    def _(t):
        slot = t % 2

        @pl.when(t < STEPS - 1)
        def _():
            for cp in loads(t + 1):
                cp.start(priority=1)

        for cp in loads(t):
            cp.wait()
        g = dot(n2_s[...], weights(slot, 0, PAIR))
        u = dot(n2_s[...], weights(slot, PAIR, 2 * PAIR))
        dhid = dot(dy[...], weights(slot, 2 * PAIR, 3 * PAIR))
        sig = jax.nn.sigmoid(g)
        silu = g * sig
        act[t, 0:ROWS, 2 * PAIR :] = (silu * u).astype(BF)
        act[t, 0:ROWS, 0:PAIR] = (dhid * u * sig * (1.0 + g * (1.0 - sig))).astype(BF)
        act[t, 0:ROWS, PAIR : 2 * PAIR] = (dhid * silu).astype(BF)
        act_send(t).start()
        acc[...] += dot(act[t, 0:ROWS, 2 * PAIR :], weights(slot, 2 * PAIR, 3 * PAIR), NT)
        dn2[...] += dot(act[t, 0:ROWS, 0 : 2 * PAIR], weights(slot, 0, 2 * PAIR), NT)

    h = h_s[...]
    r2 = mean_square_scale(h)
    hn = h * r2
    e = dn2[...]
    gain_o[...] = jnp.sum(e * hn, axis=0, keepdims=True)
    e = e * fgain[...]
    dh = dy[...].astype(F32) + r2 * (e - hn * jnp.mean(e * hn, axis=-1, keepdims=True))
    dh_o[...] = dh
    dhl_s[...] = dh.astype(BF)

    def block_at(n):
        return (col + 1 + n) % NC

    def do_send(n):
        c = block_at(n)
        return remote(do_s.at[c], g_o.at[col], do_ssem.at[n], do_rsem.at[n], (row, c))

    @pl.loop(0, NC)
    def _(n):
        c = block_at(n)
        cols = pl.ds(pl.multiple_of(256 * place(c), 256), 256)
        do_s[c] = dot(dhl_s[...], wo_v[:, cols]).astype(BF)

        @pl.when(n < NC - 1)
        def _():
            do_send(n).start()

    mine = pltpu.make_async_copy(do_s.at[col], g_o.at[col], do_lsem)
    mine.start()
    take = onehot(slt[:, :1].astype(F32).astype(I32) == iota((ROWS, ROWS), 1))
    out_s[...] = dot(take, acc[...].astype(BF)).astype(BF).reshape(out_s.shape)
    back = swap_over("row", out_s, got, *row_sems)
    a, b = halves_of(dhl_s[...].astype(F32))
    dhlh[0] = a.astype(BF)
    dhlh[1] = b.astype(BF)
    cp = mate_send(3, dhlh.at[1 - k], dhl_m)
    cp.start()
    to_mate.append(cp)
    for cp in to_mate:
        cp.wait()
    stack_tokens(k, n2h, n2_m, nt_s)
    stack_tokens(k, dyh, dy_m, yt_s)

    def stores(t):
        slot = t % 2
        return [
            pltpu.make_async_copy(
                w_v.at[slot, pl.ds(0, 512), src],
                parts[i].at[2 * t + j, :, dst],
                g_sem.at[slot, 5 * j + n],
            )
            for j in range(2)
            for n, (i, dst, src) in enumerate(lanes_of(FFN_GRADS, j))
        ]

    @pl.loop(0, STEPS)
    def _(t):
        slot = t % 2

        @pl.when(t >= 2)
        def _():
            for cp in stores(t - 2):
                cp.wait()

        act_send(t).wait()
        gu = 2 * PAIR
        g = dot(nt_s[...], act[t, :, 0:gu]).astype(BF)
        w_v[slot, 0:512, 0:gu] = g
        g = dot(yt_s[...], act[t, :, gu:]).astype(BF)
        w_v[slot, 0:512, gu:] = g
        for cp in stores(t):
            cp.start()

    for t in (STEPS - 2, STEPS - 1):
        for cp in stores(t):
            cp.wait()
    for n in range(NC - 1):
        do_send(n).wait()
    for cp in [mine] + back:
        cp.wait()


def front_kernel(
    t_row, lens, tokens, grads, again, fgain, qgain, kgain, freq, w_q, w_k, w_v, w_o, w_g, w_u, w_d,
    oa, raw, x_o, n1h, cos, sin, slt, qkv_o, o_t, lse, a0, a1, a2,
    dh_o, dhlh, gain_o, g_o, got, oa_m, dhl_m, p0, p1, p2, f0, f1, f2,
    sent, came, dy_s, dyh, kv_s, u0_s, u1_s, u2_s, n1_s, src_s, raw_s, wq_v, wkv_v, qkv, o_s, s_v,
    own_sem, w_sem, keep_sem, out_ssem, out_rsem, out_lsem, o_ssem, o_rsem, o_lsem, *rest,
):
    at = where_am_i()
    sems, rest = rest[:22], rest[22:]
    row, col = lax.axis_index("row"), lax.axis_index("col")
    here = block_index({a: at[a] for a in "xyz"}, at["k"])
    near = [device(moved(at, "z", 1)), device(moved(at, "z", -1))]
    peers = near + row_peers(at) + col_peers(at)
    greet(peers)
    kv_s[:, :HEAD] = w_k[...]
    kv_s[:, HEAD:] = w_v[...]
    for i, at_lane, part, lane, n in pieces_of(FFN):
        src = (w_g, w_u, w_d)[part]
        (u0_s, u1_s, u2_s)[i][:, at_lane : at_lane + n] = src[:, lane : lane + n]
    pairs = zip((w_q, kv_s, w_o, u0_s, u1_s, u2_s), (a0, a1, a2, f0, f1, f2))
    own = [
        pltpu.make_async_copy(src, dst.at[here], own_sem.at[i])
        for i, (src, dst) in enumerate(pairs)
    ]
    for cp in own:
        cp.start()
    spot, _ = slots_sent(t_row[...])
    sel = spot == iota((ROWS, ROWS), 0)
    pick = onehot(sel)
    slot = jnp.sum(jnp.where(sel, t_row[...] % ROWS, 0).astype(F32), axis=1, keepdims=True)
    met(peers)
    attn = Gather(at, (a0, a1, a2), sems[6:10], own=(w_q, kv_s, w_o), split=True)
    lines = Gather(at, (f0, f1, f2), sems[10:14], (0, 1), own=(u0_s, u1_s, u2_s), split=True)
    planes = [
        Gather(at, (f0, f1), sems[14:18], (2,), orders=ORDERS[:2]),
        Gather(at, (f2,), sems[18:22], (2,), orders=ORDERS[2:]),
    ]
    steps = attn.all()
    more = lines.lines()
    next(steps)
    next(more)
    message = (NR, 16, WIDTH)
    sent[0, :, :, 0:WIDTH] = dot(pick, tokens[...]).astype(BF).reshape(message)
    sent[0, :, :, WIDTH:] = (
        jnp.broadcast_to(slot, (ROWS, HEAD)).astype(BF).reshape((NR, 16, HEAD))
    )
    cps = swap_over("row", sent.at[0], came.at[0], *sems[0:3])
    next(steps)
    next(more)
    for cp in own:
        cp.wait()
    for _ in range(5):
        next(steps)
        next(more, None)
    slots = col * ROWS + iota((ROWS, HEAD), 0)
    pos = (slots - first_slots(lambda j: lens[0, j], slots)).astype(F32)
    angle = pos * freq[...]
    cos[...] = jnp.cos(angle)
    sine = jnp.sin(angle)
    sin[...] = jnp.where(iota((ROWS, HEAD), 1) < HEAD // 2, -sine, sine)
    sent[1, :, :, 0:WIDTH] = dot(pick, grads[...]).astype(BF).reshape(message)
    for cp in cps:
        cp.wait()
    local = came[0, :, :, WIDTH:].reshape(ROWS, HEAD)
    slt[...] = local
    put = onehot(local[:, :1].astype(F32).astype(I32) == iota((ROWS, ROWS), 1))
    x = dot(put, came[0, :, :, 0:WIDTH].reshape(ROWS, WIDTH), TN)
    x_o[...] = x.astype(BF)
    n1 = x * mean_square_scale(x) * again[...]
    n1_s[...] = n1.astype(BF)
    a, b = halves_of(n1)
    n1h[0] = a.astype(BF)
    n1h[1] = b.astype(BF)
    in_turn(steps, more)

    def block_at(i):
        return (col + 1 + i) % NC

    slabs = [a.reshape(NC, WIDTH, 256) for a in (a0, a1)]

    def loads(i):
        c, slot = block_at(i), i % 2
        return [
            pltpu.make_async_copy(slabs[0].at[place(c)], wq_v.at[slot], w_sem.at[0, slot]),
            pltpu.make_async_copy(slabs[1].at[place(c)], wkv_v.at[slot], w_sem.at[1, slot]),
        ]

    def sends(i):
        c = block_at(i)
        return remote(src_s.at[c], qkv.at[col], out_ssem.at[i], out_rsem.at[i], (row, c))

    for cp in attn.late:
        cp.wait()
    planes[1].send(2, None)
    for cp in loads(0):
        cp.start(priority=1)

    def columns(i):
        c = block_at(i)

        @pl.when(i < NC - 1)
        def _():
            for cp in loads(i + 1):
                cp.start(priority=1)

        for cp in loads(i):
            cp.wait()
        n = n1_s[...]
        q = dot(n, wq_v[i % 2])
        kv = dot(n, wkv_v[i % 2])
        raw_s[c, :, 0:256] = q
        raw_s[c, :, 256:384] = kv[:, :HEAD]
        pieces = ((q[:, :HEAD], qgain), (q[:, HEAD:], qgain), (kv[:, :HEAD], kgain))
        for j, (v, gain) in enumerate(pieces):
            v = v * mean_square_scale(v) * gain[...]
            v = v * cos[...] + pltpu.roll(v, HEAD // 2, 1) * sin[...]
            src_s[c, :, j * HEAD : (j + 1) * HEAD] = v.astype(BF)
        src_s[c, :, 3 * HEAD :] = kv[:, HEAD:].astype(BF)

        @pl.when(i < NC - 1)
        def _():
            sends(i).start()

    pl.loop(0, NC)(columns)
    mine = pltpu.make_async_copy(src_s.at[col], qkv.at[col], out_lsem)
    mine.start()
    keep = [pltpu.make_async_copy(raw_s, raw, keep_sem.at[0])]
    keep[0].start()
    cps = swap_over("row", sent.at[1, :, :, pl.ds(0, WIDTH)], came.at[1, :, :, pl.ds(0, WIDTH)], *sems[3:6])
    planes[0].send(2, None)
    for i in range(NC - 1):
        sends(i).wait()
    mine.wait()
    keep.append(pltpu.make_async_copy(qkv, qkv_o, keep_sem.at[1]))
    keep[1].start()

    scale = HEAD**-0.5 * LOG2E

    def o_sends(n):
        c = block_at(n)
        return remote(o_s.at[c], oa.at[col], o_ssem.at[n], o_rsem.at[n], (row, c))

    def queries(n):
        i = block_at(n)
        q = stacked(qkv[i, :, 0 : 2 * HEAD])
        start = first_slots(lambda j: lens[0, j], group_slots(i))
        j0 = jnp.maximum(i - (SPAN - 1), 0)
        m = None
        for d in range(SPAN):
            s = dot(qkv[j0 + d, :, 2 * HEAD : 3 * HEAD], q, NT) * scale
            s = jnp.where(allowed(i, j0 + d, start), s, -1e30)
            s_v[d] = s
            top = jnp.max(s, axis=0, keepdims=True)
            m = top if m is None else jnp.maximum(m, top)
        total = jnp.zeros((1, QK), F32)
        acc = jnp.zeros((HEAD, QK), F32)
        for d in range(SPAN):
            p = jnp.exp2(s_v[d] - m)
            total = total + jnp.sum(p, axis=0, keepdims=True)
            acc = acc + dot(qkv[j0 + d, :, 3 * HEAD :], p.astype(BF), TN)
        o = acc / total
        o_t[i] = o
        lse[i] = m + jnp.log2(total)
        back = o.T
        o_s[i] = jnp.concatenate([back[:ROWS], back[ROWS:]], axis=1).astype(BF)

        @pl.when(n < NC - 1)
        def _():
            o_sends(n).start()

    ffn = middle_steps(
        at, slt, x_o, dy_s, dyh, fgain, oa, a2, f0, f1, f2,
        dh_o, dhlh, gain_o, g_o, got, oa_m, dhl_m, p0, p1, p2, *rest,
    )
    next(ffn)
    pl.loop(0, NC)(queries)
    planes[1].pass_on(2, None)
    planes[0].pass_on(2, None)
    mine = pltpu.make_async_copy(o_s.at[col], oa.at[col], o_lsem)
    mine.start()
    for cp in cps:
        cp.wait()
    dy = dot(put, came[1, :, :, 0:WIDTH].reshape(ROWS, WIDTH), TN)
    dy_s[...] = dy.astype(BF)
    a, b = halves_of(dy)
    dyh[0] = a.astype(BF)
    dyh[1] = b.astype(BF)
    for n in range(NC - 1):
        o_sends(n).wait()
    for cp in [mine] + keep:
        cp.wait()
    next(ffn)
    planes[0].arrived(2, None)
    planes[1].arrived(2, None)
    for g in [lines] + planes:
        g.drain()
    for cp in attn.sent:
        cp.wait_send()
    next(ffn, None)


def front(target, lens, tokens, grads, again, fgain, qgain, kgain, *weights):
    freq = ROPE_BASE ** (-(np.arange(HEAD) % (HEAD // 2)).astype(np.float32) * 2.0 / HEAD)
    freq = jnp.asarray(freq.astype(np.float32).reshape(1, HEAD))
    vm = pltpu.VMEM
    outs = [
        (HBM, sds((NC, ROWS, 256))),
        (HBM, sds((NC, ROWS, 384), F32)),
        (VMEM, sds((ROWS, WIDTH))),
        (VMEM, sds((2, ROWS, 512))),
        (VMEM, sds((ROWS, HEAD), F32)),
        (VMEM, sds((ROWS, HEAD), F32)),
        (VMEM, sds((ROWS, HEAD))),
        (HBM, sds((NC, ROWS, 512))),
        (VMEM, sds((NC, HEAD, QK), F32)),
        (VMEM, sds((NC, 1, QK), F32)),
    ]
    outs += [(HBM, gather_shape(w)) for w in ATTN]
    outs += [
        (VMEM, sds((ROWS, WIDTH), F32)),
        (VMEM, sds((2, ROWS, 512))),
        (VMEM, sds((1, WIDTH), F32)),
        (HBM, sds((NC, ROWS, 256))),
        (HBM, sds((NR, 16, WIDTH))),
        (HBM, sds((NC, ROWS, 256))),
        (HBM, sds((ROWS, 512))),
    ]
    outs += [(HBM, sds((4, 2, 4, 2, 64, w))) for w in FFN_GRADS]
    outs += [(HBM, gather_shape(w)) for w in FFN]
    return pl.pallas_call(
        front_kernel,
        name="front",
        out_shape=[shape for _, shape in outs],
        in_specs=[VMEM, pl.BlockSpec(memory_space=pltpu.SMEM)]
        + [VMEM] * 7
        + [HBM, VMEM, VMEM, HBM]
        + [VMEM] * 3,
        out_specs=[space for space, _ in outs],
        scratch_shapes=[vm((2, NR, 16, WIDTH + HEAD), BF)] * 2
        + [vm((ROWS, WIDTH), BF), vm((2, ROWS, 512), BF)]
        + [vm((64, w), BF) for w in (256,) + FFN]
        + [
            vm((ROWS, WIDTH), BF),
            vm((NC, ROWS, 512), BF),
            vm((NC, ROWS, 384), F32),
            vm((2, WIDTH, 256), BF),
            vm((2, WIDTH, 256), BF),
            vm((NC, ROWS, 512), BF),
            vm((NC, ROWS, 256), BF),
            vm((SPAN, ROWS, QK), F32),
        ]
        + [DMA((6,)), DMA((2, 2)), DMA((2,))]
        + swap_sems("col") * 2
        + swap_sems("row") * 2
        + gather_sems(36, 16)
        + gather_sems(20, 0)
        + gather_sems(4, 4, 2)
        + gather_sems(4, 4, 1)
        + [
            vm((ROWS, 2048), BF),
            vm((WIDTH, 2048), BF),
            vm((2, WIDTH, 3 * PAIR), BF),
            vm((ROWS, WIDTH), F32),
            vm((ROWS, WIDTH), F32),
            vm((ROWS, WIDTH), F32),
            vm((ROWS, WIDTH), BF),
            vm((ROWS, WIDTH), BF),
            vm((STEPS, 2 * ROWS, 3 * PAIR), BF),
            vm((2, ROWS, 512), BF),
            vm((ROWS, 512), BF),
            vm((ROWS, 512), BF),
            vm((NC, ROWS, 256), BF),
            vm((NR, 16, WIDTH), BF),
            vm((512, 2 * ROWS), BF),
            vm((512, 2 * ROWS), BF),
            DMA((NC,)),
            DMA((NC,)),
            DMA((2, 10)),
            DMA((2, 10)),
            DMA((STEPS,)),
            DMA((STEPS,)),
            DMA((4,)),
            DMA((4,)),
        ]
        + swap_sems("col")
        + swap_sems("row"),
        compiler_params=params(1, 63),
    )(target.reshape(1, ROWS), lens, tokens, grads, again, fgain, qgain, kgain, freq, *weights)


def gain_steps(at, pieces, room, total, ssem, rsem):
    p = at["x"]
    lane = 0
    for ref in pieces:
        room[0, p, :, lane : lane + ref.shape[1]] = ref[...]
        lane += ref.shape[1]
    for t, a in enumerate("xyzk"):
        p = at[a]
        others = (1, 2, 3) if a != "k" else (1,)
        if t > 0:
            room[t, p] = total[...]
        step = []
        for d in others:
            to = device(moved(at, a, d)) if a != "k" else device(mate(at))
            sems = ssem.at[t, d - 1], rsem.at[t, d - 1]
            cp = remote(room.at[t, p], room.at[t, p], *sems, to)
            cp.start()
            step.append(cp)
        yield
        for cp in step:
            cp.wait()
        acc = room[t, 0]
        for j in range(1, len(others) + 1):
            acc = acc + room[t, j]
        total[...] = acc


def back_kernel(
    lens, qkv, d_o, lse, slt, x, dh, again, qgain, kgain, cos, sin, gain_f, n1h, dhlh, dhl_m,
    o_t, raw, wq, wkv, oa, oa_m, p0, p1, p2,
    r0, r1, r2, t0, t1, t2, got, gsum,
    out_s, qs, dos, delta, dq, first, came, draw, w_v, raw_v, acc, dx_s, gain_a, gain_qk,
    n1_m, nt_s, ht_s, oa_v, o_v, a0, a1, a2, room,
    kv_ssem, kv_rsem, kv_lsem, q_ssem, q_rsem, q_lsem, w_sem, m_ssem, m_rsem, n_ssem, n_rsem, oa_sem, o_sem,
    g_ssem, g_rsem, *rest,
):
    at = where_am_i()
    row, col, k = lax.axis_index("row"), lax.axis_index("col"), at["k"]
    to = device(mate(at))
    row_sems, rest = rest[:3], rest[3:]
    a_sems, f_sems, rest = rest[:3], rest[3:6], rest[6:]
    na = len(scatter_buffers(ATTN))
    a_bufs, f_bufs = rest[:na], rest[na:]
    near = [device(moved(at, "z", 1)), device(moved(at, "z", -1))]
    peers = near + row_peers(at) + col_peers(at)
    greet(peers)

    scale = HEAD**-0.5

    def o_load(i):
        return pltpu.make_async_copy(o_t.at[i], o_v.at[i % 2], o_sem.at[i % 2])

    o_load(0).start()

    @pl.loop(0, NC)
    def _(i):
        @pl.when(i < NC - 1)
        def _():
            o_load(i + 1).start()

        qs[i] = stacked(qkv[i, :, 0 : 2 * HEAD])
        g = stacked(d_o[i])
        dos[i] = g
        o_load(i).wait()
        delta[i] = jnp.sum(g.astype(F32).T * o_v[i % 2], axis=0, keepdims=True)
        dq[i] = jnp.zeros((HEAD, QK), F32)
        first[i] = first_slots(lambda n: lens[0, n], group_slots(i))

    met(peers)
    ffn = run_scatter(at, (p0, p1, p2), (t0, t1, t2), f_bufs, f_sems)
    next(ffn)
    swap_n1 = remote(n1h.at[1 - k], n1_m, n_ssem, n_rsem, to)
    swap_n1.start()

    def block_at(n):
        return (col + 1 + n) % NC

    lanes_q, lanes_kv = pl.ds(0, 2 * HEAD), pl.ds(2 * HEAD, 2 * HEAD)
    every = (slice(None),)

    def sends(n, lanes, ssem, rsem):
        c = block_at(n)
        src, dst = out_s.at[(c,) + every + (lanes,)], came.at[(col,) + every + (lanes,)]
        return remote(src, dst, ssem.at[n], rsem.at[n], (row, c))

    def sends_kv(n):
        return sends(n, lanes_kv, kv_ssem, kv_rsem)

    def sends_q(n):
        return sends(n, lanes_q, q_ssem, q_rsem)

    def keys(n):
        j = block_at(n)
        key = qkv[j, :, 2 * HEAD : 3 * HEAD]
        value = qkv[j, :, 3 * HEAD :]
        key_t = key.astype(F32).T.astype(BF)

        def step(i, carry):
            dk, dv = carry
            s = dot(key, qs[i], NT) * (scale * LOG2E) - lse[i]
            p = jnp.where(allowed(i, j, first[i]), jnp.exp2(s), 0.0)
            ds = (p * (dot(value, dos[i], NT) - delta[i]) * scale).astype(BF)
            dv = dv + dot(p.astype(BF), dos[i])
            dk = dk + dot(ds, qs[i])
            dq[i] += dot(key_t, ds)
            return dk, dv

        zero = jnp.zeros((ROWS, HEAD), F32)
        dk, dv = lax.fori_loop(j, jnp.minimum(j + SPAN, NC), step, (zero, zero))
        out_s[j, :, 2 * HEAD : 3 * HEAD] = dk.astype(BF)
        out_s[j, :, 3 * HEAD :] = dv.astype(BF)

        @pl.when(n < NC - 1)
        def _():
            sends_kv(n).start()

        pl.when(complete(n))(lambda: queries(n))

    start = block_at(0)

    def complete(n):
        j = block_at(n)
        return (j < start) | (jnp.maximum(j - (SPAN - 1), 0) >= start)

    def queries(n):
        i = block_at(n)
        done = dq[i].T
        out_s[i, :, 0:HEAD] = done[:ROWS].astype(BF)
        out_s[i, :, HEAD : 2 * HEAD] = done[ROWS:].astype(BF)

        @pl.when(n < NC - 1)
        def _():
            sends_q(n).start()

    pl.loop(0, NC)(keys)

    @pl.loop(0, NC)
    def _(n):
        pl.when(jnp.logical_not(complete(n)))(lambda: queries(n))

    mine = []
    for lanes, sem in ((lanes_kv, kv_lsem), (lanes_q, q_lsem)):
        here = (col,) + every + (lanes,)
        mine.append(pltpu.make_async_copy(out_s.at[here], came.at[here], sem))
    for cp in mine:
        cp.start()

    def comes_from(n):
        return (col - 1 - n + NC) % NC

    def oa_loads(n):
        slot = n % 2
        return [
            pltpu.make_async_copy(src.at[n], oa_v.at[slot, pl.ds(ROWS * i, ROWS)], oa_sem.at[i, slot])
            for i, src in enumerate((oa, oa_m))
        ]

    def loads(n):
        c, slot = comes_from(n), n % 2
        return [
            pltpu.make_async_copy(wq.at[place(c)], w_v.at[slot, :, pl.ds(0, 256)], w_sem.at[0, slot]),
            pltpu.make_async_copy(
                wkv.at[place(c)], w_v.at[slot, :, pl.ds(256, 256)], w_sem.at[1, slot]
            ),
            pltpu.make_async_copy(raw.at[c], raw_v.at[slot], w_sem.at[2, slot]),
        ]

    for cp in oa_loads(0) + loads(0):
        cp.start(priority=1)
    stack_tokens(k, dhlh, dhl_m, ht_s)

    @pl.loop(0, NC)
    def _(n):
        @pl.when(n < NC - 1)
        def _():
            for cp in oa_loads(n + 1):
                cp.start(priority=1)

        for cp in oa_loads(n):
            cp.wait()
        a2[n % 4, n // 4] = dot(ht_s[...], oa_v[n % 2]).astype(BF).reshape(4, 2, 64, 256)

    swap_n1.wait()
    stack_tokens(k, n1h, n1_m, nt_s)
    acc[...] = jnp.zeros_like(acc)
    gain_qk[...] = jnp.zeros_like(gain_qk)
    next(ffn)

    def to_mate(n):
        c = comes_from(n)
        src, dst = draw.at[c, pl.ds(0, ROWS)], draw.at[c, pl.ds(ROWS, ROWS)]
        return remote(src, dst, m_ssem.at[n], m_rsem.at[n], to)

    def weights_of(n):
        c = comes_from(n)
        to_mate(n).wait()
        g = dot(nt_s[...], draw[c]).astype(BF)
        a0[c % 4, c // 4] = g[:, 0:256].reshape(4, 2, 64, 256)
        a1[c % 4, c // 4] = g[:, 256:].reshape(4, 2, 64, 256)

    @pl.loop(0, NC)
    def _(n):
        c, slot = comes_from(n), n % 2

        @pl.when(n < NC - 1)
        def _():
            for cp in loads(n + 1):
                cp.start(priority=1)
            sends_kv(n).wait_recv()
            sends_q(n).wait_recv()

        @pl.when(n == NC - 1)
        def _():
            for cp in mine:
                cp.wait()

        for cp in loads(n):
            cp.wait()
        for i, gain in enumerate((qgain, qgain, kgain)):
            cols = slice(i * HEAD, (i + 1) * HEAD)
            v = raw_v[slot, :, cols]
            r = mean_square_scale(v)
            xn = v * r
            dn = unrope(came[c, :, cols].astype(F32), cos[...], sin[...])
            lanes = slice(0, HEAD) if i < 2 else slice(HEAD, 2 * HEAD)
            gain_qk[:, lanes] += jnp.sum(dn * xn, axis=0, keepdims=True)
            e = dn * gain[...]
            e = r * (e - xn * jnp.mean(e * xn, axis=-1, keepdims=True))
            draw[c, 0:ROWS, cols] = e.astype(BF)
        draw[c, 0:ROWS, 3 * HEAD :] = came[c, :, 3 * HEAD :]
        to_mate(n).start()
        acc[...] += dot(draw[c, 0:ROWS, :], w_v[slot], NT)

        @pl.when(n > 0)
        def _():
            weights_of(n - 1)

    weights_of(NC - 1)
    attn = run_scatter(at, (a0, a1, a2), (r0, r1, r2), a_bufs, a_sems, True)
    next(attn)

    xv = x[...].astype(F32)
    inverse = mean_square_scale(xv)
    xn = xv * inverse
    e = acc[...]
    gain_a[...] = jnp.sum(e * xn, axis=0, keepdims=True)
    gains = gain_steps(at, (gain_a, gain_f, gain_qk), room, gsum, g_ssem, g_rsem)
    next(gains)
    e = e * again[...]
    dx = dh[...] + inverse * (e - xn * jnp.mean(e * xn, axis=-1, keepdims=True))
    take = onehot(slt[:, :1].astype(F32).astype(I32) == iota((ROWS, ROWS), 1))
    dx_s[...] = dot(take, dx.astype(BF)).astype(BF).reshape(dx_s.shape)
    back = swap_over("row", dx_s, got, *row_sems)
    in_turn(attn, gains, ffn)
    for n in range(NC - 1):
        sends_kv(n).wait_send()
        sends_q(n).wait_send()
    for cp in back:
        cp.wait()


def back(
    lens, qkv, d_o, o_t, lse, slt, x, dh, again, qgain, kgain, cos, sin, gain_f, n1h, dhlh, dhl_m,
    raw, wq, wkv, oa, oa_m, f_parts,
):
    vm = pltpu.VMEM
    total = 2 * WIDTH + 2 * HEAD
    return pl.pallas_call(
        back_kernel,
        name="back",
        out_shape=[sds((64, 256), F32)] * 3
        + [sds((64, w), F32) for w in FFN_GRADS]
        + [sds((NR, 16, WIDTH)), sds((1, total), F32)],
        in_specs=[pl.BlockSpec(memory_space=pltpu.SMEM)] + [VMEM] * 15 + [HBM] * 9,
        out_specs=[VMEM] * 6 + [HBM, VMEM],
        scratch_shapes=[
            vm((NC, ROWS, 512), BF),
            vm((NC, QK, HEAD), BF),
            vm((NC, QK, HEAD), BF),
            vm((NC, 1, QK), F32),
            vm((NC, HEAD, QK), F32),
            vm((NC, 1, QK), I32),
            vm((NC, ROWS, 512), BF),
            vm((NC, 2 * ROWS, 512), BF),
            vm((2, WIDTH, 512), BF),
            vm((2, ROWS, 384), F32),
            vm((ROWS, WIDTH), F32),
            vm((NR, 16, WIDTH), BF),
            vm((1, WIDTH), F32),
            vm((1, 2 * HEAD), F32),
            vm((ROWS, 512), BF),
            vm((512, 2 * ROWS), BF),
            vm((512, 2 * ROWS), BF),
            vm((2, 2 * ROWS, 256), BF),
            vm((2, HEAD, QK), F32),
        ]
        + [vm((4, 2, 4, 2, 64, 256), BF)] * 3
        + [vm((4, 4, 1, total), F32)]
        + swap_sems("col") * 2
        + [DMA((3, 2)), DMA((NC,)), DMA((NC,)), DMA, DMA, DMA((2, 2)), DMA((2,))]
        + [DMA((4, 3)), DMA((4, 3))]
        + swap_sems("row")
        + scatter_sems()
        + scatter_sems()
        + scatter_buffers(ATTN)
        + scatter_buffers(FFN_GRADS),
        compiler_params=params(6, 63),
    )(
        lens, qkv, d_o, lse, slt, x, dh, again, qgain, kgain, cos, sin, gain_f, n1h, dhlh,
        dhl_m, o_t, raw, as_slabs(wq), as_slabs(wkv), oa, oa_m, *f_parts,
    )


def arrive_kernel(
    t_row, out, dx, q, kv, o, g, u, d, gains,
    out_o, dx_o, ga, gf, gq, gk, q_o, k_o, v_o, o_o, g_o, u_o, d_o,
):
    _, spot = slots_sent(t_row[...])
    pick = onehot(spot == iota((ROWS, ROWS), 1))
    out_o[...] = dot(pick, out[...].reshape(ROWS, WIDTH)).astype(BF)
    dx_o[...] = dot(pick, dx[...].reshape(ROWS, WIDTH)).astype(BF)
    ga[...] = gains[:, 0:WIDTH]
    gf[...] = gains[:, WIDTH : 2 * WIDTH]
    gq[...] = gains[:, 2 * WIDTH : 2 * WIDTH + HEAD]
    gk[...] = gains[:, 2 * WIDTH + HEAD :]
    q_o[...] = q[...]
    k_o[...] = kv[:, :HEAD]
    v_o[...] = kv[:, HEAD:]
    o_o[...] = o[...]
    for i, at_lane, part, lane, n in pieces_of(FFN_GRADS):
        (g_o, u_o, d_o)[part][:, lane : lane + n] = (g, u, d)[i][:, at_lane : at_lane + n]


def arrive(target, *args):
    return pl.pallas_call(
        arrive_kernel,
        name="arrive",
        out_shape=[sds((ROWS, WIDTH))] * 2
        + [sds((1, n), F32) for n in (WIDTH, WIDTH, HEAD, HEAD)]
        + [
            sds(n, F32)
            for n in ((64, 256), (64, 128), (64, 128), (64, 256), (64, 384), (64, 384), (64, 384))
        ],
        in_specs=[VMEM] * 10,
        out_specs=[VMEM] * 13,
        compiler_params=params(),
    )(target.reshape(1, ROWS), *args)


def local(
    tokens, grad_out, target, lengths, attn_gain, ffn_gain, q_gain, k_gain,
    w_query, key_matrix, value_matrix, w_out, w_gate, w_up, w_down,
):
    again, fgain = attn_gain.reshape(1, WIDTH), ffn_gain.reshape(1, WIDTH)
    qgain, kgain = q_gain.reshape(1, HEAD), k_gain.reshape(1, HEAD)

    oa, raw, x, n1h, cos, sin, slt, qkv, o_t, lse, wq, wkv, _, dh, dhlh, gain_f, g_o, got_out, oa_m, dhl_m, *rest = front(
        target, lengths, tokens, grad_out, again, fgain, qgain, kgain,
        w_query, key_matrix, value_matrix, w_out.T, w_gate, w_up, w_down.T,
    )
    f_parts = rest[:3]
    r_q, r_kv, r_o, r_g, r_u, r_d, got_dx, gains = back(
        lengths, qkv, g_o, o_t, lse, slt, x, dh, again, qgain, kgain, cos, sin, gain_f, n1h, dhlh,
        dhl_m, raw, wq, wkv, oa, oa_m, f_parts,
    )
    output, input_grad, ga, gf, gq, gk, g_q, g_k, g_v, g_o, g_g, g_u, g_d = arrive(
        target, got_out, got_dx, r_q, r_kv, r_o, r_g, r_u, r_d, gains
    )
    return (
        output, input_grad, ga[0], gf[0], gq[0], gk[0], g_q, g_k, g_v, g_o.T, g_g, g_u, g_d.T,
    )


def solution(mesh):
    both = P(("row", "col"), None)
    by_row, by_col = P("row", "col"), P("col", "row")
    weights = (by_row, by_row, by_row, by_col, by_row, by_row, by_col)
    return jax.shard_map(
        local,
        mesh=mesh,
        in_specs=(both, both, P(("row", "col")), P("row", None), P(), P(), P(), P()) + weights,
        out_specs=(both, both, P(), P(), P(), P()) + weights,
        check_vma=False,
    )
```
